32 devices in a mesh: rhs: 2 (over x), row: 8 (over z, y), col: 2 (over core).
Axes of the slice: x: 2, y: 2, z: 4, core: 2. Of those that a mesh axis runs over, the one named last changes fastest.
Arguments:
- tiles: bfloat16 [2080, 128, 128], P(('row', 'col')), as said below
- tile_rows: int32 [2080], P(('row', 'col')), may hold values from 0 to 3, as said below
- tile_cols: int32 [2080], P(('row', 'col')), may hold values from 0 to 31
- tile_count: int32 [16], P(('row', 'col')), may hold values from 2 to 130, as said below
- signs: int32 [64, 4096], P('rhs', ('row', 'col')), parts along dimension 0, may hold values from -1 to 1, as said below
- vertex_weight: float32 [4096], P(('row', 'col')), as said below
- column_scale: float32 [64], P('rhs'), parts along dimension 0, may hold values from 0.3 to 3
Outputs:
- solution: float32 [64, 4096], P('rhs', ('row', 'col')), parts along dimension 0
- residual: float32 [64, 4096], P('rhs', ('row', 'col')), parts along dimension 0
The draws below stay inside these ranges and needn't reach their ends.
There are 2 independent parts, one for each index of `rhs`. The reference program is written for one: setup_inputs(seed, part) draws one part's arguments, and reference() takes and returns one part's arrays. A program takes and returns all parts, laid end to end along the dimension named above; an argument that names none is the same for every part. Nothing has to cross between parts.
Inputs may be any that keep to these rules, and one draw needn't show every extreme that they name: Live tiles pair up: a live slot holding block (i, j) has a live partner slot holding block (j, i) whose tile is its transpose, and a tile of a block (i, i) is symmetric. Every diagonal entry of A exceeds the sum of the magnitudes of the other entries of its row; off-diagonal entries are at most 0. Padded slots hold arbitrary finite values. A live slot of a device in row group r, col index c lies in block row r * 4 + tile_rows and in a block column b with (b // 2) % 2 == c. `tile_count`: live slots come first on each device; every device holds the diagonal tile of each block b of its row group with (b // 2) % 2 equal to its col index. `signs`: every entry is -1 or 1. `vertex_weight`: every weight lies between 0.2 and 3.
All inputs are finite; a program needn't handle non-finite values.
Results may differ from the reference program's by a relative error of at most 0.01.
The reference program's roundings to bfloat16 on the way count: a program that leaves them out, or rounds other values in their place, can miss the bound.
Values may be sent and summed in bfloat16 or wider, within the bound.
No kernel may reach another device: no remote copies, remote signals or barrier semaphores. Data moves between devices by JAX's collectives and lax.ppermute only.
A program may use at most 64 MiB of HBM per device.

```python
import math
import jax
import jax.numpy as jnp
from jax import lax

TILE = 128
SKETCH = 32
NEIGH = 64
ITERS = 3
BLOCKS_DEV = 2
GROUP_BLOCKS = 4
PART_DEVICES = 16
NBLOCKS = 32
VERTS = 4096
SLOTS = 130
SLOTS_ALL = 2080
N_ROW = 8
N_COL = 2


def tile_plan(key):
    key = jax.random.fold_in(key, 101)
    devices = N_ROW * N_COL
    group_blocks = N_COL * BLOCKS_DEV
    total_blocks = devices * BLOCKS_DEV
    cand_width = NEIGH + 1
    spread = jax.random.randint(jax.random.fold_in(key, 1), (NEIGH,), 0, total_blocks // 2)
    low_part = spread % BLOCKS_DEV
    high_part = spread // BLOCKS_DEV
    high_part = high_part.at[0].set(N_ROW // 2).at[1].set(1)
    parity = jnp.arange(NEIGH, dtype=jnp.int32) % 2
    xor_masks = high_part * group_blocks + parity * BLOCKS_DEV + low_part
    xor_masks = jnp.where(xor_masks == 0, group_blocks, xor_masks)
    hub_group = jax.random.randint(jax.random.fold_in(key, 2), (), 0, N_ROW)
    degree = jax.random.randint(jax.random.fold_in(key, 3), (total_blocks,), max(2, NEIGH // 8), NEIGH // 2 + 1)
    block_ids = jnp.arange(total_blocks, dtype=jnp.int32)
    degree = jnp.where(block_ids // group_blocks == hub_group, NEIGH, degree)
    partner = jnp.bitwise_xor(block_ids[:, None], xor_masks[None, :])
    present = jnp.arange(NEIGH, dtype=jnp.int32)[None, :] < jnp.maximum(degree[:, None], degree[partner])
    row_tiles = 1 + jnp.sum(present.astype(jnp.int32), axis=1)
    cand_cols = jnp.concatenate([block_ids[:, None], partner], axis=1)
    cand_live = jnp.concatenate([jnp.ones((total_blocks, 1), bool), present], axis=1)
    cand_diag = jnp.concatenate([jnp.ones((total_blocks, 1), bool), jnp.zeros((total_blocks, NEIGH), bool)], axis=1)
    cand_rows = jnp.broadcast_to(block_ids[:, None], (total_blocks, cand_width))
    cand_side = cand_cols // BLOCKS_DEV % N_COL
    pad_rows = jax.random.randint(jax.random.fold_in(key, 4), (N_ROW, N_COL, SLOTS), 0, group_blocks)
    pad_cols = jax.random.randint(jax.random.fold_in(key, 5), (N_ROW, N_COL, SLOTS), 0, total_blocks)
    usable_all = []
    rows_all = []
    cols_all = []
    diag_all = []
    for column in range(N_COL):
        usable = (cand_live & (cand_side == column)).reshape(N_ROW, group_blocks * cand_width)
        ranking = jnp.argsort(1 - usable.astype(jnp.int32), axis=1, stable=True)[:, :SLOTS]

        def gather_slots(values_in):
            return jnp.take_along_axis(values_in.reshape(N_ROW, group_blocks * cand_width), ranking, axis=1)
        usable_all.append(gather_slots(usable))
        rows_all.append(gather_slots(cand_rows))
        cols_all.append(gather_slots(cand_cols))
        diag_all.append(gather_slots(cand_diag))
    is_live = jnp.stack(usable_all, axis=1)
    group_ids = jnp.arange(N_ROW, dtype=jnp.int32)[:, None, None]
    global_rows = jnp.where(is_live, jnp.stack(rows_all, axis=1), group_ids * group_blocks + pad_rows)
    columns = jnp.where(is_live, jnp.stack(cols_all, axis=1), pad_cols)
    on_diag = is_live & jnp.stack(diag_all, axis=1)
    counts = jnp.sum(is_live.astype(jnp.int32), axis=2).reshape(devices)
    local_rows = global_rows % group_blocks
    return (local_rows.reshape(-1).astype(jnp.int32), global_rows.reshape(-1).astype(jnp.int32), columns.reshape(-1).astype(jnp.int32), counts.astype(jnp.int32), on_diag.reshape(-1), is_live.reshape(-1), row_tiles)


def draw_tile_rows(key, part):
    return tile_plan(key)[0]


def draw_tile_cols(key, part):
    return tile_plan(key)[2]


def draw_tile_count(key, part):
    return tile_plan(key)[3]


def draw_tiles(key, part):
    local_rows, global_rows, columns, counts, on_diag, is_live, row_tiles = tile_plan(key)
    key = jax.random.fold_in(key, 5)
    total_blocks = N_ROW * N_COL * BLOCKS_DEV
    perm_count = max(2, TILE // 8)
    step = 2.0 / (NEIGH * perm_count)
    weight_low = 16
    first_block = jnp.minimum(global_rows, columns)
    second_block = jnp.maximum(global_rows, columns)
    pair_ids = jnp.where(is_live, first_block * total_blocks + second_block, total_blocks * total_blocks + jnp.arange(SLOTS_ALL, dtype=jnp.int32))
    flips = global_rows > columns
    shift_key = jax.random.fold_in(key, 9)
    identity = jnp.eye(TILE, dtype=bool)
    row_index = jnp.broadcast_to(jnp.arange(TILE, dtype=jnp.int32)[None, :], (perm_count, TILE)).reshape(-1)

    def make_tile(inputs):
        pair_id, flip, diag_flag, block_row = inputs
        pair_key = jax.random.fold_in(key, pair_id)
        perm_keys = jax.random.split(jax.random.fold_in(pair_key, 1), perm_count)
        perms = jax.vmap(lambda single: jax.random.permutation(single, TILE))(perm_keys).astype(jnp.int32)
        levels = jax.random.randint(jax.random.fold_in(pair_key, 2), (perm_count, TILE), weight_low, 65)
        weights = levels.astype(jnp.float32) / 64.0
        raw = jnp.zeros((TILE, TILE), jnp.float32).at[row_index, perms.reshape(-1)].add(weights.reshape(-1))
        raw = jnp.where(flip, raw.T, raw)
        raw = jnp.where(diag_flag, 0.5 * (raw + raw.T), raw)
        shift = jnp.exp(jax.random.uniform(jax.random.fold_in(shift_key, block_row), (TILE,), jnp.float32, math.log(0.02), math.log(0.5)))
        diag_values = 2.0 * row_tiles[block_row].astype(jnp.float32) / NEIGH + shift
        values = jnp.where(diag_flag & identity, diag_values[:, None], -step * raw)
        return values.astype(jnp.bfloat16)
    return lax.map(make_tile, (pair_ids, flips, on_diag, global_rows))


def draw_signs(key, part):
    key = jax.random.fold_in(key, 11)
    draws = jax.random.randint(key, (SKETCH, VERTS), 0, 4)
    return jnp.where(draws == 0, -1, 1).astype(jnp.int32)


def draw_vertex_weight(key, part):
    key = jax.random.fold_in(key, 13)
    position = jnp.arange(VERTS, dtype=jnp.float32) / VERTS
    noise = jax.random.uniform(key, (VERTS,), jnp.float32, math.log(0.3), 0.0)
    return jnp.exp(math.log(3.0) * position + noise)


def setup_inputs(seed: int = 0, part: int = 0) -> dict:
    key_list = jax.random.split(jax.random.key(seed), 8)
    part_keys = jax.random.split(jax.random.fold_in(key_list[7], part), 8)
    tiles = draw_tiles(jax.random.fold_in(key_list[7], 71), part)
    tile_rows = draw_tile_rows(jax.random.fold_in(key_list[7], 71), part)
    tile_cols = draw_tile_cols(jax.random.fold_in(key_list[7], 71), part)
    tile_count = draw_tile_count(jax.random.fold_in(key_list[7], 71), part)
    signs = draw_signs(jax.random.fold_in(jax.random.fold_in(key_list[7], part), 71), part)
    vertex_weight = draw_vertex_weight(jax.random.fold_in(key_list[7], 71), part)
    column_scale = jnp.clip(jnp.exp(jax.random.uniform(part_keys[6], (SKETCH,), jnp.float32, math.log(0.3), math.log(3.0))), 0.3, 3.0)
    return {"tiles": tiles, "tile_rows": tile_rows, "tile_cols": tile_cols, "tile_count": tile_count, "signs": signs, "vertex_weight": vertex_weight, "column_scale": column_scale}


def gram_of(left, right):
    return jnp.dot(left.astype(jnp.float32), right.T.astype(jnp.float32), precision=lax.Precision.HIGHEST, preferred_element_type=jnp.float32)

def full_dot(left, right):
    return jnp.dot(left.astype(jnp.float32), right.astype(jnp.float32), precision=lax.Precision.HIGHEST, preferred_element_type=jnp.float32)

def solve_spd(matrix, target):
    symmetric = 0.5 * (matrix + matrix.T)
    factor = jnp.linalg.cholesky(symmetric)
    return jax.scipy.linalg.cho_solve((factor, True), target)

def apply_matrix(direction, tiles, tile_rows, tile_cols, tile_count):
    rounded = direction.astype(jnp.bfloat16).astype(jnp.float32)
    column_blocks = rounded.reshape(SKETCH, NBLOCKS, TILE)
    device_tiles = tiles.reshape(PART_DEVICES, SLOTS, TILE, TILE)
    device_rows = tile_rows.reshape(PART_DEVICES, SLOTS)
    device_cols = tile_cols.reshape(PART_DEVICES, SLOTS)
    device_ids = jnp.arange(PART_DEVICES, dtype=jnp.int32)
    slot_ids = jnp.arange(SLOTS, dtype=jnp.int32)

    def per_device(running, inputs):
        block_tiles, block_rows, block_cols, live_count, device_id = inputs
        picked = jnp.take(column_blocks, block_cols, axis=1)
        product = jnp.einsum('gab,sgb->sga', block_tiles.astype(jnp.float32), picked, precision=lax.Precision.HIGHEST)
        keep_mask = (slot_ids < live_count).astype(jnp.float32)
        product = product * keep_mask[None, :, None]
        target = device_id // N_COL * GROUP_BLOCKS + block_rows
        return (running.at[:, target, :].add(product), None)
    initial = jnp.zeros((SKETCH, NBLOCKS, TILE), jnp.float32)
    total, unused = lax.scan(per_device, initial, (device_tiles, device_rows, device_cols, tile_count, device_ids))
    return total.reshape(SKETCH, VERTS)

def reference(tiles, tile_rows, tile_cols, tile_count, signs, vertex_weight, column_scale):
    right_side = signs.astype(jnp.float32) * vertex_weight[None, :] * column_scale[:, None]
    solution = jnp.zeros_like(right_side)
    residual = right_side
    direction = right_side
    norm_now = gram_of(residual, residual)
    for iteration in range(ITERS):
        image = apply_matrix(direction, tiles, tile_rows, tile_cols, tile_count)
        curvature = gram_of(direction, image)
        alpha = solve_spd(curvature, norm_now)
        solution = solution + full_dot(alpha.T, direction)
        residual = residual - full_dot(alpha.T, image)
        if iteration + 1 < ITERS:
            norm_next = gram_of(residual, residual)
            beta = solve_spd(norm_now, norm_next)
            direction = residual + full_dot(beta.T, direction)
            norm_now = norm_next
    return (solution, residual)
```

```python
import functools

import jax
import jax.numpy as jnp
from jax import lax
from jax.experimental import pallas as pl
from jax.experimental.pallas import tpu as pltpu
from jax.sharding import PartitionSpec as P

ITERS = 3
LANES = 128
PIVOTS = 8
F32 = jnp.float32
BF16 = jnp.bfloat16
VMEM_BYTES = 60 * 1024 * 1024

VMEM = pl.BlockSpec(memory_space=pltpu.VMEM)
SMEM = pl.BlockSpec(memory_space=pltpu.SMEM)
ANY = pl.BlockSpec(memory_space=pl.ANY)
PARAMS = pltpu.CompilerParams(vmem_limit_bytes=VMEM_BYTES)


def mul(left, right):
    return jnp.dot(left, right, precision=lax.Precision.HIGHEST, preferred_element_type=F32)


def mul_t(left, right):
    return lax.dot_general(
        left,
        right,
        (((1,), (1,)), ((), ())),
        precision=lax.Precision.HIGHEST,
        preferred_element_type=F32,
    )


def widen(matrix):
    rows, columns = matrix.shape
    return jnp.concatenate([matrix, jnp.zeros((rows, LANES - columns), F32)], axis=1)


def solve_wide(matrix, target):
    size = matrix.shape[0]
    row_ids = lax.broadcasted_iota(jnp.int32, (size, LANES), 0)
    lane_ids = lax.broadcasted_iota(jnp.int32, (size, LANES), 1)
    work = jnp.where(lane_ids < size, matrix, pltpu.roll(target, size, 1))
    for base in range(0, size, PIVOTS):
        columns = [
            jnp.broadcast_to(work[:, base + i : base + i + 1], (size, LANES))
            for i in range(PIVOTS)
        ]
        for i in range(PIVOTS):
            pivot = base + i
            here = row_ids == pivot
            inverse = 1.0 / columns[i][pivot : pivot + 1, :]
            row = work[pivot : pivot + 1, :] * inverse
            work = jnp.where(here, row, work - columns[i] * row)
            for later in range(i + 1, PIVOTS):
                entry = columns[later][pivot : pivot + 1, :] * inverse
                columns[later] = jnp.where(here, entry, columns[later] - columns[i] * entry)
    return pltpu.roll(work, LANES - size, 1)


def dense_kernel(
    rows_dev, col_devices, row_devices,
    place_ref, count_ref, rows_ref, cols_ref, tiles_ref, out_ref, total,
):
    tile = tiles_ref.shape[1]
    blocks = rows_dev // tile
    row_place = place_ref[0]
    col_place = place_ref[1]
    col_blocks, row_blocks = total.shape[:2]

    def clear(index, carry):
        for b in range(row_blocks):
            total[index, b] = jnp.zeros((tile, tile), F32)
        return carry

    lax.fori_loop(0, col_blocks, clear, 0)

    def add(slot, carry):
        row = rows_ref[slot]
        column = cols_ref[slot]
        side = lax.rem(row // blocks + col_devices - col_place, col_devices)
        row_at = side * blocks + lax.rem(row, blocks)
        owner = column // (blocks * col_devices)
        step = lax.rem(row_place + row_devices - owner, row_devices)
        column_at = step * blocks + lax.rem(column, blocks)
        total[column_at, row_at] = total[column_at, row_at] + tiles_ref[slot].astype(F32)
        return carry

    lax.fori_loop(0, count_ref[0], add, 0)

    def split(index, carry):
        start = pl.multiple_of(index * tile, tile)
        for b in range(row_blocks):
            value = total[index, b].T
            high = value.astype(BF16)
            low = (value - high.astype(F32)).astype(BF16)
            out_ref[0, pl.ds(start, tile), pl.ds(b * tile, tile)] = high
            out_ref[1, pl.ds(start, tile), pl.ds(b * tile, tile)] = low
        return carry

    lax.fori_loop(0, col_blocks, split, 0)


def apply_dense(directions, matrix):
    width = directions[0].shape[1]
    total = None
    for k, direction in enumerate(directions):
        rounded = direction.astype(BF16)
        for part in range(2):
            term = jnp.dot(
                rounded,
                matrix[part, k * width : (k + 1) * width, :],
                preferred_element_type=F32,
            )
            total = term if total is None else total + term
    return total


def first_kernel(pieces, *refs):
    blocks = refs[: pieces + 1]
    dense_ref, out_ref, state_ref, matrix, sem = refs[pieces + 1 :]
    copy = pltpu.make_async_copy(dense_ref, matrix, sem)
    copy.start()
    values = [ref[...] for ref in blocks]
    for k, value in enumerate(values):
        state_ref[k] = value
    half = mul_t(values[0], values[0])
    for value in values[1:pieces]:
        half = half + mul_t(value, value)
    rows = 2 * values[0].shape[1]
    out_ref[:, rows:] = widen(half)
    copy.wait()
    out_ref[:, :rows] = apply_dense(values[:pieces], matrix)


def image_kernel(first, mine_ref, other_ref, direction_ref, residual_ref, *outs):
    out_ref, far_ref = outs[:2]
    last = direction_ref.shape[0] - 1
    width = direction_ref.shape[2]
    near = mine_ref[:, :width] + other_ref[:, width : 2 * width]
    far = mine_ref[:, width : 2 * width] + other_ref[:, :width]
    far_ref[...] = far
    out_ref[:, :width] = near
    if first:
        outs[2][...] = mine_ref[:, 2 * width :] + other_ref[:, 2 * width :]
    image = jnp.concatenate([near, far], axis=1)
    direction = jnp.concatenate([direction_ref[0], direction_ref[last]], axis=1)
    curvature = 0.5 * (mul_t(image, direction) + mul_t(direction, image))
    residual = jnp.concatenate([residual_ref[0], residual_ref[last]], axis=1)
    size = curvature.shape[0]
    grams = [
        curvature,
        mul_t(image, residual),
        mul_t(image, image),
        jnp.zeros((size, LANES - 3 * size), F32),
    ]
    out_ref[:, width:] = jnp.concatenate(grams, axis=1)


def inverse_kernel(norm_ref, out_ref):
    size = norm_ref.shape[0]
    norm = norm_ref[...]
    small = norm[:, :size]
    norm = widen(0.5 * (small + small.T))
    unit = lax.broadcasted_iota(jnp.int32, norm.shape, 0) == lax.broadcasted_iota(
        jnp.int32, norm.shape, 1
    )
    out_ref[...] = solve_wide(norm, jnp.where(unit, 1.0, 0.0))


def in_order(place_ref, parts, held):
    pieces = len(parts)
    for k, part in enumerate(parts):
        held[k] = part
    total = None
    for device in range(pieces):
        value = held[lax.rem(place_ref[0] + (pieces - device), pieces)]
        total = value if total is None else total + value
    return total


def step_kernel(pieces, with_solution, place_ref, *refs):
    images = refs[:pieces]
    refs = refs[pieces:]
    far_ref, direction_ref, residual_ref, norm_ref, inverse_ref, dense_ref = refs[:6]
    refs = refs[6:]
    if with_solution:
        solution_ref, refs = refs[0], refs[1:]
    out_ref, new_direction, new_residual, new_norm, new_solution, matrix, held, sem = refs
    copy = pltpu.make_async_copy(dense_ref, matrix, sem)
    copy.start()
    size, width = far_ref.shape
    grams = in_order(place_ref, [ref[:, width:] for ref in images], held)
    norm = norm_ref[...]
    alpha = solve_wide(grams, norm)[:, :size]
    alpha_t = alpha.T
    image_residual = pltpu.roll(grams, LANES - size, 1)[:, :size]
    image_image = pltpu.roll(grams, LANES - 2 * size, 1)[:, :size]
    cross = mul(alpha_t, image_residual)
    next_norm = norm[:, :size] - (cross + cross.T) + mul(alpha_t, mul(image_image, alpha))
    new_norm[...] = widen(next_norm)
    beta_t = mul(next_norm, inverse_ref[:, :size])
    step = mul(alpha_t, direction_ref[0])
    new_solution[...] = solution_ref[...] + step if with_solution else step
    directions = []
    for k in range(pieces + 1):
        image = images[k][:, :width] if k < pieces else far_ref[...]
        residual = residual_ref[k] - mul(alpha_t, image)
        direction = residual + mul(beta_t, direction_ref[k])
        new_residual[k] = residual
        new_direction[k] = direction
        directions.append(direction)
    copy.wait()
    out_ref[...] = apply_dense(directions[:pieces], matrix)


def last_image_kernel(mine_ref, other_ref, direction_ref, near_ref, gram_ref):
    last = direction_ref.shape[0] - 1
    width = direction_ref.shape[2]
    near = mine_ref[:, :width] + other_ref[:, width : 2 * width]
    far = mine_ref[:, width : 2 * width] + other_ref[:, :width]
    near_ref[...] = near
    image = jnp.concatenate([near, far], axis=1)
    direction = jnp.concatenate([direction_ref[0], direction_ref[last]], axis=1)
    gram_ref[...] = widen(0.5 * (mul_t(image, direction) + mul_t(direction, image)))


def last_kernel(pieces, place_ref, *refs):
    parts = refs[:pieces]
    image_ref, direction_ref, residual_ref, norm_ref, solution_ref = refs[pieces : pieces + 5]
    new_solution, new_residual, held = refs[pieces + 5 :]
    size = image_ref.shape[0]
    curvature = in_order(place_ref, [ref[...] for ref in parts], held)
    alpha_t = solve_wide(curvature, norm_ref[...])[:, :size].T
    new_solution[...] = solution_ref[...] + mul(alpha_t, direction_ref[0])
    new_residual[...] = residual_ref[0] - mul(alpha_t, image_ref[...])


def shape(*dims, dtype=F32):
    return jax.ShapeDtypeStruct(dims, dtype)


def per_device(tiles, tile_rows, tile_cols, tile_count, signs, vertex_weight, column_scale):
    sketch, rows_dev = signs.shape
    tile = tiles.shape[1]
    pieces = lax.axis_size("row")
    col_devices = lax.axis_size("col")
    group = col_devices * rows_dev
    depth = pieces * rows_dev
    place = jnp.stack([lax.axis_index("row"), lax.axis_index("col")]).astype(jnp.int32)

    def around(value):
        received = [
            lax.ppermute(value, "row", [(i, (i + k) % pieces) for i in range(pieces)])
            for k in range(1, pieces)
        ]
        return [value] + received

    def across(value):
        return lax.ppermute(
            value, "col", [(i, (i + 1) % col_devices) for i in range(col_devices)]
        )

    right_side = signs.astype(F32) * vertex_weight[None, :] * column_scale[:, None]
    blocks = around(right_side) + [across(right_side)]

    dense = pl.pallas_call(
        functools.partial(dense_kernel, rows_dev, col_devices, pieces),
        out_shape=shape(2, depth, group, dtype=BF16),
        in_specs=[SMEM, SMEM, SMEM, SMEM, VMEM],
        out_specs=VMEM,
        scratch_shapes=[pltpu.VMEM((depth // tile, group // tile, tile, tile), F32)],
        compiler_params=PARAMS,
        cost_estimate=pl.CostEstimate(
            flops=4 * tiles.size, bytes_accessed=4 * tiles.size, transcendentals=0
        ),
        name="dense",
    )(place, tile_count, tile_rows, tile_cols, tiles)

    matrix_scratch = [pltpu.VMEM((2, depth, group), BF16)]
    state = shape(pieces + 1, sketch, rows_dev)
    small = shape(sketch, LANES)
    piece = shape(sketch, rows_dev)

    partial_sum, direction = pl.pallas_call(
        functools.partial(first_kernel, pieces),
        out_shape=(shape(sketch, group + LANES), state),
        in_specs=[VMEM] * (pieces + 1) + [ANY],
        out_specs=(VMEM, VMEM),
        scratch_shapes=matrix_scratch + [pltpu.SemaphoreType.DMA],
        compiler_params=PARAMS,
        name="first",
    )(*blocks, dense)
    residual = direction
    norm = None
    solution = None
    for iteration in range(ITERS):
        other = across(partial_sum)
        if iteration == ITERS - 1:
            break
        outs = pl.pallas_call(
            functools.partial(image_kernel, iteration == 0),
            out_shape=(shape(sketch, rows_dev + LANES), piece) + ((small,) if iteration == 0 else ()),
            in_specs=[VMEM] * 4,
            out_specs=(VMEM,) * (3 if iteration == 0 else 2),
            compiler_params=PARAMS,
            name="image",
        )(partial_sum, other, direction, residual)
        image, far = outs[:2]
        if iteration == 0:
            norm = outs[2]
        images = around(image)
        inverse = pl.pallas_call(
            inverse_kernel,
            out_shape=small,
            in_specs=[VMEM],
            out_specs=VMEM,
            compiler_params=PARAMS,
            name="inverse",
        )(norm)
        given = (solution,) if iteration else ()
        partial_sum, direction, residual, norm, solution = pl.pallas_call(
            functools.partial(step_kernel, pieces, iteration > 0),
            out_shape=(shape(sketch, group), state, state, small, piece),
            in_specs=[SMEM] + [VMEM] * (pieces + 5) + [ANY] + [VMEM] * len(given),
            out_specs=(VMEM,) * 5,
            scratch_shapes=matrix_scratch
            + [pltpu.VMEM((pieces, sketch, LANES), F32), pltpu.SemaphoreType.DMA],
            compiler_params=PARAMS,
            name="step",
        )(place, *images, far, direction, residual, norm, inverse, dense, *given)
    image, gram = pl.pallas_call(
        last_image_kernel,
        out_shape=(piece, small),
        in_specs=[VMEM] * 3,
        out_specs=(VMEM, VMEM),
        compiler_params=PARAMS,
        name="last_image",
    )(partial_sum, other, direction)
    return pl.pallas_call(
        functools.partial(last_kernel, pieces),
        out_shape=(piece, piece),
        in_specs=[SMEM] + [VMEM] * (pieces + 5),
        out_specs=(VMEM, VMEM),
        scratch_shapes=[pltpu.VMEM((pieces, sketch, LANES), F32)],
        compiler_params=PARAMS,
        name="last",
    )(place, *around(gram), image, direction, residual, norm, solution)


def solution(mesh):
    return jax.shard_map(
        per_device,
        mesh=mesh,
        in_specs=(
            P(("row", "col"), None, None),
            P(("row", "col")),
            P(("row", "col")),
            P(("row", "col")),
            P("rhs", ("row", "col")),
            P(("row", "col")),
            P("rhs"),
        ),
        out_specs=(P("rhs", ("row", "col")), P("rhs", ("row", "col"))),
        check_vma=False,
    )
```

```python
import functools

import jax
import jax.numpy as jnp
from jax import lax
from jax.experimental import pallas as pl
from jax.experimental.pallas import tpu as pltpu
from jax.sharding import PartitionSpec as P

ITERS = 3
LANES = 128
PIVOTS = 8
F32 = jnp.float32
BF16 = jnp.bfloat16
SPARE_BYTES = 4 * 1024 * 1024

VMEM = pl.BlockSpec(memory_space=pltpu.VMEM)
SMEM = pl.BlockSpec(memory_space=pltpu.SMEM)


def params(*arrays):
    used = sum(a.size * jnp.dtype(a.dtype).itemsize for a in arrays)
    return pltpu.CompilerParams(vmem_limit_bytes=used + SPARE_BYTES)


def mul(left, right):
    return jnp.dot(left, right, precision=lax.Precision.HIGHEST, preferred_element_type=F32)


def mul_t(left, right):
    return lax.dot_general(
        left,
        right,
        (((1,), (1,)), ((), ())),
        precision=lax.Precision.HIGHEST,
        preferred_element_type=F32,
    )


def widen(matrix):
    rows, columns = matrix.shape
    return jnp.concatenate([matrix, jnp.zeros((rows, LANES - columns), F32)], axis=1)


def solve_wide(matrix, target):
    size = matrix.shape[0]
    row_ids = lax.broadcasted_iota(jnp.int32, (size, LANES), 0)
    lane_ids = lax.broadcasted_iota(jnp.int32, (size, LANES), 1)
    work = jnp.where(lane_ids < size, matrix, pltpu.roll(target, size, 1))
    for base in range(0, size, PIVOTS):
        columns = [
            jnp.broadcast_to(work[:, base + i : base + i + 1], (size, LANES))
            for i in range(PIVOTS)
        ]
        for i in range(PIVOTS):
            pivot = base + i
            here = row_ids == pivot
            inverse = 1.0 / columns[i][pivot : pivot + 1, :]
            row = work[pivot : pivot + 1, :] * inverse
            work = jnp.where(here, row, work - columns[i] * row)
            for later in range(i + 1, PIVOTS):
                entry = columns[later][pivot : pivot + 1, :] * inverse
                columns[later] = jnp.where(here, entry, columns[later] - columns[i] * entry)
    return pltpu.roll(work, LANES - size, 1)


def dense_kernel(
    rows_dev, col_devices, place_ref, count_ref, rows_ref, cols_ref, tiles_ref, out_ref, total
):
    tile = tiles_ref.shape[1]
    blocks = rows_dev // tile
    col_place = place_ref[1]
    col_blocks, row_blocks = total.shape[:2]

    def clear(index, carry):
        for b in range(row_blocks):
            total[index, b] = jnp.zeros((tile, tile), F32)
        return carry

    lax.fori_loop(0, col_blocks, clear, 0)

    def add(slot, carry):
        row = rows_ref[slot]
        column = cols_ref[slot]
        side = lax.rem(row // blocks + col_devices - col_place, col_devices)
        row_at = side * blocks + lax.rem(row, blocks)
        owner = column // (blocks * col_devices)
        column_at = owner * blocks + lax.rem(column, blocks)
        total[column_at, row_at] = total[column_at, row_at] + tiles_ref[slot].astype(F32)
        return carry

    lax.fori_loop(0, count_ref[0], add, 0)

    def split(index, carry):
        start = pl.multiple_of(index * tile, tile)
        for b in range(row_blocks):
            value = total[index, b].T
            high = value.astype(BF16)
            low = (value - high.astype(F32)).astype(BF16)
            out_ref[0, pl.ds(start, tile), pl.ds(b * tile, tile)] = high
            out_ref[1, pl.ds(start, tile), pl.ds(b * tile, tile)] = low
        return carry

    lax.fori_loop(0, col_blocks, split, 0)


def apply_dense(directions, matrix):
    width = directions[0].shape[1]
    total = None
    for k, direction in enumerate(directions):
        rounded = direction.astype(BF16)
        for part in range(2):
            term = jnp.dot(
                rounded,
                matrix[part, k * width : (k + 1) * width, :],
                preferred_element_type=F32,
            )
            total = term if total is None else total + term
    return total


def first_kernel(pieces, blocks_ref, far_ref, matrix, out_ref, state_ref):
    values = [blocks_ref[k] for k in range(pieces)] + [far_ref[...]]
    for k, value in enumerate(values):
        state_ref[k] = value
    half = mul_t(values[0], values[0])
    for value in values[1:pieces]:
        half = half + mul_t(value, value)
    rows = 2 * values[0].shape[1]
    out_ref[:, rows:] = widen(half)
    out_ref[:, :rows] = apply_dense(values[:pieces], matrix)


def image_kernel(first, place_ref, mine_ref, other_ref, direction_ref, residual_ref, *outs):
    out_ref, far_ref = outs[:2]
    here = place_ref[0]
    last = direction_ref.shape[0] - 1
    width = direction_ref.shape[2]
    near = mine_ref[:, :width] + other_ref[:, width : 2 * width]
    far = mine_ref[:, width : 2 * width] + other_ref[:, :width]
    far_ref[...] = far
    if first:
        outs[2][...] = mine_ref[:, 2 * width :] + other_ref[:, 2 * width :]
    image = jnp.concatenate([near, far], axis=1)
    direction = jnp.concatenate([direction_ref[here], direction_ref[last]], axis=1)
    curvature = 0.5 * (mul_t(image, direction) + mul_t(direction, image))
    residual = jnp.concatenate([residual_ref[here], residual_ref[last]], axis=1)
    size = curvature.shape[0]
    grams = [
        curvature,
        mul_t(image, residual),
        mul_t(image, image),
        jnp.zeros((size, LANES - 3 * size), F32),
    ]
    payload = jnp.concatenate([near] + grams, axis=1)
    for k in range(out_ref.shape[0]):
        out_ref[k] = payload


def inverse_kernel(norm_ref, out_ref):
    size = norm_ref.shape[0]
    norm = norm_ref[...]
    small = norm[:, :size]
    norm = widen(0.5 * (small + small.T))
    unit = lax.broadcasted_iota(jnp.int32, norm.shape, 0) == lax.broadcasted_iota(
        jnp.int32, norm.shape, 1
    )
    out_ref[...] = solve_wide(norm, jnp.where(unit, 1.0, 0.0))


def add_up(values):
    total = values[0]
    for value in values[1:]:
        total = total + value
    return total


def step_kernel(pieces, with_solution, place_ref, *refs):
    images_ref, far_ref, direction_ref, residual_ref, norm_ref, inverse_ref, matrix = refs[:7]
    refs = refs[7:]
    if with_solution:
        solution_ref, refs = refs[0], refs[1:]
    out_ref, new_direction, new_residual, new_norm, new_solution = refs
    size, width = far_ref.shape
    grams = add_up([images_ref[k, :, width:] for k in range(pieces)])
    norm = norm_ref[...]
    alpha = solve_wide(grams, norm)[:, :size]
    alpha_t = alpha.T
    image_residual = pltpu.roll(grams, LANES - size, 1)[:, :size]
    image_image = pltpu.roll(grams, LANES - 2 * size, 1)[:, :size]
    cross = mul(alpha_t, image_residual)
    next_norm = norm[:, :size] - (cross + cross.T) + mul(alpha_t, mul(image_image, alpha))
    new_norm[...] = widen(next_norm)
    beta_t = mul(next_norm, inverse_ref[:, :size])
    step = mul(alpha_t, direction_ref[place_ref[0]])
    new_solution[...] = solution_ref[...] + step if with_solution else step
    directions = []
    for k in range(pieces + 1):
        image = images_ref[k, :, :width] if k < pieces else far_ref[...]
        residual = residual_ref[k] - mul(alpha_t, image)
        direction = residual + mul(beta_t, direction_ref[k])
        new_residual[k] = residual
        new_direction[k] = direction
        directions.append(direction)
    out_ref[...] = apply_dense(directions[:pieces], matrix)


def last_image_kernel(place_ref, mine_ref, other_ref, direction_ref, near_ref, gram_ref):
    here = place_ref[0]
    last = direction_ref.shape[0] - 1
    width = direction_ref.shape[2]
    near = mine_ref[:, :width] + other_ref[:, width : 2 * width]
    far = mine_ref[:, width : 2 * width] + other_ref[:, :width]
    near_ref[...] = near
    image = jnp.concatenate([near, far], axis=1)
    direction = jnp.concatenate([direction_ref[here], direction_ref[last]], axis=1)
    gram = widen(0.5 * (mul_t(image, direction) + mul_t(direction, image)))
    for k in range(gram_ref.shape[0]):
        gram_ref[k] = gram


def last_kernel(
    pieces, place_ref, grams_ref, image_ref, direction_ref, residual_ref, norm_ref, solution_ref,
    new_solution, new_residual,
):
    here = place_ref[0]
    size = image_ref.shape[0]
    curvature = add_up([grams_ref[k] for k in range(pieces)])
    alpha_t = solve_wide(curvature, norm_ref[...])[:, :size].T
    new_solution[...] = solution_ref[...] + mul(alpha_t, direction_ref[here])
    new_residual[...] = residual_ref[here] - mul(alpha_t, image_ref[...])


def shape(*dims, dtype=F32):
    return jax.ShapeDtypeStruct(dims, dtype)


def per_device(tiles, tile_rows, tile_cols, tile_count, signs, vertex_weight, column_scale):
    sketch, rows_dev = signs.shape
    tile = tiles.shape[1]
    pieces = lax.axis_size("row")
    col_devices = lax.axis_size("col")
    group = col_devices * rows_dev
    depth = pieces * rows_dev
    place = jnp.stack([lax.axis_index("row"), lax.axis_index("col")]).astype(jnp.int32)

    def around(values):
        return lax.all_to_all(values, "row", 0, 0)

    def across(value):
        return lax.ppermute(
            value, "col", [(i, (i + 1) % col_devices) for i in range(col_devices)]
        )

    right_side = signs.astype(F32) * vertex_weight[None, :] * column_scale[:, None]
    far_side = across(right_side)
    blocks = around(jnp.broadcast_to(right_side[None], (pieces, sketch, rows_dev)))

    matrix = shape(2, depth, group, dtype=BF16)
    dense = pl.pallas_call(
        functools.partial(dense_kernel, rows_dev, col_devices),
        out_shape=matrix,
        in_specs=[SMEM, SMEM, SMEM, SMEM, VMEM],
        out_specs=VMEM,
        scratch_shapes=[pltpu.VMEM((depth // tile, group // tile, tile, tile), F32)],
        compiler_params=params(tiles, matrix, matrix),
        cost_estimate=pl.CostEstimate(
            flops=4 * tiles.size, bytes_accessed=4 * tiles.size, transcendentals=0
        ),
        name="dense",
    )(place, tile_count, tile_rows, tile_cols, tiles)

    state = shape(pieces + 1, sketch, rows_dev)
    small = shape(sketch, LANES)
    piece = shape(sketch, rows_dev)
    payload = shape(pieces, sketch, rows_dev + LANES)

    partial_sum, direction = pl.pallas_call(
        functools.partial(first_kernel, pieces),
        out_shape=(shape(sketch, group + LANES), state),
        in_specs=[VMEM] * 3,
        out_specs=(VMEM, VMEM),
        compiler_params=params(matrix, state, state),
        name="first",
    )(blocks, far_side, dense)
    residual = direction
    norm = None
    solution = None
    for iteration in range(ITERS - 1):
        first = iteration == 0
        outs = pl.pallas_call(
            functools.partial(image_kernel, first),
            out_shape=(payload, piece) + ((small,) if first else ()),
            in_specs=[SMEM] + [VMEM] * 4,
            out_specs=(VMEM,) * (3 if first else 2),
            compiler_params=params(payload, state, state),
            name="image",
        )(place, partial_sum, across(partial_sum), direction, residual)
        payloads, far = outs[:2]
        if first:
            norm = outs[2]
        inverse = pl.pallas_call(
            inverse_kernel,
            out_shape=small,
            in_specs=[VMEM],
            out_specs=VMEM,
            compiler_params=params(),
            name="inverse",
        )(norm)
        given = () if first else (solution,)
        partial_sum, direction, residual, norm, solution = pl.pallas_call(
            functools.partial(step_kernel, pieces, not first),
            out_shape=(shape(sketch, group), state, state, small, piece),
            in_specs=[SMEM] + [VMEM] * (7 + len(given)),
            out_specs=(VMEM,) * 5,
            compiler_params=params(payload, matrix, state, state, state, state),
            name="step",
        )(place, around(payloads), far, direction, residual, norm, inverse, dense, *given)
    image, grams = pl.pallas_call(
        last_image_kernel,
        out_shape=(piece, shape(pieces, sketch, LANES)),
        in_specs=[SMEM] + [VMEM] * 3,
        out_specs=(VMEM, VMEM),
        compiler_params=params(state),
        name="last_image",
    )(place, partial_sum, across(partial_sum), direction)
    return pl.pallas_call(
        functools.partial(last_kernel, pieces),
        out_shape=(piece, piece),
        in_specs=[SMEM] + [VMEM] * 6,
        out_specs=(VMEM, VMEM),
        compiler_params=params(payload, state, state),
        name="last",
    )(place, around(grams), image, direction, residual, norm, solution)


def solution(mesh):
    return jax.shard_map(
        per_device,
        mesh=mesh,
        in_specs=(
            P(("row", "col"), None, None),
            P(("row", "col")),
            P(("row", "col")),
            P(("row", "col")),
            P("rhs", ("row", "col")),
            P(("row", "col")),
            P("rhs"),
        ),
        out_specs=(P("rhs", ("row", "col")), P("rhs", ("row", "col"))),
        check_vma=False,
    )
```

```python
import functools

import jax
import jax.numpy as jnp
from jax import lax
from jax.experimental import pallas as pl
from jax.experimental.pallas import tpu as pltpu
from jax.sharding import PartitionSpec as P

ITERS = 3
LANES = 128
PIVOTS = 8
CHUNKS = 5
F32 = jnp.float32
BF16 = jnp.bfloat16
SPARE_BYTES = 4 * 1024 * 1024

VMEM = pl.BlockSpec(memory_space=pltpu.VMEM)
SMEM = pl.BlockSpec(memory_space=pltpu.SMEM)
HBM = pl.BlockSpec(memory_space=pltpu.HBM)


def params(*arrays):
    used = sum(a.size * jnp.dtype(a.dtype).itemsize for a in arrays)
    return pltpu.CompilerParams(vmem_limit_bytes=used + SPARE_BYTES)


def split(value):
    high = value.astype(BF16)
    rest = value - high.astype(F32)
    middle = rest.astype(BF16)
    low = (rest - middle.astype(F32)).astype(BF16)
    return high, middle, low


def mul(left, right):
    return jnp.dot(left, right, precision=lax.Precision.HIGHEST, preferred_element_type=F32)


def factor(left):
    high, middle, low = split(left)
    return jnp.concatenate([high, high, middle, high, middle, low], axis=1)


def times(prepared, right):
    high, middle, low = split(right)
    stacked = jnp.concatenate([high, middle, high, low, middle, high], axis=0)
    return jnp.dot(prepared, stacked, preferred_element_type=F32)


def grams(left, rights):
    size = left.shape[0]
    parts = [split(right) for right in rights]
    parts = parts + [parts[0]] * (LANES // size - len(parts))
    stacked = jnp.concatenate([part[i] for i in range(3) for part in parts], axis=0)
    every = lax.dot_general(
        jnp.concatenate(split(left), axis=0),
        stacked,
        (((1,), (1,)), ((), ())),
        preferred_element_type=F32,
    )
    rows = every[2 * size :] + every[size : 2 * size] + every[:size]
    return rows[:, 2 * LANES :] + rows[:, LANES : 2 * LANES] + rows[:, :LANES]


def widen(matrix):
    rows, columns = matrix.shape
    return jnp.concatenate([matrix, jnp.zeros((rows, LANES - columns), F32)], axis=1)


def symmetric(matrix):
    return 0.5 * (matrix + matrix.T)


def solve_wide(matrix, target):
    size = matrix.shape[0]
    row_ids = lax.broadcasted_iota(jnp.int32, (size, LANES), 0)
    lane_ids = lax.broadcasted_iota(jnp.int32, (size, LANES), 1)
    work = jnp.where(lane_ids < size, matrix, pltpu.roll(target, size, 1))
    for base in range(0, size, PIVOTS):
        columns = [
            jnp.broadcast_to(work[:, base + i : base + i + 1], (size, LANES))
            for i in range(PIVOTS)
        ]
        for i in range(PIVOTS):
            pivot = base + i
            here = row_ids == pivot
            inverse = 1.0 / columns[i][pivot : pivot + 1, :]
            row = work[pivot : pivot + 1, :] * inverse
            work = jnp.where(here, row, work - columns[i] * row)
            for later in range(i + 1, PIVOTS):
                entry = columns[later][pivot : pivot + 1, :] * inverse
                columns[later] = jnp.where(here, entry, columns[later] - columns[i] * entry)
    return pltpu.roll(work, LANES - size, 1)


def add_up(values):
    values = list(values)
    while len(values) > 1:
        pairs = [values[i] + values[i + 1] for i in range(0, len(values) - 1, 2)]
        values = pairs + values[len(values) - len(values) % 2 :]
    return values[0]


def dense_kernel(rows_dev, col_devices, lists_ref, tiles_ref, out_ref, held, total, sems):
    slots, tile = tiles_ref.shape[:2]
    blocks = rows_dev // tile
    live = lists_ref[2 * slots]
    row_place = lists_ref[2 * slots + 1]
    col_place = lists_ref[2 * slots + 2]
    col_blocks, row_blocks = total.shape[:2]
    chunk = -(-slots // CHUNKS)
    copies = []
    for c in range(CHUNKS):
        part = pl.ds(c * chunk, min(chunk, slots - c * chunk))
        copies.append(pltpu.make_async_copy(tiles_ref.at[part], held.at[part], sems.at[c]))
        copies[c].start()

    def clear(index, carry):
        for b in range(row_blocks):
            total[index, b] = jnp.zeros((tile, tile), F32)
        return carry

    lax.fori_loop(0, col_blocks, clear, 0)

    def add(slot, carry):
        row = lists_ref[slot]
        column = lists_ref[slots + slot]
        side = lax.rem(row // blocks + col_devices - col_place, col_devices)
        row_at = side * blocks + lax.rem(row, blocks)
        owner = column // (blocks * col_devices)
        column_at = (owner ^ row_place) * blocks + lax.rem(column, blocks)
        total[column_at, row_at] = total[column_at, row_at] + held[slot].astype(F32)
        return carry

    for c in range(CHUNKS):
        copies[c].wait()
        lax.fori_loop(c * chunk, jnp.minimum(live, min((c + 1) * chunk, slots)), add, 0)

    def part(index, carry):
        start = pl.multiple_of(index * tile, tile)
        for b in range(row_blocks):
            value = total[index, b].T
            high = value.astype(BF16)
            low = (value - high.astype(F32)).astype(BF16)
            out_ref[0, pl.ds(start, tile), pl.ds(b * tile, tile)] = high
            out_ref[1, pl.ds(start, tile), pl.ds(b * tile, tile)] = low
        return carry

    lax.fori_loop(0, col_blocks, part, 0)


def apply_dense(directions, matrix):
    width = directions[0].shape[1]
    total = None
    for k, direction in enumerate(directions):
        rounded = direction.astype(BF16)
        for part in range(2):
            term = jnp.dot(
                rounded,
                matrix[part, k * width : (k + 1) * width, :],
                preferred_element_type=F32,
            )
            total = term if total is None else total + term
    return total


def first_kernel(pieces, *refs):
    values = [ref[...] for ref in refs[: pieces + 1]]
    matrix, out_ref, state_ref = refs[pieces + 1 :]
    for k, value in enumerate(values):
        state_ref[k] = value
    rows = 2 * values[0].shape[1]
    out_ref[:, rows:] = add_up([grams(value, [value]) for value in values[:pieces]])
    out_ref[:, :rows] = apply_dense(values[:pieces], matrix)


def add_halves(mine_ref, other_ref, width):
    near = mine_ref[:, :width] + other_ref[:, width : 2 * width]
    far = mine_ref[:, width : 2 * width] + other_ref[:, :width]
    return near, far


def image_kernel(first, mine_ref, other_ref, direction_ref, residual_ref, *outs):
    out_ref, far_ref = outs[:2]
    last = direction_ref.shape[0] - 1
    size, width = direction_ref.shape[1:]
    near, far = add_halves(mine_ref, other_ref, width)
    far_ref[...] = far
    if first:
        outs[2][...] = mine_ref[:, 2 * width :] + other_ref[:, 2 * width :]
    for i in range(width // LANES):
        out_ref[i * size : (i + 1) * size] = near[:, i * LANES : (i + 1) * LANES]
    near_part = grams(near, [direction_ref[0], residual_ref[0], near])
    far_part = grams(far, [direction_ref[last], residual_ref[last], far])
    out_ref[width // LANES * size :] = near_part + far_part


def inverse_kernel(norm_ref, out_ref):
    norm = widen(symmetric(norm_ref[:, : norm_ref.shape[0]]))
    unit = lax.broadcasted_iota(jnp.int32, norm.shape, 0) == lax.broadcasted_iota(
        jnp.int32, norm.shape, 1
    )
    out_ref[...] = solve_wide(norm, jnp.where(unit, 1.0, 0.0))


def step_kernel(pieces, with_solution, *refs):
    images = refs[:pieces]
    far_ref, direction_ref, residual_ref, norm_ref, inverse_ref, matrix = refs[pieces : pieces + 6]
    refs = refs[pieces + 6 :]
    if with_solution:
        solution_ref, refs = refs[0], refs[1:]
    out_ref, new_direction, new_residual, new_norm, new_solution = refs
    size, width = far_ref.shape
    parts = width // LANES
    products = add_up([ref[parts * size :] for ref in images])
    norm = norm_ref[...]
    alpha = solve_wide(widen(symmetric(products[:, :size])), norm)[:, :size]
    alpha_t = alpha.T
    image_residual = pltpu.roll(products, LANES - size, 1)[:, :size]
    image_image = pltpu.roll(products, LANES - 2 * size, 1)[:, :size]
    cross = mul(alpha_t, image_residual)
    next_norm = norm[:, :size] - (cross + cross.T) + mul(alpha_t, mul(image_image, alpha))
    new_norm[...] = widen(next_norm)
    beta_t = factor(mul(next_norm, inverse_ref[:, :size]))
    alpha_t = factor(alpha_t)
    step = times(alpha_t, direction_ref[0])
    new_solution[...] = solution_ref[...] + step if with_solution else step
    directions = []
    for k in range(pieces + 1):
        if k < pieces:
            image = jnp.concatenate(
                [images[k][i * size : (i + 1) * size] for i in range(parts)], axis=1
            )
        else:
            image = far_ref[...]
        residual = residual_ref[k] - times(alpha_t, image)
        direction = residual + times(beta_t, direction_ref[k])
        new_residual[k] = residual
        new_direction[k] = direction
        directions.append(direction)
    out_ref[...] = apply_dense(directions[:pieces], matrix)


def last_image_kernel(mine_ref, other_ref, direction_ref, near_ref, gram_ref):
    last = direction_ref.shape[0] - 1
    near, far = add_halves(mine_ref, other_ref, direction_ref.shape[2])
    near_ref[...] = near
    gram_ref[...] = grams(near, [direction_ref[0]]) + grams(far, [direction_ref[last]])


def last_kernel(pieces, *refs):
    image_ref, direction_ref, residual_ref, norm_ref, solution_ref = refs[pieces : pieces + 5]
    new_solution, new_residual = refs[pieces + 5 :]
    size = image_ref.shape[0]
    curvature = add_up([ref[:, :size] for ref in refs[:pieces]])
    alpha_t = factor(solve_wide(widen(symmetric(curvature)), norm_ref[...])[:, :size].T)
    new_solution[...] = solution_ref[...] + times(alpha_t, direction_ref[0])
    new_residual[...] = residual_ref[0] - times(alpha_t, image_ref[...])


def shape(*dims, dtype=F32):
    return jax.ShapeDtypeStruct(dims, dtype)


def per_device(tiles, tile_rows, tile_cols, tile_count, signs, vertex_weight, column_scale):
    sketch, rows_dev = signs.shape
    tile = tiles.shape[1]
    pieces = lax.axis_size("row")
    col_devices = lax.axis_size("col")
    group = col_devices * rows_dev
    depth = pieces * rows_dev

    def swap(value, mask):
        return lax.ppermute(value, "row", [(i, i ^ mask) for i in range(pieces)])

    def around(value, forward=True):
        if not forward:
            return [value] + [swap(value, k) for k in range(1, pieces)]
        even = [value] + [swap(value, k) for k in range(2, pieces, 2)]
        odd = [swap(piece, 1) for piece in even]
        return [piece for pair in zip(even, odd) for piece in pair]

    def across(value):
        return lax.ppermute(
            value, "col", [(i, (i + 1) % col_devices) for i in range(col_devices)]
        )

    right_side = signs.astype(F32) * vertex_weight[None, :] * column_scale[:, None]
    blocks = around(right_side, forward=False) + [across(right_side)]

    matrix = shape(2, depth, group, dtype=BF16)
    total = shape(depth // tile, group // tile, tile, tile)
    place = jnp.stack([lax.axis_index("row"), lax.axis_index("col")]).astype(jnp.int32)
    lists = jnp.concatenate([tile_rows, tile_cols, tile_count, place])
    dense = pl.pallas_call(
        functools.partial(dense_kernel, rows_dev, col_devices),
        out_shape=matrix,
        in_specs=[SMEM, HBM],
        out_specs=VMEM,
        scratch_shapes=[
            pltpu.VMEM(tiles.shape, BF16),
            pltpu.VMEM(total.shape, F32),
            pltpu.SemaphoreType.DMA((CHUNKS,)),
        ],
        compiler_params=params(tiles, total, matrix),
        cost_estimate=pl.CostEstimate(
            flops=4 * tiles.size, bytes_accessed=4 * tiles.size, transcendentals=0
        ),
        name="dense",
    )(lists, pltpu.with_memory_space_constraint(tiles, pltpu.HBM))

    state = shape(pieces + 1, sketch, rows_dev)
    small = shape(sketch, LANES)
    piece = shape(sketch, rows_dev)
    payload = shape(sketch * (rows_dev // LANES + 1), LANES)

    partial_sum, direction = pl.pallas_call(
        functools.partial(first_kernel, pieces),
        out_shape=(shape(sketch, group + LANES), state),
        in_specs=[VMEM] * (pieces + 2),
        out_specs=(VMEM, VMEM),
        compiler_params=params(matrix, state, state),
        name="first",
    )(*blocks, dense)
    residual = direction
    norm = None
    solution = None
    for iteration in range(ITERS - 1):
        first = iteration == 0
        outs = pl.pallas_call(
            functools.partial(image_kernel, first),
            out_shape=(payload, piece) + ((small,) if first else ()),
            in_specs=[VMEM] * 4,
            out_specs=(VMEM,) * (3 if first else 2),
            compiler_params=params(state, state),
            name="image",
        )(partial_sum, across(partial_sum), direction, residual)
        image, far = outs[:2]
        if first:
            norm = outs[2]
        inverse = pl.pallas_call(
            inverse_kernel,
            out_shape=small,
            in_specs=[VMEM],
            out_specs=VMEM,
            compiler_params=params(),
            name="inverse",
        )(norm)
        given = () if first else (solution,)
        partial_sum, direction, residual, norm, solution = pl.pallas_call(
            functools.partial(step_kernel, pieces, not first),
            out_shape=(shape(sketch, group), state, state, small, piece),
            in_specs=[VMEM] * (pieces + 6 + len(given)),
            out_specs=(VMEM,) * 5,
            compiler_params=params(matrix, state, state, state, state, state),
            name="step",
        )(*around(image), far, direction, residual, norm, inverse, dense, *given)
    image, gram = pl.pallas_call(
        last_image_kernel,
        out_shape=(piece, small),
        in_specs=[VMEM] * 3,
        out_specs=(VMEM, VMEM),
        compiler_params=params(state),
        name="last_image",
    )(partial_sum, across(partial_sum), direction)
    return pl.pallas_call(
        functools.partial(last_kernel, pieces),
        out_shape=(piece, piece),
        in_specs=[VMEM] * (pieces + 5),
        out_specs=(VMEM, VMEM),
        compiler_params=params(state, state, state),
        name="last",
    )(*around(gram), image, direction, residual, norm, solution)


def solution(mesh):
    return jax.shard_map(
        per_device,
        mesh=mesh,
        in_specs=(
            P(("row", "col"), None, None),
            P(("row", "col")),
            P(("row", "col")),
            P(("row", "col")),
            P("rhs", ("row", "col")),
            P(("row", "col")),
            P("rhs"),
        ),
        out_specs=(P("rhs", ("row", "col")), P("rhs", ("row", "col"))),
        check_vma=False,
    )
```

```python
import functools

import jax
import jax.numpy as jnp
from jax import lax
from jax.experimental import pallas as pl
from jax.experimental.pallas import tpu as pltpu
from jax.sharding import PartitionSpec as P

ITERS = 3
LANES = 128
PIVOTS = 8
CHUNKS = 5
F32 = jnp.float32
BF16 = jnp.bfloat16
SPARE_BYTES = 4 * 1024 * 1024

VMEM = pl.BlockSpec(memory_space=pltpu.VMEM)
SMEM = pl.BlockSpec(memory_space=pltpu.SMEM)
HBM = pl.BlockSpec(memory_space=pltpu.HBM)
ANY = pl.BlockSpec(memory_space=pl.ANY)


def params(*arrays):
    used = sum(a.size * jnp.dtype(a.dtype).itemsize for a in arrays)
    return pltpu.CompilerParams(vmem_limit_bytes=used + SPARE_BYTES)


def split(value):
    high = value.astype(BF16)
    rest = value - high.astype(F32)
    middle = rest.astype(BF16)
    low = (rest - middle.astype(F32)).astype(BF16)
    return high, middle, low


def mul(left, right):
    return jnp.dot(left, right, precision=lax.Precision.HIGHEST, preferred_element_type=F32)


def factor(left):
    high, middle, low = split(left)
    return jnp.concatenate([high, high, middle, high, middle, low], axis=1)


def times(prepared, right):
    high, middle, low = split(right)
    stacked = jnp.concatenate([high, middle, high, low, middle, high], axis=0)
    return jnp.dot(prepared, stacked, preferred_element_type=F32)


def grams(left, rights):
    size = left.shape[0]
    parts = [split(right) for right in rights]
    parts = parts + [parts[0]] * (LANES // size - len(parts))
    stacked = jnp.concatenate([part[i] for i in range(3) for part in parts], axis=0)
    every = lax.dot_general(
        jnp.concatenate(split(left), axis=0),
        stacked,
        (((1,), (1,)), ((), ())),
        preferred_element_type=F32,
    )
    rows = every[2 * size :] + every[size : 2 * size] + every[:size]
    return rows[:, 2 * LANES :] + rows[:, LANES : 2 * LANES] + rows[:, :LANES]


def widen(matrix):
    rows, columns = matrix.shape
    return jnp.concatenate([matrix, jnp.zeros((rows, LANES - columns), F32)], axis=1)


def pack(matrix):
    rows = matrix.shape[0]
    wide = widen(matrix)
    folds = LANES // rows
    height = rows // folds
    total = wide[:height]
    for i in range(1, folds):
        total = total + pltpu.roll(wide[i * height : (i + 1) * height], i * rows, 1)
    return total


def unpack(folded, size):
    folds = LANES // size
    parts = [folded] + [pltpu.roll(folded, LANES - i * size, 1) for i in range(1, folds)]
    return jnp.concatenate(parts, axis=0)[:, :size]


def symmetric(matrix):
    return 0.5 * (matrix + matrix.T)


def solve_wide(matrix, target):
    size = matrix.shape[0]
    row_ids = lax.broadcasted_iota(jnp.int32, (size, LANES), 0)
    lane_ids = lax.broadcasted_iota(jnp.int32, (size, LANES), 1)
    work = jnp.where(lane_ids < size, matrix, pltpu.roll(target, size, 1))
    for base in range(0, size, PIVOTS):
        columns = [
            jnp.broadcast_to(work[:, base + i : base + i + 1], (size, LANES))
            for i in range(PIVOTS)
        ]
        for i in range(PIVOTS):
            pivot = base + i
            here = row_ids == pivot
            inverse = 1.0 / columns[i][pivot : pivot + 1, :]
            row = work[pivot : pivot + 1, :] * inverse
            work = jnp.where(here, row, work - columns[i] * row)
            for later in range(i + 1, PIVOTS):
                entry = columns[later][pivot : pivot + 1, :] * inverse
                columns[later] = jnp.where(here, entry, columns[later] - columns[i] * entry)
    return pltpu.roll(work, LANES - size, 1)


def add_up(values):
    values = list(values)
    while len(values) > 1:
        pairs = [values[i] + values[i + 1] for i in range(0, len(values) - 1, 2)]
        values = pairs + values[len(values) - len(values) % 2 :]
    return values[0]


def gather_kernel(rows_dev, count_ref, rows_hbm, cols_hbm, tiles_ref, total, *scratch):
    held, rows_ref, cols_ref, sems, list_sems = scratch
    slots, tile = tiles_ref.shape[:2]
    blocks = rows_dev // tile
    row_place = lax.axis_index("row")
    col_place = lax.axis_index("col")
    col_devices = lax.axis_size("col")
    row_blocks = col_devices * blocks
    chunk = -(-slots // CHUNKS)
    lists = [
        pltpu.make_async_copy(source, target, list_sems.at[i])
        for i, (source, target) in enumerate(((rows_hbm, rows_ref), (cols_hbm, cols_ref)))
    ]
    for copy in lists:
        copy.start()
    copies = []
    for c in range(CHUNKS):
        part = pl.ds(c * chunk, min(chunk, slots - c * chunk))
        copies.append(pltpu.make_async_copy(tiles_ref.at[part], held.at[part], sems.at[c]))
        copies[c].start()

    def clear(index, carry):
        for b in range(row_blocks):
            total[index * row_blocks + b] = jnp.zeros((tile, tile), F32)
        return carry

    lax.fori_loop(0, total.shape[0] // row_blocks, clear, 0)
    for copy in lists:
        copy.wait()
    live = count_ref[0]

    def add(slot, carry):
        row = rows_ref[slot]
        column = cols_ref[slot]
        side = lax.rem(row // blocks + col_devices - col_place, col_devices)
        owner = column // (blocks * col_devices)
        column_at = (owner ^ row_place) * blocks + lax.rem(column, blocks)
        at = column_at * row_blocks + side * blocks + lax.rem(row, blocks)
        total[at] = total[at] + held[slot].astype(F32)
        return carry

    for c in range(CHUNKS):
        copies[c].wait()
        lax.fori_loop(c * chunk, jnp.minimum(live, min((c + 1) * chunk, slots)), add, 0)


def dense_kernel(total, joined_ref, out_ref):
    tile = total.shape[1]
    row_blocks = out_ref.shape[2] // tile

    def part(index, carry):
        start = pl.multiple_of(index * tile, tile)
        for b in range(row_blocks):
            value = total[index * row_blocks + b].T
            high = value.astype(BF16)
            low = (value - high.astype(F32)).astype(BF16)
            out_ref[0, pl.ds(start, tile), pl.ds(b * tile, tile)] = high
            out_ref[1, pl.ds(start, tile), pl.ds(b * tile, tile)] = low
        return carry

    lax.fori_loop(0, total.shape[0] // row_blocks, part, 0)


def join_kernel(*refs):
    for k, ref in enumerate(refs[:-2]):
        refs[-1][k] = ref[...]


def apply_dense(directions, matrix):
    width = directions[0].shape[1]
    total = None
    for k, direction in enumerate(directions):
        rounded = direction.astype(BF16)
        for part in range(2):
            term = jnp.dot(
                rounded,
                matrix[part, k * width : (k + 1) * width, :],
                preferred_element_type=F32,
            )
            total = term if total is None else total + term
    return total


def first_kernel(even_ref, odd_ref, far_ref, matrix, out_ref, state_ref):
    pieces = 2 * even_ref.shape[0]
    values = [(odd_ref if k % 2 else even_ref)[k // 2] for k in range(pieces)]
    for k, value in enumerate(values + [far_ref[...]]):
        state_ref[k] = value
    rows = 2 * values[0].shape[1]
    out_ref[:, rows:] = add_up([grams(value, [value]) for value in values])
    out_ref[:, :rows] = apply_dense(values, matrix)


def add_halves(mine_ref, other_ref, width):
    near = mine_ref[:, :width] + other_ref[:, width : 2 * width]
    far = mine_ref[:, width : 2 * width] + other_ref[:, :width]
    return near, far


def image_kernel(first, mine_ref, other_ref, direction_ref, residual_ref, *outs):
    out_ref, far_ref = outs[:2]
    last = direction_ref.shape[0] - 1
    size, width = direction_ref.shape[1:]
    near, far = add_halves(mine_ref, other_ref, width)
    far_ref[...] = far
    if first:
        outs[2][...] = mine_ref[:, 2 * width :] + other_ref[:, 2 * width :]
    for i in range(width // LANES):
        out_ref[i * size : (i + 1) * size] = near[:, i * LANES : (i + 1) * LANES]
    near_part = grams(near, [direction_ref[0], residual_ref[0], near])
    far_part = grams(far, [direction_ref[last], residual_ref[last], far])
    out_ref[width // LANES * size :] = near_part + far_part


def inverse_kernel(norm_ref, out_ref):
    norm = widen(symmetric(norm_ref[:, : norm_ref.shape[0]]))
    unit = lax.broadcasted_iota(jnp.int32, norm.shape, 0) == lax.broadcasted_iota(
        jnp.int32, norm.shape, 1
    )
    out_ref[...] = solve_wide(norm, jnp.where(unit, 1.0, 0.0))


def step_kernel(pieces, with_solution, last, *refs):
    images = refs[:pieces]
    far_ref, direction_ref, residual_ref, norm_ref, inverse_ref, matrix = refs[pieces : pieces + 6]
    refs = refs[pieces + 6 :]
    if with_solution:
        solution_ref, refs = refs[0], refs[1:]
    out_ref, new_direction, new_residual, new_norm, new_solution = refs[:5]
    size, width = far_ref.shape
    parts = width // LANES
    products = add_up([ref[parts * size :] for ref in images])
    norm = norm_ref[...]
    alpha = solve_wide(widen(symmetric(products[:, :size])), norm)[:, :size]
    alpha_t = alpha.T
    image_residual = pltpu.roll(products, LANES - size, 1)[:, :size]
    image_image = pltpu.roll(products, LANES - 2 * size, 1)[:, :size]
    cross = mul(alpha_t, image_residual)
    next_norm = norm[:, :size] - (cross + cross.T) + mul(alpha_t, mul(image_image, alpha))
    new_norm[...] = widen(next_norm)
    beta_t = factor(mul(next_norm, inverse_ref[:, :size]))
    alpha_t = factor(alpha_t)
    step = times(alpha_t, direction_ref[0])
    new_solution[...] = solution_ref[...] + step if with_solution else step
    directions = []
    for k in range(pieces + 1):
        if k < pieces:
            image = jnp.concatenate(
                [images[k][i * size : (i + 1) * size] for i in range(parts)], axis=1
            )
        else:
            image = far_ref[...]
        residual = residual_ref[k] - times(alpha_t, image)
        direction = residual + times(beta_t, direction_ref[k])
        if k < new_residual.shape[0]:
            new_residual[k] = residual
            new_direction[k] = direction
        directions.append(direction)
    image = apply_dense(directions[:pieces], matrix)
    out_ref[...] = image
    if last:
        near = grams(image[:, :width], [directions[0]])
        far = grams(image[:, width:], [directions[pieces]])
        gram = pack((near + far)[:, :size])
        for k in range(refs[5].shape[0]):
            refs[5][k] = gram


def last_kernel(
    grams_ref, mine_ref, other_ref, direction_ref, residual_ref, norm_ref, solution_ref,
    new_solution, new_residual,
):
    size, width = solution_ref.shape
    curvature = unpack(add_up([grams_ref[k] for k in range(grams_ref.shape[0])]), size)
    alpha_t = factor(solve_wide(widen(symmetric(curvature)), norm_ref[...])[:, :size].T)
    new_solution[...] = solution_ref[...] + times(alpha_t, direction_ref[0])
    image = mine_ref[:, :width] + other_ref[:, width:]
    new_residual[...] = residual_ref[0] - times(alpha_t, image)


def shape(*dims, dtype=F32):
    return jax.ShapeDtypeStruct(dims, dtype)


def per_device(tiles, tile_rows, tile_cols, tile_count, signs, vertex_weight, column_scale):
    sketch, rows_dev = signs.shape
    tile = tiles.shape[1]
    pieces = lax.axis_size("row")
    col_devices = lax.axis_size("col")
    group = col_devices * rows_dev
    depth = pieces * rows_dev

    def swap(value, mask):
        return lax.ppermute(value, "row", [(i, i ^ mask) for i in range(pieces)])

    def around(value):
        even = [value] + [swap(value, k) for k in range(2, pieces, 2)]
        odd = [swap(piece, 1) for piece in even]
        return [piece for pair in zip(even, odd) for piece in pair]

    def across(value):
        return lax.ppermute(
            value, "col", [(i, (i + 1) % col_devices) for i in range(col_devices)]
        )

    right_side = signs.astype(F32) * vertex_weight[None, :] * column_scale[:, None]
    far_side = across(right_side)
    even = [right_side] + [swap(right_side, k) for k in range(2, pieces, 2)]

    matrix = shape(2, depth, group, dtype=BF16)
    total = shape(depth // tile * (group // tile), tile, tile)
    lists = [tile_rows, tile_cols]
    blocks_sum = pl.pallas_call(
        functools.partial(gather_kernel, rows_dev),
        out_shape=total,
        in_specs=[SMEM] + [HBM] * 3,
        out_specs=VMEM,
        scratch_shapes=[
            pltpu.VMEM(tiles.shape, BF16),
            pltpu.SMEM(tile_rows.shape, jnp.int32),
            pltpu.SMEM(tile_cols.shape, jnp.int32),
            pltpu.SemaphoreType.DMA((CHUNKS,)),
            pltpu.SemaphoreType.DMA((len(lists),)),
        ],
        compiler_params=params(tiles, total),
        cost_estimate=pl.CostEstimate(
            flops=4 * tiles.size, bytes_accessed=4 * tiles.size, transcendentals=0
        ),
        name="gather",
    )(tile_count, *[pltpu.with_memory_space_constraint(x, pltpu.HBM) for x in lists + [tiles]])
    joined = shape(pieces // 2, sketch, rows_dev)
    even = pl.pallas_call(
        join_kernel,
        out_shape=joined,
        in_specs=[VMEM] * (pieces // 2) + [ANY],
        out_specs=VMEM,
        compiler_params=params(joined, joined),
        name="join",
    )(*even, blocks_sum)
    odd = swap(even, 1)
    dense = pl.pallas_call(
        dense_kernel,
        out_shape=matrix,
        in_specs=[VMEM, ANY],
        out_specs=VMEM,
        compiler_params=params(total, matrix),
        cost_estimate=pl.CostEstimate(
            flops=4 * tiles.size, bytes_accessed=4 * tiles.size, transcendentals=0
        ),
        name="dense",
    )(blocks_sum, even)

    state = shape(pieces + 1, sketch, rows_dev)
    small = shape(sketch, LANES)
    piece = shape(sketch, rows_dev)
    payload = shape(sketch * (rows_dev // LANES + 1), LANES)

    partial_sum, direction = pl.pallas_call(
        first_kernel,
        out_shape=(shape(sketch, group + LANES), state),
        in_specs=[VMEM] * 4,
        out_specs=(VMEM, VMEM),
        compiler_params=params(matrix, state, state),
        name="first",
    )(even, odd, far_side, dense)
    residual = direction
    norm = None
    solution = None
    for iteration in range(ITERS - 1):
        first = iteration == 0
        outs = pl.pallas_call(
            functools.partial(image_kernel, first),
            out_shape=(payload, piece) + ((small,) if first else ()),
            in_specs=[VMEM] * 4,
            out_specs=(VMEM,) * (3 if first else 2),
            compiler_params=params(state, state),
            name="image",
        )(partial_sum, across(partial_sum), direction, residual)
        image, far = outs[:2]
        if first:
            norm = outs[2]
        inverse = pl.pallas_call(
            inverse_kernel,
            out_shape=small,
            in_specs=[VMEM],
            out_specs=VMEM,
            compiler_params=params(),
            name="inverse",
        )(norm)
        last = iteration == ITERS - 2
        given = () if first else (solution,)
        kept = shape(1, sketch, rows_dev) if last else state
        gram = shape(pieces * col_devices, sketch * sketch // LANES, LANES)
        outs = pl.pallas_call(
            functools.partial(step_kernel, pieces, not first, last),
            out_shape=(shape(sketch, group), kept, kept, small, piece) + ((gram,) if last else ()),
            in_specs=[VMEM] * (pieces + 6 + len(given)),
            out_specs=(VMEM,) * (6 if last else 5),
            compiler_params=params(matrix, state, state, state, state, state),
            name="step",
        )(*around(image), far, direction, residual, norm, inverse, dense, *given)
        partial_sum, direction, residual, norm, solution = outs[:5]
    other = across(partial_sum)
    every = lax.all_to_all(outs[5], ("row", "col"), 0, 0)
    return pl.pallas_call(
        last_kernel,
        out_shape=(piece, piece),
        in_specs=[VMEM] * 7,
        out_specs=(VMEM, VMEM),
        compiler_params=params(state, state),
        name="last",
    )(every, partial_sum, other, direction, residual, norm, solution)


def solution(mesh):
    return jax.shard_map(
        per_device,
        mesh=mesh,
        in_specs=(
            P(("row", "col"), None, None),
            P(("row", "col")),
            P(("row", "col")),
            P(("row", "col")),
            P("rhs", ("row", "col")),
            P(("row", "col")),
            P("rhs"),
        ),
        out_specs=(P("rhs", ("row", "col")), P("rhs", ("row", "col"))),
        check_vma=False,
    )
```

```python
import functools

import jax
import jax.numpy as jnp
from jax import lax
from jax.experimental import pallas as pl
from jax.experimental.pallas import tpu as pltpu
from jax.sharding import PartitionSpec as P

ITERS = 3
LANES = 128
PIVOTS = 8
CHUNKS = 5
F32 = jnp.float32
BF16 = jnp.bfloat16
SPARE_BYTES = 4 * 1024 * 1024

VMEM = pl.BlockSpec(memory_space=pltpu.VMEM)
SMEM = pl.BlockSpec(memory_space=pltpu.SMEM)
HBM = pl.BlockSpec(memory_space=pltpu.HBM)
ANY = pl.BlockSpec(memory_space=pl.ANY)


def params(*arrays):
    used = sum(a.size * jnp.dtype(a.dtype).itemsize for a in arrays)
    return pltpu.CompilerParams(vmem_limit_bytes=used + SPARE_BYTES)


def split(value):
    high = value.astype(BF16)
    rest = value - high.astype(F32)
    middle = rest.astype(BF16)
    low = (rest - middle.astype(F32)).astype(BF16)
    return high, middle, low


def mul(left, right):
    return jnp.dot(left, right, precision=lax.Precision.HIGHEST, preferred_element_type=F32)


def factor(left):
    high, middle, low = split(left)
    return jnp.concatenate([high, high, middle, high, middle, low], axis=1)


def times(prepared, right):
    high, middle, low = split(right)
    stacked = jnp.concatenate([high, middle, high, low, middle, high], axis=0)
    return jnp.dot(prepared, stacked, preferred_element_type=F32)


def grams(left, rights):
    size = left.shape[0]
    parts = [split(right) for right in rights]
    parts = parts + [parts[0]] * (LANES // size - len(parts))
    stacked = jnp.concatenate([part[i] for i in range(3) for part in parts], axis=0)
    every = lax.dot_general(
        jnp.concatenate(split(left), axis=0),
        stacked,
        (((1,), (1,)), ((), ())),
        preferred_element_type=F32,
    )
    rows = every[2 * size :] + every[size : 2 * size] + every[:size]
    return rows[:, 2 * LANES :] + rows[:, LANES : 2 * LANES] + rows[:, :LANES]


def widen(matrix):
    rows, columns = matrix.shape
    return jnp.concatenate([matrix, jnp.zeros((rows, LANES - columns), F32)], axis=1)


def pack(matrix):
    rows = matrix.shape[0]
    wide = widen(matrix)
    folds = LANES // rows
    height = rows // folds
    total = wide[:height]
    for i in range(1, folds):
        total = total + pltpu.roll(wide[i * height : (i + 1) * height], i * rows, 1)
    return total


def unpack(folded, size):
    folds = LANES // size
    parts = [folded] + [pltpu.roll(folded, LANES - i * size, 1) for i in range(1, folds)]
    return jnp.concatenate(parts, axis=0)[:, :size]


def symmetric(matrix):
    return 0.5 * (matrix + matrix.T)


def solve_wide(matrix, target):
    size = matrix.shape[0]
    row_ids = lax.broadcasted_iota(jnp.int32, (size, LANES), 0)
    lane_ids = lax.broadcasted_iota(jnp.int32, (size, LANES), 1)
    work = jnp.where(lane_ids < size, matrix, pltpu.roll(target, size, 1))
    for base in range(0, size, PIVOTS):
        columns = [
            jnp.broadcast_to(work[:, base + i : base + i + 1], (size, LANES))
            for i in range(PIVOTS)
        ]
        for i in range(PIVOTS):
            pivot = base + i
            here = row_ids == pivot
            inverse = 1.0 / columns[i][pivot : pivot + 1, :]
            row = work[pivot : pivot + 1, :] * inverse
            work = jnp.where(here, row, work - columns[i] * row)
            for later in range(i + 1, PIVOTS):
                entry = columns[later][pivot : pivot + 1, :] * inverse
                columns[later] = jnp.where(here, entry, columns[later] - columns[i] * entry)
    return pltpu.roll(work, LANES - size, 1)


def add_up(values):
    values = list(values)
    while len(values) > 1:
        pairs = [values[i] + values[i + 1] for i in range(0, len(values) - 1, 2)]
        values = pairs + values[len(values) - len(values) % 2 :]
    return values[0]


def gather_kernel(rows_dev, count_ref, rows_hbm, cols_hbm, tiles_ref, total, *scratch):
    held, rows_ref, cols_ref, sems, list_sems = scratch
    slots, tile = tiles_ref.shape[:2]
    blocks = rows_dev // tile
    row_place = lax.axis_index("row")
    col_place = lax.axis_index("col")
    col_devices = lax.axis_size("col")
    row_blocks = col_devices * blocks
    chunk = -(-slots // CHUNKS)
    lists = [
        pltpu.make_async_copy(source, target, list_sems.at[i])
        for i, (source, target) in enumerate(((rows_hbm, rows_ref), (cols_hbm, cols_ref)))
    ]
    for copy in lists:
        copy.start()
    live = count_ref[0]
    copies = []
    for c in range(CHUNKS):
        part = pl.ds(c * chunk, min(chunk, slots - c * chunk))
        copies.append(pltpu.make_async_copy(tiles_ref.at[part], held.at[part], sems.at[c]))

        @pl.when(c * chunk < live)
        def _():
            copies[c].start()

    def clear(index, carry):
        for b in range(row_blocks):
            total[index * row_blocks + b] = jnp.zeros((tile, tile), F32)
        return carry

    lax.fori_loop(0, total.shape[0] // row_blocks, clear, 0)
    for copy in lists:
        copy.wait()

    def place(slot):
        row = rows_ref[slot]
        column = cols_ref[slot]
        side = lax.rem(row // blocks + col_devices - col_place, col_devices)
        owner = column // (blocks * col_devices)
        column_at = (owner ^ row_place) * blocks + lax.rem(column, blocks)
        return column_at * row_blocks + side * blocks + lax.rem(row, blocks)

    def add(slot, at):
        value = total[at] + held[slot].astype(F32)
        following = place(jnp.minimum(slot + 1, slots - 1))
        total[at] = value
        return following

    at = place(0)
    for c in range(CHUNKS):

        @pl.when(c * chunk < live)
        def _():
            copies[c].wait()

        at = lax.fori_loop(c * chunk, jnp.minimum(live, min((c + 1) * chunk, slots)), add, at)


def dense_kernel(total, joined_ref, out_ref):
    tile = total.shape[1]
    row_blocks = out_ref.shape[2] // tile

    def part(index, carry):
        start = pl.multiple_of(index * tile, tile)
        for b in range(row_blocks):
            value = total[index * row_blocks + b].T
            high = value.astype(BF16)
            low = (value - high.astype(F32)).astype(BF16)
            out_ref[0, pl.ds(start, tile), pl.ds(b * tile, tile)] = high
            out_ref[1, pl.ds(start, tile), pl.ds(b * tile, tile)] = low
        return carry

    lax.fori_loop(0, total.shape[0] // row_blocks, part, 0)


def join_kernel(*refs):
    for k, ref in enumerate(refs[:-2]):
        refs[-1][k] = ref[...]


def apply_dense(directions, matrix):
    width = directions[0].shape[1]
    total = None
    for k, direction in enumerate(directions):
        rounded = direction.astype(BF16)
        for part in range(2):
            term = jnp.dot(
                rounded,
                matrix[part, k * width : (k + 1) * width, :],
                preferred_element_type=F32,
            )
            total = term if total is None else total + term
    return total


def first_kernel(even_ref, odd_ref, far_ref, matrix, out_ref, state_ref):
    pieces = 2 * even_ref.shape[0]
    values = [(odd_ref if k % 2 else even_ref)[k // 2] for k in range(pieces)]
    for k, value in enumerate(values + [far_ref[...]]):
        state_ref[k] = value
    rows = 2 * values[0].shape[1]
    out_ref[:, rows:] = add_up([grams(value, [value]) for value in values])
    out_ref[:, :rows] = apply_dense(values, matrix)


def add_halves(mine_ref, other_ref, width):
    near = mine_ref[:, :width] + other_ref[:, width : 2 * width]
    far = mine_ref[:, width : 2 * width] + other_ref[:, :width]
    return near, far


def image_kernel(first, mine_ref, other_ref, direction_ref, *outs):
    out_ref, far_ref = outs[:2]
    last = direction_ref.shape[0] - 1
    size, width = direction_ref.shape[1:]
    near, far = add_halves(mine_ref, other_ref, width)
    far_ref[...] = far
    if first:
        outs[2][...] = mine_ref[:, 2 * width :] + other_ref[:, 2 * width :]
    for i in range(width // LANES):
        out_ref[i * size : (i + 1) * size] = near[:, i * LANES : (i + 1) * LANES]
    product = grams(near, [direction_ref[0]]) + grams(far, [direction_ref[last]])
    out_ref[width // LANES * size :] = pack(product[:, :size])


def inverse_kernel(norm_ref, out_ref):
    norm = widen(symmetric(norm_ref[:, : norm_ref.shape[0]]))
    unit = lax.broadcasted_iota(jnp.int32, norm.shape, 0) == lax.broadcasted_iota(
        jnp.int32, norm.shape, 1
    )
    out_ref[...] = solve_wide(norm, jnp.where(unit, 1.0, 0.0))


def residual_kernel(pieces, with_solution, last, *refs):
    images = refs[:pieces]
    far_ref, direction_ref, residual_ref, norm_ref = refs[pieces : pieces + 4]
    refs = refs[pieces + 4 :]
    if with_solution:
        solution_ref, refs = refs[0], refs[1:]
    new_residual, half_ref, new_solution = refs[:3]
    size, width = far_ref.shape
    parts = width // LANES
    curvature = unpack(add_up([ref[parts * size :] for ref in images]), size)
    alpha = solve_wide(widen(symmetric(curvature)), norm_ref[...])[:, :size]
    alpha_t = factor(alpha.T)
    products = []
    for k in range(pieces + 1):
        if k < pieces:
            image = jnp.concatenate(
                [images[k][i * size : (i + 1) * size] for i in range(parts)], axis=1
            )
        else:
            image = far_ref[...]
        residual = residual_ref[k] - times(alpha_t, image)
        new_residual[k] = residual
        if last and k == 0:
            refs[3][...] = residual
        if k < pieces:
            products.append(grams(residual, [residual]))
    half_ref[...] = pack(add_up(products)[:, :size])
    step = times(alpha_t, direction_ref[0])
    new_solution[...] = solution_ref[...] + step if with_solution else step


def direction_kernel(
    pieces, last, mine_ref, other_ref, inverse_ref, residual_ref, direction_ref, matrix, *outs
):
    out_ref, new_direction, new_norm = outs[:3]
    size, width = residual_ref.shape[1:]
    next_norm = unpack(mine_ref[...] + other_ref[...], size)
    new_norm[...] = widen(next_norm)
    beta_t = factor(mul(next_norm, inverse_ref[:, :size]))
    directions = []
    for k in range(pieces + 1):
        direction = residual_ref[k] + times(beta_t, direction_ref[k])
        if k < new_direction.shape[0]:
            new_direction[k] = direction
        directions.append(direction)
    image = apply_dense(directions[:pieces], matrix)
    out_ref[...] = image
    if last:
        near = grams(image[:, :width], [directions[0]])
        far = grams(image[:, width:], [directions[pieces]])
        gram = pack((near + far)[:, :size])
        for k in range(outs[3].shape[0]):
            outs[3][k] = gram


def last_kernel(
    grams_ref, mine_ref, other_ref, direction_ref, residual_ref, norm_ref, solution_ref,
    new_solution, new_residual,
):
    size, width = solution_ref.shape
    curvature = unpack(add_up([grams_ref[k] for k in range(grams_ref.shape[0])]), size)
    alpha_t = factor(solve_wide(widen(symmetric(curvature)), norm_ref[...])[:, :size].T)
    new_solution[...] = solution_ref[...] + times(alpha_t, direction_ref[0])
    image = mine_ref[:, :width] + other_ref[:, width:]
    new_residual[...] = residual_ref[...] - times(alpha_t, image)


def shape(*dims, dtype=F32):
    return jax.ShapeDtypeStruct(dims, dtype)


def per_device(tiles, tile_rows, tile_cols, tile_count, signs, vertex_weight, column_scale):
    sketch, rows_dev = signs.shape
    tile = tiles.shape[1]
    pieces = lax.axis_size("row")
    col_devices = lax.axis_size("col")
    group = col_devices * rows_dev
    depth = pieces * rows_dev

    def swap(value, mask):
        return lax.ppermute(value, "row", [(i, i ^ mask) for i in range(pieces)])

    def around(value):
        got = {0: value}
        half = pieces // 2
        for k in (*range(2, half), 1, half, half - 1):
            if k not in got:
                got[k] = swap(value, k)
        for k in range(half + 1, pieces):
            mask = half if k == pieces - 1 else k - half
            got[k] = swap(got[k ^ mask], mask)
        return [got[k] for k in range(pieces)]

    def across(value):
        return lax.ppermute(
            value, "col", [(i, (i + 1) % col_devices) for i in range(col_devices)]
        )

    right_side = signs.astype(F32) * vertex_weight[None, :] * column_scale[:, None]
    far_side = across(right_side)
    even = [right_side] + [swap(right_side, k) for k in range(2, pieces, 2)]

    matrix = shape(2, depth, group, dtype=BF16)
    total = shape(depth // tile * (group // tile), tile, tile)
    lists = [tile_rows, tile_cols]
    blocks_sum = pl.pallas_call(
        functools.partial(gather_kernel, rows_dev),
        out_shape=total,
        in_specs=[SMEM] + [HBM] * 3,
        out_specs=VMEM,
        scratch_shapes=[
            pltpu.VMEM(tiles.shape, BF16),
            pltpu.SMEM(tile_rows.shape, jnp.int32),
            pltpu.SMEM(tile_cols.shape, jnp.int32),
            pltpu.SemaphoreType.DMA((CHUNKS,)),
            pltpu.SemaphoreType.DMA((len(lists),)),
        ],
        compiler_params=params(tiles, total),
        cost_estimate=pl.CostEstimate(
            flops=4 * tiles.size, bytes_accessed=4 * tiles.size, transcendentals=0
        ),
        name="gather",
    )(tile_count, *[pltpu.with_memory_space_constraint(x, pltpu.HBM) for x in lists + [tiles]])
    joined = shape(pieces // 2, sketch, rows_dev)
    even = pl.pallas_call(
        join_kernel,
        out_shape=joined,
        in_specs=[VMEM] * (pieces // 2) + [ANY],
        out_specs=VMEM,
        compiler_params=params(joined, joined),
        name="join",
    )(*even, blocks_sum)
    odd = swap(even, 1)
    dense = pl.pallas_call(
        dense_kernel,
        out_shape=matrix,
        in_specs=[VMEM, ANY],
        out_specs=VMEM,
        compiler_params=params(total, matrix),
        cost_estimate=pl.CostEstimate(
            flops=4 * tiles.size, bytes_accessed=4 * tiles.size, transcendentals=0
        ),
        name="dense",
    )(blocks_sum, even)

    state = shape(pieces + 1, sketch, rows_dev)
    small = shape(sketch, LANES)
    piece = shape(sketch, rows_dev)
    packed = shape(sketch * sketch // LANES, LANES)
    payload = shape(sketch * (rows_dev // LANES) + packed.shape[0], LANES)

    partial_sum, direction = pl.pallas_call(
        first_kernel,
        out_shape=(shape(sketch, group + LANES), state),
        in_specs=[VMEM] * 4,
        out_specs=(VMEM, VMEM),
        compiler_params=params(matrix, state, state),
        name="first",
    )(even, odd, far_side, dense)
    residual = direction
    norm = None
    solution = None
    for iteration in range(ITERS - 1):
        first = iteration == 0
        last = iteration == ITERS - 2
        outs = pl.pallas_call(
            functools.partial(image_kernel, first),
            out_shape=(payload, piece) + ((small,) if first else ()),
            in_specs=[VMEM] * 3,
            out_specs=(VMEM,) * (3 if first else 2),
            compiler_params=params(state, state),
            name="image",
        )(partial_sum, across(partial_sum), direction)
        image, far = outs[:2]
        if first:
            norm = outs[2]
        inverse = pl.pallas_call(
            inverse_kernel,
            out_shape=small,
            in_specs=[VMEM],
            out_specs=VMEM,
            compiler_params=params(),
            name="inverse",
        )(norm)
        given = () if first else (solution,)
        residual, half, solution, *own = pl.pallas_call(
            functools.partial(residual_kernel, pieces, not first, last),
            out_shape=(state, packed, piece) + ((piece,) if last else ()),
            in_specs=[VMEM] * (pieces + 4 + len(given)),
            out_specs=(VMEM,) * (4 if last else 3),
            compiler_params=params(state, state, state, state),
            name="residual",
        )(*around(image), far, direction, residual, norm, *given)
        kept = shape(1, sketch, rows_dev) if last else state
        gram = shape(pieces * col_devices, *packed.shape)
        outs = pl.pallas_call(
            functools.partial(direction_kernel, pieces, last),
            out_shape=(shape(sketch, group), kept, small) + ((gram,) if last else ()),
            in_specs=[VMEM] * 6,
            out_specs=(VMEM,) * (4 if last else 3),
            compiler_params=params(matrix, state, state, state),
            name="direction",
        )(half, across(half), inverse, residual, direction, dense)
        partial_sum, direction, norm = outs[:3]
    other = across(partial_sum)
    every = lax.all_to_all(outs[3], ("row", "col"), 0, 0)
    return pl.pallas_call(
        last_kernel,
        out_shape=(piece, piece),
        in_specs=[VMEM] * 7,
        out_specs=(VMEM, VMEM),
        compiler_params=params(state, state),
        name="last",
    )(every, partial_sum, other, direction, *own, norm, solution)


def solution(mesh):
    return jax.shard_map(
        per_device,
        mesh=mesh,
        in_specs=(
            P(("row", "col"), None, None),
            P(("row", "col")),
            P(("row", "col")),
            P(("row", "col")),
            P("rhs", ("row", "col")),
            P(("row", "col")),
            P("rhs"),
        ),
        out_specs=(P("rhs", ("row", "col")), P("rhs", ("row", "col"))),
        check_vma=False,
    )
```

```python
import functools

import jax
import jax.numpy as jnp
from jax import lax
from jax.experimental import pallas as pl
from jax.experimental.pallas import tpu as pltpu
from jax.sharding import PartitionSpec as P

ITERS = 3
LANES = 128
PIVOTS = 8
CHUNKS = 5
F32 = jnp.float32
BF16 = jnp.bfloat16
SPARE_BYTES = 4 * 1024 * 1024

VMEM = pl.BlockSpec(memory_space=pltpu.VMEM)
SMEM = pl.BlockSpec(memory_space=pltpu.SMEM)
HBM = pl.BlockSpec(memory_space=pltpu.HBM)
ANY = pl.BlockSpec(memory_space=pl.ANY)


def params(*arrays):
    used = sum(a.size * jnp.dtype(a.dtype).itemsize for a in arrays)
    return pltpu.CompilerParams(vmem_limit_bytes=used + SPARE_BYTES)


def split(value):
    high = value.astype(BF16)
    rest = value - high.astype(F32)
    middle = rest.astype(BF16)
    low = (rest - middle.astype(F32)).astype(BF16)
    return high, middle, low


def mul(left, right):
    return jnp.dot(left, right, precision=lax.Precision.HIGHEST, preferred_element_type=F32)


def stack(left):
    high, middle, low = split(left)
    return jnp.concatenate([high, high, middle, high, middle, low], axis=0)


def times(stacked, right):
    high, middle, low = split(right)
    return lax.dot_general(
        stacked,
        jnp.concatenate([high, middle, high, low, middle, high], axis=0),
        (((0,), (0,)), ((), ())),
        preferred_element_type=F32,
    )


def gram_parts(left, right):
    size, width = left.shape
    filler = jnp.zeros((LANES - 3 * size, width), BF16)
    every = lax.dot_general(
        jnp.concatenate(split(left), axis=0),
        jnp.concatenate([*split(right), filler], axis=0),
        (((1,), (1,)), ((), ())),
        preferred_element_type=F32,
    )
    return every[2 * size :] + every[size : 2 * size] + every[:size]


def symmetric_parts(left, right):
    return 0.5 * (gram_parts(left, right) + gram_parts(right, left))


def finish(parts, place=0):
    size = parts.shape[0]

    def block(index):
        shift = (place - index) * size % LANES
        return pltpu.roll(parts, shift, 1) if shift else parts

    return block(2) + block(1) + block(0)


def pack(wide):
    rows = wide.shape[0]
    folds = LANES // rows
    height = rows // folds
    lanes = lax.broadcasted_iota(jnp.int32, wide.shape, 1)
    wide = jnp.where(lanes < rows, wide, 0.0)
    total = wide[:height]
    for i in range(1, folds):
        total = total + pltpu.roll(wide[i * height : (i + 1) * height], i * rows, 1)
    return total


def unpack(folded, size, place=0):
    parts = []
    for i in range(LANES // size):
        shift = (place - i) * size % LANES
        parts.append(pltpu.roll(folded, shift, 1) if shift else folded)
    return jnp.concatenate(parts, axis=0)


def solve_wide(target, matrix):
    size = matrix.shape[0]
    row_ids = lax.broadcasted_iota(jnp.int32, (size, LANES), 0)
    lane_ids = lax.broadcasted_iota(jnp.int32, (size, LANES), 1)
    work = jnp.where(lane_ids < size, target, matrix)
    for base in range(0, size, PIVOTS):
        columns = [
            jnp.broadcast_to(work[:, size + base + i : size + base + i + 1], (size, LANES))
            for i in range(PIVOTS)
        ]
        for i in range(PIVOTS):
            pivot = base + i
            here = row_ids == pivot
            inverse = 1.0 / columns[i][pivot : pivot + 1, :]
            row = work[pivot : pivot + 1, :] * inverse
            work = jnp.where(here, row, work - columns[i] * row)
            for later in range(i + 1, PIVOTS):
                entry = columns[later][pivot : pivot + 1, :] * inverse
                columns[later] = jnp.where(here, entry, columns[later] - columns[i] * entry)
    return work


def add_up(values):
    values = list(values)
    while len(values) > 1:
        pairs = [values[i] + values[i + 1] for i in range(0, len(values) - 1, 2)]
        values = pairs + values[len(values) - len(values) % 2 :]
    return values[0]


def gather_kernel(rows_dev, count_ref, rows_hbm, cols_hbm, tiles_ref, total, *scratch):
    held, rows_ref, cols_ref, sems, list_sems = scratch
    slots, tile = tiles_ref.shape[:2]
    blocks = rows_dev // tile
    row_place = lax.axis_index("row")
    col_place = lax.axis_index("col")
    col_devices = lax.axis_size("col")
    row_blocks = col_devices * blocks
    chunk = -(-slots // CHUNKS)
    lists = [
        pltpu.make_async_copy(source, target, list_sems.at[i])
        for i, (source, target) in enumerate(((rows_hbm, rows_ref), (cols_hbm, cols_ref)))
    ]
    for copy in lists:
        copy.start()
    live = count_ref[0]
    copies = []
    for c in range(CHUNKS):
        part = pl.ds(c * chunk, min(chunk, slots - c * chunk))
        copies.append(pltpu.make_async_copy(tiles_ref.at[part], held.at[part], sems.at[c]))

        @pl.when(c * chunk < live)
        def _():
            copies[c].start()

    def clear(index, carry):
        for b in range(row_blocks):
            total[index * row_blocks + b] = jnp.zeros((tile, tile), F32)
        return carry

    lax.fori_loop(0, total.shape[0] // row_blocks, clear, 0)
    for copy in lists:
        copy.wait()

    def place(slot):
        row = rows_ref[slot]
        column = cols_ref[slot]
        side = lax.rem(row // blocks + col_devices - col_place, col_devices)
        owner = column // (blocks * col_devices)
        column_at = (owner ^ row_place) * blocks + lax.rem(column, blocks)
        return column_at * row_blocks + side * blocks + lax.rem(row, blocks)

    def add(slot, at):
        value = total[at] + held[slot].astype(F32)
        following = place(jnp.minimum(slot + 1, slots - 1))
        total[at] = value
        return following

    at = place(0)
    for c in range(CHUNKS):

        @pl.when(c * chunk < live)
        def _():
            copies[c].wait()

        at = lax.fori_loop(c * chunk, jnp.minimum(live, min((c + 1) * chunk, slots)), add, at)


def dense_kernel(total, joined_ref, out_ref):
    tile = total.shape[1]
    row_blocks = out_ref.shape[2] // tile

    def part(index, carry):
        start = pl.multiple_of(index * tile, tile)
        for b in range(row_blocks):
            value = total[index * row_blocks + b].T
            high = value.astype(BF16)
            low = (value - high.astype(F32)).astype(BF16)
            out_ref[0, pl.ds(start, tile), pl.ds(b * tile, tile)] = high
            out_ref[1, pl.ds(start, tile), pl.ds(b * tile, tile)] = low
        return carry

    lax.fori_loop(0, total.shape[0] // row_blocks, part, 0)


def join_kernel(*refs):
    for k, ref in enumerate(refs[:-2]):
        refs[-1][k] = ref[...]


def apply_dense(directions, matrix):
    width = directions[0].shape[1]
    total = None
    for k, direction in enumerate(directions):
        rounded = direction.astype(BF16)
        for part in range(2):
            term = jnp.dot(
                rounded,
                matrix[part, k * width : (k + 1) * width, :],
                preferred_element_type=F32,
            )
            total = term if total is None else total + term
    return total


def first_kernel(even_ref, odd_ref, far_ref, matrix, out_ref, state_ref):
    pieces = 2 * even_ref.shape[0]
    values = [(odd_ref if k % 2 else even_ref)[k // 2] for k in range(pieces)]
    for k, value in enumerate(values + [far_ref[...]]):
        state_ref[k] = value
    rows = 2 * values[0].shape[1]
    joined = jnp.concatenate(values, axis=1)
    out_ref[:, rows:] = gram_parts(joined, joined)
    out_ref[:, :rows] = apply_dense(values, matrix)


def add_halves(mine_ref, other_ref, width):
    near = mine_ref[:, :width] + other_ref[:, width : 2 * width]
    far = mine_ref[:, width : 2 * width] + other_ref[:, :width]
    return near, far


def image_kernel(first, mine_ref, other_ref, direction_ref, *outs):
    out_ref, far_ref = outs[:2]
    last = direction_ref.shape[0] - 1
    size, width = direction_ref.shape[1:]
    near, far = add_halves(mine_ref, other_ref, width)
    far_ref[...] = far
    if first:
        outs[2][...] = finish(mine_ref[:, 2 * width :] + other_ref[:, 2 * width :])
    for i in range(width // LANES):
        out_ref[i * size : (i + 1) * size] = near[:, i * LANES : (i + 1) * LANES]
    out_ref[width // LANES * size :] = symmetric_parts(near, direction_ref[0]) + symmetric_parts(
        far, direction_ref[last]
    )


def inverse_kernel(norm_ref, out_ref):
    norm = norm_ref[...]
    size = norm.shape[0]
    norm = 0.5 * (norm + jnp.concatenate([norm[:, :size].T, norm[:, size:]], axis=1))
    unit = lax.broadcasted_iota(jnp.int32, norm.shape, 0) == lax.broadcasted_iota(
        jnp.int32, norm.shape, 1
    )
    out_ref[...] = solve_wide(jnp.where(unit, 1.0, 0.0), pltpu.roll(norm, size, 1))


def arrivals(pieces):
    half = pieces // 2
    forwarded = [*range(half + 1, pieces - 1), pieces - 1]
    own = [k for k in range(1, half - 1)] + [half, half - 1]
    return [0, *forwarded, *own]


def residual_kernel(pieces, with_solution, last, *refs):
    images = [refs[arrivals(pieces).index(k)] for k in range(pieces)]
    far_ref, direction_ref, residual_ref, norm_ref = refs[pieces : pieces + 4]
    refs = refs[pieces + 4 :]
    if with_solution:
        solution_ref, refs = refs[0], refs[1:]
    new_residual, half_ref, new_solution = refs[:3]
    size, width = far_ref.shape
    parts = width // LANES
    curvature = finish(add_up([ref[parts * size :] for ref in images]), 1)
    alpha = stack(solve_wide(norm_ref[...], curvature)[:, :size])
    residuals = []
    for k in range(pieces + 1):
        if k < pieces:
            image = jnp.concatenate(
                [images[k][i * size : (i + 1) * size] for i in range(parts)], axis=1
            )
        else:
            image = far_ref[...]
        residual = residual_ref[k] - times(alpha, image)
        new_residual[k] = residual
        if last and k == 0:
            refs[3][...] = residual
        if k < pieces:
            residuals.append(residual)
    joined = jnp.concatenate(residuals, axis=1)
    half_ref[...] = gram_parts(joined, joined)
    step = times(alpha, direction_ref[0])
    new_solution[...] = solution_ref[...] + step if with_solution else step


def direction_kernel(
    pieces, last, mine_ref, other_ref, inverse_ref, residual_ref, direction_ref, matrix, *outs
):
    out_ref, new_direction, new_norm = outs[:3]
    size, width = residual_ref.shape[1:]
    next_norm = finish(mine_ref[...] + other_ref[...])
    new_norm[...] = next_norm
    beta = stack(mul(inverse_ref[:, :size], next_norm[:, :size]))
    directions = []
    for k in range(pieces + 1):
        direction = residual_ref[k] + times(beta, direction_ref[k])
        if k < new_direction.shape[0]:
            new_direction[k] = direction
        directions.append(direction)
    image = apply_dense(directions[:pieces], matrix)
    out_ref[...] = image
    if last:
        near = symmetric_parts(image[:, :width], directions[0])
        far = symmetric_parts(image[:, width:], directions[pieces])
        gram = pack(finish(near + far))
        for k in range(outs[3].shape[0]):
            outs[3][k] = gram


def last_kernel(
    grams_ref, mine_ref, other_ref, direction_ref, residual_ref, norm_ref, solution_ref,
    new_solution, new_residual,
):
    size, width = solution_ref.shape
    curvature = unpack(add_up([grams_ref[k] for k in range(grams_ref.shape[0])]), size, 1)
    alpha = stack(solve_wide(norm_ref[...], curvature)[:, :size])
    new_solution[...] = solution_ref[...] + times(alpha, direction_ref[0])
    image = mine_ref[:, :width] + other_ref[:, width:]
    new_residual[...] = residual_ref[...] - times(alpha, image)


def shape(*dims, dtype=F32):
    return jax.ShapeDtypeStruct(dims, dtype)


def per_device(tiles, tile_rows, tile_cols, tile_count, signs, vertex_weight, column_scale):
    sketch, rows_dev = signs.shape
    tile = tiles.shape[1]
    pieces = lax.axis_size("row")
    col_devices = lax.axis_size("col")
    group = col_devices * rows_dev
    depth = pieces * rows_dev

    def swap(value, mask):
        return lax.ppermute(value, "row", [(i, i ^ mask) for i in range(pieces)])

    def around(value):
        got = {0: value}
        half = pieces // 2
        for k in (*range(2, half), 1, half, half - 1):
            if k not in got:
                got[k] = swap(value, k)
        for k in range(half + 1, pieces):
            mask = half if k == pieces - 1 else k - half
            got[k] = swap(got[k ^ mask], mask)
        return [got[k] for k in range(pieces)]

    def across(value):
        return lax.ppermute(
            value, "col", [(i, (i + 1) % col_devices) for i in range(col_devices)]
        )

    right_side = signs.astype(F32) * vertex_weight[None, :] * column_scale[:, None]
    far_side = across(right_side)
    even = [right_side] + [swap(right_side, k) for k in range(2, pieces, 2)]

    matrix = shape(2, depth, group, dtype=BF16)
    total = shape(depth // tile * (group // tile), tile, tile)
    lists = [tile_rows, tile_cols]
    blocks_sum = pl.pallas_call(
        functools.partial(gather_kernel, rows_dev),
        out_shape=total,
        in_specs=[SMEM] + [HBM] * 3,
        out_specs=VMEM,
        scratch_shapes=[
            pltpu.VMEM(tiles.shape, BF16),
            pltpu.SMEM(tile_rows.shape, jnp.int32),
            pltpu.SMEM(tile_cols.shape, jnp.int32),
            pltpu.SemaphoreType.DMA((CHUNKS,)),
            pltpu.SemaphoreType.DMA((len(lists),)),
        ],
        compiler_params=params(tiles, total),
        cost_estimate=pl.CostEstimate(
            flops=4 * tiles.size, bytes_accessed=4 * tiles.size, transcendentals=0
        ),
        name="gather",
    )(tile_count, *[pltpu.with_memory_space_constraint(x, pltpu.HBM) for x in lists + [tiles]])
    joined = shape(pieces // 2, sketch, rows_dev)
    even = pl.pallas_call(
        join_kernel,
        out_shape=joined,
        in_specs=[VMEM] * (pieces // 2) + [ANY],
        out_specs=VMEM,
        compiler_params=params(joined, joined),
        name="join",
    )(*even, blocks_sum)
    odd = swap(even, 1)
    dense = pl.pallas_call(
        dense_kernel,
        out_shape=matrix,
        in_specs=[VMEM, ANY],
        out_specs=VMEM,
        compiler_params=params(total, matrix),
        cost_estimate=pl.CostEstimate(
            flops=4 * tiles.size, bytes_accessed=4 * tiles.size, transcendentals=0
        ),
        name="dense",
    )(blocks_sum, even)

    state = shape(pieces + 1, sketch, rows_dev)
    small = shape(sketch, LANES)
    piece = shape(sketch, rows_dev)
    payload = shape(sketch * (rows_dev // LANES + 1), LANES)

    partial_sum, direction = pl.pallas_call(
        first_kernel,
        out_shape=(shape(sketch, group + LANES), state),
        in_specs=[VMEM] * 4,
        out_specs=(VMEM, VMEM),
        compiler_params=params(matrix, state, state),
        name="first",
    )(even, odd, far_side, dense)
    residual = direction
    norm = None
    solution = None
    for iteration in range(ITERS - 1):
        first = iteration == 0
        last = iteration == ITERS - 2
        outs = pl.pallas_call(
            functools.partial(image_kernel, first),
            out_shape=(payload, piece) + ((small,) if first else ()),
            in_specs=[VMEM] * 3,
            out_specs=(VMEM,) * (3 if first else 2),
            compiler_params=params(state, state),
            name="image",
        )(partial_sum, across(partial_sum), direction)
        image, far = outs[:2]
        if first:
            norm = outs[2]
        inverse = pl.pallas_call(
            inverse_kernel,
            out_shape=small,
            in_specs=[VMEM],
            out_specs=VMEM,
            compiler_params=params(),
            name="inverse",
        )(norm)
        images = around(image)
        given = () if first else (solution,)
        residual, half, solution, *own = pl.pallas_call(
            functools.partial(residual_kernel, pieces, not first, last),
            out_shape=(state, small, piece) + ((piece,) if last else ()),
            in_specs=[VMEM] * (pieces + 4 + len(given)),
            out_specs=(VMEM,) * (4 if last else 3),
            compiler_params=params(state, state, state, state),
            name="residual",
        )(*[images[k] for k in arrivals(pieces)], far, direction, residual, norm, *given)
        kept = shape(1, sketch, rows_dev) if last else state
        gram = shape(pieces * col_devices, sketch * sketch // LANES, LANES)
        outs = pl.pallas_call(
            functools.partial(direction_kernel, pieces, last),
            out_shape=(shape(sketch, group), kept, small) + ((gram,) if last else ()),
            in_specs=[VMEM] * 6,
            out_specs=(VMEM,) * (4 if last else 3),
            compiler_params=params(matrix, state, state, state),
            name="direction",
        )(half, across(half), inverse, residual, direction, dense)
        partial_sum, direction, norm = outs[:3]
    other = across(partial_sum)
    every = lax.all_to_all(outs[3], ("row", "col"), 0, 0)
    return pl.pallas_call(
        last_kernel,
        out_shape=(piece, piece),
        in_specs=[VMEM] * 7,
        out_specs=(VMEM, VMEM),
        compiler_params=params(state, state),
        name="last",
    )(every, partial_sum, other, direction, *own, norm, solution)


def solution(mesh):
    return jax.shard_map(
        per_device,
        mesh=mesh,
        in_specs=(
            P(("row", "col"), None, None),
            P(("row", "col")),
            P(("row", "col")),
            P(("row", "col")),
            P("rhs", ("row", "col")),
            P(("row", "col")),
            P("rhs"),
        ),
        out_specs=(P("rhs", ("row", "col")), P("rhs", ("row", "col"))),
        check_vma=False,
    )
```

```python
import functools

import jax
import jax.numpy as jnp
from jax import lax
from jax.experimental import pallas as pl
from jax.experimental.pallas import tpu as pltpu
from jax.sharding import PartitionSpec as P

ITERS = 3
LANES = 128
PIVOTS = 8
CHUNKS = 5
F32 = jnp.float32
BF16 = jnp.bfloat16
SPARE_BYTES = 4 * 1024 * 1024

VMEM = pl.BlockSpec(memory_space=pltpu.VMEM)
SMEM = pl.BlockSpec(memory_space=pltpu.SMEM)
HBM = pl.BlockSpec(memory_space=pltpu.HBM)
ANY = pl.BlockSpec(memory_space=pl.ANY)


def params(*arrays):
    used = sum(a.size * jnp.dtype(a.dtype).itemsize for a in arrays)
    return pltpu.CompilerParams(vmem_limit_bytes=used + SPARE_BYTES)


def split(value):
    high = value.astype(BF16)
    rest = value - high.astype(F32)
    middle = rest.astype(BF16)
    low = (rest - middle.astype(F32)).astype(BF16)
    return high, middle, low


def mul(left, right):
    return jnp.dot(left, right, precision=lax.Precision.HIGHEST, preferred_element_type=F32)


def stack(left):
    high, middle, low = split(left)
    return jnp.concatenate([high, high, middle, high, middle, low], axis=0)


def times(stacked, right):
    high, middle, low = split(right)
    return lax.dot_general(
        stacked,
        jnp.concatenate([high, middle, high, low, middle, high], axis=0),
        (((0,), (0,)), ((), ())),
        preferred_element_type=F32,
    )


def gram_parts(left, right):
    size, width = left.shape
    filler = jnp.zeros((LANES - 3 * size, width), BF16)
    every = lax.dot_general(
        jnp.concatenate(split(left), axis=0),
        jnp.concatenate([*split(right), filler], axis=0),
        (((1,), (1,)), ((), ())),
        preferred_element_type=F32,
    )
    return every[2 * size :] + every[size : 2 * size] + every[:size]


def symmetric_parts(left, right):
    return 0.5 * (gram_parts(left, right) + gram_parts(right, left))


def finish(parts, place=0):
    size = parts.shape[0]

    def block(index):
        shift = (place - index) * size % LANES
        return pltpu.roll(parts, shift, 1) if shift else parts

    return block(2) + block(1) + block(0)


def pack(wide):
    rows = wide.shape[0]
    folds = LANES // rows
    height = rows // folds
    lanes = lax.broadcasted_iota(jnp.int32, wide.shape, 1)
    wide = jnp.where(lanes < rows, wide, 0.0)
    total = wide[:height]
    for i in range(1, folds):
        total = total + pltpu.roll(wide[i * height : (i + 1) * height], i * rows, 1)
    return total


def unpack(folded, size, place=0):
    parts = []
    for i in range(LANES // size):
        shift = (place - i) * size % LANES
        parts.append(pltpu.roll(folded, shift, 1) if shift else folded)
    return jnp.concatenate(parts, axis=0)


def solve_wide(target, matrix):
    size = matrix.shape[0]
    row_ids = lax.broadcasted_iota(jnp.int32, (size, LANES), 0)
    lane_ids = lax.broadcasted_iota(jnp.int32, (size, LANES), 1)
    work = jnp.where(lane_ids < size, target, matrix)
    for base in range(0, size, PIVOTS):
        columns = [
            jnp.broadcast_to(work[:, size + base + i : size + base + i + 1], (size, LANES))
            for i in range(PIVOTS)
        ]
        for i in range(PIVOTS):
            pivot = base + i
            here = row_ids == pivot
            inverse = 1.0 / columns[i][pivot : pivot + 1, :]
            row = work[pivot : pivot + 1, :] * inverse
            work = jnp.where(here, row, work - columns[i] * row)
            for later in range(i + 1, PIVOTS):
                entry = columns[later][pivot : pivot + 1, :] * inverse
                columns[later] = jnp.where(here, entry, columns[later] - columns[i] * entry)
    return work


def add_up(values):
    values = list(values)
    while len(values) > 1:
        pairs = [values[i] + values[i + 1] for i in range(0, len(values) - 1, 2)]
        values = pairs + values[len(values) - len(values) % 2 :]
    return values[0]


def add_tiles(rows_dev, lists, tiles, first_tile, start, stop, total):
    rows_ref, cols_ref = lists
    tile = total.shape[1]
    slots = rows_ref.shape[0]
    blocks = rows_dev // tile
    row_place = lax.axis_index("row")
    col_place = lax.axis_index("col")
    col_devices = lax.axis_size("col")
    row_blocks = col_devices * blocks

    def place(slot):
        row = rows_ref[slot]
        column = cols_ref[slot]
        side = lax.rem(row // blocks + col_devices - col_place, col_devices)
        owner = column // (blocks * col_devices)
        column_at = (owner ^ row_place) * blocks + lax.rem(column, blocks)
        return column_at * row_blocks + side * blocks + lax.rem(row, blocks)

    def add(slot, at):
        value = total[at] + tiles[slot - first_tile].astype(F32)
        following = place(jnp.minimum(slot + 1, slots - 1))
        total[at] = value
        return following

    lax.fori_loop(start, stop, add, place(start))


def copy_lists(hbm_refs, smem_refs, sems):
    copies = [
        pltpu.make_async_copy(source, target, sems.at[i])
        for i, (source, target) in enumerate(zip(hbm_refs, smem_refs))
    ]
    for copy in copies:
        copy.start()
    return copies


def gather_kernel(rows_dev, count_ref, rows_hbm, cols_hbm, tiles_ref, total, rest, *scratch):
    held, rows_ref, cols_ref, sems, list_sems = scratch
    live = count_ref[0]
    half = held.shape[0]
    slots, tile = tiles_ref.shape[:2]
    chunk = -(-half // CHUNKS)
    lists = copy_lists((rows_hbm, cols_hbm), (rows_ref, cols_ref), list_sems)
    copies = []
    for c in range(CHUNKS):
        part = pl.ds(c * chunk, min(chunk, half - c * chunk))
        copies.append(pltpu.make_async_copy(tiles_ref.at[part], held.at[part], sems.at[c]))

        @pl.when(c * chunk < live)
        def _():
            copies[c].start()

    last = pltpu.make_async_copy(tiles_ref.at[pl.ds(half, slots - half)], rest, sems.at[CHUNKS])

    @pl.when(half < live)
    def _():
        last.start()

    def clear(index, carry):
        total[index] = jnp.zeros((tile, tile), F32)
        return carry

    lax.fori_loop(0, total.shape[0], clear, 0, unroll=4)
    for copy in lists:
        copy.wait()
    for c in range(CHUNKS):
        start, stop = c * chunk, min((c + 1) * chunk, half)

        @pl.when(start < live)
        def _():
            copies[c].wait()
            add_tiles(
                rows_dev, (rows_ref, cols_ref), held, 0, start, jnp.minimum(live, stop), total
            )

    @pl.when(half < live)
    def _():
        last.wait()


def dense_kernel(
    rows_dev, count_ref, rows_hbm, cols_hbm, rest, total_in, joined_ref, out_ref, total, *scratch
):
    rows_ref, cols_ref, list_sems = scratch
    live = count_ref[0]
    half = rows_ref.shape[0] - rest.shape[0]
    tile = total.shape[1]
    row_blocks = out_ref.shape[2] // tile

    @pl.when(half < live)
    def _():
        lists = copy_lists((rows_hbm, cols_hbm), (rows_ref, cols_ref), list_sems)
        for copy in lists:
            copy.wait()
        add_tiles(rows_dev, (rows_ref, cols_ref), rest, half, half, live, total)

    def part(index, carry):
        start = pl.multiple_of(index * tile, tile)
        for b in range(row_blocks):
            value = total[index * row_blocks + b].T
            high = value.astype(BF16)
            low = (value - high.astype(F32)).astype(BF16)
            out_ref[0, pl.ds(start, tile), pl.ds(b * tile, tile)] = high
            out_ref[1, pl.ds(start, tile), pl.ds(b * tile, tile)] = low
        return carry

    lax.fori_loop(0, total.shape[0] // row_blocks, part, 0)


def join_kernel(*refs):
    for k, ref in enumerate(refs[:-2]):
        refs[-1][k] = ref[...]


def apply_dense(directions, matrix):
    width = directions[0].shape[1]
    total = None
    for k, direction in enumerate(directions):
        rounded = direction.astype(BF16)
        for part in range(2):
            term = jnp.dot(
                rounded,
                matrix[part, k * width : (k + 1) * width, :],
                preferred_element_type=F32,
            )
            total = term if total is None else total + term
    return total


def first_kernel(even_ref, odd_ref, matrix, out_ref, blocks_ref):
    pieces = blocks_ref.shape[0]
    values = [(odd_ref if k % 2 else even_ref)[k // 2] for k in range(pieces)]
    for k, value in enumerate(values):
        blocks_ref[k] = value
    rows = 2 * values[0].shape[1]
    joined = jnp.concatenate(values, axis=1)
    out_ref[:, rows:] = gram_parts(joined, joined)
    out_ref[:, :rows] = apply_dense(values, matrix)


def collect_kernel(near_ref, far_ref, residual_ref, direction_ref):
    pieces = near_ref.shape[0]
    for k in range(pieces):
        residual_ref[0, k] = near_ref[k]
        residual_ref[1, k] = far_ref[k]
        direction_ref[k] = near_ref[k]
    direction_ref[pieces] = far_ref[0]


def add_halves(mine_ref, other_ref, width):
    near = mine_ref[:, :width] + other_ref[:, width : 2 * width]
    far = mine_ref[:, width : 2 * width] + other_ref[:, :width]
    return near, far


def image_kernel(first, mine_ref, other_ref, near_ref, far_ref, out_ref, *norm_ref):
    core = lax.axis_index("col")
    size, width = near_ref.shape[1:]
    near, far = add_halves(mine_ref, other_ref, width)
    if first:
        norm_ref[0][...] = finish(mine_ref[:, 2 * width :] + other_ref[:, 2 * width :])
    parts = width // LANES
    for i in range(parts):
        lanes = slice(i * LANES, (i + 1) * LANES)
        for place, half in ((core, near), (1 - core, far)):
            at = pl.multiple_of((place * parts + i) * size, size)
            out_ref[pl.ds(at, size)] = half[:, lanes]
    out_ref[2 * parts * size :] = symmetric_parts(near, near_ref[0]) + symmetric_parts(
        far, far_ref[far_ref.shape[0] - 1]
    )


def inverse_kernel(norm_ref, out_ref):
    norm = norm_ref[...]
    size = norm.shape[0]
    norm = 0.5 * (norm + jnp.concatenate([norm[:, :size].T, norm[:, size:]], axis=1))
    unit = lax.broadcasted_iota(jnp.int32, norm.shape, 0) == lax.broadcasted_iota(
        jnp.int32, norm.shape, 1
    )
    out_ref[...] = solve_wide(jnp.where(unit, 1.0, 0.0), pltpu.roll(norm, size, 1))


def pick(refs, places, core, rows):
    if places[0] == places[1]:
        return refs[places[0]][rows]
    return jnp.where(core == 0, refs[places[0]][rows], refs[places[1]][rows])


def step_kernel(places, with_solution, last, *refs):
    used = 1 + max(max(pair) for pair in places)
    images, refs = refs[:used], refs[used:]
    direction_ref, residual_ref, norm_ref, inverse_ref, matrix = refs[:5]
    refs = refs[5:]
    if with_solution:
        solution_ref, refs = refs[0], refs[1:]
    out_ref, new_direction, new_residual, new_norm, new_solution = refs
    core = lax.axis_index("col")
    pieces = len(places)
    size, width = direction_ref.shape[1:]
    parts = width // LANES

    def image(k, half):
        found = []
        for i in range(parts):
            at = pl.multiple_of((half * parts + i) * size, size)
            found.append(pick(images, places[k], core, pl.ds(at, size)))
        return jnp.concatenate(found, axis=1)

    behind = slice(2 * parts * size, None)
    products = add_up([pick(images, pair, core, behind) for pair in places])
    alpha = stack(solve_wide(norm_ref[...], finish(products, 1))[:, :size])
    residuals = [
        [residual_ref[side, k] - times(alpha, image(k, half)) for k in range(pieces)]
        for side, half in enumerate((core, 1 - core))
    ]
    joined = [jnp.concatenate(values, axis=1) for values in residuals]
    next_norm = finish(gram_parts(joined[0], joined[0]) + gram_parts(joined[1], joined[1]))
    new_norm[...] = next_norm
    step = times(alpha, direction_ref[0])
    new_solution[...] = solution_ref[...] + step if with_solution else step
    beta = stack(mul(inverse_ref[:, :size], next_norm[:, :size]))
    directions = [
        residual + times(beta, direction_ref[k])
        for k, residual in enumerate(residuals[0] + residuals[1][:1])
    ]
    if last:
        new_residual[...] = residuals[0][0]
        new_direction[0] = directions[0]
        new_direction[1] = directions[pieces]
    else:
        for k in range(pieces):
            new_residual[0, k] = residuals[0][k]
            new_residual[1, k] = residuals[1][k]
        for k in range(pieces + 1):
            new_direction[k] = directions[k]
    out_ref[...] = apply_dense(directions[:pieces], matrix)


def last_image_kernel(mine_ref, other_ref, direction_ref, near_ref, gram_ref):
    near, far = add_halves(mine_ref, other_ref, direction_ref.shape[2])
    near_ref[...] = near
    gram_ref[...] = symmetric_parts(near, direction_ref[0]) + symmetric_parts(
        far, direction_ref[1]
    )


def last_kernel(places, *refs):
    used = 1 + max(max(pair) for pair in places)
    image_ref, direction_ref, residual_ref, norm_ref, solution_ref = refs[used:-2]
    new_solution, new_residual = refs[-2:]
    core = lax.axis_index("col")
    size = image_ref.shape[0]
    products = add_up([pick(refs, pair, core, slice(None)) for pair in places])
    alpha = stack(solve_wide(norm_ref[...], finish(products, 1))[:, :size])
    new_solution[...] = solution_ref[...] + times(alpha, direction_ref[0])
    new_residual[...] = residual_ref[...] - times(alpha, image_ref[...])


def shape(*dims, dtype=F32):
    return jax.ShapeDtypeStruct(dims, dtype)


def per_device(tiles, tile_rows, tile_cols, tile_count, signs, vertex_weight, column_scale):
    sketch, rows_dev = signs.shape
    tile = tiles.shape[1]
    pieces = lax.axis_size("row")
    col_devices = lax.axis_size("col")
    group = col_devices * rows_dev
    depth = pieces * rows_dev

    def swap(value, mask):
        return lax.ppermute(value, "row", [(i, i ^ mask) for i in range(pieces)])

    def across(value):
        return lax.ppermute(
            value, "col", [(i, (i + 1) % col_devices) for i in range(col_devices)]
        )

    def exchange(value):
        if pieces != 8:
            found = [value] + [swap(value, k) for k in range(1, pieces)]
            return found, [(k, k) for k in range(pieces)]
        shares = ((7, 4), (3, 5), (2, 6), (1, 0))
        fetched = []
        passed = []
        places = {0: (0, 0)}
        for turn, masks in enumerate(shares, 1):
            pairs = [
                (i * 2 + core, (i ^ mask) * 2 + core)
                for core, mask in enumerate(masks)
                if mask
                for i in range(pieces)
            ]
            fetched.append(lax.ppermute(value, ("row", "col"), pairs))
            pairs = [(core, 1 - core) for core, mask in enumerate(masks) if mask]
            passed.append(lax.ppermute(fetched[-1], "col", pairs))
            for core, mask in enumerate(masks):
                if mask:
                    here = (turn, turn + len(shares))
                    places[mask] = here if core == 0 else here[::-1]
        return [value, *fetched, *passed], [places[k] for k in range(pieces)]

    right_side = signs.astype(F32) * vertex_weight[None, :] * column_scale[:, None]
    far_side = across(right_side)[None]
    even = [right_side] + [swap(right_side, k) for k in range(2, pieces, 2)]

    matrix = shape(2, depth, group, dtype=BF16)
    total = shape(depth // tile * (group // tile), tile, tile)
    slots = tiles.shape[0]
    half = slots // 2
    rest = shape(slots - half, tile, tile, dtype=BF16)
    lists = [pltpu.with_memory_space_constraint(x, pltpu.HBM) for x in (tile_rows, tile_cols)]
    lists_scratch = [pltpu.SMEM(x.shape, jnp.int32) for x in lists]
    cost = pl.CostEstimate(
        flops=4 * tiles.size, bytes_accessed=4 * tiles.size, transcendentals=0
    )
    blocks_sum, others = pl.pallas_call(
        functools.partial(gather_kernel, rows_dev),
        out_shape=(total, rest),
        in_specs=[SMEM] + [HBM] * 3,
        out_specs=(VMEM, VMEM),
        scratch_shapes=[
            pltpu.VMEM((half, tile, tile), BF16),
            *lists_scratch,
            pltpu.SemaphoreType.DMA((CHUNKS + 1,)),
            pltpu.SemaphoreType.DMA((len(lists),)),
        ],
        compiler_params=params(tiles, total),
        cost_estimate=cost,
        name="gather",
    )(tile_count, *lists, pltpu.with_memory_space_constraint(tiles, pltpu.HBM))
    joined = shape(pieces // 2, sketch, rows_dev)
    even = pl.pallas_call(
        join_kernel,
        out_shape=joined,
        in_specs=[VMEM] * (pieces // 2) + [ANY],
        out_specs=VMEM,
        compiler_params=params(joined, joined),
        name="join",
    )(*even, blocks_sum)
    odd = swap(even, 1)
    dense, _ = pl.pallas_call(
        functools.partial(dense_kernel, rows_dev),
        out_shape=(matrix, total),
        in_specs=[SMEM] + [HBM] * 2 + [VMEM, VMEM, ANY],
        out_specs=(VMEM, VMEM),
        scratch_shapes=[*lists_scratch, pltpu.SemaphoreType.DMA((len(lists),))],
        input_output_aliases={4: 1},
        compiler_params=params(rest, total, total, matrix),
        cost_estimate=cost,
        name="dense",
    )(tile_count, *lists, others, blocks_sum, even)

    held = shape(2, pieces, sketch, rows_dev)
    state = shape(pieces + 1, sketch, rows_dev)
    small = shape(sketch, LANES)
    piece = shape(sketch, rows_dev)
    payload = shape(sketch * (2 * (rows_dev // LANES) + 1), LANES)

    partial_sum, blocks = pl.pallas_call(
        first_kernel,
        out_shape=(shape(sketch, group + LANES), shape(pieces, sketch, rows_dev)),
        in_specs=[VMEM] * 3,
        out_specs=(VMEM, VMEM),
        compiler_params=params(matrix, state, state),
        name="first",
    )(even, odd, dense)
    residual, direction = pl.pallas_call(
        collect_kernel,
        out_shape=(held, state),
        in_specs=[VMEM] * 2,
        out_specs=(VMEM, VMEM),
        compiler_params=params(held, held, state),
        name="collect",
    )(blocks, across(blocks))
    norm = None
    solution = None
    for iteration in range(ITERS - 1):
        first = iteration == 0
        last = iteration == ITERS - 2
        outs = pl.pallas_call(
            functools.partial(image_kernel, first),
            out_shape=(payload,) + ((small,) if first else ()),
            in_specs=[VMEM] * 4,
            out_specs=(VMEM,) * (2 if first else 1),
            compiler_params=params(state, payload),
            name="image",
        )(partial_sum, across(partial_sum), *((even, far_side) if first else (direction,) * 2))
        if first:
            norm = outs[1]
        found, places = exchange(outs[0])
        inverse = pl.pallas_call(
            inverse_kernel,
            out_shape=small,
            in_specs=[VMEM],
            out_specs=VMEM,
            compiler_params=params(),
            name="inverse",
        )(norm)
        given = () if first else (solution,)
        partial_sum, direction, residual, norm, solution = pl.pallas_call(
            functools.partial(step_kernel, places, not first, last),
            out_shape=(
                shape(sketch, group),
                shape(2, sketch, rows_dev) if last else state,
                piece if last else held,
                small,
                piece,
            ),
            in_specs=[VMEM] * (len(found) + 5 + len(given)),
            out_specs=(VMEM,) * 5,
            compiler_params=params(matrix, held, held, held, held, state),
            name="step",
        )(*found, direction, residual, norm, inverse, dense, *given)
    near, gram = pl.pallas_call(
        last_image_kernel,
        out_shape=(piece, small),
        in_specs=[VMEM] * 3,
        out_specs=(VMEM, VMEM),
        compiler_params=params(state),
        name="last_image",
    )(partial_sum, across(partial_sum), direction)
    found, places = exchange(gram)
    return pl.pallas_call(
        functools.partial(last_kernel, places),
        out_shape=(piece, piece),
        in_specs=[VMEM] * (len(found) + 5),
        out_specs=(VMEM, VMEM),
        compiler_params=params(state, state),
        name="last",
    )(*found, near, direction, residual, norm, solution)


def solution(mesh):
    return jax.shard_map(
        per_device,
        mesh=mesh,
        in_specs=(
            P(("row", "col"), None, None),
            P(("row", "col")),
            P(("row", "col")),
            P(("row", "col")),
            P("rhs", ("row", "col")),
            P(("row", "col")),
            P("rhs"),
        ),
        out_specs=(P("rhs", ("row", "col")), P("rhs", ("row", "col"))),
        check_vma=False,
    )
```

```python
import functools

import jax
import jax.numpy as jnp
from jax import lax
from jax.experimental import pallas as pl
from jax.experimental.pallas import tpu as pltpu
from jax.sharding import PartitionSpec as P

ITERS = 3
LANES = 128
PIVOTS = 8
CHUNKS = 5
F32 = jnp.float32
BF16 = jnp.bfloat16
SPARE_BYTES = 4 * 1024 * 1024

VMEM = pl.BlockSpec(memory_space=pltpu.VMEM)
SMEM = pl.BlockSpec(memory_space=pltpu.SMEM)
HBM = pl.BlockSpec(memory_space=pltpu.HBM)
ANY = pl.BlockSpec(memory_space=pl.ANY)


def params(*arrays):
    used = sum(a.size * jnp.dtype(a.dtype).itemsize for a in arrays)
    return pltpu.CompilerParams(vmem_limit_bytes=used + SPARE_BYTES)


def split(value):
    high = value.astype(BF16)
    rest = value - high.astype(F32)
    middle = rest.astype(BF16)
    low = (rest - middle.astype(F32)).astype(BF16)
    return high, middle, low


def mul(left, right):
    return jnp.dot(left, right, precision=lax.Precision.HIGHEST, preferred_element_type=F32)


def stack(left):
    high, middle, low = split(left)
    return jnp.concatenate([high, high, middle, high, middle, low], axis=0)


def times(stacked, right):
    high, middle, low = split(right)
    return lax.dot_general(
        stacked,
        jnp.concatenate([high, middle, high, low, middle, high], axis=0),
        (((0,), (0,)), ((), ())),
        preferred_element_type=F32,
    )


def gram_parts(left, right):
    size, width = left.shape
    filler = jnp.zeros((LANES - 3 * size, width), BF16)
    every = lax.dot_general(
        jnp.concatenate(split(left), axis=0),
        jnp.concatenate([*split(right), filler], axis=0),
        (((1,), (1,)), ((), ())),
        preferred_element_type=F32,
    )
    return every[2 * size :] + every[size : 2 * size] + every[:size]


def symmetric_parts(left, right):
    return 0.5 * (gram_parts(left, right) + gram_parts(right, left))


def finish(parts, place=0):
    size = parts.shape[0]

    def block(index):
        shift = (place - index) * size % LANES
        return pltpu.roll(parts, shift, 1) if shift else parts

    return block(2) + block(1) + block(0)


def pack(wide):
    rows = wide.shape[0]
    folds = LANES // rows
    height = rows // folds
    lanes = lax.broadcasted_iota(jnp.int32, wide.shape, 1)
    wide = jnp.where(lanes < rows, wide, 0.0)
    total = wide[:height]
    for i in range(1, folds):
        total = total + pltpu.roll(wide[i * height : (i + 1) * height], i * rows, 1)
    return total


def unpack(folded, size, place=0):
    parts = []
    for i in range(LANES // size):
        shift = (place - i) * size % LANES
        parts.append(pltpu.roll(folded, shift, 1) if shift else folded)
    return jnp.concatenate(parts, axis=0)


def solve_wide(target, matrix):
    size = matrix.shape[0]
    row_ids = lax.broadcasted_iota(jnp.int32, (size, LANES), 0)
    lane_ids = lax.broadcasted_iota(jnp.int32, (size, LANES), 1)
    work = jnp.where(lane_ids < size, target, matrix)
    for base in range(0, size, PIVOTS):
        columns = [
            jnp.broadcast_to(work[:, size + base + i : size + base + i + 1], (size, LANES))
            for i in range(PIVOTS)
        ]
        for i in range(PIVOTS):
            pivot = base + i
            here = row_ids == pivot
            inverse = 1.0 / columns[i][pivot : pivot + 1, :]
            row = work[pivot : pivot + 1, :] * inverse
            work = jnp.where(here, row, work - columns[i] * row)
            for later in range(i + 1, PIVOTS):
                entry = columns[later][pivot : pivot + 1, :] * inverse
                columns[later] = jnp.where(here, entry, columns[later] - columns[i] * entry)
    return work


def add_up(values):
    values = list(values)
    while len(values) > 1:
        pairs = [values[i] + values[i + 1] for i in range(0, len(values) - 1, 2)]
        values = pairs + values[len(values) - len(values) % 2 :]
    return values[0]


def add_tiles(rows_dev, lists, tiles, first_tile, start, stop, total):
    rows_ref, cols_ref = lists
    tile = total.shape[1]
    slots = rows_ref.shape[0]
    blocks = rows_dev // tile
    row_place = lax.axis_index("row")
    col_place = lax.axis_index("col")
    col_devices = lax.axis_size("col")
    row_blocks = col_devices * blocks

    def place(slot):
        row = rows_ref[slot]
        column = cols_ref[slot]
        side = lax.rem(row // blocks + col_devices - col_place, col_devices)
        owner = column // (blocks * col_devices)
        column_at = (owner ^ row_place) * blocks + lax.rem(column, blocks)
        return column_at * row_blocks + side * blocks + lax.rem(row, blocks)

    def add(slot, at):
        value = total[at] + tiles[slot - first_tile].astype(F32)
        following = place(jnp.minimum(slot + 1, slots - 1))
        total[at] = value
        return following

    lax.fori_loop(start, stop, add, place(start))


def copy_lists(hbm_refs, smem_refs, sems):
    copies = [
        pltpu.make_async_copy(source, target, sems.at[i])
        for i, (source, target) in enumerate(zip(hbm_refs, smem_refs))
    ]
    for copy in copies:
        copy.start()
    return copies


def gather_kernel(rows_dev, count_ref, rows_hbm, cols_hbm, tiles_ref, total, rest, *scratch):
    held, rows_ref, cols_ref, sems, list_sems = scratch
    live = count_ref[0]
    half = held.shape[0]
    slots, tile = tiles_ref.shape[:2]
    chunk = -(-half // CHUNKS)
    lists = copy_lists((rows_hbm, cols_hbm), (rows_ref, cols_ref), list_sems)
    copies = []
    for c in range(CHUNKS):
        part = pl.ds(c * chunk, min(chunk, half - c * chunk))
        copies.append(pltpu.make_async_copy(tiles_ref.at[part], held.at[part], sems.at[c]))

        @pl.when(c * chunk < live)
        def _():
            copies[c].start()

    last = pltpu.make_async_copy(tiles_ref.at[pl.ds(half, slots - half)], rest, sems.at[CHUNKS])

    @pl.when(half < live)
    def _():
        last.start()

    def clear(index, carry):
        total[index] = jnp.zeros((tile, tile), F32)
        return carry

    lax.fori_loop(0, total.shape[0], clear, 0, unroll=4)
    for copy in lists:
        copy.wait()
    for c in range(CHUNKS):
        start, stop = c * chunk, min((c + 1) * chunk, half)

        @pl.when(start < live)
        def _():
            copies[c].wait()
            add_tiles(
                rows_dev, (rows_ref, cols_ref), held, 0, start, jnp.minimum(live, stop), total
            )

    @pl.when(half < live)
    def _():
        last.wait()


def dense_kernel(
    rows_dev, count_ref, rows_hbm, cols_hbm, rest, total_in, joined_ref, out_ref, total, *scratch
):
    rows_ref, cols_ref, list_sems = scratch
    live = count_ref[0]
    half = rows_ref.shape[0] - rest.shape[0]
    tile = total.shape[1]
    row_blocks = out_ref.shape[2] // tile

    @pl.when(half < live)
    def _():
        lists = copy_lists((rows_hbm, cols_hbm), (rows_ref, cols_ref), list_sems)
        for copy in lists:
            copy.wait()
        add_tiles(rows_dev, (rows_ref, cols_ref), rest, half, half, live, total)

    def part(index, carry):
        start = pl.multiple_of(index * tile, tile)
        for b in range(row_blocks):
            value = total[index * row_blocks + b].T
            high = value.astype(BF16)
            low = (value - high.astype(F32)).astype(BF16)
            out_ref[0, pl.ds(start, tile), pl.ds(b * tile, tile)] = high
            out_ref[1, pl.ds(start, tile), pl.ds(b * tile, tile)] = low
        return carry

    lax.fori_loop(0, total.shape[0] // row_blocks, part, 0)


def join_kernel(*refs):
    for k, ref in enumerate(refs[:-2]):
        refs[-1][k] = ref[...]


def apply_dense(directions, matrix):
    width = directions[0].shape[1]
    total = None
    for k, direction in enumerate(directions):
        rounded = direction.astype(BF16)
        for part in range(2):
            term = jnp.dot(
                rounded,
                matrix[part, k * width : (k + 1) * width, :],
                preferred_element_type=F32,
            )
            total = term if total is None else total + term
    return total


def first_kernel(even_ref, odd_ref, matrix, out_ref, blocks_ref):
    pieces = blocks_ref.shape[0]
    values = [(odd_ref if k % 2 else even_ref)[k // 2] for k in range(pieces)]
    for k, value in enumerate(values):
        blocks_ref[k] = value
    rows = 2 * values[0].shape[1]
    joined = jnp.concatenate(values, axis=1)
    out_ref[:, rows:] = gram_parts(joined, joined)
    out_ref[:, :rows] = apply_dense(values, matrix)


def collect_kernel(near_ref, far_ref, residual_ref, direction_ref):
    pieces = near_ref.shape[0]
    for k in range(pieces):
        residual_ref[0, k] = near_ref[k]
        residual_ref[1, k] = far_ref[k]
        direction_ref[k] = near_ref[k]
    direction_ref[pieces] = far_ref[0]


def add_halves(mine_ref, other_ref, width):
    near = mine_ref[:, :width] + other_ref[:, width : 2 * width]
    far = mine_ref[:, width : 2 * width] + other_ref[:, :width]
    return near, far


def image_kernel(first, mine_ref, other_ref, near_ref, far_ref, *refs):
    out_ref, norm_ref = refs[1:3] if first else (refs[0], None)
    core = lax.axis_index("col")
    size, width = near_ref.shape[1:]
    near, far = add_halves(mine_ref, other_ref, width)
    if first:
        norm_ref[...] = finish(mine_ref[:, 2 * width :] + other_ref[:, 2 * width :])
    parts = width // LANES
    for i in range(parts):
        lanes = slice(i * LANES, (i + 1) * LANES)
        for place, half in ((core, near), (1 - core, far)):
            at = pl.multiple_of((place * parts + i) * size, size)
            out_ref[pl.ds(at, size)] = half[:, lanes]
    out_ref[2 * parts * size :] = symmetric_parts(near, near_ref[0]) + symmetric_parts(
        far, far_ref[far_ref.shape[0] - 1]
    )


def inverse_kernel(norm_ref, out_ref):
    norm = norm_ref[...]
    size = norm.shape[0]
    norm = 0.5 * (norm + jnp.concatenate([norm[:, :size].T, norm[:, size:]], axis=1))
    unit = lax.broadcasted_iota(jnp.int32, norm.shape, 0) == lax.broadcasted_iota(
        jnp.int32, norm.shape, 1
    )
    out_ref[...] = solve_wide(jnp.where(unit, 1.0, 0.0), pltpu.roll(norm, size, 1))


def pick(refs, places, core, rows):
    if places[0] == places[1]:
        return refs[places[0]][rows]
    return jnp.where(core == 0, refs[places[0]][rows], refs[places[1]][rows])


def step_kernel(places, with_solution, last, *refs):
    used = 1 + max(max(pair) for pair in places)
    images, refs = refs[:used], refs[used:]
    direction_ref, residual_ref, norm_ref, inverse_ref, matrix = refs[:5]
    refs = refs[5:]
    if with_solution:
        solution_ref, refs = refs[0], refs[1:]
    out_ref, new_direction, new_residual, new_norm, new_solution = refs
    core = lax.axis_index("col")
    pieces = len(places)
    size, width = direction_ref.shape[1:]
    parts = width // LANES

    def image(k, half):
        found = []
        for i in range(parts):
            at = pl.multiple_of((half * parts + i) * size, size)
            found.append(pick(images, places[k], core, pl.ds(at, size)))
        return jnp.concatenate(found, axis=1)

    behind = slice(2 * parts * size, None)
    products = add_up([pick(images, pair, core, behind) for pair in places])
    alpha = stack(solve_wide(norm_ref[...], finish(products, 1))[:, :size])
    residuals = [
        [residual_ref[side, k] - times(alpha, image(k, half)) for k in range(pieces)]
        for side, half in enumerate((core, 1 - core))
    ]
    joined = [jnp.concatenate(values, axis=1) for values in residuals]
    next_norm = finish(gram_parts(joined[0], joined[0]) + gram_parts(joined[1], joined[1]))
    new_norm[...] = next_norm
    step = times(alpha, direction_ref[0])
    new_solution[...] = solution_ref[...] + step if with_solution else step
    beta = stack(mul(inverse_ref[:, :size], next_norm[:, :size]))
    directions = [
        residual + times(beta, direction_ref[k])
        for k, residual in enumerate(residuals[0] + residuals[1][:1])
    ]
    if last:
        new_residual[...] = residuals[0][0]
        new_direction[0] = directions[0]
        new_direction[1] = directions[pieces]
    else:
        for k in range(pieces):
            new_residual[0, k] = residuals[0][k]
            new_residual[1, k] = residuals[1][k]
        for k in range(pieces + 1):
            new_direction[k] = directions[k]
    out_ref[...] = apply_dense(directions[:pieces], matrix)


def last_image_kernel(mine_ref, other_ref, direction_ref, near_ref, gram_ref):
    near, far = add_halves(mine_ref, other_ref, direction_ref.shape[2])
    near_ref[...] = near
    gram_ref[...] = symmetric_parts(near, direction_ref[0]) + symmetric_parts(
        far, direction_ref[1]
    )


def last_kernel(places, *refs):
    used = 1 + max(max(pair) for pair in places)
    image_ref, direction_ref, residual_ref, norm_ref, solution_ref = refs[used:-2]
    new_solution, new_residual = refs[-2:]
    core = lax.axis_index("col")
    size = image_ref.shape[0]
    products = add_up([pick(refs, pair, core, slice(None)) for pair in places])
    alpha = stack(solve_wide(norm_ref[...], finish(products, 1))[:, :size])
    new_solution[...] = solution_ref[...] + times(alpha, direction_ref[0])
    new_residual[...] = residual_ref[...] - times(alpha, image_ref[...])


def shape(*dims, dtype=F32):
    return jax.ShapeDtypeStruct(dims, dtype)


def per_device(tiles, tile_rows, tile_cols, tile_count, signs, vertex_weight, column_scale):
    sketch, rows_dev = signs.shape
    tile = tiles.shape[1]
    pieces = lax.axis_size("row")
    col_devices = lax.axis_size("col")
    group = col_devices * rows_dev
    depth = pieces * rows_dev

    def swap(value, mask):
        return lax.ppermute(value, "row", [(i, i ^ mask) for i in range(pieces)])

    def across(value):
        return lax.ppermute(
            value, "col", [(i, (i + 1) % col_devices) for i in range(col_devices)]
        )

    def exchange(value):
        if pieces != 8:
            found = [value] + [swap(value, k) for k in range(1, pieces)]
            return found, [(k, k) for k in range(pieces)]
        shares = ((7, 4), (3, 5), (2, 6), (1, 1))
        fetched = []
        passed = []
        places = {0: (0, 0)}
        for turn, masks in enumerate(shares, 1):
            pairs = [
                (i * 2 + core, (i ^ mask) * 2 + core)
                for core, mask in enumerate(masks)
                for i in range(pieces)
            ]
            fetched.append(lax.ppermute(value, ("row", "col"), pairs))
            if masks[0] == masks[1]:
                places[masks[0]] = (turn, turn)
            else:
                passed.append(across(fetched[-1]))
                places[masks[0]] = (turn, turn + len(shares))
                places[masks[1]] = (turn + len(shares), turn)
        return [value, *fetched, *passed], [places[k] for k in range(pieces)]

    right_side = signs.astype(F32) * vertex_weight[None, :] * column_scale[:, None]
    far_side = across(right_side)[None]
    even = [right_side] + [swap(right_side, k) for k in range(2, pieces, 2)]

    matrix = shape(2, depth, group, dtype=BF16)
    total = shape(depth // tile * (group // tile), tile, tile)
    slots = tiles.shape[0]
    half = slots // 2
    rest = shape(slots - half, tile, tile, dtype=BF16)
    lists = [pltpu.with_memory_space_constraint(x, pltpu.HBM) for x in (tile_rows, tile_cols)]
    lists_scratch = [pltpu.SMEM(x.shape, jnp.int32) for x in lists]
    cost = pl.CostEstimate(
        flops=4 * tiles.size, bytes_accessed=4 * tiles.size, transcendentals=0
    )
    blocks_sum, others = pl.pallas_call(
        functools.partial(gather_kernel, rows_dev),
        out_shape=(total, rest),
        in_specs=[SMEM] + [HBM] * 3,
        out_specs=(VMEM, VMEM),
        scratch_shapes=[
            pltpu.VMEM((half, tile, tile), BF16),
            *lists_scratch,
            pltpu.SemaphoreType.DMA((CHUNKS + 1,)),
            pltpu.SemaphoreType.DMA((len(lists),)),
        ],
        compiler_params=params(tiles, total),
        cost_estimate=cost,
        name="gather",
    )(tile_count, *lists, pltpu.with_memory_space_constraint(tiles, pltpu.HBM))
    joined = shape(pieces // 2, sketch, rows_dev)
    even = pl.pallas_call(
        join_kernel,
        out_shape=joined,
        in_specs=[VMEM] * (pieces // 2) + [ANY],
        out_specs=VMEM,
        compiler_params=params(joined, joined),
        name="join",
    )(*even, blocks_sum)
    odd = swap(even, 1)
    dense, _ = pl.pallas_call(
        functools.partial(dense_kernel, rows_dev),
        out_shape=(matrix, total),
        in_specs=[SMEM] + [HBM] * 2 + [VMEM, VMEM, ANY],
        out_specs=(VMEM, VMEM),
        scratch_shapes=[*lists_scratch, pltpu.SemaphoreType.DMA((len(lists),))],
        input_output_aliases={4: 1},
        compiler_params=params(rest, total, total, matrix),
        cost_estimate=cost,
        name="dense",
    )(tile_count, *lists, others, blocks_sum, even)

    held = shape(2, pieces, sketch, rows_dev)
    state = shape(pieces + 1, sketch, rows_dev)
    small = shape(sketch, LANES)
    piece = shape(sketch, rows_dev)
    payload = shape(sketch * (2 * (rows_dev // LANES) + 1), LANES)

    partial_sum, blocks = pl.pallas_call(
        first_kernel,
        out_shape=(shape(sketch, group + LANES), shape(pieces, sketch, rows_dev)),
        in_specs=[VMEM] * 3,
        out_specs=(VMEM, VMEM),
        compiler_params=params(matrix, state, state),
        name="first",
    )(even, odd, dense)
    norm = None
    solution = None
    direction = None
    for iteration in range(ITERS - 1):
        first = iteration == 0
        last = iteration == ITERS - 2
        sums = (partial_sum, across(partial_sum))
        given = (even, far_side, blocks) if first else (direction, direction)
        outs = pl.pallas_call(
            functools.partial(image_kernel, first),
            out_shape=(payload, small, blocks) if first else (payload,),
            in_specs=[VMEM] * 4 + [ANY] * (len(given) - 2),
            out_specs=(VMEM, VMEM, ANY) if first else (VMEM,),
            input_output_aliases={4: 2} if first else {},
            compiler_params=params(state, payload),
            name="image",
        )(*sums, *given)
        if first:
            norm, blocks = outs[1:]
            residual, direction = pl.pallas_call(
                collect_kernel,
                out_shape=(held, state),
                in_specs=[VMEM] * 2,
                out_specs=(VMEM, VMEM),
                compiler_params=params(held, held, state),
                name="collect",
            )(blocks, across(blocks))
        found, places = exchange(outs[0])
        inverse = pl.pallas_call(
            inverse_kernel,
            out_shape=small,
            in_specs=[VMEM],
            out_specs=VMEM,
            compiler_params=params(),
            name="inverse",
        )(norm)
        given = () if first else (solution,)
        partial_sum, direction, residual, norm, solution = pl.pallas_call(
            functools.partial(step_kernel, places, not first, last),
            out_shape=(
                shape(sketch, group),
                shape(2, sketch, rows_dev) if last else state,
                piece if last else held,
                small,
                piece,
            ),
            in_specs=[VMEM] * (len(found) + 5 + len(given)),
            out_specs=(VMEM,) * 5,
            compiler_params=params(matrix, held, held, held, held, state),
            name="step",
        )(*found, direction, residual, norm, inverse, dense, *given)
    near, gram = pl.pallas_call(
        last_image_kernel,
        out_shape=(piece, small),
        in_specs=[VMEM] * 3,
        out_specs=(VMEM, VMEM),
        compiler_params=params(state),
        name="last_image",
    )(partial_sum, across(partial_sum), direction)
    found, places = exchange(gram)
    return pl.pallas_call(
        functools.partial(last_kernel, places),
        out_shape=(piece, piece),
        in_specs=[VMEM] * (len(found) + 5),
        out_specs=(VMEM, VMEM),
        compiler_params=params(state, state),
        name="last",
    )(*found, near, direction, residual, norm, solution)


def solution(mesh):
    return jax.shard_map(
        per_device,
        mesh=mesh,
        in_specs=(
            P(("row", "col"), None, None),
            P(("row", "col")),
            P(("row", "col")),
            P(("row", "col")),
            P("rhs", ("row", "col")),
            P(("row", "col")),
            P("rhs"),
        ),
        out_specs=(P("rhs", ("row", "col")), P("rhs", ("row", "col"))),
        check_vma=False,
    )
```

```python
import functools

import jax
import jax.numpy as jnp
from jax import lax
from jax.experimental import pallas as pl
from jax.experimental.pallas import tpu as pltpu
from jax.sharding import PartitionSpec as P

ITERS = 3
LANES = 128
PIVOTS = 8
CHUNKS = 5
F32 = jnp.float32
BF16 = jnp.bfloat16
SPARE_BYTES = 4 * 1024 * 1024

VMEM = pl.BlockSpec(memory_space=pltpu.VMEM)
SMEM = pl.BlockSpec(memory_space=pltpu.SMEM)
HBM = pl.BlockSpec(memory_space=pltpu.HBM)
ANY = pl.BlockSpec(memory_space=pl.ANY)


def params(*arrays):
    used = sum(a.size * jnp.dtype(a.dtype).itemsize for a in arrays)
    return pltpu.CompilerParams(vmem_limit_bytes=used + SPARE_BYTES)


def split(value):
    high = value.astype(BF16)
    rest = value - high.astype(F32)
    middle = rest.astype(BF16)
    low = (rest - middle.astype(F32)).astype(BF16)
    return high, middle, low


def mul(left, right):
    return jnp.dot(left, right, precision=lax.Precision.HIGHEST, preferred_element_type=F32)


def stack(left):
    high, middle, low = [part.astype(F32) for part in split(left)]
    parts = jnp.concatenate([high, high, middle, high, middle, low], axis=0)
    return parts.T.astype(BF16)


def times(stacked, right):
    high, middle, low = split(right)
    parts = jnp.concatenate([high, middle, high, low, middle, high], axis=0)
    return jnp.dot(stacked, parts, preferred_element_type=F32)


def gram_parts(left, right):
    size, width = left.shape
    filler = jnp.zeros((LANES - 3 * size, width), BF16)
    every = lax.dot_general(
        jnp.concatenate(split(left), axis=0),
        jnp.concatenate([*split(right), filler], axis=0),
        (((1,), (1,)), ((), ())),
        preferred_element_type=F32,
    )
    return every[2 * size :] + every[size : 2 * size] + every[:size]


def symmetric_parts(left, right):
    return 0.5 * (gram_parts(left, right) + gram_parts(right, left))


def finish(parts, place=0):
    size = parts.shape[0]

    def block(index):
        shift = (place - index) * size % LANES
        return pltpu.roll(parts, shift, 1) if shift else parts

    return block(2) + block(1) + block(0)


def pack(wide):
    rows = wide.shape[0]
    folds = LANES // rows
    height = rows // folds
    lanes = lax.broadcasted_iota(jnp.int32, wide.shape, 1)
    wide = jnp.where(lanes < rows, wide, 0.0)
    total = wide[:height]
    for i in range(1, folds):
        total = total + pltpu.roll(wide[i * height : (i + 1) * height], i * rows, 1)
    return total


def unpack(folded, size, place=0):
    parts = []
    for i in range(LANES // size):
        shift = (place - i) * size % LANES
        parts.append(pltpu.roll(folded, shift, 1) if shift else folded)
    return jnp.concatenate(parts, axis=0)


def solve_wide(target, matrix):
    size = matrix.shape[0]
    row_ids = lax.broadcasted_iota(jnp.int32, (size, LANES), 0)
    lane_ids = lax.broadcasted_iota(jnp.int32, (size, LANES), 1)
    work = jnp.where(lane_ids < size, target, matrix)
    for base in range(0, size, PIVOTS):
        columns = [
            jnp.broadcast_to(work[:, size + base + i : size + base + i + 1], (size, LANES))
            for i in range(PIVOTS)
        ]
        for i in range(PIVOTS):
            pivot = base + i
            here = row_ids == pivot
            inverse = 1.0 / columns[i][pivot : pivot + 1, :]
            row = work[pivot : pivot + 1, :] * inverse
            work = jnp.where(here, row, work - columns[i] * row)
            for later in range(i + 1, PIVOTS):
                entry = columns[later][pivot : pivot + 1, :] * inverse
                columns[later] = jnp.where(here, entry, columns[later] - columns[i] * entry)
    return work


def add_up(values):
    values = list(values)
    while len(values) > 1:
        pairs = [values[i] + values[i + 1] for i in range(0, len(values) - 1, 2)]
        values = pairs + values[len(values) - len(values) % 2 :]
    return values[0]


def add_tiles(rows_dev, lists, tiles, first_tile, start, stop, total):
    rows_ref, cols_ref = lists
    tile = total.shape[1]
    slots = rows_ref.shape[0]
    blocks = rows_dev // tile
    row_place = lax.axis_index("row")
    col_place = lax.axis_index("col")
    col_devices = lax.axis_size("col")
    row_blocks = col_devices * blocks

    def place(slot):
        row = rows_ref[slot]
        column = cols_ref[slot]
        side = lax.rem(row // blocks + col_devices - col_place, col_devices)
        owner = column // (blocks * col_devices)
        column_at = (owner ^ row_place) * blocks + lax.rem(column, blocks)
        return column_at * row_blocks + side * blocks + lax.rem(row, blocks)

    def add(slot, at):
        value = total[at] + tiles[slot - first_tile].astype(F32)
        following = place(jnp.minimum(slot + 1, slots - 1))
        total[at] = value
        return following

    lax.fori_loop(start, stop, add, place(start))


def copy_lists(hbm_refs, smem_refs, sems):
    copies = [
        pltpu.make_async_copy(source, target, sems.at[i])
        for i, (source, target) in enumerate(zip(hbm_refs, smem_refs))
    ]
    for copy in copies:
        copy.start()
    return copies


def gather_kernel(rows_dev, count_ref, rows_hbm, cols_hbm, tiles_ref, total, rest, *scratch):
    held, rows_ref, cols_ref, sems, list_sems = scratch
    live = count_ref[0]
    half = held.shape[0]
    slots, tile = tiles_ref.shape[:2]
    chunk = -(-half // CHUNKS)
    lists = copy_lists((rows_hbm, cols_hbm), (rows_ref, cols_ref), list_sems)
    copies = []
    for c in range(CHUNKS):
        part = pl.ds(c * chunk, min(chunk, half - c * chunk))
        copies.append(pltpu.make_async_copy(tiles_ref.at[part], held.at[part], sems.at[c]))

        @pl.when(c * chunk < live)
        def _():
            copies[c].start()

    last = pltpu.make_async_copy(tiles_ref.at[pl.ds(half, slots - half)], rest, sems.at[CHUNKS])

    @pl.when(half < live)
    def _():
        last.start()

    def clear(index, carry):
        total[index] = jnp.zeros((tile, tile), F32)
        return carry

    lax.fori_loop(0, total.shape[0], clear, 0, unroll=4)
    for copy in lists:
        copy.wait()
    for c in range(CHUNKS):
        start, stop = c * chunk, min((c + 1) * chunk, half)

        @pl.when(start < live)
        def _():
            copies[c].wait()
            add_tiles(
                rows_dev, (rows_ref, cols_ref), held, 0, start, jnp.minimum(live, stop), total
            )

    @pl.when(half < live)
    def _():
        last.wait()


def dense_kernel(
    rows_dev, count_ref, rows_hbm, cols_hbm, rest, total_in, joined_ref, out_ref, total, *scratch
):
    rows_ref, cols_ref, list_sems = scratch
    live = count_ref[0]
    half = rows_ref.shape[0] - rest.shape[0]
    tile = total.shape[1]
    row_blocks = out_ref.shape[2] // tile

    @pl.when(half < live)
    def _():
        lists = copy_lists((rows_hbm, cols_hbm), (rows_ref, cols_ref), list_sems)
        for copy in lists:
            copy.wait()
        add_tiles(rows_dev, (rows_ref, cols_ref), rest, half, half, live, total)

    def part(index, carry):
        start = pl.multiple_of(index * tile, tile)
        for b in range(row_blocks):
            value = total[index * row_blocks + b].T
            high = value.astype(BF16)
            low = (value - high.astype(F32)).astype(BF16)
            out_ref[0, pl.ds(start, tile), pl.ds(b * tile, tile)] = high
            out_ref[1, pl.ds(start, tile), pl.ds(b * tile, tile)] = low
        return carry

    lax.fori_loop(0, total.shape[0] // row_blocks, part, 0)


def join_kernel(*refs):
    for k, ref in enumerate(reversed(refs[:-2])):
        refs[-1][k] = ref[...]


def apply_dense(directions, matrix):
    rounded = jnp.concatenate([direction.astype(BF16) for direction in directions], axis=1)
    high, low = [
        jnp.dot(rounded, matrix[part], preferred_element_type=F32) for part in range(2)
    ]
    return high + low


def first_kernel(even_ref, odd_ref, matrix, out_ref, blocks_ref):
    pieces = blocks_ref.shape[0]
    values = [(odd_ref if k % 2 else even_ref)[k // 2] for k in range(pieces)]
    for k, value in enumerate(values):
        blocks_ref[k] = value
    rows = 2 * values[0].shape[1]
    joined = jnp.concatenate(values, axis=1)
    out_ref[:, rows:] = gram_parts(joined, joined)
    out_ref[:, :rows] = apply_dense(values, matrix)


def collect_kernel(near_ref, far_ref, residual_ref, direction_ref):
    pieces = near_ref.shape[0]
    for k in range(pieces):
        residual_ref[0, k] = near_ref[k]
        residual_ref[1, k] = far_ref[k]
        direction_ref[k] = near_ref[k]
    direction_ref[pieces] = far_ref[0]


def add_halves(mine_ref, other_ref, width):
    near = mine_ref[:, :width] + other_ref[:, width : 2 * width]
    far = mine_ref[:, width : 2 * width] + other_ref[:, :width]
    return near, far


def image_kernel(first, mine_ref, other_ref, near_ref, far_ref, *refs):
    out_ref, norm_ref = refs[1:3] if first else (refs[0], None)
    core = lax.axis_index("col")
    size, width = near_ref.shape[1:]
    near, far = add_halves(mine_ref, other_ref, width)
    if first:
        norm_ref[...] = finish(mine_ref[:, 2 * width :] + other_ref[:, 2 * width :])
    parts = width // LANES
    for i in range(parts):
        lanes = slice(i * LANES, (i + 1) * LANES)
        for place, half in ((core, near), (1 - core, far)):
            at = pl.multiple_of((place * parts + i) * size, size)
            out_ref[pl.ds(at, size)] = half[:, lanes]
    products = symmetric_parts(near, near_ref[0]) + symmetric_parts(
        far, far_ref[far_ref.shape[0] - 1]
    )
    out_ref[2 * parts * size :] = pack(finish(products))


def inverse_kernel(norm_ref, out_ref):
    norm = norm_ref[...]
    size = norm.shape[0]
    norm = 0.5 * (norm + jnp.concatenate([norm[:, :size].T, norm[:, size:]], axis=1))
    unit = lax.broadcasted_iota(jnp.int32, norm.shape, 0) == lax.broadcasted_iota(
        jnp.int32, norm.shape, 1
    )
    out_ref[...] = solve_wide(jnp.where(unit, 1.0, 0.0), pltpu.roll(norm, size, 1))


def pick(refs, places, core, rows):
    if places[0] == places[1]:
        return refs[places[0]][rows]
    return jnp.where(core == 0, refs[places[0]][rows], refs[places[1]][rows])


def step_kernel(places, with_solution, last, *refs):
    used = 1 + max(max(pair) for pair in places)
    images, refs = refs[:used], refs[used:]
    direction_ref, residual_ref, norm_ref, inverse_ref, matrix = refs[:5]
    refs = refs[5:]
    if with_solution:
        solution_ref, refs = refs[0], refs[1:]
    out_ref, new_direction, new_residual, new_norm, new_solution = refs
    core = lax.axis_index("col")
    pieces = len(places)
    size, width = direction_ref.shape[1:]
    parts = width // LANES

    def image(k, half):
        found = []
        for i in range(parts):
            at = pl.multiple_of((half * parts + i) * size, size)
            found.append(pick(images, places[k], core, pl.ds(at, size)))
        return jnp.concatenate(found, axis=1)

    behind = slice(2 * parts * size, None)
    products = add_up([pick(images, pair, core, behind) for pair in places])
    alpha = stack(solve_wide(norm_ref[...], unpack(products, size, 1))[:, :size])
    residuals = [
        [residual_ref[side, k] - times(alpha, image(k, half)) for k in range(pieces)]
        for side, half in enumerate((core, 1 - core))
    ]
    joined = [jnp.concatenate(values, axis=1) for values in residuals]
    next_norm = finish(gram_parts(joined[0], joined[0]) + gram_parts(joined[1], joined[1]))
    new_norm[...] = next_norm
    step = times(alpha, direction_ref[0])
    new_solution[...] = solution_ref[...] + step if with_solution else step
    beta = stack(mul(inverse_ref[:, :size], next_norm[:, :size]))
    directions = [
        residual + times(beta, direction_ref[k])
        for k, residual in enumerate(residuals[0] + residuals[1][:1])
    ]
    if last:
        new_residual[...] = residuals[0][0]
        new_direction[0] = directions[0]
        new_direction[1] = directions[pieces]
    else:
        for k in range(pieces):
            new_residual[0, k] = residuals[0][k]
            new_residual[1, k] = residuals[1][k]
        for k in range(pieces + 1):
            new_direction[k] = directions[k]
    out_ref[...] = apply_dense(directions[:pieces], matrix)


def last_image_kernel(mine_ref, other_ref, direction_ref, near_ref, gram_ref):
    near, far = add_halves(mine_ref, other_ref, direction_ref.shape[2])
    near_ref[...] = near
    products = symmetric_parts(near, direction_ref[0]) + symmetric_parts(far, direction_ref[1])
    gram_ref[...] = pack(finish(products))


def last_kernel(places, *refs):
    used = 1 + max(max(pair) for pair in places)
    image_ref, direction_ref, residual_ref, norm_ref, solution_ref = refs[used:-2]
    new_solution, new_residual = refs[-2:]
    core = lax.axis_index("col")
    size = image_ref.shape[0]
    products = add_up([pick(refs, pair, core, slice(None)) for pair in places])
    alpha = stack(solve_wide(norm_ref[...], unpack(products, size, 1))[:, :size])
    new_solution[...] = solution_ref[...] + times(alpha, direction_ref[0])
    new_residual[...] = residual_ref[...] - times(alpha, image_ref[...])


def shape(*dims, dtype=F32):
    return jax.ShapeDtypeStruct(dims, dtype)


def per_device(tiles, tile_rows, tile_cols, tile_count, signs, vertex_weight, column_scale):
    sketch, rows_dev = signs.shape
    tile = tiles.shape[1]
    pieces = lax.axis_size("row")
    col_devices = lax.axis_size("col")
    group = col_devices * rows_dev
    depth = pieces * rows_dev

    def swap(value, mask):
        return lax.ppermute(value, "row", [(i, i ^ mask) for i in range(pieces)])

    def across(value):
        return lax.ppermute(
            value, "col", [(i, (i + 1) % col_devices) for i in range(col_devices)]
        )

    def exchange(value):
        if pieces != 8:
            found = [value] + [swap(value, k) for k in range(1, pieces)]
            return found, [(k, k) for k in range(pieces)]
        shares = ((7, 4), (3, 5), (2, 6), (1, 1))
        fetched = []
        passed = []
        places = {0: (0, 0)}
        for turn, masks in enumerate(shares, 1):
            pairs = [
                (i * 2 + core, (i ^ mask) * 2 + core)
                for core, mask in enumerate(masks)
                for i in range(pieces)
            ]
            fetched.append(lax.ppermute(value, ("row", "col"), pairs))
            if masks[0] == masks[1]:
                places[masks[0]] = (turn, turn)
            else:
                passed.append(across(fetched[-1]))
                places[masks[0]] = (turn, turn + len(shares))
                places[masks[1]] = (turn + len(shares), turn)
        return [value, *fetched, *passed], [places[k] for k in range(pieces)]

    right_side = signs.astype(F32) * vertex_weight[None, :] * column_scale[:, None]
    far_side = across(right_side)[None]
    even = [right_side] + [swap(right_side, k) for k in range(2, pieces, 2)]

    matrix = shape(2, depth, group, dtype=BF16)
    total = shape(depth // tile * (group // tile), tile, tile)
    slots = tiles.shape[0]
    half = slots // 2
    rest = shape(slots - half, tile, tile, dtype=BF16)
    lists = [pltpu.with_memory_space_constraint(x, pltpu.HBM) for x in (tile_rows, tile_cols)]
    lists_scratch = [pltpu.SMEM(x.shape, jnp.int32) for x in lists]
    cost = pl.CostEstimate(
        flops=4 * tiles.size, bytes_accessed=4 * tiles.size, transcendentals=0
    )
    blocks_sum, others = pl.pallas_call(
        functools.partial(gather_kernel, rows_dev),
        out_shape=(total, rest),
        in_specs=[SMEM] + [HBM] * 3,
        out_specs=(VMEM, VMEM),
        scratch_shapes=[
            pltpu.VMEM((half, tile, tile), BF16),
            *lists_scratch,
            pltpu.SemaphoreType.DMA((CHUNKS + 1,)),
            pltpu.SemaphoreType.DMA((len(lists),)),
        ],
        compiler_params=params(tiles, total),
        cost_estimate=cost,
        name="gather",
    )(tile_count, *lists, pltpu.with_memory_space_constraint(tiles, pltpu.HBM))
    joined = shape(pieces // 2, sketch, rows_dev)
    even = pl.pallas_call(
        join_kernel,
        out_shape=joined,
        in_specs=[VMEM] * (pieces // 2) + [ANY],
        out_specs=VMEM,
        compiler_params=params(joined, joined),
        name="join",
    )(*reversed(even), blocks_sum)
    odd = swap(even, 1)
    dense, _ = pl.pallas_call(
        functools.partial(dense_kernel, rows_dev),
        out_shape=(matrix, total),
        in_specs=[SMEM] + [HBM] * 2 + [VMEM, VMEM, ANY],
        out_specs=(VMEM, VMEM),
        scratch_shapes=[*lists_scratch, pltpu.SemaphoreType.DMA((len(lists),))],
        input_output_aliases={4: 1},
        compiler_params=params(rest, total, total, matrix),
        cost_estimate=cost,
        name="dense",
    )(tile_count, *lists, others, blocks_sum, even)

    held = shape(2, pieces, sketch, rows_dev)
    state = shape(pieces + 1, sketch, rows_dev)
    small = shape(sketch, LANES)
    piece = shape(sketch, rows_dev)
    packed = shape(sketch * sketch // LANES, LANES)
    payload = shape(2 * sketch * (rows_dev // LANES) + packed.shape[0], LANES)

    partial_sum, blocks = pl.pallas_call(
        first_kernel,
        out_shape=(shape(sketch, group + LANES), shape(pieces, sketch, rows_dev)),
        in_specs=[VMEM] * 3,
        out_specs=(VMEM, VMEM),
        compiler_params=params(matrix, state, state),
        name="first",
    )(even, odd, dense)
    norm = None
    solution = None
    direction = None
    for iteration in range(ITERS - 1):
        first = iteration == 0
        last = iteration == ITERS - 2
        sums = (partial_sum, across(partial_sum))
        given = (even, far_side, blocks) if first else (direction, direction)
        outs = pl.pallas_call(
            functools.partial(image_kernel, first),
            out_shape=(payload, small, blocks) if first else (payload,),
            in_specs=[VMEM] * 4 + [ANY] * (len(given) - 2),
            out_specs=(VMEM, VMEM, ANY) if first else (VMEM,),
            input_output_aliases={4: 2} if first else {},
            compiler_params=params(state, payload),
            name="image",
        )(*sums, *given)
        if first:
            norm, blocks = outs[1:]
            residual, direction = pl.pallas_call(
                collect_kernel,
                out_shape=(held, state),
                in_specs=[VMEM] * 2,
                out_specs=(VMEM, VMEM),
                compiler_params=params(held, held, state),
                name="collect",
            )(blocks, across(blocks))
        found, places = exchange(outs[0])
        inverse = pl.pallas_call(
            inverse_kernel,
            out_shape=small,
            in_specs=[VMEM],
            out_specs=VMEM,
            compiler_params=params(),
            name="inverse",
        )(norm)
        given = () if first else (solution,)
        partial_sum, direction, residual, norm, solution = pl.pallas_call(
            functools.partial(step_kernel, places, not first, last),
            out_shape=(
                shape(sketch, group),
                shape(2, sketch, rows_dev) if last else state,
                piece if last else held,
                small,
                piece,
            ),
            in_specs=[VMEM] * (len(found) + 5 + len(given)),
            out_specs=(VMEM,) * 5,
            compiler_params=params(matrix, held, held, held, held, state),
            name="step",
        )(*found, direction, residual, norm, inverse, dense, *given)
    near, gram = pl.pallas_call(
        last_image_kernel,
        out_shape=(piece, packed),
        in_specs=[VMEM] * 3,
        out_specs=(VMEM, VMEM),
        compiler_params=params(state),
        name="last_image",
    )(partial_sum, across(partial_sum), direction)
    found, places = exchange(gram)
    return pl.pallas_call(
        functools.partial(last_kernel, places),
        out_shape=(piece, piece),
        in_specs=[VMEM] * (len(found) + 5),
        out_specs=(VMEM, VMEM),
        compiler_params=params(state, state),
        name="last",
    )(*found, near, direction, residual, norm, solution)


def solution(mesh):
    return jax.shard_map(
        per_device,
        mesh=mesh,
        in_specs=(
            P(("row", "col"), None, None),
            P(("row", "col")),
            P(("row", "col")),
            P(("row", "col")),
            P("rhs", ("row", "col")),
            P(("row", "col")),
            P("rhs"),
        ),
        out_specs=(P("rhs", ("row", "col")), P("rhs", ("row", "col"))),
        check_vma=False,
    )
```

```python
import functools

import jax
import jax.numpy as jnp
from jax import lax
from jax.experimental import pallas as pl
from jax.experimental.pallas import tpu as pltpu
from jax.sharding import PartitionSpec as P

ITERS = 3
LANES = 128
SUBLANES = 8
PIVOTS = 8
CHUNKS = 5
F32 = jnp.float32
BF16 = jnp.bfloat16
SPARE_BYTES = 4 * 1024 * 1024

VMEM = pl.BlockSpec(memory_space=pltpu.VMEM)
SMEM = pl.BlockSpec(memory_space=pltpu.SMEM)
HBM = pl.BlockSpec(memory_space=pltpu.HBM)
ANY = pl.BlockSpec(memory_space=pl.ANY)


def params(*arrays):
    used = sum(a.size * jnp.dtype(a.dtype).itemsize for a in arrays)
    return pltpu.CompilerParams(vmem_limit_bytes=used + SPARE_BYTES)


def split(value):
    high = value.astype(BF16)
    rest = value - high.astype(F32)
    middle = rest.astype(BF16)
    low = (rest - middle.astype(F32)).astype(BF16)
    return high, middle, low


def mul(left, right):
    return jnp.dot(left, right, precision=lax.Precision.HIGHEST, preferred_element_type=F32)


def stack(left):
    high, middle, low = [part.astype(F32) for part in split(left)]
    parts = jnp.concatenate([high, high, middle, high, middle, low], axis=0)
    return parts.T.astype(BF16)


def times(stacked, right):
    high, middle, low = split(right)
    parts = jnp.concatenate([high, middle, high, low, middle, high], axis=0)
    return jnp.dot(stacked, parts, preferred_element_type=F32)


def gram_parts(left, right):
    size, width = left.shape
    filler = jnp.zeros((LANES - 3 * size, width), BF16)
    every = lax.dot_general(
        jnp.concatenate(split(left), axis=0),
        jnp.concatenate([*split(right), filler], axis=0),
        (((1,), (1,)), ((), ())),
        preferred_element_type=F32,
    )
    return every[2 * size :] + every[size : 2 * size] + every[:size]


def symmetric_parts(left, right):
    return 0.5 * (gram_parts(left, right) + gram_parts(right, left))


def finish(parts, place=0):
    size = parts.shape[0]

    def block(index):
        shift = (place - index) * size % LANES
        return pltpu.roll(parts, shift, 1) if shift else parts

    return block(2) + block(1) + block(0)


def pack(wide):
    rows = wide.shape[0]
    folds = LANES // rows
    height = rows // folds
    lanes = lax.broadcasted_iota(jnp.int32, wide.shape, 1)
    wide = jnp.where(lanes < rows, wide, 0.0)
    total = wide[:height]
    for i in range(1, folds):
        total = total + pltpu.roll(wide[i * height : (i + 1) * height], i * rows, 1)
    return total


def unpack(folded, size, place=0):
    parts = []
    for i in range(LANES // size):
        shift = (place - i) * size % LANES
        parts.append(pltpu.roll(folded, shift, 1) if shift else folded)
    return jnp.concatenate(parts, axis=0)


def solve_wide(target, matrix):
    size = matrix.shape[0]
    groups = (size // SUBLANES, SUBLANES, LANES)
    row_ids = (
        lax.broadcasted_iota(jnp.int32, groups, 0) * SUBLANES
        + lax.broadcasted_iota(jnp.int32, groups, 1)
    )
    lane_ids = lax.broadcasted_iota(jnp.int32, (size, LANES), 1)
    work = jnp.where(lane_ids < size, target, matrix).reshape(groups)
    scale = jnp.zeros(groups, F32)

    def spread(value, row):
        at = row % SUBLANES
        return jnp.broadcast_to(value[row // SUBLANES, at : at + 1], (SUBLANES, LANES))

    for base in range(size, 2 * size, PIVOTS):
        columns = [
            jnp.broadcast_to(work[:, :, base + i : base + i + 1], groups) for i in range(PIVOTS)
        ]
        for i in range(PIVOTS):
            pivot = base - size + i
            here = row_ids == pivot
            inverse = pltpu.reciprocal(spread(columns[i], pivot), full_range=False)
            factors = jnp.where(here, 0.0, columns[i])
            work = work - factors * (spread(work, pivot) * inverse)[None]
            scale = jnp.where(here, inverse[None], scale)
            for later in range(i + 1, PIVOTS):
                entry = spread(columns[later], pivot) * inverse
                columns[later] = columns[later] - factors * entry[None]
    return (work * scale).reshape(size, LANES)


def add_up(values):
    values = list(values)
    while len(values) > 1:
        pairs = [values[i] + values[i + 1] for i in range(0, len(values) - 1, 2)]
        values = pairs + values[len(values) - len(values) % 2 :]
    return values[0]


def add_tiles(rows_dev, lists, tiles, first_tile, start, stop, total):
    rows_ref, cols_ref = lists
    tile = total.shape[1]
    slots = rows_ref.shape[0]
    blocks = rows_dev // tile
    row_place = lax.axis_index("row")
    col_place = lax.axis_index("col")
    col_devices = lax.axis_size("col")
    row_blocks = col_devices * blocks

    def place(slot):
        row = rows_ref[slot]
        column = cols_ref[slot]
        side = lax.rem(row // blocks + col_devices - col_place, col_devices)
        owner = column // (blocks * col_devices)
        column_at = (owner ^ row_place) * blocks + lax.rem(column, blocks)
        return column_at * row_blocks + side * blocks + lax.rem(row, blocks)

    def add(slot, at):
        value = total[at] + tiles[slot - first_tile].astype(F32)
        following = place(jnp.minimum(slot + 1, slots - 1))
        total[at] = value
        return following

    lax.fori_loop(start, stop, add, place(start))


def copy_lists(hbm_refs, smem_refs, sems):
    copies = [
        pltpu.make_async_copy(source, target, sems.at[i])
        for i, (source, target) in enumerate(zip(hbm_refs, smem_refs))
    ]
    for copy in copies:
        copy.start()
    return copies


def gather_kernel(rows_dev, count_ref, rows_hbm, cols_hbm, tiles_ref, total, rest, *scratch):
    held, rows_ref, cols_ref, sems, list_sems = scratch
    live = count_ref[0]
    half = held.shape[0]
    slots, tile = tiles_ref.shape[:2]
    chunk = -(-half // CHUNKS)
    lists = copy_lists((rows_hbm, cols_hbm), (rows_ref, cols_ref), list_sems)
    copies = []
    for c in range(CHUNKS):
        part = pl.ds(c * chunk, min(chunk, half - c * chunk))
        copies.append(pltpu.make_async_copy(tiles_ref.at[part], held.at[part], sems.at[c]))

        @pl.when(c * chunk < live)
        def _():
            copies[c].start()

    last = pltpu.make_async_copy(tiles_ref.at[pl.ds(half, slots - half)], rest, sems.at[CHUNKS])

    @pl.when(half < live)
    def _():
        last.start()

    def clear(index, carry):
        total[index] = jnp.zeros((tile, tile), F32)
        return carry

    lax.fori_loop(0, total.shape[0], clear, 0, unroll=4)
    for copy in lists:
        copy.wait()
    for c in range(CHUNKS):
        start, stop = c * chunk, min((c + 1) * chunk, half)

        @pl.when(start < live)
        def _():
            copies[c].wait()
            add_tiles(
                rows_dev, (rows_ref, cols_ref), held, 0, start, jnp.minimum(live, stop), total
            )

    @pl.when(half < live)
    def _():
        last.wait()


def dense_kernel(
    rows_dev, count_ref, rows_hbm, cols_hbm, rest, total_in, joined_ref, out_ref, total, *scratch
):
    rows_ref, cols_ref, list_sems = scratch
    live = count_ref[0]
    half = rows_ref.shape[0] - rest.shape[0]
    tile = total.shape[1]
    row_blocks = out_ref.shape[2] // tile

    @pl.when(half < live)
    def _():
        lists = copy_lists((rows_hbm, cols_hbm), (rows_ref, cols_ref), list_sems)
        for copy in lists:
            copy.wait()
        add_tiles(rows_dev, (rows_ref, cols_ref), rest, half, half, live, total)

    def part(index, carry):
        start = pl.multiple_of(index * tile, tile)
        for b in range(row_blocks):
            value = total[index * row_blocks + b].T
            high = value.astype(BF16)
            low = (value - high.astype(F32)).astype(BF16)
            out_ref[0, pl.ds(start, tile), pl.ds(b * tile, tile)] = high
            out_ref[1, pl.ds(start, tile), pl.ds(b * tile, tile)] = low
        return carry

    lax.fori_loop(0, total.shape[0] // row_blocks, part, 0)


def join_kernel(*refs):
    for k, ref in enumerate(reversed(refs[:-2])):
        refs[-1][k] = ref[...]


def apply_dense(directions, matrix):
    rounded = jnp.concatenate([direction.astype(BF16) for direction in directions], axis=1)
    high, low = [
        jnp.dot(rounded, matrix[part], preferred_element_type=F32) for part in range(2)
    ]
    return high + low


def first_kernel(even_ref, odd_ref, matrix, out_ref, blocks_ref):
    pieces = blocks_ref.shape[0]
    values = [(odd_ref if k % 2 else even_ref)[k // 2] for k in range(pieces)]
    for k, value in enumerate(values):
        blocks_ref[k] = value
    rows = 2 * values[0].shape[1]
    joined = jnp.concatenate(values, axis=1)
    out_ref[:, rows:] = gram_parts(joined, joined)
    out_ref[:, :rows] = apply_dense(values, matrix)


def collect_kernel(near_ref, far_ref, residual_ref, direction_ref):
    pieces = near_ref.shape[0]
    for k in range(pieces):
        residual_ref[0, k] = near_ref[k]
        residual_ref[1, k] = far_ref[k]
        direction_ref[k] = near_ref[k]
    direction_ref[pieces] = far_ref[0]


def add_halves(mine_ref, other_ref, width):
    near = mine_ref[:, :width] + other_ref[:, width : 2 * width]
    far = mine_ref[:, width : 2 * width] + other_ref[:, :width]
    return near, far


def image_kernel(first, mine_ref, other_ref, near_ref, far_ref, *refs):
    out_ref, norm_ref = refs[1:3] if first else (refs[0], None)
    core = lax.axis_index("col")
    size, width = near_ref.shape[1:]
    near, far = add_halves(mine_ref, other_ref, width)
    if first:
        norm_ref[...] = finish(mine_ref[:, 2 * width :] + other_ref[:, 2 * width :])
    parts = width // LANES
    for i in range(parts):
        lanes = slice(i * LANES, (i + 1) * LANES)
        for place, half in ((core, near), (1 - core, far)):
            at = pl.multiple_of((place * parts + i) * size, size)
            out_ref[pl.ds(at, size)] = half[:, lanes]
    products = symmetric_parts(near, near_ref[0]) + symmetric_parts(
        far, far_ref[far_ref.shape[0] - 1]
    )
    out_ref[2 * parts * size :] = pack(finish(products))


def inverse_kernel(norm_ref, out_ref):
    norm = norm_ref[...]
    size = norm.shape[0]
    norm = 0.5 * (norm + jnp.concatenate([norm[:, :size].T, norm[:, size:]], axis=1))
    unit = lax.broadcasted_iota(jnp.int32, norm.shape, 0) == lax.broadcasted_iota(
        jnp.int32, norm.shape, 1
    )
    out_ref[...] = solve_wide(jnp.where(unit, 1.0, 0.0), pltpu.roll(norm, size, 1))


def pick(refs, places, core, rows):
    if places[0] == places[1]:
        return refs[places[0]][rows]
    return jnp.where(core == 0, refs[places[0]][rows], refs[places[1]][rows])


def step_kernel(places, with_solution, last, *refs):
    used = 1 + max(max(pair) for pair in places)
    images, refs = refs[:used], refs[used:]
    direction_ref, residual_ref, norm_ref, inverse_ref, matrix = refs[:5]
    refs = refs[5:]
    if with_solution:
        solution_ref, refs = refs[0], refs[1:]
    out_ref, new_direction, new_residual, new_norm, new_solution = refs
    core = lax.axis_index("col")
    pieces = len(places)
    size, width = direction_ref.shape[1:]
    parts = width // LANES

    def image(k, half):
        found = []
        for i in range(parts):
            at = pl.multiple_of((half * parts + i) * size, size)
            found.append(pick(images, places[k], core, pl.ds(at, size)))
        return jnp.concatenate(found, axis=1)

    behind = slice(2 * parts * size, None)
    products = add_up([pick(images, pair, core, behind) for pair in places])
    alpha = stack(solve_wide(norm_ref[...], unpack(products, size, 1))[:, :size])
    residuals = [
        [residual_ref[side, k] - times(alpha, image(k, half)) for k in range(pieces)]
        for side, half in enumerate((core, 1 - core))
    ]
    joined = [jnp.concatenate(values, axis=1) for values in residuals]
    next_norm = finish(gram_parts(joined[0], joined[0]) + gram_parts(joined[1], joined[1]))
    new_norm[...] = next_norm
    step = times(alpha, direction_ref[0])
    new_solution[...] = solution_ref[...] + step if with_solution else step
    beta = stack(mul(inverse_ref[:, :size], next_norm[:, :size]))
    directions = [
        residual + times(beta, direction_ref[k])
        for k, residual in enumerate(residuals[0] + residuals[1][:1])
    ]
    if last:
        new_residual[...] = residuals[0][0]
        new_direction[0] = directions[0]
        new_direction[1] = directions[pieces]
    else:
        for k in range(pieces):
            new_residual[0, k] = residuals[0][k]
            new_residual[1, k] = residuals[1][k]
        for k in range(pieces + 1):
            new_direction[k] = directions[k]
    out_ref[...] = apply_dense(directions[:pieces], matrix)


def last_image_kernel(mine_ref, other_ref, direction_ref, near_ref, gram_ref):
    near, far = add_halves(mine_ref, other_ref, direction_ref.shape[2])
    near_ref[...] = near
    products = symmetric_parts(near, direction_ref[0]) + symmetric_parts(far, direction_ref[1])
    gram_ref[...] = pack(finish(products))


def last_kernel(places, *refs):
    used = 1 + max(max(pair) for pair in places)
    image_ref, direction_ref, residual_ref, norm_ref, solution_ref = refs[used:-2]
    new_solution, new_residual = refs[-2:]
    core = lax.axis_index("col")
    size = image_ref.shape[0]
    products = add_up([pick(refs, pair, core, slice(None)) for pair in places])
    alpha = stack(solve_wide(norm_ref[...], unpack(products, size, 1))[:, :size])
    new_solution[...] = solution_ref[...] + times(alpha, direction_ref[0])
    new_residual[...] = residual_ref[...] - times(alpha, image_ref[...])


def shape(*dims, dtype=F32):
    return jax.ShapeDtypeStruct(dims, dtype)


def per_device(tiles, tile_rows, tile_cols, tile_count, signs, vertex_weight, column_scale):
    sketch, rows_dev = signs.shape
    tile = tiles.shape[1]
    pieces = lax.axis_size("row")
    col_devices = lax.axis_size("col")
    group = col_devices * rows_dev
    depth = pieces * rows_dev

    def swap(value, mask):
        return lax.ppermute(value, "row", [(i, i ^ mask) for i in range(pieces)])

    def across(value):
        return lax.ppermute(
            value, "col", [(i, (i + 1) % col_devices) for i in range(col_devices)]
        )

    def exchange(value):
        if pieces != 8:
            found = [value] + [swap(value, k) for k in range(1, pieces)]
            return found, [(k, k) for k in range(pieces)]
        shares = ((7, 5), (3, 6), (2, 4), (1, 1))
        fetched = []
        passed = []
        places = {0: (0, 0)}
        for turn, masks in enumerate(shares, 1):
            pairs = [
                (i * 2 + core, (i ^ mask) * 2 + core)
                for core, mask in enumerate(masks)
                for i in range(pieces)
            ]
            fetched.append(lax.ppermute(value, ("row", "col"), pairs))
            if masks[0] == masks[1]:
                places[masks[0]] = (turn, turn)
            else:
                passed.append(across(fetched[-1]))
                places[masks[0]] = (turn, turn + len(shares))
                places[masks[1]] = (turn + len(shares), turn)
        return [value, *fetched, *passed], [places[k] for k in range(pieces)]

    right_side = signs.astype(F32) * vertex_weight[None, :] * column_scale[:, None]
    far_side = across(right_side)[None]
    even = [right_side] + [swap(right_side, k) for k in range(2, pieces, 2)]

    matrix = shape(2, depth, group, dtype=BF16)
    total = shape(depth // tile * (group // tile), tile, tile)
    slots = tiles.shape[0]
    half = slots // 2
    rest = shape(slots - half, tile, tile, dtype=BF16)
    lists = [pltpu.with_memory_space_constraint(x, pltpu.HBM) for x in (tile_rows, tile_cols)]
    lists_scratch = [pltpu.SMEM(x.shape, jnp.int32) for x in lists]
    cost = pl.CostEstimate(
        flops=4 * tiles.size, bytes_accessed=4 * tiles.size, transcendentals=0
    )
    blocks_sum, others = pl.pallas_call(
        functools.partial(gather_kernel, rows_dev),
        out_shape=(total, rest),
        in_specs=[SMEM] + [HBM] * 3,
        out_specs=(VMEM, VMEM),
        scratch_shapes=[
            pltpu.VMEM((half, tile, tile), BF16),
            *lists_scratch,
            pltpu.SemaphoreType.DMA((CHUNKS + 1,)),
            pltpu.SemaphoreType.DMA((len(lists),)),
        ],
        compiler_params=params(tiles, total),
        cost_estimate=cost,
        name="gather",
    )(tile_count, *lists, pltpu.with_memory_space_constraint(tiles, pltpu.HBM))
    joined = shape(pieces // 2, sketch, rows_dev)
    even = pl.pallas_call(
        join_kernel,
        out_shape=joined,
        in_specs=[VMEM] * (pieces // 2) + [ANY],
        out_specs=VMEM,
        compiler_params=params(joined, joined),
        name="join",
    )(*reversed(even), blocks_sum)
    odd = swap(even, 1)
    dense, _ = pl.pallas_call(
        functools.partial(dense_kernel, rows_dev),
        out_shape=(matrix, total),
        in_specs=[SMEM] + [HBM] * 2 + [VMEM, VMEM, ANY],
        out_specs=(VMEM, VMEM),
        scratch_shapes=[*lists_scratch, pltpu.SemaphoreType.DMA((len(lists),))],
        input_output_aliases={4: 1},
        compiler_params=params(rest, total, total, matrix),
        cost_estimate=cost,
        name="dense",
    )(tile_count, *lists, others, blocks_sum, even)

    held = shape(2, pieces, sketch, rows_dev)
    state = shape(pieces + 1, sketch, rows_dev)
    small = shape(sketch, LANES)
    piece = shape(sketch, rows_dev)
    packed = shape(sketch * sketch // LANES, LANES)
    payload = shape(2 * sketch * (rows_dev // LANES) + packed.shape[0], LANES)

    partial_sum, blocks = pl.pallas_call(
        first_kernel,
        out_shape=(shape(sketch, group + LANES), shape(pieces, sketch, rows_dev)),
        in_specs=[VMEM] * 3,
        out_specs=(VMEM, VMEM),
        compiler_params=params(matrix, state, state),
        name="first",
    )(even, odd, dense)
    norm = None
    solution = None
    direction = None
    for iteration in range(ITERS - 1):
        first = iteration == 0
        last = iteration == ITERS - 2
        sums = (partial_sum, across(partial_sum))
        given = (even, far_side, blocks) if first else (direction, direction)
        outs = pl.pallas_call(
            functools.partial(image_kernel, first),
            out_shape=(payload, small, blocks) if first else (payload,),
            in_specs=[VMEM] * 4 + [ANY] * (len(given) - 2),
            out_specs=(VMEM, VMEM, ANY) if first else (VMEM,),
            input_output_aliases={4: 2} if first else {},
            compiler_params=params(state, payload),
            name="image",
        )(*sums, *given)
        if first:
            norm, blocks = outs[1:]
            residual, direction = pl.pallas_call(
                collect_kernel,
                out_shape=(held, state),
                in_specs=[VMEM] * 2,
                out_specs=(VMEM, VMEM),
                compiler_params=params(held, held, state),
                name="collect",
            )(blocks, across(blocks))
        found, places = exchange(outs[0])
        inverse = pl.pallas_call(
            inverse_kernel,
            out_shape=small,
            in_specs=[VMEM],
            out_specs=VMEM,
            compiler_params=params(),
            name="inverse",
        )(norm)
        given = () if first else (solution,)
        partial_sum, direction, residual, norm, solution = pl.pallas_call(
            functools.partial(step_kernel, places, not first, last),
            out_shape=(
                shape(sketch, group),
                shape(2, sketch, rows_dev) if last else state,
                piece if last else held,
                small,
                piece,
            ),
            in_specs=[VMEM] * (len(found) + 5 + len(given)),
            out_specs=(VMEM,) * 5,
            compiler_params=params(matrix, held, held, held, held, state),
            name="step",
        )(*found, direction, residual, norm, inverse, dense, *given)
    near, gram = pl.pallas_call(
        last_image_kernel,
        out_shape=(piece, packed),
        in_specs=[VMEM] * 3,
        out_specs=(VMEM, VMEM),
        compiler_params=params(state),
        name="last_image",
    )(partial_sum, across(partial_sum), direction)
    found, places = exchange(gram)
    return pl.pallas_call(
        functools.partial(last_kernel, places),
        out_shape=(piece, piece),
        in_specs=[VMEM] * (len(found) + 5),
        out_specs=(VMEM, VMEM),
        compiler_params=params(state, state),
        name="last",
    )(*found, near, direction, residual, norm, solution)


def solution(mesh):
    return jax.shard_map(
        per_device,
        mesh=mesh,
        in_specs=(
            P(("row", "col"), None, None),
            P(("row", "col")),
            P(("row", "col")),
            P(("row", "col")),
            P("rhs", ("row", "col")),
            P(("row", "col")),
            P("rhs"),
        ),
        out_specs=(P("rhs", ("row", "col")), P("rhs", ("row", "col"))),
        check_vma=False,
    )
```

```python
import functools

import jax
import jax.numpy as jnp
from jax import lax
from jax.experimental import pallas as pl
from jax.experimental.pallas import tpu as pltpu
from jax.sharding import PartitionSpec as P

ITERS = 3
LANES = 128
PIVOTS = 8
CHUNKS = 5
F32 = jnp.float32
BF16 = jnp.bfloat16
SPARE_BYTES = 4 * 1024 * 1024

VMEM = pl.BlockSpec(memory_space=pltpu.VMEM)
SMEM = pl.BlockSpec(memory_space=pltpu.SMEM)
HBM = pl.BlockSpec(memory_space=pltpu.HBM)
ANY = pl.BlockSpec(memory_space=pl.ANY)


def params(*arrays):
    used = sum(a.size * jnp.dtype(a.dtype).itemsize for a in arrays)
    return pltpu.CompilerParams(vmem_limit_bytes=used + SPARE_BYTES)


def split(value):
    high = value.astype(BF16)
    rest = value - high.astype(F32)
    middle = rest.astype(BF16)
    low = (rest - middle.astype(F32)).astype(BF16)
    return high, middle, low


def mul(left, right):
    return jnp.dot(left, right, precision=lax.Precision.HIGHEST, preferred_element_type=F32)


def stack(left):
    high, middle, low = [part.astype(F32) for part in split(left)]
    parts = jnp.concatenate([high, high, middle, high, middle, low], axis=0)
    return parts.T.astype(BF16)


def times(stacked, right):
    high, middle, low = split(right)
    parts = jnp.concatenate([high, middle, high, low, middle, high], axis=0)
    return jnp.dot(stacked, parts, preferred_element_type=F32)


def gram_parts(left, right):
    size, width = left.shape
    filler = jnp.zeros((LANES - 3 * size, width), BF16)
    every = lax.dot_general(
        jnp.concatenate(split(left), axis=0),
        jnp.concatenate([*split(right), filler], axis=0),
        (((1,), (1,)), ((), ())),
        preferred_element_type=F32,
    )
    return every[2 * size :] + every[size : 2 * size] + every[:size]


def symmetric_parts(left, right):
    return 0.5 * (gram_parts(left, right) + gram_parts(right, left))


def finish(parts, place=0):
    size = parts.shape[0]

    def block(index):
        shift = (place - index) * size % LANES
        return pltpu.roll(parts, shift, 1) if shift else parts

    return block(2) + block(1) + block(0)


def pack(wide):
    rows = wide.shape[0]
    folds = LANES // rows
    height = rows // folds
    lanes = lax.broadcasted_iota(jnp.int32, wide.shape, 1)
    wide = jnp.where(lanes < rows, wide, 0.0)
    total = wide[:height]
    for i in range(1, folds):
        total = total + pltpu.roll(wide[i * height : (i + 1) * height], i * rows, 1)
    return total


def unpack(folded, size, place=0):
    parts = []
    for i in range(LANES // size):
        shift = (place - i) * size % LANES
        parts.append(pltpu.roll(folded, shift, 1) if shift else folded)
    return jnp.concatenate(parts, axis=0)


def solve_wide(target, matrix):
    size = matrix.shape[0]
    row_ids = lax.broadcasted_iota(jnp.int32, (size, LANES), 0)
    lane_ids = lax.broadcasted_iota(jnp.int32, (size, LANES), 1)
    work = jnp.where(lane_ids < size, target, matrix)
    for base in range(0, size, PIVOTS):
        columns = [
            jnp.broadcast_to(work[:, size + base + i : size + base + i + 1], (size, LANES))
            for i in range(PIVOTS)
        ]
        for i in range(PIVOTS):
            pivot = base + i
            here = row_ids == pivot
            inverse = pltpu.reciprocal(columns[i][pivot : pivot + 1, :], full_range=False)
            row = work[pivot : pivot + 1, :] * inverse
            work = jnp.where(here, row, work - columns[i] * row)
            for later in range(i + 1, PIVOTS):
                entry = columns[later][pivot : pivot + 1, :] * inverse
                columns[later] = jnp.where(here, entry, columns[later] - columns[i] * entry)
    return work


def add_up(values):
    values = list(values)
    while len(values) > 1:
        pairs = [values[i] + values[i + 1] for i in range(0, len(values) - 1, 2)]
        values = pairs + values[len(values) - len(values) % 2 :]
    return values[0]


def add_tiles(rows_dev, lists, tiles, first_tile, start, stop, total):
    rows_ref, cols_ref = lists
    tile = total.shape[1]
    slots = rows_ref.shape[0]
    blocks = rows_dev // tile
    row_place = lax.axis_index("row")
    col_place = lax.axis_index("col")
    col_devices = lax.axis_size("col")
    row_blocks = col_devices * blocks

    def place(slot):
        row = rows_ref[slot]
        column = cols_ref[slot]
        side = lax.rem(row // blocks + col_devices - col_place, col_devices)
        owner = column // (blocks * col_devices)
        column_at = (owner ^ row_place) * blocks + lax.rem(column, blocks)
        return column_at * row_blocks + side * blocks + lax.rem(row, blocks)

    def after(slot):
        return place(jnp.minimum(slot, slots - 1))

    def add(turn, places):
        slot = start + 2 * turn
        values = [tiles[slot + i - first_tile].astype(F32) for i in range(2)]
        following = (after(slot + 2), after(slot + 3))
        for at, value in zip(places, values):
            total[at] = total[at] + value
        return following

    places = lax.fori_loop(0, (stop - start) // 2, add, (after(start), after(start + 1)))

    @pl.when(lax.rem(stop - start, 2) == 1)
    def _():
        total[places[0]] = total[places[0]] + tiles[stop - 1 - first_tile].astype(F32)


def copy_lists(hbm_refs, smem_refs, sems):
    copies = [
        pltpu.make_async_copy(source, target, sems.at[i])
        for i, (source, target) in enumerate(zip(hbm_refs, smem_refs))
    ]
    for copy in copies:
        copy.start()
    return copies


def gather_kernel(rows_dev, count_ref, rows_hbm, cols_hbm, tiles_ref, total, rest, *scratch):
    held, rows_ref, cols_ref, sems, list_sems = scratch
    live = count_ref[0]
    half = held.shape[0]
    slots, tile = tiles_ref.shape[:2]
    chunk = -(-half // CHUNKS)
    lists = copy_lists((rows_hbm, cols_hbm), (rows_ref, cols_ref), list_sems)
    copies = []
    for c in range(CHUNKS):
        part = pl.ds(c * chunk, min(chunk, half - c * chunk))
        copies.append(pltpu.make_async_copy(tiles_ref.at[part], held.at[part], sems.at[c]))

        @pl.when(c * chunk < live)
        def _():
            copies[c].start()

    last = pltpu.make_async_copy(tiles_ref.at[pl.ds(half, slots - half)], rest, sems.at[CHUNKS])

    @pl.when(half < live)
    def _():
        last.start()

    def clear(index, carry):
        total[index] = jnp.zeros((tile, tile), F32)
        return carry

    lax.fori_loop(0, total.shape[0], clear, 0, unroll=4)
    for copy in lists:
        copy.wait()
    for c in range(CHUNKS):
        start, stop = c * chunk, min((c + 1) * chunk, half)

        @pl.when(start < live)
        def _():
            copies[c].wait()
            add_tiles(
                rows_dev, (rows_ref, cols_ref), held, 0, start, jnp.minimum(live, stop), total
            )

    @pl.when(half < live)
    def _():
        last.wait()


def dense_kernel(
    rows_dev, count_ref, rows_hbm, cols_hbm, rest, total_in, joined_ref, out_ref, total, *scratch
):
    rows_ref, cols_ref, list_sems = scratch
    live = count_ref[0]
    half = rows_ref.shape[0] - rest.shape[0]
    tile = total.shape[1]
    row_blocks = out_ref.shape[2] // tile

    @pl.when(half < live)
    def _():
        lists = copy_lists((rows_hbm, cols_hbm), (rows_ref, cols_ref), list_sems)
        for copy in lists:
            copy.wait()
        add_tiles(rows_dev, (rows_ref, cols_ref), rest, half, half, live, total)

    def part(index, carry):
        start = pl.multiple_of(index * tile, tile)
        for b in range(row_blocks):
            value = total[index * row_blocks + b].T
            high = value.astype(BF16)
            low = (value - high.astype(F32)).astype(BF16)
            out_ref[0, pl.ds(start, tile), pl.ds(b * tile, tile)] = high
            out_ref[1, pl.ds(start, tile), pl.ds(b * tile, tile)] = low
        return carry

    lax.fori_loop(0, total.shape[0] // row_blocks, part, 0)


def join_kernel(*refs):
    for k, ref in enumerate(reversed(refs[:-2])):
        refs[-1][k] = ref[...]


def apply_dense(directions, matrix):
    rounded = jnp.concatenate([direction.astype(BF16) for direction in directions], axis=1)
    high, low = [
        jnp.dot(rounded, matrix[part], preferred_element_type=F32) for part in range(2)
    ]
    return high + low


def first_kernel(even_ref, odd_ref, matrix, out_ref, blocks_ref):
    pieces = blocks_ref.shape[0]
    values = [(odd_ref if k % 2 else even_ref)[k // 2] for k in range(pieces)]
    for k, value in enumerate(values):
        blocks_ref[k] = value
    rows = 2 * values[0].shape[1]
    joined = jnp.concatenate(values, axis=1)
    out_ref[:, rows:] = gram_parts(joined, joined)
    out_ref[:, :rows] = apply_dense(values, matrix)


def collect_kernel(near_ref, far_ref, residual_ref, direction_ref):
    pieces = near_ref.shape[0]
    for k in range(pieces):
        residual_ref[0, k] = near_ref[k]
        residual_ref[1, k] = far_ref[k]
        direction_ref[k] = near_ref[k]
    direction_ref[pieces] = far_ref[0]


def add_halves(mine_ref, other_ref, width):
    near = mine_ref[:, :width] + other_ref[:, width : 2 * width]
    far = mine_ref[:, width : 2 * width] + other_ref[:, :width]
    return near, far


def image_kernel(first, mine_ref, other_ref, near_ref, far_ref, *refs):
    out_ref, norm_ref = refs[1:3] if first else (refs[0], None)
    core = lax.axis_index("col")
    size, width = near_ref.shape[1:]
    near, far = add_halves(mine_ref, other_ref, width)
    if first:
        norm_ref[...] = finish(mine_ref[:, 2 * width :] + other_ref[:, 2 * width :])
    parts = width // LANES
    for i in range(parts):
        lanes = slice(i * LANES, (i + 1) * LANES)
        for place, half in ((core, near), (1 - core, far)):
            at = pl.multiple_of((place * parts + i) * size, size)
            out_ref[pl.ds(at, size)] = half[:, lanes]
    products = symmetric_parts(near, near_ref[0]) + symmetric_parts(
        far, far_ref[far_ref.shape[0] - 1]
    )
    out_ref[2 * parts * size :] = pack(finish(products))


def inverse_kernel(norm_ref, out_ref):
    norm = norm_ref[...]
    size = norm.shape[0]
    norm = 0.5 * (norm + jnp.concatenate([norm[:, :size].T, norm[:, size:]], axis=1))
    unit = lax.broadcasted_iota(jnp.int32, norm.shape, 0) == lax.broadcasted_iota(
        jnp.int32, norm.shape, 1
    )
    out_ref[...] = solve_wide(jnp.where(unit, 1.0, 0.0), pltpu.roll(norm, size, 1))


def pick(refs, places, core, rows):
    if places[0] == places[1]:
        return refs[places[0]][rows]
    return jnp.where(core == 0, refs[places[0]][rows], refs[places[1]][rows])


def step_kernel(places, with_solution, last, *refs):
    used = 1 + max(max(pair) for pair in places)
    images, refs = refs[:used], refs[used:]
    direction_ref, residual_ref, norm_ref, inverse_ref, matrix = refs[:5]
    refs = refs[5:]
    if with_solution:
        solution_ref, refs = refs[0], refs[1:]
    out_ref, new_direction, new_residual, new_norm, new_solution = refs
    core = lax.axis_index("col")
    pieces = len(places)
    size, width = direction_ref.shape[1:]
    parts = width // LANES

    def image(k, half):
        found = []
        for i in range(parts):
            at = pl.multiple_of((half * parts + i) * size, size)
            found.append(pick(images, places[k], core, pl.ds(at, size)))
        return jnp.concatenate(found, axis=1)

    behind = slice(2 * parts * size, None)
    products = add_up([pick(images, pair, core, behind) for pair in places])
    alpha = stack(solve_wide(norm_ref[...], unpack(products, size, 1))[:, :size])
    residuals = [
        [residual_ref[side, k] - times(alpha, image(k, half)) for k in range(pieces)]
        for side, half in enumerate((core, 1 - core))
    ]
    joined = [jnp.concatenate(values, axis=1) for values in residuals]
    next_norm = finish(gram_parts(joined[0], joined[0]) + gram_parts(joined[1], joined[1]))
    new_norm[...] = next_norm
    step = times(alpha, direction_ref[0])
    new_solution[...] = solution_ref[...] + step if with_solution else step
    beta = stack(mul(inverse_ref[:, :size], next_norm[:, :size]))
    directions = [
        residual + times(beta, direction_ref[k])
        for k, residual in enumerate(residuals[0] + residuals[1][:1])
    ]
    if last:
        new_residual[...] = residuals[0][0]
        new_direction[0] = directions[0]
        new_direction[1] = directions[pieces]
    else:
        for k in range(pieces):
            new_residual[0, k] = residuals[0][k]
            new_residual[1, k] = residuals[1][k]
        for k in range(pieces + 1):
            new_direction[k] = directions[k]
    out_ref[...] = apply_dense(directions[:pieces], matrix)


def last_image_kernel(mine_ref, other_ref, direction_ref, near_ref, gram_ref):
    near, far = add_halves(mine_ref, other_ref, direction_ref.shape[2])
    near_ref[...] = near
    products = symmetric_parts(near, direction_ref[0]) + symmetric_parts(far, direction_ref[1])
    gram_ref[...] = pack(finish(products))


def last_kernel(places, *refs):
    used = 1 + max(max(pair) for pair in places)
    image_ref, direction_ref, residual_ref, norm_ref, solution_ref = refs[used:-2]
    new_solution, new_residual = refs[-2:]
    core = lax.axis_index("col")
    size = image_ref.shape[0]
    products = add_up([pick(refs, pair, core, slice(None)) for pair in places])
    alpha = stack(solve_wide(norm_ref[...], unpack(products, size, 1))[:, :size])
    new_solution[...] = solution_ref[...] + times(alpha, direction_ref[0])
    new_residual[...] = residual_ref[...] - times(alpha, image_ref[...])


def shape(*dims, dtype=F32):
    return jax.ShapeDtypeStruct(dims, dtype)


def per_device(tiles, tile_rows, tile_cols, tile_count, signs, vertex_weight, column_scale):
    sketch, rows_dev = signs.shape
    tile = tiles.shape[1]
    pieces = lax.axis_size("row")
    col_devices = lax.axis_size("col")
    group = col_devices * rows_dev
    depth = pieces * rows_dev

    def swap(value, mask):
        return lax.ppermute(value, "row", [(i, i ^ mask) for i in range(pieces)])

    def across(value):
        return lax.ppermute(
            value, "col", [(i, (i + 1) % col_devices) for i in range(col_devices)]
        )

    def exchange(value):
        if pieces != 8:
            found = [value] + [swap(value, k) for k in range(1, pieces)]
            return found, [(k, k) for k in range(pieces)]
        shares = ((7, 5), (3, 6), (2, 4), (1, 1))
        fetched = []
        passed = []
        places = {0: (0, 0)}
        for turn, masks in enumerate(shares, 1):
            pairs = [
                (i * 2 + core, (i ^ mask) * 2 + core)
                for core, mask in enumerate(masks)
                for i in range(pieces)
            ]
            fetched.append(lax.ppermute(value, ("row", "col"), pairs))
            if masks[0] == masks[1]:
                places[masks[0]] = (turn, turn)
            else:
                passed.append(across(fetched[-1]))
                places[masks[0]] = (turn, turn + len(shares))
                places[masks[1]] = (turn + len(shares), turn)
        return [value, *fetched, *passed], [places[k] for k in range(pieces)]

    right_side = signs.astype(F32) * vertex_weight[None, :] * column_scale[:, None]
    far_side = across(right_side)[None]
    even = [right_side] + [swap(right_side, k) for k in range(2, pieces, 2)]

    matrix = shape(2, depth, group, dtype=BF16)
    total = shape(depth // tile * (group // tile), tile, tile)
    slots = tiles.shape[0]
    half = slots // 2
    rest = shape(slots - half, tile, tile, dtype=BF16)
    lists = [pltpu.with_memory_space_constraint(x, pltpu.HBM) for x in (tile_rows, tile_cols)]
    lists_scratch = [pltpu.SMEM(x.shape, jnp.int32) for x in lists]
    cost = pl.CostEstimate(
        flops=4 * tiles.size, bytes_accessed=4 * tiles.size, transcendentals=0
    )
    blocks_sum, others = pl.pallas_call(
        functools.partial(gather_kernel, rows_dev),
        out_shape=(total, rest),
        in_specs=[SMEM] + [HBM] * 3,
        out_specs=(VMEM, VMEM),
        scratch_shapes=[
            pltpu.VMEM((half, tile, tile), BF16),
            *lists_scratch,
            pltpu.SemaphoreType.DMA((CHUNKS + 1,)),
            pltpu.SemaphoreType.DMA((len(lists),)),
        ],
        compiler_params=params(tiles, total),
        cost_estimate=cost,
        name="gather",
    )(tile_count, *lists, pltpu.with_memory_space_constraint(tiles, pltpu.HBM))
    joined = shape(pieces // 2, sketch, rows_dev)
    even = pl.pallas_call(
        join_kernel,
        out_shape=joined,
        in_specs=[VMEM] * (pieces // 2) + [ANY],
        out_specs=VMEM,
        compiler_params=params(joined, joined),
        name="join",
    )(*reversed(even), blocks_sum)
    odd = swap(even, 1)
    dense, _ = pl.pallas_call(
        functools.partial(dense_kernel, rows_dev),
        out_shape=(matrix, total),
        in_specs=[SMEM] + [HBM] * 2 + [VMEM, VMEM, ANY],
        out_specs=(VMEM, VMEM),
        scratch_shapes=[*lists_scratch, pltpu.SemaphoreType.DMA((len(lists),))],
        input_output_aliases={4: 1},
        compiler_params=params(rest, total, total, matrix),
        cost_estimate=cost,
        name="dense",
    )(tile_count, *lists, others, blocks_sum, even)

    held = shape(2, pieces, sketch, rows_dev)
    state = shape(pieces + 1, sketch, rows_dev)
    small = shape(sketch, LANES)
    piece = shape(sketch, rows_dev)
    packed = shape(sketch * sketch // LANES, LANES)
    payload = shape(2 * sketch * (rows_dev // LANES) + packed.shape[0], LANES)

    partial_sum, blocks = pl.pallas_call(
        first_kernel,
        out_shape=(shape(sketch, group + LANES), shape(pieces, sketch, rows_dev)),
        in_specs=[VMEM] * 3,
        out_specs=(VMEM, VMEM),
        compiler_params=params(matrix, state, state),
        name="first",
    )(even, odd, dense)
    norm = None
    solution = None
    direction = None
    for iteration in range(ITERS - 1):
        first = iteration == 0
        last = iteration == ITERS - 2
        sums = (partial_sum, across(partial_sum))
        given = (even, far_side, blocks) if first else (direction, direction)
        outs = pl.pallas_call(
            functools.partial(image_kernel, first),
            out_shape=(payload, small, blocks) if first else (payload,),
            in_specs=[VMEM] * 4 + [ANY] * (len(given) - 2),
            out_specs=(VMEM, VMEM, ANY) if first else (VMEM,),
            input_output_aliases={4: 2} if first else {},
            compiler_params=params(state, payload),
            name="image",
        )(*sums, *given)
        if first:
            norm, blocks = outs[1:]
            residual, direction = pl.pallas_call(
                collect_kernel,
                out_shape=(held, state),
                in_specs=[VMEM] * 2,
                out_specs=(VMEM, VMEM),
                compiler_params=params(held, held, state),
                name="collect",
            )(blocks, across(blocks))
        found, places = exchange(outs[0])
        inverse = pl.pallas_call(
            inverse_kernel,
            out_shape=small,
            in_specs=[VMEM],
            out_specs=VMEM,
            compiler_params=params(),
            name="inverse",
        )(norm)
        given = () if first else (solution,)
        partial_sum, direction, residual, norm, solution = pl.pallas_call(
            functools.partial(step_kernel, places, not first, last),
            out_shape=(
                shape(sketch, group),
                shape(2, sketch, rows_dev) if last else state,
                piece if last else held,
                small,
                piece,
            ),
            in_specs=[VMEM] * (len(found) + 5 + len(given)),
            out_specs=(VMEM,) * 5,
            compiler_params=params(matrix, held, held, held, held, state),
            name="step",
        )(*found, direction, residual, norm, inverse, dense, *given)
    near, gram = pl.pallas_call(
        last_image_kernel,
        out_shape=(piece, packed),
        in_specs=[VMEM] * 3,
        out_specs=(VMEM, VMEM),
        compiler_params=params(state),
        name="last_image",
    )(partial_sum, across(partial_sum), direction)
    found, places = exchange(gram)
    return pl.pallas_call(
        functools.partial(last_kernel, places),
        out_shape=(piece, piece),
        in_specs=[VMEM] * (len(found) + 5),
        out_specs=(VMEM, VMEM),
        compiler_params=params(state, state),
        name="last",
    )(*found, near, direction, residual, norm, solution)


def solution(mesh):
    return jax.shard_map(
        per_device,
        mesh=mesh,
        in_specs=(
            P(("row", "col"), None, None),
            P(("row", "col")),
            P(("row", "col")),
            P(("row", "col")),
            P("rhs", ("row", "col")),
            P(("row", "col")),
            P("rhs"),
        ),
        out_specs=(P("rhs", ("row", "col")), P("rhs", ("row", "col"))),
        check_vma=False,
    )
```

```python
import functools

import jax
import jax.numpy as jnp
from jax import lax
from jax.experimental import pallas as pl
from jax.experimental.pallas import tpu as pltpu
from jax.sharding import PartitionSpec as P

ITERS = 3
LANES = 128
PIVOTS = 8
CHUNKS = 5
F32 = jnp.float32
BF16 = jnp.bfloat16
SPARE_BYTES = 4 * 1024 * 1024

VMEM = pl.BlockSpec(memory_space=pltpu.VMEM)
SMEM = pl.BlockSpec(memory_space=pltpu.SMEM)
HBM = pl.BlockSpec(memory_space=pltpu.HBM)
ANY = pl.BlockSpec(memory_space=pl.ANY)


def params(*arrays):
    used = sum(a.size * jnp.dtype(a.dtype).itemsize for a in arrays)
    return pltpu.CompilerParams(vmem_limit_bytes=used + SPARE_BYTES)


def split(value):
    high = value.astype(BF16)
    rest = value - high.astype(F32)
    middle = rest.astype(BF16)
    low = (rest - middle.astype(F32)).astype(BF16)
    return high, middle, low


def mul(left, right):
    return jnp.dot(left, right, precision=lax.Precision.HIGHEST, preferred_element_type=F32)


def stack(left):
    high, middle, low = [part.astype(F32) for part in split(left)]
    parts = jnp.concatenate([high, high, middle, high, middle, low], axis=0)
    return parts.T.astype(BF16)


def times(stacked, right):
    high, middle, low = split(right)
    parts = jnp.concatenate([high, middle, high, low, middle, high], axis=0)
    return jnp.dot(stacked, parts, preferred_element_type=F32)


def gram_parts(left, right):
    size, width = left.shape
    filler = jnp.zeros((LANES - 3 * size, width), BF16)
    every = lax.dot_general(
        jnp.concatenate(split(left), axis=0),
        jnp.concatenate([*split(right), filler], axis=0),
        (((1,), (1,)), ((), ())),
        preferred_element_type=F32,
    )
    return every[2 * size :] + every[size : 2 * size] + every[:size]


def symmetric_parts(left, right):
    return 0.5 * (gram_parts(left, right) + gram_parts(right, left))


def finish(parts, place=0):
    size = parts.shape[0]

    def block(index):
        shift = (place - index) * size % LANES
        return pltpu.roll(parts, shift, 1) if shift else parts

    return block(2) + block(1) + block(0)


def pack(wide):
    rows = wide.shape[0]
    folds = LANES // rows
    height = rows // folds
    lanes = lax.broadcasted_iota(jnp.int32, wide.shape, 1)
    wide = jnp.where(lanes < rows, wide, 0.0)
    total = wide[:height]
    for i in range(1, folds):
        total = total + pltpu.roll(wide[i * height : (i + 1) * height], i * rows, 1)
    return total


def unpack(folded, size, place=0):
    parts = []
    for i in range(LANES // size):
        shift = (place - i) * size % LANES
        parts.append(pltpu.roll(folded, shift, 1) if shift else folded)
    return jnp.concatenate(parts, axis=0)


def solve_wide(target, matrix):
    size = matrix.shape[0]
    row_ids = lax.broadcasted_iota(jnp.int32, (size, LANES), 0)
    lane_ids = lax.broadcasted_iota(jnp.int32, (size, LANES), 1)
    work = jnp.where(lane_ids < size, target, matrix)
    for base in range(0, size, PIVOTS):
        columns = [
            jnp.broadcast_to(work[:, size + base + i : size + base + i + 1], (size, LANES))
            for i in range(PIVOTS)
        ]
        for i in range(PIVOTS):
            pivot = base + i
            here = row_ids == pivot
            inverse = pltpu.reciprocal(columns[i][pivot : pivot + 1, :], full_range=False)
            row = work[pivot : pivot + 1, :] * inverse
            work = jnp.where(here, row, work - columns[i] * row)
            for later in range(i + 1, PIVOTS):
                entry = columns[later][pivot : pivot + 1, :] * inverse
                columns[later] = jnp.where(here, entry, columns[later] - columns[i] * entry)
    return work


def add_up(values):
    values = list(values)
    while len(values) > 1:
        pairs = [values[i] + values[i + 1] for i in range(0, len(values) - 1, 2)]
        values = pairs + values[len(values) - len(values) % 2 :]
    return values[0]


def add_tiles(rows_dev, lists, tiles, first_tile, start, stop, total):
    rows_ref, cols_ref = lists
    tile = total.shape[1]
    slots = rows_ref.shape[0]
    blocks = rows_dev // tile
    row_place = lax.axis_index("row")
    col_place = lax.axis_index("col")
    col_devices = lax.axis_size("col")
    row_blocks = col_devices * blocks

    def place(slot):
        row = rows_ref[slot]
        column = cols_ref[slot]
        side = lax.rem(row // blocks + col_devices - col_place, col_devices)
        owner = column // (blocks * col_devices)
        column_at = (owner ^ row_place) * blocks + lax.rem(column, blocks)
        return column_at * row_blocks + side * blocks + lax.rem(row, blocks)

    def after(slot):
        return place(jnp.minimum(slot, slots - 1))

    def add(turn, places):
        slot = start + 2 * turn
        values = [tiles[slot + i - first_tile].astype(F32) for i in range(2)]
        following = (after(slot + 2), after(slot + 3))
        for at, value in zip(places, values):
            total[at] = total[at] + value
        return following

    places = lax.fori_loop(0, (stop - start) // 2, add, (after(start), after(start + 1)))

    @pl.when(lax.rem(stop - start, 2) == 1)
    def _():
        total[places[0]] = total[places[0]] + tiles[stop - 1 - first_tile].astype(F32)


def copy_lists(hbm_refs, smem_refs, sems):
    copies = [
        pltpu.make_async_copy(source, target, sems.at[i])
        for i, (source, target) in enumerate(zip(hbm_refs, smem_refs))
    ]
    for copy in copies:
        copy.start()
    return copies


def gather_kernel(rows_dev, count_ref, rows_hbm, cols_hbm, tiles_ref, total, rest, *scratch):
    held, rows_ref, cols_ref, sems, list_sems = scratch
    live = count_ref[0]
    half = held.shape[0]
    slots, tile = tiles_ref.shape[:2]
    chunk = -(-half // CHUNKS)
    lists = copy_lists((rows_hbm, cols_hbm), (rows_ref, cols_ref), list_sems)
    copies = []
    for c in range(CHUNKS):
        part = pl.ds(c * chunk, min(chunk, half - c * chunk))
        copies.append(pltpu.make_async_copy(tiles_ref.at[part], held.at[part], sems.at[c]))

        @pl.when(c * chunk < live)
        def _():
            copies[c].start()

    last = pltpu.make_async_copy(tiles_ref.at[pl.ds(half, slots - half)], rest, sems.at[CHUNKS])

    @pl.when(half < live)
    def _():
        last.start()

    def clear(index, carry):
        total[index] = jnp.zeros((tile, tile), F32)
        return carry

    lax.fori_loop(0, total.shape[0], clear, 0, unroll=4)
    for copy in lists:
        copy.wait()
    for c in range(CHUNKS):
        start, stop = c * chunk, min((c + 1) * chunk, half)

        @pl.when(start < live)
        def _():
            copies[c].wait()
            add_tiles(
                rows_dev, (rows_ref, cols_ref), held, 0, start, jnp.minimum(live, stop), total
            )

    @pl.when(half < live)
    def _():
        last.wait()


def dense_kernel(
    rows_dev, count_ref, rows_hbm, cols_hbm, rest, total_in, joined_ref, out_ref, total, *scratch
):
    rows_ref, cols_ref, list_sems = scratch
    live = count_ref[0]
    half = rows_ref.shape[0] - rest.shape[0]
    tile = total.shape[1]
    row_blocks = out_ref.shape[2] // tile

    @pl.when(half < live)
    def _():
        lists = copy_lists((rows_hbm, cols_hbm), (rows_ref, cols_ref), list_sems)
        for copy in lists:
            copy.wait()
        add_tiles(rows_dev, (rows_ref, cols_ref), rest, half, half, live, total)

    def part(index, carry):
        start = pl.multiple_of(index * tile, tile)
        for b in range(row_blocks):
            value = total[index * row_blocks + b].T
            high = value.astype(BF16)
            low = (value - high.astype(F32)).astype(BF16)
            out_ref[0, pl.ds(start, tile), pl.ds(b * tile, tile)] = high
            out_ref[1, pl.ds(start, tile), pl.ds(b * tile, tile)] = low
        return carry

    lax.fori_loop(0, total.shape[0] // row_blocks, part, 0)


def join_kernel(order, *refs):
    for k, ref in zip(order, refs):
        refs[-1][k] = ref[...]


def apply_dense(directions, matrix):
    rounded = jnp.concatenate([direction.astype(BF16) for direction in directions], axis=1)
    high, low = [
        jnp.dot(rounded, matrix[part], preferred_element_type=F32) for part in range(2)
    ]
    return high + low


def first_kernel(even_ref, odd_ref, matrix, out_ref, blocks_ref):
    pieces = blocks_ref.shape[0]
    values = [(odd_ref if k % 2 else even_ref)[k // 2] for k in range(pieces)]
    for k, value in enumerate(values):
        blocks_ref[k] = value
    rows = 2 * values[0].shape[1]
    joined = jnp.concatenate(values, axis=1)
    out_ref[:, rows:] = gram_parts(joined, joined)
    out_ref[:, :rows] = apply_dense(values, matrix)


def collect_kernel(near_ref, far_ref, residual_ref, direction_ref):
    pieces = near_ref.shape[0]
    for k in range(pieces):
        residual_ref[0, k] = near_ref[k]
        residual_ref[1, k] = far_ref[k]
        direction_ref[k] = near_ref[k]
    direction_ref[pieces] = far_ref[0]


def add_halves(mine_ref, other_ref, width):
    near = mine_ref[:, :width] + other_ref[:, width : 2 * width]
    far = mine_ref[:, width : 2 * width] + other_ref[:, :width]
    return near, far


def image_kernel(first, mine_ref, other_ref, near_ref, far_ref, *refs):
    out_ref, norm_ref = refs if first else (refs[0], None)
    core = lax.axis_index("col")
    size, width = near_ref.shape[1:]
    near, far = add_halves(mine_ref, other_ref, width)
    if first:
        norm_ref[...] = finish(mine_ref[:, 2 * width :] + other_ref[:, 2 * width :])
    parts = width // LANES
    for i in range(parts):
        lanes = slice(i * LANES, (i + 1) * LANES)
        for place, half in ((core, near), (1 - core, far)):
            at = pl.multiple_of((place * parts + i) * size, size)
            out_ref[pl.ds(at, size)] = half[:, lanes]
    products = symmetric_parts(near, near_ref[0]) + symmetric_parts(
        far, far_ref[far_ref.shape[0] - 1]
    )
    out_ref[2 * parts * size :] = pack(finish(products))


def inverse_kernel(norm_ref, out_ref):
    norm = norm_ref[...]
    size = norm.shape[0]
    norm = 0.5 * (norm + jnp.concatenate([norm[:, :size].T, norm[:, size:]], axis=1))
    unit = lax.broadcasted_iota(jnp.int32, norm.shape, 0) == lax.broadcasted_iota(
        jnp.int32, norm.shape, 1
    )
    out_ref[...] = solve_wide(jnp.where(unit, 1.0, 0.0), pltpu.roll(norm, size, 1))


def pick(refs, places, core, rows):
    if places[0] == places[1]:
        return refs[places[0]][rows]
    return jnp.where(core == 0, refs[places[0]][rows], refs[places[1]][rows])


def step_kernel(used, places, with_solution, last, *refs):
    images, refs = refs[:used], refs[used:]
    direction_ref, residual_ref, norm_ref, inverse_ref, matrix = refs[:5]
    refs = refs[5:]
    if with_solution:
        solution_ref, refs = refs[0], refs[1:]
    out_ref, new_direction, new_residual, new_norm, new_solution = refs
    core = lax.axis_index("col")
    pieces = len(places)
    size, width = direction_ref.shape[1:]
    parts = width // LANES

    def image(k, half):
        found = []
        for i in range(parts):
            at = pl.multiple_of((half * parts + i) * size, size)
            found.append(pick(images, places[k], core, pl.ds(at, size)))
        return jnp.concatenate(found, axis=1)

    behind = slice(2 * parts * size, None)
    products = add_up([pick(images, pair, core, behind) for pair in places])
    alpha = stack(solve_wide(norm_ref[...], unpack(products, size, 1))[:, :size])
    residuals = [
        [residual_ref[side, k] - times(alpha, image(k, half)) for k in range(pieces)]
        for side, half in enumerate((core, 1 - core))
    ]
    joined = [jnp.concatenate(values, axis=1) for values in residuals]
    next_norm = finish(gram_parts(joined[0], joined[0]) + gram_parts(joined[1], joined[1]))
    new_norm[...] = next_norm
    step = times(alpha, direction_ref[0])
    new_solution[...] = solution_ref[...] + step if with_solution else step
    beta = stack(mul(inverse_ref[:, :size], next_norm[:, :size]))
    directions = [
        residual + times(beta, direction_ref[k])
        for k, residual in enumerate(residuals[0] + residuals[1][:1])
    ]
    if last:
        new_residual[...] = residuals[0][0]
        new_direction[0] = directions[0]
        new_direction[1] = directions[pieces]
    else:
        for k in range(pieces):
            new_residual[0, k] = residuals[0][k]
            new_residual[1, k] = residuals[1][k]
        for k in range(pieces + 1):
            new_direction[k] = directions[k]
    out_ref[...] = apply_dense(directions[:pieces], matrix)


def last_image_kernel(mine_ref, other_ref, direction_ref, near_ref, gram_ref):
    near, far = add_halves(mine_ref, other_ref, direction_ref.shape[2])
    near_ref[...] = near
    products = symmetric_parts(near, direction_ref[0]) + symmetric_parts(far, direction_ref[1])
    gram_ref[...] = pack(finish(products))


def last_kernel(used, places, *refs):
    image_ref, direction_ref, residual_ref, norm_ref, solution_ref = refs[used:-2]
    new_solution, new_residual = refs[-2:]
    core = lax.axis_index("col")
    size = image_ref.shape[0]
    products = add_up([pick(refs, pair, core, slice(None)) for pair in places])
    alpha = stack(solve_wide(norm_ref[...], unpack(products, size, 1))[:, :size])
    new_solution[...] = solution_ref[...] + times(alpha, direction_ref[0])
    new_residual[...] = residual_ref[...] - times(alpha, image_ref[...])


def shape(*dims, dtype=F32):
    return jax.ShapeDtypeStruct(dims, dtype)


def per_device(tiles, tile_rows, tile_cols, tile_count, signs, vertex_weight, column_scale):
    sketch, rows_dev = signs.shape
    tile = tiles.shape[1]
    pieces = lax.axis_size("row")
    col_devices = lax.axis_size("col")
    group = col_devices * rows_dev
    depth = pieces * rows_dev

    def swap(value, mask):
        return lax.ppermute(value, "row", [(i, i ^ mask) for i in range(pieces)])

    def across(value):
        return lax.ppermute(
            value, "col", [(i, (i + 1) % col_devices) for i in range(col_devices)]
        )

    def exchange(value):
        if pieces != 8:
            found = [value] + [swap(value, k) for k in range(1, pieces)]
            return found, [(k, k) for k in range(pieces)]
        turns = ((2, 4), (7, 6), (1, 2))

        def fetch(source, masks):
            pairs = [
                (i * 2 + core, (i ^ mask) * 2 + core)
                for core, mask in enumerate(masks)
                for i in range(pieces)
            ]
            return lax.ppermute(source, ("row", "col"), pairs)

        fetched = [fetch(value, masks) for masks in turns]
        fetched.append(fetch(fetched[0], (1, 1)))
        found = [value, *fetched, *map(across, fetched)]
        places = [(0, 0), (3, 7), (1, 5), (4, 8), (5, 1), (8, 4), (6, 2), (2, 6)]
        return found, places

    right_side = signs.astype(F32) * vertex_weight[None, :] * column_scale[:, None]
    far_side = across(right_side)[None]
    even = [right_side] + [swap(right_side, k) for k in range(2, pieces, 2)]

    matrix = shape(2, depth, group, dtype=BF16)
    total = shape(depth // tile * (group // tile), tile, tile)
    slots = tiles.shape[0]
    half = slots // 2
    rest = shape(slots - half, tile, tile, dtype=BF16)
    lists = [pltpu.with_memory_space_constraint(x, pltpu.HBM) for x in (tile_rows, tile_cols)]
    lists_scratch = [pltpu.SMEM(x.shape, jnp.int32) for x in lists]
    cost = pl.CostEstimate(
        flops=4 * tiles.size, bytes_accessed=4 * tiles.size, transcendentals=0
    )
    blocks_sum, others = pl.pallas_call(
        functools.partial(gather_kernel, rows_dev),
        out_shape=(total, rest),
        in_specs=[SMEM] + [HBM] * 3,
        out_specs=(VMEM, VMEM),
        scratch_shapes=[
            pltpu.VMEM((half, tile, tile), BF16),
            *lists_scratch,
            pltpu.SemaphoreType.DMA((CHUNKS + 1,)),
            pltpu.SemaphoreType.DMA((len(lists),)),
        ],
        compiler_params=params(tiles, total),
        cost_estimate=cost,
        name="gather",
    )(tile_count, *lists, pltpu.with_memory_space_constraint(tiles, pltpu.HBM))
    joined = shape(pieces // 2, sketch, rows_dev)
    order = [*range(pieces // 4, pieces // 2), *range(1, pieces // 4), 0]
    even = pl.pallas_call(
        functools.partial(join_kernel, order),
        out_shape=joined,
        in_specs=[VMEM] * (pieces // 2) + [ANY],
        out_specs=VMEM,
        compiler_params=params(joined, joined),
        name="join",
    )(*[even[k] for k in order], blocks_sum)
    odd = swap(even, 1)
    dense, _ = pl.pallas_call(
        functools.partial(dense_kernel, rows_dev),
        out_shape=(matrix, total),
        in_specs=[SMEM] + [HBM] * 2 + [VMEM, VMEM, ANY],
        out_specs=(VMEM, VMEM),
        scratch_shapes=[*lists_scratch, pltpu.SemaphoreType.DMA((len(lists),))],
        input_output_aliases={4: 1},
        compiler_params=params(rest, total, total, matrix),
        cost_estimate=cost,
        name="dense",
    )(tile_count, *lists, others, blocks_sum, even)

    held = shape(2, pieces, sketch, rows_dev)
    state = shape(pieces + 1, sketch, rows_dev)
    small = shape(sketch, LANES)
    piece = shape(sketch, rows_dev)
    packed = shape(sketch * sketch // LANES, LANES)
    payload = shape(2 * sketch * (rows_dev // LANES) + packed.shape[0], LANES)

    partial_sum, blocks = pl.pallas_call(
        first_kernel,
        out_shape=(shape(sketch, group + LANES), shape(pieces, sketch, rows_dev)),
        in_specs=[VMEM] * 3,
        out_specs=(VMEM, VMEM),
        compiler_params=params(matrix, state, state),
        name="first",
    )(even, odd, dense)
    norm = None
    solution = None
    direction = None
    for iteration in range(ITERS - 1):
        first = iteration == 0
        last = iteration == ITERS - 2
        sums = (partial_sum, across(partial_sum))
        given = (even, far_side) if first else (direction, direction)
        outs = pl.pallas_call(
            functools.partial(image_kernel, first),
            out_shape=(payload, small) if first else (payload,),
            in_specs=[VMEM] * 4,
            out_specs=(VMEM, VMEM) if first else (VMEM,),
            compiler_params=params(state, payload),
            name="image",
        )(*sums, *given)
        found, places = exchange(outs[0])
        if first:
            norm = outs[1]
            residual, direction = pl.pallas_call(
                collect_kernel,
                out_shape=(held, state),
                in_specs=[VMEM] * 2,
                out_specs=(VMEM, VMEM),
                compiler_params=params(held, held, state),
                name="collect",
            )(blocks, across(blocks))
        inverse = pl.pallas_call(
            inverse_kernel,
            out_shape=small,
            in_specs=[VMEM],
            out_specs=VMEM,
            compiler_params=params(),
            name="inverse",
        )(norm)
        given = () if first else (solution,)
        partial_sum, direction, residual, norm, solution = pl.pallas_call(
            functools.partial(step_kernel, len(found), places, not first, last),
            out_shape=(
                shape(sketch, group),
                shape(2, sketch, rows_dev) if last else state,
                piece if last else held,
                small,
                piece,
            ),
            in_specs=[VMEM] * (len(found) + 5 + len(given)),
            out_specs=(VMEM,) * 5,
            compiler_params=params(matrix, held, held, held, held, state),
            name="step",
        )(*found, direction, residual, norm, inverse, dense, *given)
    near, gram = pl.pallas_call(
        last_image_kernel,
        out_shape=(piece, packed),
        in_specs=[VMEM] * 3,
        out_specs=(VMEM, VMEM),
        compiler_params=params(state),
        name="last_image",
    )(partial_sum, across(partial_sum), direction)
    found, places = exchange(gram)
    return pl.pallas_call(
        functools.partial(last_kernel, len(found), places),
        out_shape=(piece, piece),
        in_specs=[VMEM] * (len(found) + 5),
        out_specs=(VMEM, VMEM),
        compiler_params=params(state, state),
        name="last",
    )(*found, near, direction, residual, norm, solution)


def solution(mesh):
    return jax.shard_map(
        per_device,
        mesh=mesh,
        in_specs=(
            P(("row", "col"), None, None),
            P(("row", "col")),
            P(("row", "col")),
            P(("row", "col")),
            P("rhs", ("row", "col")),
            P(("row", "col")),
            P("rhs"),
        ),
        out_specs=(P("rhs", ("row", "col")), P("rhs", ("row", "col"))),
        check_vma=False,
    )
```

```python
import functools

import jax
import jax.numpy as jnp
from jax import lax
from jax.experimental import pallas as pl
from jax.experimental.pallas import tpu as pltpu
from jax.sharding import PartitionSpec as P

ITERS = 3
LANES = 128
PIVOTS = 8
CHUNKS = 5
F32 = jnp.float32
BF16 = jnp.bfloat16
SPARE_BYTES = 4 * 1024 * 1024

VMEM = pl.BlockSpec(memory_space=pltpu.VMEM)
SMEM = pl.BlockSpec(memory_space=pltpu.SMEM)
HBM = pl.BlockSpec(memory_space=pltpu.HBM)
ANY = pl.BlockSpec(memory_space=pl.ANY)


def params(*arrays):
    used = sum(a.size * jnp.dtype(a.dtype).itemsize for a in arrays)
    return pltpu.CompilerParams(vmem_limit_bytes=used + SPARE_BYTES)


def split(value):
    high = value.astype(BF16)
    rest = value - high.astype(F32)
    middle = rest.astype(BF16)
    low = (rest - middle.astype(F32)).astype(BF16)
    return high, middle, low


def mul(left, right):
    return jnp.dot(left, right, precision=lax.Precision.HIGHEST, preferred_element_type=F32)


def stack(left):
    high, middle, low = [part.astype(F32) for part in split(left)]
    parts = jnp.concatenate([high, high, middle, high, middle, low], axis=0)
    return parts.T.astype(BF16)


def times(stacked, right):
    high, middle, low = split(right)
    parts = jnp.concatenate([high, middle, high, low, middle, high], axis=0)
    return jnp.dot(stacked, parts, preferred_element_type=F32)


def gram_parts(left, right):
    size, width = left.shape
    filler = jnp.zeros((LANES - 3 * size, width), BF16)
    every = lax.dot_general(
        jnp.concatenate(split(left), axis=0),
        jnp.concatenate([*split(right), filler], axis=0),
        (((1,), (1,)), ((), ())),
        preferred_element_type=F32,
    )
    return every[2 * size :] + every[size : 2 * size] + every[:size]


def symmetric_parts(left, right):
    return 0.5 * (gram_parts(left, right) + gram_parts(right, left))


def finish(parts, place=0):
    size = parts.shape[0]

    def block(index):
        shift = (place - index) * size % LANES
        return pltpu.roll(parts, shift, 1) if shift else parts

    return block(2) + block(1) + block(0)


def pack(wide):
    rows = wide.shape[0]
    folds = LANES // rows
    height = rows // folds
    lanes = lax.broadcasted_iota(jnp.int32, wide.shape, 1)
    wide = jnp.where(lanes < rows, wide, 0.0)
    total = wide[:height]
    for i in range(1, folds):
        total = total + pltpu.roll(wide[i * height : (i + 1) * height], i * rows, 1)
    return total


def unpack(folded, size, place=0):
    parts = []
    for i in range(LANES // size):
        shift = (place - i) * size % LANES
        parts.append(pltpu.roll(folded, shift, 1) if shift else folded)
    return jnp.concatenate(parts, axis=0)


def solve_wide(target, matrix):
    size = matrix.shape[0]
    row_ids = lax.broadcasted_iota(jnp.int32, (size, LANES), 0)
    lane_ids = lax.broadcasted_iota(jnp.int32, (size, LANES), 1)
    work = jnp.where(lane_ids < size, target, matrix)
    work = work * pltpu.reciprocal(work[:1, size : size + 1], full_range=False)
    for base in range(0, size, PIVOTS):
        columns = [
            jnp.broadcast_to(work[:, size + base + i : size + base + i + 1], (size, LANES))
            for i in range(PIVOTS)
        ]
        for i in range(0, PIVOTS, 2):
            first = base + i
            one, two = columns[i : i + 2]
            here = row_ids == first
            below = row_ids == first + 1
            row, next_row = slice(first, first + 1), slice(first + 1, first + 2)
            a, b, c, d = one[row], two[row], one[next_row], two[next_row]
            inverse = pltpu.reciprocal(a * d - b * c, full_range=False)

            def eliminate(value):
                up, low = value[row], value[next_row]
                up, low = (d * up - b * low) * inverse, (a * low - c * up) * inverse
                rest = value - one * up - two * low
                return jnp.where(here, up, jnp.where(below, low, rest))

            work = eliminate(work)
            for later in range(i + 2, PIVOTS):
                columns[later] = eliminate(columns[later])
    return work


def add_up(values):
    values = list(values)
    while len(values) > 1:
        pairs = [values[i] + values[i + 1] for i in range(0, len(values) - 1, 2)]
        values = pairs + values[len(values) - len(values) % 2 :]
    return values[0]


def add_tiles(rows_dev, lists, tiles, first_tile, start, stop, total):
    rows_ref, cols_ref = lists
    tile = total.shape[1]
    slots = rows_ref.shape[0]
    blocks = rows_dev // tile
    row_place = lax.axis_index("row")
    col_place = lax.axis_index("col")
    col_devices = lax.axis_size("col")
    row_blocks = col_devices * blocks

    def place(slot):
        row = rows_ref[slot]
        column = cols_ref[slot]
        side = lax.rem(row // blocks + col_devices - col_place, col_devices)
        owner = column // (blocks * col_devices)
        column_at = (owner ^ row_place) * blocks + lax.rem(column, blocks)
        return column_at * row_blocks + side * blocks + lax.rem(row, blocks)

    def after(slot):
        return place(jnp.minimum(slot, slots - 1))

    def add(turn, places):
        slot = start + 2 * turn
        values = [tiles[slot + i - first_tile].astype(F32) for i in range(2)]
        following = (after(slot + 2), after(slot + 3))
        for at, value in zip(places, values):
            total[at] = total[at] + value
        return following

    places = lax.fori_loop(0, (stop - start) // 2, add, (after(start), after(start + 1)))

    @pl.when(lax.rem(stop - start, 2) == 1)
    def _():
        total[places[0]] = total[places[0]] + tiles[stop - 1 - first_tile].astype(F32)


def copy_lists(hbm_refs, smem_refs, sems):
    copies = [
        pltpu.make_async_copy(source, target, sems.at[i])
        for i, (source, target) in enumerate(zip(hbm_refs, smem_refs))
    ]
    for copy in copies:
        copy.start()
    return copies


def gather_kernel(rows_dev, count_ref, rows_hbm, cols_hbm, tiles_ref, total, rest, *scratch):
    held, rows_ref, cols_ref, sems, list_sems = scratch
    live = count_ref[0]
    half = held.shape[0]
    slots, tile = tiles_ref.shape[:2]
    chunk = -(-half // CHUNKS)
    lists = copy_lists((rows_hbm, cols_hbm), (rows_ref, cols_ref), list_sems)
    copies = []
    for c in range(CHUNKS):
        part = pl.ds(c * chunk, min(chunk, half - c * chunk))
        copies.append(pltpu.make_async_copy(tiles_ref.at[part], held.at[part], sems.at[c]))

        @pl.when(c * chunk < live)
        def _():
            copies[c].start()

    last = pltpu.make_async_copy(tiles_ref.at[pl.ds(half, slots - half)], rest, sems.at[CHUNKS])

    @pl.when(half < live)
    def _():
        last.start()

    def clear(index, carry):
        total[index] = jnp.zeros((tile, tile), F32)
        return carry

    lax.fori_loop(0, total.shape[0], clear, 0, unroll=4)
    for copy in lists:
        copy.wait()
    for c in range(CHUNKS):
        start, stop = c * chunk, min((c + 1) * chunk, half)

        @pl.when(start < live)
        def _():
            copies[c].wait()
            add_tiles(
                rows_dev, (rows_ref, cols_ref), held, 0, start, jnp.minimum(live, stop), total
            )

    @pl.when(half < live)
    def _():
        last.wait()


def dense_kernel(
    rows_dev, count_ref, rows_hbm, cols_hbm, rest, total_in, joined_ref, out_ref, total, *scratch
):
    rows_ref, cols_ref, list_sems = scratch
    live = count_ref[0]
    half = rows_ref.shape[0] - rest.shape[0]
    tile = total.shape[1]
    row_blocks = out_ref.shape[2] // tile

    @pl.when(half < live)
    def _():
        lists = copy_lists((rows_hbm, cols_hbm), (rows_ref, cols_ref), list_sems)
        for copy in lists:
            copy.wait()
        add_tiles(rows_dev, (rows_ref, cols_ref), rest, half, half, live, total)

    def part(index, carry):
        start = pl.multiple_of(index * tile, tile)
        for b in range(row_blocks):
            value = total[index * row_blocks + b].T
            high = value.astype(BF16)
            low = (value - high.astype(F32)).astype(BF16)
            out_ref[0, pl.ds(start, tile), pl.ds(b * tile, tile)] = high
            out_ref[1, pl.ds(start, tile), pl.ds(b * tile, tile)] = low
        return carry

    lax.fori_loop(0, total.shape[0] // row_blocks, part, 0)


def join_kernel(order, *refs):
    for k, ref in zip(order, refs):
        refs[-1][k] = ref[...]


def apply_dense(directions, matrix):
    rounded = jnp.concatenate([direction.astype(BF16) for direction in directions], axis=1)
    high, low = [
        jnp.dot(rounded, matrix[part], preferred_element_type=F32) for part in range(2)
    ]
    return high + low


def first_kernel(even_ref, odd_ref, matrix, out_ref, blocks_ref):
    pieces = blocks_ref.shape[0]
    values = [(odd_ref if k % 2 else even_ref)[k // 2] for k in range(pieces)]
    for k, value in enumerate(values):
        blocks_ref[k] = value
    rows = 2 * values[0].shape[1]
    joined = jnp.concatenate(values, axis=1)
    out_ref[:, rows:] = gram_parts(joined, joined)
    out_ref[:, :rows] = apply_dense(values, matrix)


def collect_kernel(near_ref, far_ref, residual_ref, direction_ref):
    pieces = near_ref.shape[0]
    for k in range(pieces):
        residual_ref[0, k] = near_ref[k]
        residual_ref[1, k] = far_ref[k]
        direction_ref[k] = near_ref[k]
    direction_ref[pieces] = far_ref[0]


def add_halves(mine_ref, other_ref, width):
    near = mine_ref[:, :width] + other_ref[:, width : 2 * width]
    far = mine_ref[:, width : 2 * width] + other_ref[:, :width]
    return near, far


def image_kernel(first, mine_ref, other_ref, near_ref, far_ref, *refs):
    out_ref, norm_ref = refs if first else (refs[0], None)
    core = lax.axis_index("col")
    size, width = near_ref.shape[1:]
    near, far = add_halves(mine_ref, other_ref, width)
    if first:
        norm_ref[...] = finish(mine_ref[:, 2 * width :] + other_ref[:, 2 * width :])
    parts = width // LANES
    for i in range(parts):
        lanes = slice(i * LANES, (i + 1) * LANES)
        for place, half in ((core, near), (1 - core, far)):
            at = pl.multiple_of((place * parts + i) * size, size)
            out_ref[pl.ds(at, size)] = half[:, lanes]
    products = symmetric_parts(near, near_ref[0]) + symmetric_parts(
        far, far_ref[far_ref.shape[0] - 1]
    )
    out_ref[2 * parts * size :] = pack(finish(products))


def inverse_kernel(norm_ref, out_ref):
    norm = norm_ref[...]
    size = norm.shape[0]
    norm = 0.5 * (norm + jnp.concatenate([norm[:, :size].T, norm[:, size:]], axis=1))
    unit = lax.broadcasted_iota(jnp.int32, norm.shape, 0) == lax.broadcasted_iota(
        jnp.int32, norm.shape, 1
    )
    out_ref[...] = solve_wide(jnp.where(unit, 1.0, 0.0), pltpu.roll(norm, size, 1))


def pick(refs, places, core, rows):
    if places[0] == places[1]:
        return refs[places[0]][rows]
    return jnp.where(core == 0, refs[places[0]][rows], refs[places[1]][rows])


def step_kernel(used, places, with_solution, last, *refs):
    images, refs = refs[:used], refs[used:]
    direction_ref, residual_ref, norm_ref, inverse_ref, matrix = refs[:5]
    refs = refs[5:]
    if with_solution:
        solution_ref, refs = refs[0], refs[1:]
    out_ref, new_direction, new_residual, new_norm, new_solution = refs
    core = lax.axis_index("col")
    pieces = len(places)
    size, width = direction_ref.shape[1:]
    parts = width // LANES

    def image(k, half):
        found = []
        for i in range(parts):
            at = pl.multiple_of((half * parts + i) * size, size)
            found.append(pick(images, places[k], core, pl.ds(at, size)))
        return jnp.concatenate(found, axis=1)

    behind = slice(2 * parts * size, None)
    products = add_up([pick(images, pair, core, behind) for pair in places])
    alpha = stack(solve_wide(norm_ref[...], unpack(products, size, 1))[:, :size])
    residuals = [
        [residual_ref[side, k] - times(alpha, image(k, half)) for k in range(pieces)]
        for side, half in enumerate((core, 1 - core))
    ]
    joined = [jnp.concatenate(values, axis=1) for values in residuals]
    next_norm = finish(gram_parts(joined[0], joined[0]) + gram_parts(joined[1], joined[1]))
    new_norm[...] = next_norm
    step = times(alpha, direction_ref[0])
    new_solution[...] = solution_ref[...] + step if with_solution else step
    beta = stack(mul(inverse_ref[:, :size], next_norm[:, :size]))
    directions = [
        residual + times(beta, direction_ref[k])
        for k, residual in enumerate(residuals[0] + residuals[1][:1])
    ]
    if last:
        new_residual[...] = residuals[0][0]
        new_direction[0] = directions[0]
        new_direction[1] = directions[pieces]
    else:
        for k in range(pieces):
            new_residual[0, k] = residuals[0][k]
            new_residual[1, k] = residuals[1][k]
        for k in range(pieces + 1):
            new_direction[k] = directions[k]
    out_ref[...] = apply_dense(directions[:pieces], matrix)


def last_image_kernel(mine_ref, other_ref, direction_ref, near_ref, gram_ref):
    near, far = add_halves(mine_ref, other_ref, direction_ref.shape[2])
    near_ref[...] = near
    products = symmetric_parts(near, direction_ref[0]) + symmetric_parts(far, direction_ref[1])
    gram_ref[...] = pack(finish(products))


def last_kernel(used, places, *refs):
    image_ref, direction_ref, residual_ref, norm_ref, solution_ref = refs[used:-2]
    new_solution, new_residual = refs[-2:]
    core = lax.axis_index("col")
    size = image_ref.shape[0]
    products = add_up([pick(refs, pair, core, slice(None)) for pair in places])
    alpha = stack(solve_wide(norm_ref[...], unpack(products, size, 1))[:, :size])
    new_solution[...] = solution_ref[...] + times(alpha, direction_ref[0])
    new_residual[...] = residual_ref[...] - times(alpha, image_ref[...])


def shape(*dims, dtype=F32):
    return jax.ShapeDtypeStruct(dims, dtype)


def per_device(tiles, tile_rows, tile_cols, tile_count, signs, vertex_weight, column_scale):
    sketch, rows_dev = signs.shape
    tile = tiles.shape[1]
    pieces = lax.axis_size("row")
    col_devices = lax.axis_size("col")
    group = col_devices * rows_dev
    depth = pieces * rows_dev

    def swap(value, mask):
        return lax.ppermute(value, "row", [(i, i ^ mask) for i in range(pieces)])

    def across(value):
        return lax.ppermute(
            value, "col", [(i, (i + 1) % col_devices) for i in range(col_devices)]
        )

    def exchange(value):
        if pieces != 8:
            found = [value] + [swap(value, k) for k in range(1, pieces)]
            return found, [(k, k) for k in range(pieces)]
        turns = ((7, 5), (3, 6), (2, 4), (1, 1))
        fetched = []
        passed = []
        places = {0: (0, 0)}
        for turn, masks in enumerate(turns, 1):
            pairs = [
                (i * 2 + core, (i ^ mask) * 2 + core)
                for core, mask in enumerate(masks)
                for i in range(pieces)
            ]
            fetched.append(lax.ppermute(value, ("row", "col"), pairs))
            if masks[0] == masks[1]:
                places[masks[0]] = (turn, turn)
            else:
                passed.append(across(fetched[-1]))
                places[masks[0]] = (turn, turn + len(turns))
                places[masks[1]] = (turn + len(turns), turn)
        return [value, *fetched, *passed], [places[k] for k in range(pieces)]

    right_side = signs.astype(F32) * vertex_weight[None, :] * column_scale[:, None]
    far_side = across(right_side)[None]
    even = [right_side] + [swap(right_side, k) for k in range(2, pieces, 2)]

    matrix = shape(2, depth, group, dtype=BF16)
    total = shape(depth // tile * (group // tile), tile, tile)
    slots = tiles.shape[0]
    half = slots // 2
    rest = shape(slots - half, tile, tile, dtype=BF16)
    lists = [pltpu.with_memory_space_constraint(x, pltpu.HBM) for x in (tile_rows, tile_cols)]
    lists_scratch = [pltpu.SMEM(x.shape, jnp.int32) for x in lists]
    cost = pl.CostEstimate(
        flops=4 * tiles.size, bytes_accessed=4 * tiles.size, transcendentals=0
    )
    blocks_sum, others = pl.pallas_call(
        functools.partial(gather_kernel, rows_dev),
        out_shape=(total, rest),
        in_specs=[SMEM] + [HBM] * 3,
        out_specs=(VMEM, VMEM),
        scratch_shapes=[
            pltpu.VMEM((half, tile, tile), BF16),
            *lists_scratch,
            pltpu.SemaphoreType.DMA((CHUNKS + 1,)),
            pltpu.SemaphoreType.DMA((len(lists),)),
        ],
        compiler_params=params(tiles, total),
        cost_estimate=cost,
        name="gather",
    )(tile_count, *lists, pltpu.with_memory_space_constraint(tiles, pltpu.HBM))
    joined = shape(pieces // 2, sketch, rows_dev)
    order = [*range(pieces // 4, pieces // 2), *range(1, pieces // 4), 0]
    even = pl.pallas_call(
        functools.partial(join_kernel, order),
        out_shape=joined,
        in_specs=[VMEM] * (pieces // 2) + [ANY],
        out_specs=VMEM,
        compiler_params=params(joined, joined),
        name="join",
    )(*[even[k] for k in order], blocks_sum)
    odd = swap(even, 1)
    dense, _ = pl.pallas_call(
        functools.partial(dense_kernel, rows_dev),
        out_shape=(matrix, total),
        in_specs=[SMEM] + [HBM] * 2 + [VMEM, VMEM, ANY],
        out_specs=(VMEM, VMEM),
        scratch_shapes=[*lists_scratch, pltpu.SemaphoreType.DMA((len(lists),))],
        input_output_aliases={4: 1},
        compiler_params=params(rest, total, total, matrix),
        cost_estimate=cost,
        name="dense",
    )(tile_count, *lists, others, blocks_sum, even)

    held = shape(2, pieces, sketch, rows_dev)
    state = shape(pieces + 1, sketch, rows_dev)
    small = shape(sketch, LANES)
    piece = shape(sketch, rows_dev)
    packed = shape(sketch * sketch // LANES, LANES)
    payload = shape(2 * sketch * (rows_dev // LANES) + packed.shape[0], LANES)

    partial_sum, blocks = pl.pallas_call(
        first_kernel,
        out_shape=(shape(sketch, group + LANES), shape(pieces, sketch, rows_dev)),
        in_specs=[VMEM] * 3,
        out_specs=(VMEM, VMEM),
        compiler_params=params(matrix, state, state),
        name="first",
    )(even, odd, dense)
    norm = None
    solution = None
    direction = None
    for iteration in range(ITERS - 1):
        first = iteration == 0
        last = iteration == ITERS - 2
        sums = (partial_sum, across(partial_sum))
        given = (even, far_side) if first else (direction, direction)
        outs = pl.pallas_call(
            functools.partial(image_kernel, first),
            out_shape=(payload, small) if first else (payload,),
            in_specs=[VMEM] * 4,
            out_specs=(VMEM, VMEM) if first else (VMEM,),
            compiler_params=params(state, payload),
            name="image",
        )(*sums, *given)
        found, places = exchange(outs[0])
        if first:
            norm = outs[1]
            residual, direction = pl.pallas_call(
                collect_kernel,
                out_shape=(held, state),
                in_specs=[VMEM] * 2,
                out_specs=(VMEM, VMEM),
                compiler_params=params(held, held, state),
                name="collect",
            )(blocks, across(blocks))
        inverse = pl.pallas_call(
            inverse_kernel,
            out_shape=small,
            in_specs=[VMEM],
            out_specs=VMEM,
            compiler_params=params(),
            name="inverse",
        )(norm)
        given = () if first else (solution,)
        partial_sum, direction, residual, norm, solution = pl.pallas_call(
            functools.partial(step_kernel, len(found), places, not first, last),
            out_shape=(
                shape(sketch, group),
                shape(2, sketch, rows_dev) if last else state,
                piece if last else held,
                small,
                piece,
            ),
            in_specs=[VMEM] * (len(found) + 5 + len(given)),
            out_specs=(VMEM,) * 5,
            compiler_params=params(matrix, held, held, held, held, state),
            name="step",
        )(*found, direction, residual, norm, inverse, dense, *given)
    near, gram = pl.pallas_call(
        last_image_kernel,
        out_shape=(piece, packed),
        in_specs=[VMEM] * 3,
        out_specs=(VMEM, VMEM),
        compiler_params=params(state),
        name="last_image",
    )(partial_sum, across(partial_sum), direction)
    found, places = exchange(gram)
    return pl.pallas_call(
        functools.partial(last_kernel, len(found), places),
        out_shape=(piece, piece),
        in_specs=[VMEM] * (len(found) + 5),
        out_specs=(VMEM, VMEM),
        compiler_params=params(state, state),
        name="last",
    )(*found, near, direction, residual, norm, solution)


def solution(mesh):
    return jax.shard_map(
        per_device,
        mesh=mesh,
        in_specs=(
            P(("row", "col"), None, None),
            P(("row", "col")),
            P(("row", "col")),
            P(("row", "col")),
            P("rhs", ("row", "col")),
            P(("row", "col")),
            P("rhs"),
        ),
        out_specs=(P("rhs", ("row", "col")), P("rhs", ("row", "col"))),
        check_vma=False,
    )
```

```python
import functools

import jax
import jax.numpy as jnp
from jax import lax
from jax.experimental import pallas as pl
from jax.experimental.pallas import tpu as pltpu
from jax.sharding import PartitionSpec as P

ITERS = 3
LANES = 128
PIVOTS = 8
CHUNKS = 5
F32 = jnp.float32
BF16 = jnp.bfloat16
SPARE_BYTES = 4 * 1024 * 1024

VMEM = pl.BlockSpec(memory_space=pltpu.VMEM)
SMEM = pl.BlockSpec(memory_space=pltpu.SMEM)
HBM = pl.BlockSpec(memory_space=pltpu.HBM)
ANY = pl.BlockSpec(memory_space=pl.ANY)


def params(*arrays):
    used = sum(a.size * jnp.dtype(a.dtype).itemsize for a in arrays)
    return pltpu.CompilerParams(vmem_limit_bytes=used + SPARE_BYTES)


def split(value):
    high = value.astype(BF16)
    rest = value - high.astype(F32)
    middle = rest.astype(BF16)
    low = (rest - middle.astype(F32)).astype(BF16)
    return high, middle, low


def mul(left, right):
    return jnp.dot(left, right, precision=lax.Precision.HIGHEST, preferred_element_type=F32)


def stack(left):
    high, middle, low = [part.astype(F32) for part in split(left)]
    parts = jnp.concatenate([high, high, middle, high, middle, low], axis=0)
    return parts.T.astype(BF16)


def times(stacked, right):
    high, middle, low = split(right)
    parts = jnp.concatenate([high, middle, high, low, middle, high], axis=0)
    return jnp.dot(stacked, parts, preferred_element_type=F32)


def gram_parts(left, right):
    size, width = left.shape
    filler = jnp.zeros((LANES - 3 * size, width), BF16)
    every = lax.dot_general(
        jnp.concatenate(split(left), axis=0),
        jnp.concatenate([*split(right), filler], axis=0),
        (((1,), (1,)), ((), ())),
        preferred_element_type=F32,
    )
    return every[2 * size :] + every[size : 2 * size] + every[:size]


def symmetric_parts(left, right):
    return 0.5 * (gram_parts(left, right) + gram_parts(right, left))


def finish(parts, place=0):
    size = parts.shape[0]

    def block(index):
        shift = (place - index) * size % LANES
        return pltpu.roll(parts, shift, 1) if shift else parts

    return block(2) + block(1) + block(0)


def pack(wide):
    rows = wide.shape[0]
    folds = LANES // rows
    height = rows // folds
    lanes = lax.broadcasted_iota(jnp.int32, wide.shape, 1)
    wide = jnp.where(lanes < rows, wide, 0.0)
    total = wide[:height]
    for i in range(1, folds):
        total = total + pltpu.roll(wide[i * height : (i + 1) * height], i * rows, 1)
    return total


def unpack(folded, size, place=0):
    parts = []
    for i in range(LANES // size):
        shift = (place - i) * size % LANES
        parts.append(pltpu.roll(folded, shift, 1) if shift else folded)
    return jnp.concatenate(parts, axis=0)


def solve_wide(target, matrix):
    size = matrix.shape[0]
    row_ids = lax.broadcasted_iota(jnp.int32, (size, LANES), 0)
    lane_ids = lax.broadcasted_iota(jnp.int32, (size, LANES), 1)
    work = jnp.where(lane_ids < size, target, matrix)
    for base in range(0, size, PIVOTS):
        columns = [
            jnp.broadcast_to(work[:, size + base + i : size + base + i + 1], (size, LANES))
            for i in range(PIVOTS)
        ]
        for i in range(PIVOTS):
            pivot = base + i
            here = row_ids == pivot
            inverse = pltpu.reciprocal(columns[i][pivot : pivot + 1, :], full_range=False)
            row = work[pivot : pivot + 1, :] * inverse
            work = jnp.where(here, row, work - columns[i] * row)
            for later in range(i + 1, PIVOTS):
                entry = columns[later][pivot : pivot + 1, :] * inverse
                columns[later] = jnp.where(here, entry, columns[later] - columns[i] * entry)
    return work


def add_up(values):
    values = list(values)
    while len(values) > 1:
        pairs = [values[i] + values[i + 1] for i in range(0, len(values) - 1, 2)]
        values = pairs + values[len(values) - len(values) % 2 :]
    return values[0]


def add_tiles(rows_dev, lists, tiles, first_tile, start, stop, total):
    rows_ref, cols_ref = lists
    tile = total.shape[1]
    slots = rows_ref.shape[0]
    blocks = rows_dev // tile
    row_place = lax.axis_index("row")
    col_place = lax.axis_index("col")
    col_devices = lax.axis_size("col")
    row_blocks = col_devices * blocks

    def place(slot):
        row = rows_ref[slot]
        column = cols_ref[slot]
        side = lax.rem(row // blocks + col_devices - col_place, col_devices)
        owner = column // (blocks * col_devices)
        column_at = (owner ^ row_place) * blocks + lax.rem(column, blocks)
        return column_at * row_blocks + side * blocks + lax.rem(row, blocks)

    def after(slot):
        return place(jnp.minimum(slot, slots - 1))

    def add(turn, places):
        slot = start + 2 * turn
        values = [tiles[slot + i - first_tile].astype(F32) for i in range(2)]
        following = (after(slot + 2), after(slot + 3))
        for at, value in zip(places, values):
            total[at] = total[at] + value
        return following

    places = lax.fori_loop(0, (stop - start) // 2, add, (after(start), after(start + 1)))

    @pl.when(lax.rem(stop - start, 2) == 1)
    def _():
        total[places[0]] = total[places[0]] + tiles[stop - 1 - first_tile].astype(F32)


def copy_lists(hbm_refs, smem_refs, sems):
    copies = [
        pltpu.make_async_copy(source, target, sems.at[i])
        for i, (source, target) in enumerate(zip(hbm_refs, smem_refs))
    ]
    for copy in copies:
        copy.start()
    return copies


def gather_kernel(rows_dev, count_ref, rows_hbm, cols_hbm, tiles_ref, total, rest, *scratch):
    held, rows_ref, cols_ref, sems, list_sems = scratch
    live = count_ref[0]
    half = held.shape[0]
    slots, tile = tiles_ref.shape[:2]
    chunk = -(-half // CHUNKS)
    lists = copy_lists((rows_hbm, cols_hbm), (rows_ref, cols_ref), list_sems)
    copies = []
    for c in range(CHUNKS):
        part = pl.ds(c * chunk, min(chunk, half - c * chunk))
        copies.append(pltpu.make_async_copy(tiles_ref.at[part], held.at[part], sems.at[c]))

        @pl.when(c * chunk < live)
        def _():
            copies[c].start()

    last = pltpu.make_async_copy(tiles_ref.at[pl.ds(half, slots - half)], rest, sems.at[CHUNKS])

    @pl.when(half < live)
    def _():
        last.start()

    def clear(index, carry):
        total[index] = jnp.zeros((tile, tile), F32)
        return carry

    lax.fori_loop(0, total.shape[0], clear, 0, unroll=4)
    for copy in lists:
        copy.wait()
    for c in range(CHUNKS):
        start, stop = c * chunk, min((c + 1) * chunk, half)

        @pl.when(start < live)
        def _():
            copies[c].wait()
            add_tiles(
                rows_dev, (rows_ref, cols_ref), held, 0, start, jnp.minimum(live, stop), total
            )

    @pl.when(half < live)
    def _():
        last.wait()


def dense_kernel(
    rows_dev, count_ref, rows_hbm, cols_hbm, rest, total_in, joined_ref, out_ref, total, *scratch
):
    rows_ref, cols_ref, list_sems = scratch
    live = count_ref[0]
    half = rows_ref.shape[0] - rest.shape[0]
    tile = total.shape[1]
    row_blocks = out_ref.shape[2] // tile

    @pl.when(half < live)
    def _():
        lists = copy_lists((rows_hbm, cols_hbm), (rows_ref, cols_ref), list_sems)
        for copy in lists:
            copy.wait()
        add_tiles(rows_dev, (rows_ref, cols_ref), rest, half, half, live, total)

    def part(index, carry):
        start = pl.multiple_of(index * tile, tile)
        for b in range(row_blocks):
            value = total[index * row_blocks + b].T
            high = value.astype(BF16)
            low = (value - high.astype(F32)).astype(BF16)
            out_ref[0, pl.ds(start, tile), pl.ds(b * tile, tile)] = high
            out_ref[1, pl.ds(start, tile), pl.ds(b * tile, tile)] = low
        return carry

    lax.fori_loop(0, total.shape[0] // row_blocks, part, 0)


def join_kernel(order, *refs):
    for k, ref in zip(order, refs):
        refs[-1][k] = ref[...]


def apply_dense(directions, matrix):
    rounded = jnp.concatenate([direction.astype(BF16) for direction in directions], axis=1)
    high, low = [
        jnp.dot(rounded, matrix[part], preferred_element_type=F32) for part in range(2)
    ]
    return high + low


def first_kernel(even_ref, odd_ref, matrix, out_ref, blocks_ref):
    pieces = blocks_ref.shape[0]
    values = [(odd_ref if k % 2 else even_ref)[k // 2] for k in range(pieces)]
    for k, value in enumerate(values):
        blocks_ref[k] = value
    rows = 2 * values[0].shape[1]
    joined = jnp.concatenate(values, axis=1)
    out_ref[:, rows:] = gram_parts(joined, joined)
    out_ref[:, :rows] = apply_dense(values, matrix)


def collect_kernel(near_ref, far_ref, residual_ref, direction_ref):
    pieces = near_ref.shape[0]
    for k in range(pieces):
        residual_ref[0, k] = near_ref[k]
        residual_ref[1, k] = far_ref[k]
        direction_ref[k] = near_ref[k]
    direction_ref[pieces] = far_ref[0]


def add_halves(mine_ref, other_ref, width):
    near = mine_ref[:, :width] + other_ref[:, width : 2 * width]
    far = mine_ref[:, width : 2 * width] + other_ref[:, :width]
    return near, far


def image_kernel(first, mine_ref, other_ref, near_ref, far_ref, *refs):
    out_ref, norm_ref = refs if first else (refs[0], None)
    core = lax.axis_index("col")
    size, width = near_ref.shape[1:]
    near, far = add_halves(mine_ref, other_ref, width)
    if first:
        norm_ref[...] = finish(mine_ref[:, 2 * width :] + other_ref[:, 2 * width :])
    parts = width // LANES
    for i in range(parts):
        lanes = slice(i * LANES, (i + 1) * LANES)
        for place, half in ((core, near), (1 - core, far)):
            at = pl.multiple_of((place * parts + i) * size, size)
            out_ref[pl.ds(at, size)] = half[:, lanes]
    products = symmetric_parts(near, near_ref[0]) + symmetric_parts(
        far, far_ref[far_ref.shape[0] - 1]
    )
    out_ref[2 * parts * size :] = pack(finish(products))


def inverse_kernel(norm_ref, out_ref):
    norm = norm_ref[...]
    size = norm.shape[0]
    norm = 0.5 * (norm + jnp.concatenate([norm[:, :size].T, norm[:, size:]], axis=1))
    unit = lax.broadcasted_iota(jnp.int32, norm.shape, 0) == lax.broadcasted_iota(
        jnp.int32, norm.shape, 1
    )
    out_ref[...] = solve_wide(jnp.where(unit, 1.0, 0.0), pltpu.roll(norm, size, 1))


def pick(refs, places, core, rows):
    if places[0] == places[1]:
        return refs[places[0]][rows]
    return jnp.where(core == 0, refs[places[0]][rows], refs[places[1]][rows])


def step_kernel(used, places, with_solution, last, *refs):
    images, refs = refs[:used], refs[used:]
    direction_ref, residual_ref, norm_ref, inverse_ref, matrix = refs[:5]
    refs = refs[5:]
    if with_solution:
        solution_ref, refs = refs[0], refs[1:]
    out_ref, new_direction, new_residual, new_norm, new_solution = refs
    core = lax.axis_index("col")
    pieces = len(places)
    size, width = direction_ref.shape[1:]
    parts = width // LANES

    def image(k, half):
        found = []
        for i in range(parts):
            at = pl.multiple_of((half * parts + i) * size, size)
            found.append(pick(images, places[k], core, pl.ds(at, size)))
        return jnp.concatenate(found, axis=1)

    behind = slice(2 * parts * size, None)
    products = add_up([pick(images, pair, core, behind) for pair in places])
    alpha = stack(solve_wide(norm_ref[...], unpack(products, size, 1))[:, :size])
    residuals = [
        [residual_ref[side, k] - times(alpha, image(k, half)) for k in range(pieces)]
        for side, half in enumerate((core, 1 - core))
    ]
    joined = [jnp.concatenate(values, axis=1) for values in residuals]
    next_norm = finish(gram_parts(joined[0], joined[0]) + gram_parts(joined[1], joined[1]))
    new_norm[...] = next_norm
    step = times(alpha, direction_ref[0])
    new_solution[...] = solution_ref[...] + step if with_solution else step
    beta = stack(mul(inverse_ref[:, :size], next_norm[:, :size]))
    directions = [
        residual + times(beta, direction_ref[k])
        for k, residual in enumerate(residuals[0] + residuals[1][:1])
    ]
    if last:
        new_residual[...] = residuals[0][0]
        new_direction[0] = directions[0]
        new_direction[1] = directions[pieces]
    else:
        for k in range(pieces):
            new_residual[0, k] = residuals[0][k]
            new_residual[1, k] = residuals[1][k]
        for k in range(pieces + 1):
            new_direction[k] = directions[k]
    out_ref[...] = apply_dense(directions[:pieces], matrix)


def last_image_kernel(mine_ref, other_ref, direction_ref, near_ref, gram_ref):
    near, far = add_halves(mine_ref, other_ref, direction_ref.shape[2])
    near_ref[...] = near
    products = symmetric_parts(near, direction_ref[0]) + symmetric_parts(far, direction_ref[1])
    gram_ref[...] = pack(finish(products))


def last_kernel(used, places, *refs):
    image_ref, direction_ref, residual_ref, norm_ref, solution_ref = refs[used:-2]
    new_solution, new_residual = refs[-2:]
    core = lax.axis_index("col")
    size = image_ref.shape[0]
    products = add_up([pick(refs, pair, core, slice(None)) for pair in places])
    alpha = stack(solve_wide(norm_ref[...], unpack(products, size, 1))[:, :size])
    new_solution[...] = solution_ref[...] + times(alpha, direction_ref[0])
    new_residual[...] = residual_ref[...] - times(alpha, image_ref[...])


def shape(*dims, dtype=F32):
    return jax.ShapeDtypeStruct(dims, dtype)


def per_device(tiles, tile_rows, tile_cols, tile_count, signs, vertex_weight, column_scale):
    sketch, rows_dev = signs.shape
    tile = tiles.shape[1]
    pieces = lax.axis_size("row")
    col_devices = lax.axis_size("col")
    group = col_devices * rows_dev
    depth = pieces * rows_dev

    def swap(value, mask):
        return lax.ppermute(value, "row", [(i, i ^ mask) for i in range(pieces)])

    def across(value):
        return lax.ppermute(
            value, "col", [(i, (i + 1) % col_devices) for i in range(col_devices)]
        )

    def exchange(value):
        if pieces != 8:
            found = [value] + [swap(value, k) for k in range(1, pieces)]
            return found, [(k, k) for k in range(pieces)]
        turns = ((7, 5), (3, 6), (2, 4), (1, 1))
        fetched = []
        passed = []
        places = {0: (0, 0)}
        for turn, masks in enumerate(turns, 1):
            pairs = [
                (i * 2 + core, (i ^ mask) * 2 + core)
                for core, mask in enumerate(masks)
                for i in range(pieces)
            ]
            fetched.append(lax.ppermute(value, ("row", "col"), pairs))
            if masks[0] == masks[1]:
                places[masks[0]] = (turn, turn)
            else:
                passed.append(across(fetched[-1]))
                places[masks[0]] = (turn, turn + len(turns))
                places[masks[1]] = (turn + len(turns), turn)
        return [value, *fetched, *passed], [places[k] for k in range(pieces)]

    right_side = signs.astype(F32) * vertex_weight[None, :] * column_scale[:, None]
    far_side = across(right_side)[None]
    even = [right_side] + [swap(right_side, k) for k in range(2, pieces, 2)]

    matrix = shape(2, depth, group, dtype=BF16)
    total = shape(depth // tile * (group // tile), tile, tile)
    slots = tiles.shape[0]
    half = slots * 3 // 8
    rest = shape(slots - half, tile, tile, dtype=BF16)
    lists = [pltpu.with_memory_space_constraint(x, pltpu.HBM) for x in (tile_rows, tile_cols)]
    lists_scratch = [pltpu.SMEM(x.shape, jnp.int32) for x in lists]
    cost = pl.CostEstimate(
        flops=4 * tiles.size, bytes_accessed=4 * tiles.size, transcendentals=0
    )
    blocks_sum, others = pl.pallas_call(
        functools.partial(gather_kernel, rows_dev),
        out_shape=(total, rest),
        in_specs=[SMEM] + [HBM] * 3,
        out_specs=(VMEM, VMEM),
        scratch_shapes=[
            pltpu.VMEM((half, tile, tile), BF16),
            *lists_scratch,
            pltpu.SemaphoreType.DMA((CHUNKS + 1,)),
            pltpu.SemaphoreType.DMA((len(lists),)),
        ],
        compiler_params=params(tiles, total),
        cost_estimate=cost,
        name="gather",
    )(tile_count, *lists, pltpu.with_memory_space_constraint(tiles, pltpu.HBM))
    joined = shape(pieces // 2, sketch, rows_dev)
    order = [*range(pieces // 4, pieces // 2), *range(1, pieces // 4), 0]
    even = pl.pallas_call(
        functools.partial(join_kernel, order),
        out_shape=joined,
        in_specs=[VMEM] * (pieces // 2) + [ANY],
        out_specs=VMEM,
        compiler_params=params(joined, joined),
        name="join",
    )(*[even[k] for k in order], blocks_sum)
    odd = swap(even, 1)
    dense, _ = pl.pallas_call(
        functools.partial(dense_kernel, rows_dev),
        out_shape=(matrix, total),
        in_specs=[SMEM] + [HBM] * 2 + [VMEM, VMEM, ANY],
        out_specs=(VMEM, VMEM),
        scratch_shapes=[*lists_scratch, pltpu.SemaphoreType.DMA((len(lists),))],
        input_output_aliases={4: 1},
        compiler_params=params(rest, total, total, matrix),
        cost_estimate=cost,
        name="dense",
    )(tile_count, *lists, others, blocks_sum, even)

    held = shape(2, pieces, sketch, rows_dev)
    state = shape(pieces + 1, sketch, rows_dev)
    small = shape(sketch, LANES)
    piece = shape(sketch, rows_dev)
    packed = shape(sketch * sketch // LANES, LANES)
    payload = shape(2 * sketch * (rows_dev // LANES) + packed.shape[0], LANES)

    partial_sum, blocks = pl.pallas_call(
        first_kernel,
        out_shape=(shape(sketch, group + LANES), shape(pieces, sketch, rows_dev)),
        in_specs=[VMEM] * 3,
        out_specs=(VMEM, VMEM),
        compiler_params=params(matrix, state, state),
        name="first",
    )(even, odd, dense)
    norm = None
    solution = None
    direction = None
    for iteration in range(ITERS - 1):
        first = iteration == 0
        last = iteration == ITERS - 2
        sums = (partial_sum, across(partial_sum))
        given = (even, far_side) if first else (direction, direction)
        outs = pl.pallas_call(
            functools.partial(image_kernel, first),
            out_shape=(payload, small) if first else (payload,),
            in_specs=[VMEM] * 4,
            out_specs=(VMEM, VMEM) if first else (VMEM,),
            compiler_params=params(state, payload),
            name="image",
        )(*sums, *given)
        found, places = exchange(outs[0])
        if first:
            norm = outs[1]
            residual, direction = pl.pallas_call(
                collect_kernel,
                out_shape=(held, state),
                in_specs=[VMEM] * 2,
                out_specs=(VMEM, VMEM),
                compiler_params=params(held, held, state),
                name="collect",
            )(blocks, across(blocks))
        inverse = pl.pallas_call(
            inverse_kernel,
            out_shape=small,
            in_specs=[VMEM],
            out_specs=VMEM,
            compiler_params=params(),
            name="inverse",
        )(norm)
        given = () if first else (solution,)
        partial_sum, direction, residual, norm, solution = pl.pallas_call(
            functools.partial(step_kernel, len(found), places, not first, last),
            out_shape=(
                shape(sketch, group),
                shape(2, sketch, rows_dev) if last else state,
                piece if last else held,
                small,
                piece,
            ),
            in_specs=[VMEM] * (len(found) + 5 + len(given)),
            out_specs=(VMEM,) * 5,
            compiler_params=params(matrix, held, held, held, held, state),
            name="step",
        )(*found, direction, residual, norm, inverse, dense, *given)
    near, gram = pl.pallas_call(
        last_image_kernel,
        out_shape=(piece, packed),
        in_specs=[VMEM] * 3,
        out_specs=(VMEM, VMEM),
        compiler_params=params(state),
        name="last_image",
    )(partial_sum, across(partial_sum), direction)
    found, places = exchange(gram)
    return pl.pallas_call(
        functools.partial(last_kernel, len(found), places),
        out_shape=(piece, piece),
        in_specs=[VMEM] * (len(found) + 5),
        out_specs=(VMEM, VMEM),
        compiler_params=params(state, state),
        name="last",
    )(*found, near, direction, residual, norm, solution)


def solution(mesh):
    return jax.shard_map(
        per_device,
        mesh=mesh,
        in_specs=(
            P(("row", "col"), None, None),
            P(("row", "col")),
            P(("row", "col")),
            P(("row", "col")),
            P("rhs", ("row", "col")),
            P(("row", "col")),
            P("rhs"),
        ),
        out_specs=(P("rhs", ("row", "col")), P("rhs", ("row", "col"))),
        check_vma=False,
    )
```

```python
import functools

import jax
import jax.numpy as jnp
from jax import lax
from jax.experimental import pallas as pl
from jax.experimental.pallas import tpu as pltpu
from jax.sharding import PartitionSpec as P

ITERS = 3
LANES = 128
PIVOTS = 8
CHUNKS = 5
F32 = jnp.float32
BF16 = jnp.bfloat16
SPARE_BYTES = 4 * 1024 * 1024

VMEM = pl.BlockSpec(memory_space=pltpu.VMEM)
SMEM = pl.BlockSpec(memory_space=pltpu.SMEM)
HBM = pl.BlockSpec(memory_space=pltpu.HBM)
ANY = pl.BlockSpec(memory_space=pl.ANY)


def params(*arrays):
    used = sum(a.size * jnp.dtype(a.dtype).itemsize for a in arrays)
    return pltpu.CompilerParams(vmem_limit_bytes=used + SPARE_BYTES)


def split(value):
    high = value.astype(BF16)
    rest = value - high.astype(F32)
    middle = rest.astype(BF16)
    low = (rest - middle.astype(F32)).astype(BF16)
    return high, middle, low


def mul(left, right):
    return jnp.dot(left, right, precision=lax.Precision.HIGHEST, preferred_element_type=F32)


def stack(left):
    high, middle, low = [part.astype(F32) for part in split(left)]
    parts = jnp.concatenate([high, high, middle, high, middle, low], axis=0)
    return parts.T.astype(BF16)


def times(stacked, right):
    high, middle, low = split(right)
    parts = jnp.concatenate([high, middle, high, low, middle, high], axis=0)
    return jnp.dot(stacked, parts, preferred_element_type=F32)


def gram_parts(left, right):
    size, width = left.shape
    filler = jnp.zeros((LANES - 3 * size, width), BF16)
    every = lax.dot_general(
        jnp.concatenate(split(left), axis=0),
        jnp.concatenate([*split(right), filler], axis=0),
        (((1,), (1,)), ((), ())),
        preferred_element_type=F32,
    )
    return every[2 * size :] + every[size : 2 * size] + every[:size]


def symmetric_parts(left, right):
    return 0.5 * (gram_parts(left, right) + gram_parts(right, left))


def finish(parts, place=0):
    size = parts.shape[0]

    def block(index):
        shift = (place - index) * size % LANES
        return pltpu.roll(parts, shift, 1) if shift else parts

    return block(2) + block(1) + block(0)


def pack(wide):
    rows = wide.shape[0]
    folds = LANES // rows
    height = rows // folds
    lanes = lax.broadcasted_iota(jnp.int32, wide.shape, 1)
    wide = jnp.where(lanes < rows, wide, 0.0)
    total = wide[:height]
    for i in range(1, folds):
        total = total + pltpu.roll(wide[i * height : (i + 1) * height], i * rows, 1)
    return total


def unpack(folded, size, place=0):
    parts = []
    for i in range(LANES // size):
        shift = (place - i) * size % LANES
        parts.append(pltpu.roll(folded, shift, 1) if shift else folded)
    return jnp.concatenate(parts, axis=0)


def solve_wide(target, matrix):
    size = matrix.shape[0]
    row_ids = lax.broadcasted_iota(jnp.int32, (size, LANES), 0)
    lane_ids = lax.broadcasted_iota(jnp.int32, (size, LANES), 1)
    work = jnp.where(lane_ids < size, target, matrix)
    for base in range(0, size, PIVOTS):
        columns = [
            jnp.broadcast_to(work[:, size + base + i : size + base + i + 1], (size, LANES))
            for i in range(PIVOTS)
        ]
        for i in range(PIVOTS):
            pivot = base + i
            here = row_ids == pivot
            inverse = pltpu.reciprocal(columns[i][pivot : pivot + 1, :], full_range=False)
            row = work[pivot : pivot + 1, :] * inverse
            work = jnp.where(here, row, work - columns[i] * row)
            for later in range(i + 1, PIVOTS):
                entry = columns[later][pivot : pivot + 1, :] * inverse
                columns[later] = jnp.where(here, entry, columns[later] - columns[i] * entry)
    return work


def add_up(values):
    values = list(values)
    while len(values) > 1:
        pairs = [values[i] + values[i + 1] for i in range(0, len(values) - 1, 2)]
        values = pairs + values[len(values) - len(values) % 2 :]
    return values[0]


def add_tiles(rows_dev, lists, tiles, first_tile, start, stop, total):
    rows_ref, cols_ref = lists
    tile = total.shape[1]
    slots = rows_ref.shape[0]
    blocks = rows_dev // tile
    row_place = lax.axis_index("row")
    col_place = lax.axis_index("col")
    col_devices = lax.axis_size("col")
    row_blocks = col_devices * blocks

    def place(slot):
        row = rows_ref[slot]
        column = cols_ref[slot]
        side = lax.rem(row // blocks + col_devices - col_place, col_devices)
        owner = column // (blocks * col_devices)
        column_at = (owner ^ row_place) * blocks + lax.rem(column, blocks)
        return column_at * row_blocks + side * blocks + lax.rem(row, blocks)

    def after(slot):
        return place(jnp.minimum(slot, slots - 1))

    def add(turn, places):
        slot = start + 2 * turn
        values = [tiles[slot + i - first_tile].astype(F32) for i in range(2)]
        following = (after(slot + 2), after(slot + 3))
        for at, value in zip(places, values):
            total[at] = total[at] + value
        return following

    places = lax.fori_loop(0, (stop - start) // 2, add, (after(start), after(start + 1)))

    @pl.when(lax.rem(stop - start, 2) == 1)
    def _():
        total[places[0]] = total[places[0]] + tiles[stop - 1 - first_tile].astype(F32)


def copy_lists(hbm_refs, smem_refs, sems):
    copies = [
        pltpu.make_async_copy(source, target, sems.at[i])
        for i, (source, target) in enumerate(zip(hbm_refs, smem_refs))
    ]
    for copy in copies:
        copy.start()
    return copies


def gather_kernel(rows_dev, count_ref, rows_hbm, cols_hbm, tiles_ref, total, rest, *scratch):
    held, rows_ref, cols_ref, sems, list_sems = scratch
    live = count_ref[0]
    half = held.shape[0]
    slots, tile = tiles_ref.shape[:2]
    chunk = -(-half // CHUNKS)
    lists = copy_lists((rows_hbm, cols_hbm), (rows_ref, cols_ref), list_sems)
    copies = []
    for c in range(CHUNKS):
        part = pl.ds(c * chunk, min(chunk, half - c * chunk))
        copies.append(pltpu.make_async_copy(tiles_ref.at[part], held.at[part], sems.at[c]))

        @pl.when(c * chunk < live)
        def _():
            copies[c].start()

    chunk_rest = -(-rest.shape[0] // CHUNKS)
    rest_copies = []
    for c in range(CHUNKS):
        start = c * chunk_rest
        length = min(chunk_rest, rest.shape[0] - start)
        copy = pltpu.make_async_copy(
            tiles_ref.at[pl.ds(half + start, length)],
            rest.at[pl.ds(start, length)],
            sems.at[CHUNKS + c],
        )
        rest_copies.append((half + start, copy))

        @pl.when(half + start < live)
        def _():
            copy.start()

    def clear(index, carry):
        total[index] = jnp.zeros((tile, tile), F32)
        return carry

    lax.fori_loop(0, total.shape[0], clear, 0, unroll=4)
    for copy in lists:
        copy.wait()
    for c in range(CHUNKS):
        start, stop = c * chunk, min((c + 1) * chunk, half)

        @pl.when(start < live)
        def _():
            copies[c].wait()
            add_tiles(
                rows_dev, (rows_ref, cols_ref), held, 0, start, jnp.minimum(live, stop), total
            )

    for start, copy in rest_copies:

        @pl.when(start < live)
        def _():
            copy.wait()


def dense_kernel(
    rows_dev, count_ref, rows_hbm, cols_hbm, rest, total_in, joined_ref, out_ref, total, *scratch
):
    rows_ref, cols_ref, list_sems = scratch
    live = count_ref[0]
    half = rows_ref.shape[0] - rest.shape[0]
    tile = total.shape[1]
    row_blocks = out_ref.shape[2] // tile

    @pl.when(half < live)
    def _():
        lists = copy_lists((rows_hbm, cols_hbm), (rows_ref, cols_ref), list_sems)
        for copy in lists:
            copy.wait()
        add_tiles(rows_dev, (rows_ref, cols_ref), rest, half, half, live, total)

    def part(index, carry):
        start = pl.multiple_of(index * tile, tile)
        for b in range(row_blocks):
            value = total[index * row_blocks + b].T
            high = value.astype(BF16)
            low = (value - high.astype(F32)).astype(BF16)
            out_ref[0, pl.ds(start, tile), pl.ds(b * tile, tile)] = high
            out_ref[1, pl.ds(start, tile), pl.ds(b * tile, tile)] = low
        return carry

    lax.fori_loop(0, total.shape[0] // row_blocks, part, 0)


def join_kernel(order, *refs):
    for k, ref in zip(order, refs):
        refs[-1][k] = ref[...]


def apply_dense(directions, matrix):
    rounded = jnp.concatenate([direction.astype(BF16) for direction in directions], axis=1)
    high, low = [
        jnp.dot(rounded, matrix[part], preferred_element_type=F32) for part in range(2)
    ]
    return high + low


def first_kernel(even_ref, odd_ref, matrix, out_ref, blocks_ref):
    pieces = blocks_ref.shape[0]
    values = [(odd_ref if k % 2 else even_ref)[k // 2] for k in range(pieces)]
    for k, value in enumerate(values):
        blocks_ref[k] = value
    rows = 2 * values[0].shape[1]
    joined = jnp.concatenate(values, axis=1)
    out_ref[:, rows:] = gram_parts(joined, joined)
    out_ref[:, :rows] = apply_dense(values, matrix)


def collect_kernel(near_ref, far_ref, residual_ref, direction_ref):
    pieces = near_ref.shape[0]
    for k in range(pieces):
        residual_ref[0, k] = near_ref[k]
        residual_ref[1, k] = far_ref[k]
        direction_ref[k] = near_ref[k]
    direction_ref[pieces] = far_ref[0]


def add_halves(mine_ref, other_ref, width):
    near = mine_ref[:, :width] + other_ref[:, width : 2 * width]
    far = mine_ref[:, width : 2 * width] + other_ref[:, :width]
    return near, far


def image_kernel(first, mine_ref, other_ref, near_ref, far_ref, *refs):
    out_ref, norm_ref = refs if first else (refs[0], None)
    core = lax.axis_index("col")
    size, width = near_ref.shape[1:]
    near, far = add_halves(mine_ref, other_ref, width)
    if first:
        norm_ref[...] = finish(mine_ref[:, 2 * width :] + other_ref[:, 2 * width :])
    parts = width // LANES
    for i in range(parts):
        lanes = slice(i * LANES, (i + 1) * LANES)
        for place, half in ((core, near), (1 - core, far)):
            at = pl.multiple_of((place * parts + i) * size, size)
            out_ref[pl.ds(at, size)] = half[:, lanes]
    products = symmetric_parts(near, near_ref[0]) + symmetric_parts(
        far, far_ref[far_ref.shape[0] - 1]
    )
    out_ref[2 * parts * size :] = pack(finish(products))


def inverse_kernel(norm_ref, out_ref):
    norm = norm_ref[...]
    size = norm.shape[0]
    norm = 0.5 * (norm + jnp.concatenate([norm[:, :size].T, norm[:, size:]], axis=1))
    unit = lax.broadcasted_iota(jnp.int32, norm.shape, 0) == lax.broadcasted_iota(
        jnp.int32, norm.shape, 1
    )
    out_ref[...] = solve_wide(jnp.where(unit, 1.0, 0.0), pltpu.roll(norm, size, 1))


def pick(refs, places, core, rows):
    if places[0] == places[1]:
        return refs[places[0]][rows]
    return jnp.where(core == 0, refs[places[0]][rows], refs[places[1]][rows])


def step_kernel(used, places, with_solution, last, *refs):
    images, refs = refs[:used], refs[used:]
    direction_ref, residual_ref, norm_ref, inverse_ref, matrix = refs[:5]
    refs = refs[5:]
    if with_solution:
        solution_ref, refs = refs[0], refs[1:]
    out_ref, new_direction, new_residual, new_norm, new_solution = refs
    core = lax.axis_index("col")
    pieces = len(places)
    size, width = direction_ref.shape[1:]
    parts = width // LANES

    def image(k, half):
        found = []
        for i in range(parts):
            at = pl.multiple_of((half * parts + i) * size, size)
            found.append(pick(images, places[k], core, pl.ds(at, size)))
        return jnp.concatenate(found, axis=1)

    behind = slice(2 * parts * size, None)
    products = add_up([pick(images, pair, core, behind) for pair in places])
    alpha = stack(solve_wide(norm_ref[...], unpack(products, size, 1))[:, :size])
    residuals = [
        [residual_ref[side, k] - times(alpha, image(k, half)) for k in range(pieces)]
        for side, half in enumerate((core, 1 - core))
    ]
    joined = [jnp.concatenate(values, axis=1) for values in residuals]
    next_norm = finish(gram_parts(joined[0], joined[0]) + gram_parts(joined[1], joined[1]))
    new_norm[...] = next_norm
    step = times(alpha, direction_ref[0])
    new_solution[...] = solution_ref[...] + step if with_solution else step
    beta = stack(mul(inverse_ref[:, :size], next_norm[:, :size]))
    directions = [
        residual + times(beta, direction_ref[k])
        for k, residual in enumerate(residuals[0] + residuals[1][:1])
    ]
    if last:
        new_residual[...] = residuals[0][0]
        new_direction[0] = directions[0]
        new_direction[1] = directions[pieces]
    else:
        for k in range(pieces):
            new_residual[0, k] = residuals[0][k]
            new_residual[1, k] = residuals[1][k]
        for k in range(pieces + 1):
            new_direction[k] = directions[k]
    out_ref[...] = apply_dense(directions[:pieces], matrix)


def last_image_kernel(mine_ref, other_ref, direction_ref, near_ref, gram_ref):
    near, far = add_halves(mine_ref, other_ref, direction_ref.shape[2])
    near_ref[...] = near
    products = symmetric_parts(near, direction_ref[0]) + symmetric_parts(far, direction_ref[1])
    gram_ref[...] = pack(finish(products))


def last_kernel(used, places, *refs):
    image_ref, direction_ref, residual_ref, norm_ref, solution_ref = refs[used:-2]
    new_solution, new_residual = refs[-2:]
    core = lax.axis_index("col")
    size = image_ref.shape[0]
    products = add_up([pick(refs, pair, core, slice(None)) for pair in places])
    alpha = stack(solve_wide(norm_ref[...], unpack(products, size, 1))[:, :size])
    new_solution[...] = solution_ref[...] + times(alpha, direction_ref[0])
    new_residual[...] = residual_ref[...] - times(alpha, image_ref[...])


def shape(*dims, dtype=F32):
    return jax.ShapeDtypeStruct(dims, dtype)


def per_device(tiles, tile_rows, tile_cols, tile_count, signs, vertex_weight, column_scale):
    sketch, rows_dev = signs.shape
    tile = tiles.shape[1]
    pieces = lax.axis_size("row")
    col_devices = lax.axis_size("col")
    group = col_devices * rows_dev
    depth = pieces * rows_dev

    def swap(value, mask):
        return lax.ppermute(value, "row", [(i, i ^ mask) for i in range(pieces)])

    def across(value):
        return lax.ppermute(
            value, "col", [(i, (i + 1) % col_devices) for i in range(col_devices)]
        )

    def exchange(value):
        if pieces != 8:
            found = [value] + [swap(value, k) for k in range(1, pieces)]
            return found, [(k, k) for k in range(pieces)]

        def fetch(source, masks):
            pairs = [
                (i * 2 + core, (i ^ mask) * 2 + core)
                for core, mask in enumerate(masks)
                for i in range(pieces)
            ]
            return lax.ppermute(source, ("row", "col"), pairs)

        fetched = [fetch(value, masks) for masks in ((1, 4), (3, 6), (2, 1))]
        fetched.append(fetch(fetched[0], (6, 1)))
        found = [value, *fetched, *map(across, fetched)]
        return found, [(0, 0), (1, 3), (3, 7), (2, 6), (5, 1), (8, 4), (6, 2), (4, 8)]

    right_side = signs.astype(F32) * vertex_weight[None, :] * column_scale[:, None]
    far_side = across(right_side)[None]
    even = [right_side] + [swap(right_side, k) for k in range(2, pieces, 2)]

    matrix = shape(2, depth, group, dtype=BF16)
    total = shape(depth // tile * (group // tile), tile, tile)
    slots = tiles.shape[0]
    half = slots * 3 // 8
    rest = shape(slots - half, tile, tile, dtype=BF16)
    lists = [pltpu.with_memory_space_constraint(x, pltpu.HBM) for x in (tile_rows, tile_cols)]
    lists_scratch = [pltpu.SMEM(x.shape, jnp.int32) for x in lists]
    cost = pl.CostEstimate(
        flops=4 * tiles.size, bytes_accessed=4 * tiles.size, transcendentals=0
    )
    blocks_sum, others = pl.pallas_call(
        functools.partial(gather_kernel, rows_dev),
        out_shape=(total, rest),
        in_specs=[SMEM] + [HBM] * 3,
        out_specs=(VMEM, VMEM),
        scratch_shapes=[
            pltpu.VMEM((half, tile, tile), BF16),
            *lists_scratch,
            pltpu.SemaphoreType.DMA((2 * CHUNKS,)),
            pltpu.SemaphoreType.DMA((len(lists),)),
        ],
        compiler_params=params(tiles, total),
        cost_estimate=cost,
        name="gather",
    )(tile_count, *lists, pltpu.with_memory_space_constraint(tiles, pltpu.HBM))
    joined = shape(pieces // 2, sketch, rows_dev)
    order = [*range(pieces // 4, pieces // 2), *range(1, pieces // 4), 0]
    even = pl.pallas_call(
        functools.partial(join_kernel, order),
        out_shape=joined,
        in_specs=[VMEM] * (pieces // 2) + [ANY],
        out_specs=VMEM,
        compiler_params=params(joined, joined),
        name="join",
    )(*[even[k] for k in order], blocks_sum)
    odd = swap(even, 1)
    dense, _ = pl.pallas_call(
        functools.partial(dense_kernel, rows_dev),
        out_shape=(matrix, total),
        in_specs=[SMEM] + [HBM] * 2 + [VMEM, VMEM, ANY],
        out_specs=(VMEM, VMEM),
        scratch_shapes=[*lists_scratch, pltpu.SemaphoreType.DMA((len(lists),))],
        input_output_aliases={4: 1},
        compiler_params=params(rest, total, total, matrix),
        cost_estimate=cost,
        name="dense",
    )(tile_count, *lists, others, blocks_sum, even)

    held = shape(2, pieces, sketch, rows_dev)
    state = shape(pieces + 1, sketch, rows_dev)
    small = shape(sketch, LANES)
    piece = shape(sketch, rows_dev)
    packed = shape(sketch * sketch // LANES, LANES)
    payload = shape(2 * sketch * (rows_dev // LANES) + packed.shape[0], LANES)

    partial_sum, blocks = pl.pallas_call(
        first_kernel,
        out_shape=(shape(sketch, group + LANES), shape(pieces, sketch, rows_dev)),
        in_specs=[VMEM] * 3,
        out_specs=(VMEM, VMEM),
        compiler_params=params(matrix, state, state),
        name="first",
    )(even, odd, dense)
    norm = None
    solution = None
    direction = None
    for iteration in range(ITERS - 1):
        first = iteration == 0
        last = iteration == ITERS - 2
        sums = (partial_sum, across(partial_sum))
        given = (even, far_side) if first else (direction, direction)
        outs = pl.pallas_call(
            functools.partial(image_kernel, first),
            out_shape=(payload, small) if first else (payload,),
            in_specs=[VMEM] * 4,
            out_specs=(VMEM, VMEM) if first else (VMEM,),
            compiler_params=params(state, payload),
            name="image",
        )(*sums, *given)
        found, places = exchange(outs[0])
        if first:
            norm = outs[1]
            residual, direction = pl.pallas_call(
                collect_kernel,
                out_shape=(held, state),
                in_specs=[VMEM] * 2,
                out_specs=(VMEM, VMEM),
                compiler_params=params(held, held, state),
                name="collect",
            )(blocks, across(blocks))
        inverse = pl.pallas_call(
            inverse_kernel,
            out_shape=small,
            in_specs=[VMEM],
            out_specs=VMEM,
            compiler_params=params(),
            name="inverse",
        )(norm)
        given = () if first else (solution,)
        partial_sum, direction, residual, norm, solution = pl.pallas_call(
            functools.partial(step_kernel, len(found), places, not first, last),
            out_shape=(
                shape(sketch, group),
                shape(2, sketch, rows_dev) if last else state,
                piece if last else held,
                small,
                piece,
            ),
            in_specs=[VMEM] * (len(found) + 5 + len(given)),
            out_specs=(VMEM,) * 5,
            compiler_params=params(matrix, held, held, held, held, state),
            name="step",
        )(*found, direction, residual, norm, inverse, dense, *given)
    near, gram = pl.pallas_call(
        last_image_kernel,
        out_shape=(piece, packed),
        in_specs=[VMEM] * 3,
        out_specs=(VMEM, VMEM),
        compiler_params=params(state),
        name="last_image",
    )(partial_sum, across(partial_sum), direction)
    found, places = exchange(gram)
    return pl.pallas_call(
        functools.partial(last_kernel, len(found), places),
        out_shape=(piece, piece),
        in_specs=[VMEM] * (len(found) + 5),
        out_specs=(VMEM, VMEM),
        compiler_params=params(state, state),
        name="last",
    )(*found, near, direction, residual, norm, solution)


def solution(mesh):
    return jax.shard_map(
        per_device,
        mesh=mesh,
        in_specs=(
            P(("row", "col"), None, None),
            P(("row", "col")),
            P(("row", "col")),
            P(("row", "col")),
            P("rhs", ("row", "col")),
            P(("row", "col")),
            P("rhs"),
        ),
        out_specs=(P("rhs", ("row", "col")), P("rhs", ("row", "col"))),
        check_vma=False,
    )
```

```python
import functools

import jax
import jax.numpy as jnp
from jax import lax
from jax.experimental import pallas as pl
from jax.experimental.pallas import tpu as pltpu
from jax.sharding import PartitionSpec as P

ITERS = 3
LANES = 128
PIVOTS = 8
CHUNKS = 5
F32 = jnp.float32
BF16 = jnp.bfloat16
SPARE_BYTES = 4 * 1024 * 1024

VMEM = pl.BlockSpec(memory_space=pltpu.VMEM)
SMEM = pl.BlockSpec(memory_space=pltpu.SMEM)
HBM = pl.BlockSpec(memory_space=pltpu.HBM)
ANY = pl.BlockSpec(memory_space=pl.ANY)


def params(*arrays):
    used = sum(a.size * jnp.dtype(a.dtype).itemsize for a in arrays)
    return pltpu.CompilerParams(vmem_limit_bytes=used + SPARE_BYTES)


def split(value):
    high = value.astype(BF16)
    rest = value - high.astype(F32)
    middle = rest.astype(BF16)
    low = (rest - middle.astype(F32)).astype(BF16)
    return high, middle, low


def mul(left, right):
    return jnp.dot(left, right, precision=lax.Precision.HIGHEST, preferred_element_type=F32)


def stack(left):
    high, middle, low = [part.astype(F32) for part in split(left)]
    parts = jnp.concatenate([high, high, middle, high, middle, low], axis=0)
    return parts.T.astype(BF16)


def times(stacked, right):
    high, middle, low = split(right)
    parts = jnp.concatenate([high, middle, high, low, middle, high], axis=0)
    return jnp.dot(stacked, parts, preferred_element_type=F32)


def stack_leading(left):
    high, middle, _ = [part.astype(F32) for part in split(left)]
    return jnp.concatenate([high, high, middle], axis=0).T.astype(BF16)


def times_leading(stacked, right):
    high, middle, _ = split(right)
    parts = jnp.concatenate([high, middle, high], axis=0)
    return jnp.dot(stacked, parts, preferred_element_type=F32)


def gram_parts(left, right):
    size, width = left.shape
    filler = jnp.zeros((LANES - 3 * size, width), BF16)
    every = lax.dot_general(
        jnp.concatenate(split(left), axis=0),
        jnp.concatenate([*split(right), filler], axis=0),
        (((1,), (1,)), ((), ())),
        preferred_element_type=F32,
    )
    return every[2 * size :] + every[size : 2 * size] + every[:size]


def symmetric_parts(left, right):
    return 0.5 * (gram_parts(left, right) + gram_parts(right, left))


def finish(parts, place=0):
    size = parts.shape[0]

    def block(index):
        shift = (place - index) * size % LANES
        return pltpu.roll(parts, shift, 1) if shift else parts

    return block(2) + block(1) + block(0)


def pack(wide):
    rows = wide.shape[0]
    folds = LANES // rows
    height = rows // folds
    lanes = lax.broadcasted_iota(jnp.int32, wide.shape, 1)
    wide = jnp.where(lanes < rows, wide, 0.0)
    total = wide[:height]
    for i in range(1, folds):
        total = total + pltpu.roll(wide[i * height : (i + 1) * height], i * rows, 1)
    return total


def unpack(folded, size, place=0):
    parts = []
    for i in range(LANES // size):
        shift = (place - i) * size % LANES
        parts.append(pltpu.roll(folded, shift, 1) if shift else folded)
    return jnp.concatenate(parts, axis=0)


def solve_wide(target, matrix):
    size = matrix.shape[0]
    row_ids = lax.broadcasted_iota(jnp.int32, (size, LANES), 0)
    lane_ids = lax.broadcasted_iota(jnp.int32, (size, LANES), 1)
    work = jnp.where(lane_ids < size, target, matrix)
    for base in range(0, size, PIVOTS):
        columns = [
            jnp.broadcast_to(work[:, size + base + i : size + base + i + 1], (size, LANES))
            for i in range(PIVOTS)
        ]
        for i in range(PIVOTS):
            pivot = base + i
            here = row_ids == pivot
            inverse = pltpu.reciprocal(columns[i][pivot : pivot + 1, :], full_range=False)
            row = work[pivot : pivot + 1, :] * inverse
            work = jnp.where(here, row, work - columns[i] * row)
            for later in range(i + 1, PIVOTS):
                entry = columns[later][pivot : pivot + 1, :] * inverse
                columns[later] = jnp.where(here, entry, columns[later] - columns[i] * entry)
    return work


def add_up(values):
    values = list(values)
    while len(values) > 1:
        pairs = [values[i] + values[i + 1] for i in range(0, len(values) - 1, 2)]
        values = pairs + values[len(values) - len(values) % 2 :]
    return values[0]


def add_tiles(rows_dev, lists, tiles, first_tile, start, stop, total):
    rows_ref, cols_ref = lists
    tile = total.shape[1]
    slots = rows_ref.shape[0]
    blocks = rows_dev // tile
    row_place = lax.axis_index("row")
    col_place = lax.axis_index("col")
    col_devices = lax.axis_size("col")
    row_blocks = col_devices * blocks

    def place(slot):
        row = rows_ref[slot]
        column = cols_ref[slot]
        side = lax.rem(row // blocks + col_devices - col_place, col_devices)
        owner = column // (blocks * col_devices)
        column_at = (owner ^ row_place) * blocks + lax.rem(column, blocks)
        return column_at * row_blocks + side * blocks + lax.rem(row, blocks)

    def after(slot):
        return place(jnp.minimum(slot, slots - 1))

    def add(turn, places):
        slot = start + 2 * turn
        values = [tiles[slot + i - first_tile].astype(F32) for i in range(2)]
        following = (after(slot + 2), after(slot + 3))
        for at, value in zip(places, values):
            total[at] = total[at] + value
        return following

    places = lax.fori_loop(0, (stop - start) // 2, add, (after(start), after(start + 1)))

    @pl.when(lax.rem(stop - start, 2) == 1)
    def _():
        total[places[0]] = total[places[0]] + tiles[stop - 1 - first_tile].astype(F32)


def copy_lists(hbm_refs, smem_refs, sems):
    copies = [
        pltpu.make_async_copy(source, target, sems.at[i])
        for i, (source, target) in enumerate(zip(hbm_refs, smem_refs))
    ]
    for copy in copies:
        copy.start()
    return copies


def gather_kernel(rows_dev, count_ref, rows_hbm, cols_hbm, tiles_ref, total, rest, *scratch):
    held, rows_ref, cols_ref, sems, list_sems = scratch
    live = count_ref[0]
    half = held.shape[0]
    slots, tile = tiles_ref.shape[:2]
    chunk = -(-half // CHUNKS)
    lists = copy_lists((rows_hbm, cols_hbm), (rows_ref, cols_ref), list_sems)
    copies = []
    for c in range(CHUNKS):
        part = pl.ds(c * chunk, min(chunk, half - c * chunk))
        copies.append(pltpu.make_async_copy(tiles_ref.at[part], held.at[part], sems.at[c]))

        @pl.when(c * chunk < live)
        def _():
            copies[c].start()

    chunk_rest = -(-rest.shape[0] // CHUNKS)
    rest_copies = []
    for c in range(CHUNKS):
        start = c * chunk_rest
        length = min(chunk_rest, rest.shape[0] - start)
        copy = pltpu.make_async_copy(
            tiles_ref.at[pl.ds(half + start, length)],
            rest.at[pl.ds(start, length)],
            sems.at[CHUNKS + c],
        )
        rest_copies.append((half + start, copy))

        @pl.when(half + start < live)
        def _():
            copy.start()

    def clear(index, carry):
        total[index] = jnp.zeros((tile, tile), F32)
        return carry

    lax.fori_loop(0, total.shape[0], clear, 0, unroll=4)
    for copy in lists:
        copy.wait()
    for c in range(CHUNKS):
        start, stop = c * chunk, min((c + 1) * chunk, half)

        @pl.when(start < live)
        def _():
            copies[c].wait()
            add_tiles(
                rows_dev, (rows_ref, cols_ref), held, 0, start, jnp.minimum(live, stop), total
            )

    for start, copy in rest_copies:

        @pl.when(start < live)
        def _():
            copy.wait()


def dense_kernel(
    rows_dev, count_ref, rows_hbm, cols_hbm, rest, total_in, joined_ref, out_ref, total, *scratch
):
    rows_ref, cols_ref, list_sems = scratch
    live = count_ref[0]
    half = rows_ref.shape[0] - rest.shape[0]
    tile = total.shape[1]
    row_blocks = out_ref.shape[2] // tile

    @pl.when(half < live)
    def _():
        lists = copy_lists((rows_hbm, cols_hbm), (rows_ref, cols_ref), list_sems)
        for copy in lists:
            copy.wait()
        add_tiles(rows_dev, (rows_ref, cols_ref), rest, half, half, live, total)

    def part(index, carry):
        start = pl.multiple_of(index * tile, tile)
        for b in range(row_blocks):
            value = total[index * row_blocks + b].T
            high = value.astype(BF16)
            low = (value - high.astype(F32)).astype(BF16)
            out_ref[0, pl.ds(start, tile), pl.ds(b * tile, tile)] = high
            out_ref[1, pl.ds(start, tile), pl.ds(b * tile, tile)] = low
        return carry

    lax.fori_loop(0, total.shape[0] // row_blocks, part, 0)


def join_kernel(order, *refs):
    for k, ref in zip(order, refs):
        refs[-1][k] = ref[...]


def apply_dense(directions, matrix):
    rounded = jnp.concatenate([direction.astype(BF16) for direction in directions], axis=1)
    high, low = [
        jnp.dot(rounded, matrix[part], preferred_element_type=F32) for part in range(2)
    ]
    return high + low


def first_kernel(even_ref, odd_ref, matrix, out_ref, odd_out_ref):
    pieces = 2 * even_ref.shape[0]
    odd_out_ref[...] = odd_ref[...]
    values = [(odd_ref if k % 2 else even_ref)[k // 2] for k in range(pieces)]
    rows = 2 * values[0].shape[1]
    joined = jnp.concatenate(values, axis=1)
    out_ref[:, rows:] = gram_parts(joined, joined)
    out_ref[:, :rows] = apply_dense(values, matrix)


def collect_kernel(even_ref, odd_ref, far_even_ref, far_odd_ref, residual_ref, direction_ref):
    pieces = 2 * even_ref.shape[0]
    for k in range(pieces):
        near = (odd_ref if k % 2 else even_ref)[k // 2]
        residual_ref[0, k] = near
        residual_ref[1, k] = (far_odd_ref if k % 2 else far_even_ref)[k // 2]
        direction_ref[k] = near
    direction_ref[pieces] = far_even_ref[0]


def add_halves(mine_ref, other_ref, width):
    near = mine_ref[:, :width] + other_ref[:, width : 2 * width]
    far = mine_ref[:, width : 2 * width] + other_ref[:, :width]
    return near, far


def image_kernel(first, mine_ref, other_ref, near_ref, far_ref, *refs):
    out_ref, norm_ref = refs if first else (refs[0], None)
    core = lax.axis_index("col")
    size, width = near_ref.shape[1:]
    near, far = add_halves(mine_ref, other_ref, width)
    if first:
        norm_ref[...] = finish(mine_ref[:, 2 * width :] + other_ref[:, 2 * width :])
    parts = width // LANES
    for i in range(parts):
        lanes = slice(i * LANES, (i + 1) * LANES)
        for place, half in ((core, near), (1 - core, far)):
            at = pl.multiple_of((place * parts + i) * size, size)
            out_ref[pl.ds(at, size)] = half[:, lanes]
    products = symmetric_parts(near, near_ref[0]) + symmetric_parts(
        far, far_ref[0 if first else far_ref.shape[0] - 1]
    )
    out_ref[2 * parts * size :] = pack(finish(products))


def inverse_kernel(norm_ref, out_ref):
    norm = norm_ref[...]
    size = norm.shape[0]
    norm = 0.5 * (norm + jnp.concatenate([norm[:, :size].T, norm[:, size:]], axis=1))
    unit = lax.broadcasted_iota(jnp.int32, norm.shape, 0) == lax.broadcasted_iota(
        jnp.int32, norm.shape, 1
    )
    out_ref[...] = solve_wide(jnp.where(unit, 1.0, 0.0), pltpu.roll(norm, size, 1))


def pick(refs, places, core, rows):
    if places[0] == places[1]:
        return refs[places[0]][rows]
    return jnp.where(core == 0, refs[places[0]][rows], refs[places[1]][rows])


def step_kernel(used, places, with_solution, last, *refs):
    images, refs = refs[:used], refs[used:]
    direction_ref, residual_ref, norm_ref, inverse_ref, matrix = refs[:5]
    refs = refs[5:]
    if with_solution:
        solution_ref, refs = refs[0], refs[1:]
    out_ref, new_direction, new_residual, new_norm, new_solution = refs
    core = lax.axis_index("col")
    pieces = len(places)
    size, width = direction_ref.shape[1:]
    parts = width // LANES

    def image(k, half):
        found = []
        for i in range(parts):
            at = pl.multiple_of((half * parts + i) * size, size)
            found.append(pick(images, places[k], core, pl.ds(at, size)))
        return jnp.concatenate(found, axis=1)

    behind = slice(2 * parts * size, None)
    products = add_up([pick(images, pair, core, behind) for pair in places])
    alpha = stack(solve_wide(norm_ref[...], unpack(products, size, 1))[:, :size])
    residuals = [
        [residual_ref[side, k] - times(alpha, image(k, half)) for k in range(pieces)]
        for side, half in enumerate((core, 1 - core))
    ]
    joined = [jnp.concatenate(values, axis=1) for values in residuals]
    next_norm = finish(gram_parts(joined[0], joined[0]) + gram_parts(joined[1], joined[1]))
    new_norm[...] = next_norm
    step = times(alpha, direction_ref[0])
    new_solution[...] = solution_ref[...] + step if with_solution else step
    beta = stack_leading(mul(inverse_ref[:, :size], next_norm[:, :size]))
    directions = [
        residual + times_leading(beta, direction_ref[k])
        for k, residual in enumerate(residuals[0] + residuals[1][:1])
    ]
    if last:
        new_residual[...] = residuals[0][0]
        new_direction[0] = directions[0]
        new_direction[1] = directions[pieces]
    else:
        for k in range(pieces):
            new_residual[0, k] = residuals[0][k]
            new_residual[1, k] = residuals[1][k]
        for k in range(pieces + 1):
            new_direction[k] = directions[k]
    out_ref[...] = apply_dense(directions[:pieces], matrix)


def last_image_kernel(mine_ref, other_ref, direction_ref, near_ref, gram_ref):
    near, far = add_halves(mine_ref, other_ref, direction_ref.shape[2])
    near_ref[...] = near
    products = symmetric_parts(near, direction_ref[0]) + symmetric_parts(far, direction_ref[1])
    gram_ref[...] = pack(finish(products))


def last_kernel(used, places, *refs):
    image_ref, direction_ref, residual_ref, norm_ref, solution_ref = refs[used:-2]
    new_solution, new_residual = refs[-2:]
    core = lax.axis_index("col")
    size = image_ref.shape[0]
    products = add_up([pick(refs, pair, core, slice(None)) for pair in places])
    alpha = stack(solve_wide(norm_ref[...], unpack(products, size, 1))[:, :size])
    new_solution[...] = solution_ref[...] + times(alpha, direction_ref[0])
    new_residual[...] = residual_ref[...] - times(alpha, image_ref[...])


def shape(*dims, dtype=F32):
    return jax.ShapeDtypeStruct(dims, dtype)


def per_device(tiles, tile_rows, tile_cols, tile_count, signs, vertex_weight, column_scale):
    sketch, rows_dev = signs.shape
    tile = tiles.shape[1]
    pieces = lax.axis_size("row")
    col_devices = lax.axis_size("col")
    group = col_devices * rows_dev
    depth = pieces * rows_dev

    def swap(value, mask):
        return lax.ppermute(value, "row", [(i, i ^ mask) for i in range(pieces)])

    def across(value):
        return lax.ppermute(
            value, "col", [(i, (i + 1) % col_devices) for i in range(col_devices)]
        )

    def exchange(value):
        if pieces != 8:
            found = [value] + [swap(value, k) for k in range(1, pieces)]
            return found, [(k, k) for k in range(pieces)]
        turns = ((7, 5), (3, 6), (2, 4), (1, 1))
        fetched = []
        passed = []
        places = {0: (0, 0)}
        for turn, masks in enumerate(turns, 1):
            pairs = [
                (i * 2 + core, (i ^ mask) * 2 + core)
                for core, mask in enumerate(masks)
                for i in range(pieces)
            ]
            fetched.append(lax.ppermute(value, ("row", "col"), pairs))
            if masks[0] == masks[1]:
                places[masks[0]] = (turn, turn)
            else:
                passed.append(across(fetched[-1]))
                places[masks[0]] = (turn, turn + len(turns))
                places[masks[1]] = (turn + len(turns), turn)
        return [value, *fetched, *passed], [places[k] for k in range(pieces)]

    right_side = signs.astype(F32) * vertex_weight[None, :] * column_scale[:, None]
    even = [right_side] + [swap(right_side, k) for k in range(2, pieces, 2)]

    matrix = shape(2, depth, group, dtype=BF16)
    total = shape(depth // tile * (group // tile), tile, tile)
    slots = tiles.shape[0]
    half = slots * 3 // 8
    rest = shape(slots - half, tile, tile, dtype=BF16)
    lists = [pltpu.with_memory_space_constraint(x, pltpu.HBM) for x in (tile_rows, tile_cols)]
    lists_scratch = [pltpu.SMEM(x.shape, jnp.int32) for x in lists]
    cost = pl.CostEstimate(
        flops=4 * tiles.size, bytes_accessed=4 * tiles.size, transcendentals=0
    )
    blocks_sum, others = pl.pallas_call(
        functools.partial(gather_kernel, rows_dev),
        out_shape=(total, rest),
        in_specs=[SMEM] + [HBM] * 3,
        out_specs=(VMEM, VMEM),
        scratch_shapes=[
            pltpu.VMEM((half, tile, tile), BF16),
            *lists_scratch,
            pltpu.SemaphoreType.DMA((2 * CHUNKS,)),
            pltpu.SemaphoreType.DMA((len(lists),)),
        ],
        compiler_params=params(tiles, total),
        cost_estimate=cost,
        name="gather",
    )(tile_count, *lists, pltpu.with_memory_space_constraint(tiles, pltpu.HBM))
    joined = shape(pieces // 2, sketch, rows_dev)
    order = [*range(pieces // 4, pieces // 2), *range(1, pieces // 4), 0]
    even = pl.pallas_call(
        functools.partial(join_kernel, order),
        out_shape=joined,
        in_specs=[VMEM] * (pieces // 2) + [ANY],
        out_specs=VMEM,
        compiler_params=params(joined, joined),
        name="join",
    )(*[even[k] for k in order], blocks_sum)
    odd = swap(even, 1)
    far_even = across(even)
    dense, _ = pl.pallas_call(
        functools.partial(dense_kernel, rows_dev),
        out_shape=(matrix, total),
        in_specs=[SMEM] + [HBM] * 2 + [VMEM, VMEM, ANY],
        out_specs=(VMEM, VMEM),
        scratch_shapes=[*lists_scratch, pltpu.SemaphoreType.DMA((len(lists),))],
        input_output_aliases={4: 1},
        compiler_params=params(rest, total, total, matrix),
        cost_estimate=cost,
        name="dense",
    )(tile_count, *lists, others, blocks_sum, even)

    held = shape(2, pieces, sketch, rows_dev)
    state = shape(pieces + 1, sketch, rows_dev)
    small = shape(sketch, LANES)
    piece = shape(sketch, rows_dev)
    packed = shape(sketch * sketch // LANES, LANES)
    payload = shape(2 * sketch * (rows_dev // LANES) + packed.shape[0], LANES)

    partial_sum, odd = pl.pallas_call(
        first_kernel,
        out_shape=(shape(sketch, group + LANES), joined),
        in_specs=[VMEM] * 3,
        out_specs=(VMEM, VMEM),
        compiler_params=params(matrix, state, state),
        name="first",
    )(even, odd, dense)
    norm = None
    solution = None
    direction = None
    for iteration in range(ITERS - 1):
        first = iteration == 0
        last = iteration == ITERS - 2
        sums = (partial_sum, across(partial_sum))
        given = (even, far_even) if first else (direction, direction)
        outs = pl.pallas_call(
            functools.partial(image_kernel, first),
            out_shape=(payload, small) if first else (payload,),
            in_specs=[VMEM] * 4,
            out_specs=(VMEM, VMEM) if first else (VMEM,),
            compiler_params=params(state, payload),
            name="image",
        )(*sums, *given)
        found, places = exchange(outs[0])
        if first:
            norm = outs[1]
            residual, direction = pl.pallas_call(
                collect_kernel,
                out_shape=(held, state),
                in_specs=[VMEM] * 4,
                out_specs=(VMEM, VMEM),
                compiler_params=params(held, held, state),
                name="collect",
            )(even, odd, far_even, across(odd))
        inverse = pl.pallas_call(
            inverse_kernel,
            out_shape=small,
            in_specs=[VMEM],
            out_specs=VMEM,
            compiler_params=params(),
            name="inverse",
        )(norm)
        given = () if first else (solution,)
        partial_sum, direction, residual, norm, solution = pl.pallas_call(
            functools.partial(step_kernel, len(found), places, not first, last),
            out_shape=(
                shape(sketch, group),
                shape(2, sketch, rows_dev) if last else state,
                piece if last else held,
                small,
                piece,
            ),
            in_specs=[VMEM] * (len(found) + 5 + len(given)),
            out_specs=(VMEM,) * 5,
            compiler_params=params(matrix, held, held, held, held, state),
            name="step",
        )(*found, direction, residual, norm, inverse, dense, *given)
    near, gram = pl.pallas_call(
        last_image_kernel,
        out_shape=(piece, packed),
        in_specs=[VMEM] * 3,
        out_specs=(VMEM, VMEM),
        compiler_params=params(state),
        name="last_image",
    )(partial_sum, across(partial_sum), direction)
    found, places = exchange(gram)
    return pl.pallas_call(
        functools.partial(last_kernel, len(found), places),
        out_shape=(piece, piece),
        in_specs=[VMEM] * (len(found) + 5),
        out_specs=(VMEM, VMEM),
        compiler_params=params(state, state),
        name="last",
    )(*found, near, direction, residual, norm, solution)


def solution(mesh):
    return jax.shard_map(
        per_device,
        mesh=mesh,
        in_specs=(
            P(("row", "col"), None, None),
            P(("row", "col")),
            P(("row", "col")),
            P(("row", "col")),
            P("rhs", ("row", "col")),
            P(("row", "col")),
            P("rhs"),
        ),
        out_specs=(P("rhs", ("row", "col")), P("rhs", ("row", "col"))),
        check_vma=False,
    )
```

```python
import functools

import jax
import jax.numpy as jnp
from jax import lax
from jax.experimental import pallas as pl
from jax.experimental.pallas import tpu as pltpu
from jax.sharding import PartitionSpec as P

ITERS = 3
LANES = 128
PIVOTS = 8
CHUNKS = 5
F32 = jnp.float32
BF16 = jnp.bfloat16
SPARE_BYTES = 4 * 1024 * 1024

VMEM = pl.BlockSpec(memory_space=pltpu.VMEM)
SMEM = pl.BlockSpec(memory_space=pltpu.SMEM)
HBM = pl.BlockSpec(memory_space=pltpu.HBM)
ANY = pl.BlockSpec(memory_space=pl.ANY)


def params(*arrays):
    used = sum(a.size * jnp.dtype(a.dtype).itemsize for a in arrays)
    return pltpu.CompilerParams(vmem_limit_bytes=used + SPARE_BYTES)


def split(value):
    high = value.astype(BF16)
    rest = value - high.astype(F32)
    middle = rest.astype(BF16)
    low = (rest - middle.astype(F32)).astype(BF16)
    return high, middle, low


def stack(left):
    high, middle, low = [part.astype(F32) for part in split(left)]
    parts = jnp.concatenate([high, high, middle, high, middle, low], axis=0)
    return parts.T.astype(BF16)


def times(stacked, right):
    high, middle, low = split(right)
    parts = jnp.concatenate([high, middle, high, low, middle, high], axis=0)
    return jnp.dot(stacked, parts, preferred_element_type=F32)


def stack_leading(left):
    high, middle, _ = [part.astype(F32) for part in split(left)]
    return jnp.concatenate([high, high, middle], axis=0).T.astype(BF16)


def times_leading(stacked, right):
    high, middle, _ = split(right)
    parts = jnp.concatenate([high, middle, high], axis=0)
    return jnp.dot(stacked, parts, preferred_element_type=F32)


def gram_parts(left, right):
    size, width = left.shape
    filler = jnp.zeros((LANES - 3 * size, width), BF16)
    every = lax.dot_general(
        jnp.concatenate(split(left), axis=0),
        jnp.concatenate([*split(right), filler], axis=0),
        (((1,), (1,)), ((), ())),
        preferred_element_type=F32,
    )
    return every[2 * size :] + every[size : 2 * size] + every[:size]


def symmetric_parts(left, right):
    return 0.5 * (gram_parts(left, right) + gram_parts(right, left))


def finish(parts, place=0):
    size = parts.shape[0]

    def block(index):
        shift = (place - index) * size % LANES
        return pltpu.roll(parts, shift, 1) if shift else parts

    return block(2) + block(1) + block(0)


def pack(wide):
    rows = wide.shape[0]
    folds = LANES // rows
    height = rows // folds
    lanes = lax.broadcasted_iota(jnp.int32, wide.shape, 1)
    wide = jnp.where(lanes < rows, wide, 0.0)
    total = wide[:height]
    for i in range(1, folds):
        total = total + pltpu.roll(wide[i * height : (i + 1) * height], i * rows, 1)
    return total


def unpack(folded, size, place=0):
    parts = []
    for i in range(LANES // size):
        shift = (place - i) * size % LANES
        parts.append(pltpu.roll(folded, shift, 1) if shift else folded)
    return jnp.concatenate(parts, axis=0)


def solve_wide(target, matrix):
    size = matrix.shape[0]
    row_ids = lax.broadcasted_iota(jnp.int32, (size, LANES), 0)
    lane_ids = lax.broadcasted_iota(jnp.int32, (size, LANES), 1)
    work = jnp.where(lane_ids < size, target, matrix)
    for base in range(0, size, PIVOTS):
        columns = [
            jnp.broadcast_to(work[:, size + base + i : size + base + i + 1], (size, LANES))
            for i in range(PIVOTS)
        ]
        for i in range(PIVOTS):
            pivot = base + i
            here = row_ids == pivot
            inverse = pltpu.reciprocal(columns[i][pivot : pivot + 1, :], full_range=False)
            row = work[pivot : pivot + 1, :] * inverse
            work = jnp.where(here, row, work - columns[i] * row)
            for later in range(i + 1, PIVOTS):
                entry = columns[later][pivot : pivot + 1, :] * inverse
                columns[later] = jnp.where(here, entry, columns[later] - columns[i] * entry)
    return work


def add_up(values):
    values = list(values)
    while len(values) > 1:
        pairs = [values[i] + values[i + 1] for i in range(0, len(values) - 1, 2)]
        values = pairs + values[len(values) - len(values) % 2 :]
    return values[0]


def add_tiles(rows_dev, lists, tiles, first_tile, start, stop, total):
    rows_ref, cols_ref = lists
    tile = total.shape[1]
    slots = rows_ref.shape[0]
    blocks = rows_dev // tile
    row_place = lax.axis_index("row")
    col_place = lax.axis_index("col")
    col_devices = lax.axis_size("col")
    row_blocks = col_devices * blocks

    def place(slot):
        row = rows_ref[slot]
        column = cols_ref[slot]
        side = lax.rem(row // blocks + col_devices - col_place, col_devices)
        owner = column // (blocks * col_devices)
        column_at = (owner ^ row_place) * blocks + lax.rem(column, blocks)
        return column_at * row_blocks + side * blocks + lax.rem(row, blocks)

    def after(slot):
        return place(jnp.minimum(slot, slots - 1))

    def add(turn, places):
        slot = start + 2 * turn
        values = [tiles[slot + i - first_tile].astype(F32) for i in range(2)]
        following = (after(slot + 2), after(slot + 3))
        for at, value in zip(places, values):
            total[at] = total[at] + value
        return following

    places = lax.fori_loop(0, (stop - start) // 2, add, (after(start), after(start + 1)))

    @pl.when(lax.rem(stop - start, 2) == 1)
    def _():
        total[places[0]] = total[places[0]] + tiles[stop - 1 - first_tile].astype(F32)


def copy_lists(hbm_refs, smem_refs, sems):
    copies = [
        pltpu.make_async_copy(source, target, sems.at[i])
        for i, (source, target) in enumerate(zip(hbm_refs, smem_refs))
    ]
    for copy in copies:
        copy.start()
    return copies


def gather_kernel(rows_dev, count_ref, rows_hbm, cols_hbm, tiles_ref, total, rest, *scratch):
    held, rows_ref, cols_ref, sems, list_sems = scratch
    live = count_ref[0]
    half = held.shape[0]
    slots, tile = tiles_ref.shape[:2]
    chunk = -(-half // CHUNKS)
    lists = copy_lists((rows_hbm, cols_hbm), (rows_ref, cols_ref), list_sems)
    copies = []
    for c in range(CHUNKS):
        part = pl.ds(c * chunk, min(chunk, half - c * chunk))
        copies.append(pltpu.make_async_copy(tiles_ref.at[part], held.at[part], sems.at[c]))

        @pl.when(c * chunk < live)
        def _():
            copies[c].start()

    chunk_rest = -(-rest.shape[0] // CHUNKS)
    rest_copies = []
    for c in range(CHUNKS):
        start = c * chunk_rest
        length = min(chunk_rest, rest.shape[0] - start)
        copy = pltpu.make_async_copy(
            tiles_ref.at[pl.ds(half + start, length)],
            rest.at[pl.ds(start, length)],
            sems.at[CHUNKS + c],
        )
        rest_copies.append((half + start, copy))

        @pl.when(half + start < live)
        def _():
            copy.start()

    def clear(index, carry):
        total[index] = jnp.zeros((tile, tile), F32)
        return carry

    lax.fori_loop(0, total.shape[0], clear, 0, unroll=4)
    for copy in lists:
        copy.wait()
    for c in range(CHUNKS):
        start, stop = c * chunk, min((c + 1) * chunk, half)

        @pl.when(start < live)
        def _():
            copies[c].wait()
            add_tiles(
                rows_dev, (rows_ref, cols_ref), held, 0, start, jnp.minimum(live, stop), total
            )

    for start, copy in rest_copies:

        @pl.when(start < live)
        def _():
            copy.wait()


def dense_kernel(
    rows_dev, count_ref, rows_hbm, cols_hbm, rest, total_in, joined_ref, out_ref, total, *scratch
):
    rows_ref, cols_ref, list_sems = scratch
    live = count_ref[0]
    half = rows_ref.shape[0] - rest.shape[0]
    tile = total.shape[1]
    row_blocks = out_ref.shape[2] // tile

    @pl.when(half < live)
    def _():
        lists = copy_lists((rows_hbm, cols_hbm), (rows_ref, cols_ref), list_sems)
        for copy in lists:
            copy.wait()
        add_tiles(rows_dev, (rows_ref, cols_ref), rest, half, half, live, total)

    def part(index, carry):
        start = pl.multiple_of(index * tile, tile)
        for b in range(row_blocks):
            value = total[index * row_blocks + b].T
            high = value.astype(BF16)
            low = (value - high.astype(F32)).astype(BF16)
            out_ref[0, pl.ds(start, tile), pl.ds(b * tile, tile)] = high
            out_ref[1, pl.ds(start, tile), pl.ds(b * tile, tile)] = low
        return carry

    lax.fori_loop(0, total.shape[0] // row_blocks, part, 0)


def join_kernel(order, *refs):
    for k, ref in zip(order, refs):
        refs[-1][k] = ref[...]


def apply_dense(directions, matrix):
    rounded = jnp.concatenate([direction.astype(BF16) for direction in directions], axis=1)
    high, low = [
        jnp.dot(rounded, matrix[part], preferred_element_type=F32) for part in range(2)
    ]
    return high + low


def first_kernel(even_ref, odd_ref, matrix, out_ref, odd_out_ref):
    pieces = 2 * even_ref.shape[0]
    odd_out_ref[...] = odd_ref[...]
    values = [(odd_ref if k % 2 else even_ref)[k // 2] for k in range(pieces)]
    rows = 2 * values[0].shape[1]
    joined = jnp.concatenate(values, axis=1)
    out_ref[:, rows:] = gram_parts(joined, joined)
    out_ref[:, :rows] = apply_dense(values, matrix)


def collect_kernel(even_ref, odd_ref, far_even_ref, far_odd_ref, residual_ref, direction_ref):
    pieces = 2 * even_ref.shape[0]
    for k in range(pieces):
        near = (odd_ref if k % 2 else even_ref)[k // 2]
        residual_ref[0, k] = near
        residual_ref[1, k] = (far_odd_ref if k % 2 else far_even_ref)[k // 2]
        direction_ref[k] = near
    direction_ref[pieces] = far_even_ref[0]


def add_halves(mine_ref, other_ref, width):
    near = mine_ref[:, :width] + other_ref[:, width : 2 * width]
    far = mine_ref[:, width : 2 * width] + other_ref[:, :width]
    return near, far


def image_kernel(first, mine_ref, other_ref, near_ref, far_ref, *refs):
    out_ref, norm_ref = refs if first else (refs[0], None)
    core = lax.axis_index("col")
    size, width = near_ref.shape[1:]
    near, far = add_halves(mine_ref, other_ref, width)
    if first:
        norm_ref[...] = finish(mine_ref[:, 2 * width :] + other_ref[:, 2 * width :])
    parts = width // LANES
    for i in range(parts):
        lanes = slice(i * LANES, (i + 1) * LANES)
        for place, half in ((core, near), (1 - core, far)):
            at = pl.multiple_of((place * parts + i) * size, size)
            out_ref[pl.ds(at, size)] = half[:, lanes]
    products = symmetric_parts(near, near_ref[0]) + symmetric_parts(
        far, far_ref[0 if first else far_ref.shape[0] - 1]
    )
    out_ref[2 * parts * size :] = pack(finish(products))


def inverse_kernel(norm_ref, out_ref):
    norm = norm_ref[...]
    size = norm.shape[0]
    norm = 0.5 * (norm + jnp.concatenate([norm[:, :size].T, norm[:, size:]], axis=1))
    unit = lax.broadcasted_iota(jnp.int32, norm.shape, 0) == lax.broadcasted_iota(
        jnp.int32, norm.shape, 1
    )
    out_ref[...] = solve_wide(jnp.where(unit, 1.0, 0.0), pltpu.roll(norm, size, 1))


def pick(refs, places, core, rows):
    if places[0] == places[1]:
        return refs[places[0]][rows]
    return jnp.where(core == 0, refs[places[0]][rows], refs[places[1]][rows])


def step_kernel(used, places, with_solution, last, *refs):
    images, refs = refs[:used], refs[used:]
    direction_ref, residual_ref, norm_ref, inverse_ref, matrix = refs[:5]
    refs = refs[5:]
    if with_solution:
        solution_ref, refs = refs[0], refs[1:]
    out_ref, new_direction, new_residual, new_norm, new_solution = refs
    core = lax.axis_index("col")
    pieces = len(places)
    size, width = direction_ref.shape[1:]
    parts = width // LANES

    def image(k, half):
        found = []
        for i in range(parts):
            at = pl.multiple_of((half * parts + i) * size, size)
            found.append(pick(images, places[k], core, pl.ds(at, size)))
        return jnp.concatenate(found, axis=1)

    behind = slice(2 * parts * size, None)
    products = add_up([pick(images, pair, core, behind) for pair in places])
    inverse = stack(inverse_ref[:, :size])
    alpha = stack(solve_wide(norm_ref[...], unpack(products, size, 1))[:, :size])
    residuals = [
        [residual_ref[side, k] - times(alpha, image(k, half)) for k in range(pieces)]
        for side, half in enumerate((core, 1 - core))
    ]
    joined = [jnp.concatenate(values, axis=1) for values in residuals]
    next_norm = finish(gram_parts(joined[0], joined[0]) + gram_parts(joined[1], joined[1]))
    new_norm[...] = next_norm
    step = times(alpha, direction_ref[0])
    new_solution[...] = solution_ref[...] + step if with_solution else step
    beta = stack_leading(times(inverse, next_norm)[:, :size])
    directions = [
        residual + times_leading(beta, direction_ref[k])
        for k, residual in enumerate(residuals[0] + residuals[1][:1])
    ]
    if last:
        new_residual[...] = residuals[0][0]
        new_direction[0] = directions[0]
        new_direction[1] = directions[pieces]
    else:
        for k in range(pieces):
            new_residual[0, k] = residuals[0][k]
            new_residual[1, k] = residuals[1][k]
        for k in range(pieces + 1):
            new_direction[k] = directions[k]
    out_ref[...] = apply_dense(directions[:pieces], matrix)


def last_image_kernel(mine_ref, other_ref, direction_ref, near_ref, gram_ref):
    near, far = add_halves(mine_ref, other_ref, direction_ref.shape[2])
    near_ref[...] = near
    products = symmetric_parts(near, direction_ref[0]) + symmetric_parts(far, direction_ref[1])
    gram_ref[...] = pack(finish(products))


def last_kernel(used, places, *refs):
    image_ref, direction_ref, residual_ref, norm_ref, solution_ref = refs[used:-2]
    new_solution, new_residual = refs[-2:]
    core = lax.axis_index("col")
    size = image_ref.shape[0]
    products = add_up([pick(refs, pair, core, slice(None)) for pair in places])
    alpha = stack(solve_wide(norm_ref[...], unpack(products, size, 1))[:, :size])
    new_solution[...] = solution_ref[...] + times(alpha, direction_ref[0])
    new_residual[...] = residual_ref[...] - times(alpha, image_ref[...])


def shape(*dims, dtype=F32):
    return jax.ShapeDtypeStruct(dims, dtype)


def per_device(tiles, tile_rows, tile_cols, tile_count, signs, vertex_weight, column_scale):
    sketch, rows_dev = signs.shape
    tile = tiles.shape[1]
    pieces = lax.axis_size("row")
    col_devices = lax.axis_size("col")
    group = col_devices * rows_dev
    depth = pieces * rows_dev

    def swap(value, mask):
        return lax.ppermute(value, "row", [(i, i ^ mask) for i in range(pieces)])

    def across(value):
        return lax.ppermute(
            value, "col", [(i, (i + 1) % col_devices) for i in range(col_devices)]
        )

    def exchange(value, turns=((7, 5), (3, 6), (2, 4), (1, 1))):
        if pieces != 8:
            found = [value] + [swap(value, k) for k in range(1, pieces)]
            return found, [(k, k) for k in range(pieces)]
        fetched = []
        passed = []
        places = {0: (0, 0)}
        for turn, masks in enumerate(turns, 1):
            pairs = [
                (i * 2 + core, (i ^ mask) * 2 + core)
                for core, mask in enumerate(masks)
                for i in range(pieces)
            ]
            fetched.append(lax.ppermute(value, ("row", "col"), pairs))
            if masks[0] == masks[1]:
                places[masks[0]] = (turn, turn)
            else:
                passed.append(across(fetched[-1]))
                places[masks[0]] = (turn, turn + len(turns))
                places[masks[1]] = (turn + len(turns), turn)
        return [value, *fetched, *passed], [places[k] for k in range(pieces)]

    right_side = signs.astype(F32) * vertex_weight[None, :] * column_scale[:, None]
    even = [right_side] + [swap(right_side, k) for k in range(2, pieces, 2)]

    matrix = shape(2, depth, group, dtype=BF16)
    total = shape(depth // tile * (group // tile), tile, tile)
    slots = tiles.shape[0]
    half = slots * 3 // 8
    rest = shape(slots - half, tile, tile, dtype=BF16)
    lists = [pltpu.with_memory_space_constraint(x, pltpu.HBM) for x in (tile_rows, tile_cols)]
    lists_scratch = [pltpu.SMEM(x.shape, jnp.int32) for x in lists]
    cost = pl.CostEstimate(
        flops=4 * tiles.size, bytes_accessed=4 * tiles.size, transcendentals=0
    )
    blocks_sum, others = pl.pallas_call(
        functools.partial(gather_kernel, rows_dev),
        out_shape=(total, rest),
        in_specs=[SMEM] + [HBM] * 3,
        out_specs=(VMEM, VMEM),
        scratch_shapes=[
            pltpu.VMEM((half, tile, tile), BF16),
            *lists_scratch,
            pltpu.SemaphoreType.DMA((2 * CHUNKS,)),
            pltpu.SemaphoreType.DMA((len(lists),)),
        ],
        compiler_params=params(tiles, total),
        cost_estimate=cost,
        name="gather",
    )(tile_count, *lists, pltpu.with_memory_space_constraint(tiles, pltpu.HBM))
    joined = shape(pieces // 2, sketch, rows_dev)
    order = [*range(pieces // 4, pieces // 2), *range(1, pieces // 4), 0]
    even = pl.pallas_call(
        functools.partial(join_kernel, order),
        out_shape=joined,
        in_specs=[VMEM] * (pieces // 2) + [ANY],
        out_specs=VMEM,
        compiler_params=params(joined, joined),
        name="join",
    )(*[even[k] for k in order], blocks_sum)
    odd = swap(even, 1)
    far_even = across(even)
    dense, _ = pl.pallas_call(
        functools.partial(dense_kernel, rows_dev),
        out_shape=(matrix, total),
        in_specs=[SMEM] + [HBM] * 2 + [VMEM, VMEM, ANY],
        out_specs=(VMEM, VMEM),
        scratch_shapes=[*lists_scratch, pltpu.SemaphoreType.DMA((len(lists),))],
        input_output_aliases={4: 1},
        compiler_params=params(rest, total, total, matrix),
        cost_estimate=cost,
        name="dense",
    )(tile_count, *lists, others, blocks_sum, even)

    held = shape(2, pieces, sketch, rows_dev)
    state = shape(pieces + 1, sketch, rows_dev)
    small = shape(sketch, LANES)
    piece = shape(sketch, rows_dev)
    packed = shape(sketch * sketch // LANES, LANES)
    payload = shape(2 * sketch * (rows_dev // LANES) + packed.shape[0], LANES)

    partial_sum, odd = pl.pallas_call(
        first_kernel,
        out_shape=(shape(sketch, group + LANES), joined),
        in_specs=[VMEM] * 3,
        out_specs=(VMEM, VMEM),
        compiler_params=params(matrix, state, state),
        name="first",
    )(even, odd, dense)
    norm = None
    solution = None
    direction = None
    for iteration in range(ITERS - 1):
        first = iteration == 0
        last = iteration == ITERS - 2
        sums = (partial_sum, across(partial_sum))
        given = (even, far_even) if first else (direction, direction)
        outs = pl.pallas_call(
            functools.partial(image_kernel, first),
            out_shape=(payload, small) if first else (payload,),
            in_specs=[VMEM] * 4,
            out_specs=(VMEM, VMEM) if first else (VMEM,),
            compiler_params=params(state, payload),
            name="image",
        )(*sums, *given)
        found, places = exchange(outs[0])
        if first:
            norm = outs[1]
            residual, direction = pl.pallas_call(
                collect_kernel,
                out_shape=(held, state),
                in_specs=[VMEM] * 4,
                out_specs=(VMEM, VMEM),
                compiler_params=params(held, held, state),
                name="collect",
            )(even, odd, far_even, across(odd))
        inverse = pl.pallas_call(
            inverse_kernel,
            out_shape=small,
            in_specs=[VMEM],
            out_specs=VMEM,
            compiler_params=params(),
            name="inverse",
        )(norm)
        given = () if first else (solution,)
        partial_sum, direction, residual, norm, solution = pl.pallas_call(
            functools.partial(step_kernel, len(found), places, not first, last),
            out_shape=(
                shape(sketch, group),
                shape(2, sketch, rows_dev) if last else state,
                piece if last else held,
                small,
                piece,
            ),
            in_specs=[VMEM] * (len(found) + 5 + len(given)),
            out_specs=(VMEM,) * 5,
            compiler_params=params(matrix, held, held, held, held, state),
            name="step",
        )(*found, direction, residual, norm, inverse, dense, *given)
    near, gram = pl.pallas_call(
        last_image_kernel,
        out_shape=(piece, packed),
        in_specs=[VMEM] * 3,
        out_specs=(VMEM, VMEM),
        compiler_params=params(state),
        name="last_image",
    )(partial_sum, across(partial_sum), direction)
    found, places = exchange(gram, ((6, 7), (3, 5), (2, 4), (1, 1)))
    return pl.pallas_call(
        functools.partial(last_kernel, len(found), places),
        out_shape=(piece, piece),
        in_specs=[VMEM] * (len(found) + 5),
        out_specs=(VMEM, VMEM),
        compiler_params=params(state, state),
        name="last",
    )(*found, near, direction, residual, norm, solution)


def solution(mesh):
    return jax.shard_map(
        per_device,
        mesh=mesh,
        in_specs=(
            P(("row", "col"), None, None),
            P(("row", "col")),
            P(("row", "col")),
            P(("row", "col")),
            P("rhs", ("row", "col")),
            P(("row", "col")),
            P("rhs"),
        ),
        out_specs=(P("rhs", ("row", "col")), P("rhs", ("row", "col"))),
        check_vma=False,
    )
```

```python
import functools

import jax
import jax.numpy as jnp
from jax import lax
from jax.experimental import pallas as pl
from jax.experimental.pallas import tpu as pltpu
from jax.sharding import PartitionSpec as P

ITERS = 3
LANES = 128
PIVOTS = 16
CHUNKS = 5
F32 = jnp.float32
BF16 = jnp.bfloat16
SPARE_BYTES = 4 * 1024 * 1024

VMEM = pl.BlockSpec(memory_space=pltpu.VMEM)
SMEM = pl.BlockSpec(memory_space=pltpu.SMEM)
HBM = pl.BlockSpec(memory_space=pltpu.HBM)
ANY = pl.BlockSpec(memory_space=pl.ANY)


def params(*arrays):
    used = sum(a.size * jnp.dtype(a.dtype).itemsize for a in arrays)
    return pltpu.CompilerParams(vmem_limit_bytes=used + SPARE_BYTES)


def split(value):
    high = value.astype(BF16)
    rest = value - high.astype(F32)
    middle = rest.astype(BF16)
    low = (rest - middle.astype(F32)).astype(BF16)
    return high, middle, low


def stack(left):
    high, middle, low = [part.astype(F32) for part in split(left)]
    parts = jnp.concatenate([high, high, middle, high, middle, low], axis=0)
    return parts.T.astype(BF16)


def times(stacked, right):
    high, middle, low = split(right)
    parts = jnp.concatenate([high, middle, high, low, middle, high], axis=0)
    return jnp.dot(stacked, parts, preferred_element_type=F32)


def stack_leading(left):
    high, middle, _ = [part.astype(F32) for part in split(left)]
    return jnp.concatenate([high, high, middle], axis=0).T.astype(BF16)


def times_leading(stacked, right):
    high, middle, _ = split(right)
    parts = jnp.concatenate([high, middle, high], axis=0)
    return jnp.dot(stacked, parts, preferred_element_type=F32)


def gram_parts(left, right):
    size, width = left.shape
    filler = jnp.zeros((LANES - 3 * size, width), BF16)
    every = lax.dot_general(
        jnp.concatenate(split(left), axis=0),
        jnp.concatenate([*split(right), filler], axis=0),
        (((1,), (1,)), ((), ())),
        preferred_element_type=F32,
    )
    return every[2 * size :] + every[size : 2 * size] + every[:size]


def symmetric_parts(left, right):
    return 0.5 * (gram_parts(left, right) + gram_parts(right, left))


def finish(parts, place=0):
    size = parts.shape[0]

    def block(index):
        shift = (place - index) * size % LANES
        return pltpu.roll(parts, shift, 1) if shift else parts

    return block(2) + block(1) + block(0)


def pack(wide):
    rows = wide.shape[0]
    folds = LANES // rows
    height = rows // folds
    lanes = lax.broadcasted_iota(jnp.int32, wide.shape, 1)
    wide = jnp.where(lanes < rows, wide, 0.0)
    total = wide[:height]
    for i in range(1, folds):
        total = total + pltpu.roll(wide[i * height : (i + 1) * height], i * rows, 1)
    return total


def unpack(folded, size, place=0):
    parts = []
    for i in range(LANES // size):
        shift = (place - i) * size % LANES
        parts.append(pltpu.roll(folded, shift, 1) if shift else folded)
    return jnp.concatenate(parts, axis=0)


def solve_wide(target, matrix):
    size = matrix.shape[0]
    row_ids = lax.broadcasted_iota(jnp.int32, (size, LANES), 0)
    lane_ids = lax.broadcasted_iota(jnp.int32, (size, LANES), 1)
    work = jnp.where(lane_ids < size, target, matrix)
    for base in range(0, size, PIVOTS):
        columns = [
            jnp.broadcast_to(work[:, size + base + i : size + base + i + 1], (size, LANES))
            for i in range(PIVOTS)
        ]
        for i in range(PIVOTS):
            pivot = base + i
            here = row_ids == pivot
            inverse = pltpu.reciprocal(columns[i][pivot : pivot + 1, :], full_range=False)
            row = work[pivot : pivot + 1, :] * inverse
            work = jnp.where(here, row, work - columns[i] * row)
            for later in range(i + 1, PIVOTS):
                entry = columns[later][pivot : pivot + 1, :] * inverse
                columns[later] = jnp.where(here, entry, columns[later] - columns[i] * entry)
    return work


def add_up(values):
    values = list(values)
    while len(values) > 1:
        pairs = [values[i] + values[i + 1] for i in range(0, len(values) - 1, 2)]
        values = pairs + values[len(values) - len(values) % 2 :]
    return values[0]


def add_tiles(rows_dev, lists, tiles, first_tile, start, stop, total):
    rows_ref, cols_ref = lists
    tile = total.shape[1]
    slots = rows_ref.shape[0]
    blocks = rows_dev // tile
    row_place = lax.axis_index("row")
    col_place = lax.axis_index("col")
    col_devices = lax.axis_size("col")
    row_blocks = col_devices * blocks

    def place(slot):
        row = rows_ref[slot]
        column = cols_ref[slot]
        side = lax.rem(row // blocks + col_devices - col_place, col_devices)
        owner = column // (blocks * col_devices)
        column_at = (owner ^ row_place) * blocks + lax.rem(column, blocks)
        return column_at * row_blocks + side * blocks + lax.rem(row, blocks)

    def after(slot):
        return place(jnp.minimum(slot, slots - 1))

    def add(turn, places):
        slot = start + 2 * turn
        values = [tiles[slot + i - first_tile].astype(F32) for i in range(2)]
        following = (after(slot + 2), after(slot + 3))
        for at, value in zip(places, values):
            total[at] = total[at] + value
        return following

    places = lax.fori_loop(0, (stop - start) // 2, add, (after(start), after(start + 1)))

    @pl.when(lax.rem(stop - start, 2) == 1)
    def _():
        total[places[0]] = total[places[0]] + tiles[stop - 1 - first_tile].astype(F32)


def copy_lists(hbm_refs, smem_refs, sems):
    copies = [
        pltpu.make_async_copy(source, target, sems.at[i])
        for i, (source, target) in enumerate(zip(hbm_refs, smem_refs))
    ]
    for copy in copies:
        copy.start()
    return copies


def gather_kernel(rows_dev, count_ref, rows_hbm, cols_hbm, tiles_ref, total, rest, *scratch):
    held, rows_ref, cols_ref, sems, list_sems = scratch
    live = count_ref[0]
    half = held.shape[0]
    slots, tile = tiles_ref.shape[:2]
    chunk = -(-half // CHUNKS)
    lists = copy_lists((rows_hbm, cols_hbm), (rows_ref, cols_ref), list_sems)
    copies = []
    for c in range(CHUNKS):
        part = pl.ds(c * chunk, min(chunk, half - c * chunk))
        copies.append(pltpu.make_async_copy(tiles_ref.at[part], held.at[part], sems.at[c]))

        @pl.when(c * chunk < live)
        def _():
            copies[c].start()

    chunk_rest = -(-rest.shape[0] // CHUNKS)
    rest_copies = []
    for c in range(CHUNKS):
        start = c * chunk_rest
        length = min(chunk_rest, rest.shape[0] - start)
        copy = pltpu.make_async_copy(
            tiles_ref.at[pl.ds(half + start, length)],
            rest.at[pl.ds(start, length)],
            sems.at[CHUNKS + c],
        )
        rest_copies.append((half + start, copy))

        @pl.when(half + start < live)
        def _():
            copy.start()

    def clear(index, carry):
        total[index] = jnp.zeros((tile, tile), F32)
        return carry

    lax.fori_loop(0, total.shape[0], clear, 0, unroll=4)
    for copy in lists:
        copy.wait()
    for c in range(CHUNKS):
        start, stop = c * chunk, min((c + 1) * chunk, half)

        @pl.when(start < live)
        def _():
            copies[c].wait()
            add_tiles(
                rows_dev, (rows_ref, cols_ref), held, 0, start, jnp.minimum(live, stop), total
            )

    for start, copy in rest_copies:

        @pl.when(start < live)
        def _():
            copy.wait()


def dense_kernel(
    rows_dev, count_ref, rows_hbm, cols_hbm, rest, total_in, joined_ref, out_ref, total, *scratch
):
    rows_ref, cols_ref, list_sems = scratch
    live = count_ref[0]
    half = rows_ref.shape[0] - rest.shape[0]
    tile = total.shape[1]
    row_blocks = out_ref.shape[2] // tile

    @pl.when(half < live)
    def _():
        lists = copy_lists((rows_hbm, cols_hbm), (rows_ref, cols_ref), list_sems)
        for copy in lists:
            copy.wait()
        add_tiles(rows_dev, (rows_ref, cols_ref), rest, half, half, live, total)

    def part(index, carry):
        start = pl.multiple_of(index * tile, tile)
        for b in range(row_blocks):
            value = total[index * row_blocks + b].T
            high = value.astype(BF16)
            low = (value - high.astype(F32)).astype(BF16)
            out_ref[0, pl.ds(start, tile), pl.ds(b * tile, tile)] = high
            out_ref[1, pl.ds(start, tile), pl.ds(b * tile, tile)] = low
        return carry

    lax.fori_loop(0, total.shape[0] // row_blocks, part, 0)


def join_kernel(order, *refs):
    for k, ref in zip(order, refs):
        refs[-1][k] = ref[...]


def apply_dense(directions, matrix):
    rounded = jnp.concatenate([direction.astype(BF16) for direction in directions], axis=1)
    high, low = [
        jnp.dot(rounded, matrix[part], preferred_element_type=F32) for part in range(2)
    ]
    return high + low


def first_kernel(even_ref, odd_ref, matrix, out_ref, odd_out_ref):
    pieces = 2 * even_ref.shape[0]
    odd_out_ref[...] = odd_ref[...]
    values = [(odd_ref if k % 2 else even_ref)[k // 2] for k in range(pieces)]
    rows = 2 * values[0].shape[1]
    joined = jnp.concatenate(values, axis=1)
    out_ref[:, rows:] = gram_parts(joined, joined)
    out_ref[:, :rows] = apply_dense(values, matrix)


def collect_kernel(even_ref, odd_ref, far_even_ref, far_odd_ref, residual_ref, direction_ref):
    pieces = 2 * even_ref.shape[0]
    for k in range(pieces):
        near = (odd_ref if k % 2 else even_ref)[k // 2]
        residual_ref[0, k] = near
        residual_ref[1, k] = (far_odd_ref if k % 2 else far_even_ref)[k // 2]
        direction_ref[k] = near
    direction_ref[pieces] = far_even_ref[0]


def add_halves(mine_ref, other_ref, width):
    near = mine_ref[:, :width] + other_ref[:, width : 2 * width]
    far = mine_ref[:, width : 2 * width] + other_ref[:, :width]
    return near, far


def image_kernel(first, mine_ref, other_ref, near_ref, far_ref, *refs):
    out_ref, norm_ref = refs if first else (refs[0], None)
    core = lax.axis_index("col")
    size, width = near_ref.shape[1:]
    near, far = add_halves(mine_ref, other_ref, width)
    if first:
        norm_ref[...] = finish(mine_ref[:, 2 * width :] + other_ref[:, 2 * width :])
    parts = width // LANES
    for i in range(parts):
        lanes = slice(i * LANES, (i + 1) * LANES)
        for place, half in ((core, near), (1 - core, far)):
            at = pl.multiple_of((place * parts + i) * size, size)
            out_ref[pl.ds(at, size)] = half[:, lanes]
    products = symmetric_parts(near, near_ref[0]) + symmetric_parts(
        far, far_ref[0 if first else far_ref.shape[0] - 1]
    )
    out_ref[2 * parts * size :] = pack(finish(products))


def inverse_kernel(norm_ref, out_ref):
    norm = norm_ref[...]
    size = norm.shape[0]
    norm = 0.5 * (norm + jnp.concatenate([norm[:, :size].T, norm[:, size:]], axis=1))
    unit = lax.broadcasted_iota(jnp.int32, norm.shape, 0) == lax.broadcasted_iota(
        jnp.int32, norm.shape, 1
    )
    out_ref[...] = solve_wide(jnp.where(unit, 1.0, 0.0), pltpu.roll(norm, size, 1))


def pick(refs, places, core, rows):
    if places[0] == places[1]:
        return refs[places[0]][rows]
    return jnp.where(core == 0, refs[places[0]][rows], refs[places[1]][rows])


def step_kernel(used, places, with_solution, last, *refs):
    images, refs = refs[:used], refs[used:]
    direction_ref, residual_ref, norm_ref, inverse_ref, matrix = refs[:5]
    refs = refs[5:]
    if with_solution:
        solution_ref, refs = refs[0], refs[1:]
    out_ref, new_direction, new_residual, new_norm, new_solution = refs
    core = lax.axis_index("col")
    pieces = len(places)
    size, width = direction_ref.shape[1:]
    parts = width // LANES

    def image(k, half):
        found = []
        for i in range(parts):
            at = pl.multiple_of((half * parts + i) * size, size)
            found.append(pick(images, places[k], core, pl.ds(at, size)))
        return jnp.concatenate(found, axis=1)

    behind = slice(2 * parts * size, None)
    products = add_up([pick(images, pair, core, behind) for pair in places])
    inverse = stack(inverse_ref[:, :size])
    alpha = stack(solve_wide(norm_ref[...], unpack(products, size, 1))[:, :size])
    residuals = [
        [residual_ref[side, k] - times(alpha, image(k, half)) for k in range(pieces)]
        for side, half in enumerate((core, 1 - core))
    ]
    joined = [jnp.concatenate(values, axis=1) for values in residuals]
    next_norm = finish(gram_parts(joined[0], joined[0]) + gram_parts(joined[1], joined[1]))
    new_norm[...] = next_norm
    step = times(alpha, direction_ref[0])
    new_solution[...] = solution_ref[...] + step if with_solution else step
    beta = stack_leading(times(inverse, next_norm)[:, :size])
    directions = [
        residual + times_leading(beta, direction_ref[k])
        for k, residual in enumerate(residuals[0] + residuals[1][:1])
    ]
    if last:
        new_residual[...] = residuals[0][0]
        new_direction[0] = directions[0]
        new_direction[1] = directions[pieces]
    else:
        for k in range(pieces):
            new_residual[0, k] = residuals[0][k]
            new_residual[1, k] = residuals[1][k]
        for k in range(pieces + 1):
            new_direction[k] = directions[k]
    out_ref[...] = apply_dense(directions[:pieces], matrix)


def last_image_kernel(mine_ref, other_ref, direction_ref, near_ref, gram_ref):
    near, far = add_halves(mine_ref, other_ref, direction_ref.shape[2])
    near_ref[...] = near
    products = symmetric_parts(near, direction_ref[0]) + symmetric_parts(far, direction_ref[1])
    gram_ref[...] = pack(finish(products))


def last_kernel(used, places, *refs):
    image_ref, direction_ref, residual_ref, norm_ref, solution_ref = refs[used:-2]
    new_solution, new_residual = refs[-2:]
    core = lax.axis_index("col")
    size = image_ref.shape[0]
    products = add_up([pick(refs, pair, core, slice(None)) for pair in places])
    alpha = stack(solve_wide(norm_ref[...], unpack(products, size, 1))[:, :size])
    new_solution[...] = solution_ref[...] + times(alpha, direction_ref[0])
    new_residual[...] = residual_ref[...] - times(alpha, image_ref[...])


def shape(*dims, dtype=F32):
    return jax.ShapeDtypeStruct(dims, dtype)


def per_device(tiles, tile_rows, tile_cols, tile_count, signs, vertex_weight, column_scale):
    sketch, rows_dev = signs.shape
    tile = tiles.shape[1]
    pieces = lax.axis_size("row")
    col_devices = lax.axis_size("col")
    group = col_devices * rows_dev
    depth = pieces * rows_dev

    def swap(value, mask):
        return lax.ppermute(value, "row", [(i, i ^ mask) for i in range(pieces)])

    def across(value):
        return lax.ppermute(
            value, "col", [(i, (i + 1) % col_devices) for i in range(col_devices)]
        )

    def exchange(value, turns=((7, 5), (3, 6), (2, 4), (1, 1))):
        if pieces != 8:
            found = [value] + [swap(value, k) for k in range(1, pieces)]
            return found, [(k, k) for k in range(pieces)]
        fetched = []
        passed = []
        places = {0: (0, 0)}
        for turn, masks in enumerate(turns, 1):
            pairs = [
                (i * 2 + core, (i ^ mask) * 2 + core)
                for core, mask in enumerate(masks)
                for i in range(pieces)
            ]
            fetched.append(lax.ppermute(value, ("row", "col"), pairs))
            if masks[0] == masks[1]:
                places[masks[0]] = (turn, turn)
            else:
                passed.append(across(fetched[-1]))
                places[masks[0]] = (turn, turn + len(turns))
                places[masks[1]] = (turn + len(turns), turn)
        return [value, *fetched, *passed], [places[k] for k in range(pieces)]

    right_side = signs.astype(F32) * vertex_weight[None, :] * column_scale[:, None]
    even = [right_side] + [swap(right_side, k) for k in range(2, pieces, 2)]

    matrix = shape(2, depth, group, dtype=BF16)
    total = shape(depth // tile * (group // tile), tile, tile)
    slots = tiles.shape[0]
    half = slots * 3 // 8
    rest = shape(slots - half, tile, tile, dtype=BF16)
    lists = [pltpu.with_memory_space_constraint(x, pltpu.HBM) for x in (tile_rows, tile_cols)]
    lists_scratch = [pltpu.SMEM(x.shape, jnp.int32) for x in lists]
    cost = pl.CostEstimate(
        flops=4 * tiles.size, bytes_accessed=4 * tiles.size, transcendentals=0
    )
    blocks_sum, others = pl.pallas_call(
        functools.partial(gather_kernel, rows_dev),
        out_shape=(total, rest),
        in_specs=[SMEM] + [HBM] * 3,
        out_specs=(VMEM, VMEM),
        scratch_shapes=[
            pltpu.VMEM((half, tile, tile), BF16),
            *lists_scratch,
            pltpu.SemaphoreType.DMA((2 * CHUNKS,)),
            pltpu.SemaphoreType.DMA((len(lists),)),
        ],
        compiler_params=params(tiles, total),
        cost_estimate=cost,
        name="gather",
    )(tile_count, *lists, pltpu.with_memory_space_constraint(tiles, pltpu.HBM))
    joined = shape(pieces // 2, sketch, rows_dev)
    order = [*range(pieces // 4, pieces // 2), *range(1, pieces // 4), 0]
    even = pl.pallas_call(
        functools.partial(join_kernel, order),
        out_shape=joined,
        in_specs=[VMEM] * (pieces // 2) + [ANY],
        out_specs=VMEM,
        compiler_params=params(joined, joined),
        name="join",
    )(*[even[k] for k in order], blocks_sum)
    odd = swap(even, 1)
    far_even = across(even)
    dense, _ = pl.pallas_call(
        functools.partial(dense_kernel, rows_dev),
        out_shape=(matrix, total),
        in_specs=[SMEM] + [HBM] * 2 + [VMEM, VMEM, ANY],
        out_specs=(VMEM, VMEM),
        scratch_shapes=[*lists_scratch, pltpu.SemaphoreType.DMA((len(lists),))],
        input_output_aliases={4: 1},
        compiler_params=params(rest, total, total, matrix),
        cost_estimate=cost,
        name="dense",
    )(tile_count, *lists, others, blocks_sum, even)

    held = shape(2, pieces, sketch, rows_dev)
    state = shape(pieces + 1, sketch, rows_dev)
    small = shape(sketch, LANES)
    piece = shape(sketch, rows_dev)
    packed = shape(sketch * sketch // LANES, LANES)
    payload = shape(2 * sketch * (rows_dev // LANES) + packed.shape[0], LANES)

    partial_sum, odd = pl.pallas_call(
        first_kernel,
        out_shape=(shape(sketch, group + LANES), joined),
        in_specs=[VMEM] * 3,
        out_specs=(VMEM, VMEM),
        compiler_params=params(matrix, state, state),
        name="first",
    )(even, odd, dense)
    norm = None
    solution = None
    direction = None
    for iteration in range(ITERS - 1):
        first = iteration == 0
        last = iteration == ITERS - 2
        sums = (partial_sum, across(partial_sum))
        given = (even, far_even) if first else (direction, direction)
        outs = pl.pallas_call(
            functools.partial(image_kernel, first),
            out_shape=(payload, small) if first else (payload,),
            in_specs=[VMEM] * 4,
            out_specs=(VMEM, VMEM) if first else (VMEM,),
            compiler_params=params(state, payload),
            name="image",
        )(*sums, *given)
        found, places = exchange(outs[0])
        if first:
            norm = outs[1]
            residual, direction = pl.pallas_call(
                collect_kernel,
                out_shape=(held, state),
                in_specs=[VMEM] * 4,
                out_specs=(VMEM, VMEM),
                compiler_params=params(held, held, state),
                name="collect",
            )(even, odd, far_even, across(odd))
        inverse = pl.pallas_call(
            inverse_kernel,
            out_shape=small,
            in_specs=[VMEM],
            out_specs=VMEM,
            compiler_params=params(),
            name="inverse",
        )(norm)
        given = () if first else (solution,)
        partial_sum, direction, residual, norm, solution = pl.pallas_call(
            functools.partial(step_kernel, len(found), places, not first, last),
            out_shape=(
                shape(sketch, group),
                shape(2, sketch, rows_dev) if last else state,
                piece if last else held,
                small,
                piece,
            ),
            in_specs=[VMEM] * (len(found) + 5 + len(given)),
            out_specs=(VMEM,) * 5,
            compiler_params=params(matrix, held, held, held, held, state),
            name="step",
        )(*found, direction, residual, norm, inverse, dense, *given)
    near, gram = pl.pallas_call(
        last_image_kernel,
        out_shape=(piece, packed),
        in_specs=[VMEM] * 3,
        out_specs=(VMEM, VMEM),
        compiler_params=params(state),
        name="last_image",
    )(partial_sum, across(partial_sum), direction)
    found, places = exchange(gram, ((6, 7), (3, 5), (2, 4), (1, 1)))
    return pl.pallas_call(
        functools.partial(last_kernel, len(found), places),
        out_shape=(piece, piece),
        in_specs=[VMEM] * (len(found) + 5),
        out_specs=(VMEM, VMEM),
        compiler_params=params(state, state),
        name="last",
    )(*found, near, direction, residual, norm, solution)


def solution(mesh):
    return jax.shard_map(
        per_device,
        mesh=mesh,
        in_specs=(
            P(("row", "col"), None, None),
            P(("row", "col")),
            P(("row", "col")),
            P(("row", "col")),
            P("rhs", ("row", "col")),
            P(("row", "col")),
            P("rhs"),
        ),
        out_specs=(P("rhs", ("row", "col")), P("rhs", ("row", "col"))),
        check_vma=False,
    )
```

```python
import functools

import jax
import jax.numpy as jnp
from jax import lax
from jax.experimental import pallas as pl
from jax.experimental.pallas import tpu as pltpu
from jax.sharding import PartitionSpec as P

ITERS = 3
LANES = 128
PIVOTS = 16
TAIL = 16
CHUNKS = 5
F32 = jnp.float32
BF16 = jnp.bfloat16
SPARE_BYTES = 4 * 1024 * 1024

VMEM = pl.BlockSpec(memory_space=pltpu.VMEM)
SMEM = pl.BlockSpec(memory_space=pltpu.SMEM)
HBM = pl.BlockSpec(memory_space=pltpu.HBM)
ANY = pl.BlockSpec(memory_space=pl.ANY)


def params(*arrays):
    used = sum(a.size * jnp.dtype(a.dtype).itemsize for a in arrays)
    return pltpu.CompilerParams(vmem_limit_bytes=used + SPARE_BYTES)


def split(value):
    high = value.astype(BF16)
    rest = value - high.astype(F32)
    middle = rest.astype(BF16)
    low = (rest - middle.astype(F32)).astype(BF16)
    return high, middle, low


def stack(left):
    high, middle, low = [part.astype(F32) for part in split(left)]
    parts = jnp.concatenate([high, high, middle, high, middle, low], axis=0)
    return parts.T.astype(BF16)


def times(stacked, right):
    high, middle, low = split(right)
    parts = jnp.concatenate([high, middle, high, low, middle, high], axis=0)
    return jnp.dot(stacked, parts, preferred_element_type=F32)


def stack_leading(left):
    high, middle, _ = [part.astype(F32) for part in split(left)]
    return jnp.concatenate([high, high, middle], axis=0).T.astype(BF16)


def times_leading(stacked, right):
    high, middle, _ = split(right)
    parts = jnp.concatenate([high, middle, high], axis=0)
    return jnp.dot(stacked, parts, preferred_element_type=F32)


def gram_parts(left, right):
    size, width = left.shape
    filler = jnp.zeros((LANES - 3 * size, width), BF16)
    every = lax.dot_general(
        jnp.concatenate(split(left), axis=0),
        jnp.concatenate([*split(right), filler], axis=0),
        (((1,), (1,)), ((), ())),
        preferred_element_type=F32,
    )
    return every[2 * size :] + every[size : 2 * size] + every[:size]


def symmetric_parts(left, right):
    return 0.5 * (gram_parts(left, right) + gram_parts(right, left))


def finish(parts, place=0):
    size = parts.shape[0]

    def block(index):
        shift = (place - index) * size % LANES
        return pltpu.roll(parts, shift, 1) if shift else parts

    return block(2) + block(1) + block(0)


def pack(wide):
    rows = wide.shape[0]
    folds = LANES // rows
    height = rows // folds
    lanes = lax.broadcasted_iota(jnp.int32, wide.shape, 1)
    wide = jnp.where(lanes < rows, wide, 0.0)
    total = wide[:height]
    for i in range(1, folds):
        total = total + pltpu.roll(wide[i * height : (i + 1) * height], i * rows, 1)
    return total


def unpack(folded, size, place=0):
    parts = []
    for i in range(LANES // size):
        shift = (place - i) * size % LANES
        parts.append(pltpu.roll(folded, shift, 1) if shift else folded)
    return jnp.concatenate(parts, axis=0)


def solve_wide(target, matrix):
    size = matrix.shape[0]
    row_ids = lax.broadcasted_iota(jnp.int32, (size, LANES), 0)
    lane_ids = lax.broadcasted_iota(jnp.int32, (size, LANES), 1)
    work = jnp.where(lane_ids < size, target, matrix)
    for base in range(0, size, PIVOTS):
        columns = [
            jnp.broadcast_to(work[:, size + base + i : size + base + i + 1], (size, LANES))
            for i in range(PIVOTS)
        ]
        for i in range(PIVOTS):
            pivot = base + i
            here = row_ids == pivot
            inverse = pltpu.reciprocal(columns[i][pivot : pivot + 1, :], full_range=False)
            row = work[pivot : pivot + 1, :] * inverse
            work = jnp.where(here, row, work - columns[i] * row)
            for later in range(i + 1, PIVOTS):
                entry = columns[later][pivot : pivot + 1, :] * inverse
                columns[later] = jnp.where(here, entry, columns[later] - columns[i] * entry)
    return work


def add_up(values):
    values = list(values)
    while len(values) > 1:
        pairs = [values[i] + values[i + 1] for i in range(0, len(values) - 1, 2)]
        values = pairs + values[len(values) - len(values) % 2 :]
    return values[0]


def add_tiles(rows_dev, lists, tiles, first_tile, start, stop, total):
    rows_ref, cols_ref = lists
    tile = total.shape[1]
    slots = rows_ref.shape[0]
    blocks = rows_dev // tile
    row_place = lax.axis_index("row")
    col_place = lax.axis_index("col")
    col_devices = lax.axis_size("col")
    row_blocks = col_devices * blocks

    def place(slot):
        row = rows_ref[slot]
        column = cols_ref[slot]
        side = lax.rem(row // blocks + col_devices - col_place, col_devices)
        owner = column // (blocks * col_devices)
        column_at = (owner ^ row_place) * blocks + lax.rem(column, blocks)
        return column_at * row_blocks + side * blocks + lax.rem(row, blocks)

    def after(slot):
        return place(jnp.minimum(slot, slots - 1))

    def add(turn, places):
        slot = start + 2 * turn
        values = [tiles[slot + i - first_tile].astype(F32) for i in range(2)]
        following = (after(slot + 2), after(slot + 3))
        for at, value in zip(places, values):
            total[at] = total[at] + value
        return following

    places = lax.fori_loop(0, (stop - start) // 2, add, (after(start), after(start + 1)))

    @pl.when(lax.rem(stop - start, 2) == 1)
    def _():
        total[places[0]] = total[places[0]] + tiles[stop - 1 - first_tile].astype(F32)


def copy_lists(hbm_refs, smem_refs, sems):
    copies = [
        pltpu.make_async_copy(source, target, sems.at[i])
        for i, (source, target) in enumerate(zip(hbm_refs, smem_refs))
    ]
    for copy in copies:
        copy.start()
    return copies


def gather_kernel(rows_dev, count_ref, rows_hbm, cols_hbm, tiles_ref, total, rest, *scratch):
    held, rows_ref, cols_ref, sems, list_sems = scratch
    live = count_ref[0]
    half = held.shape[0]
    slots, tile = tiles_ref.shape[:2]
    chunk = -(-half // CHUNKS)
    lists = copy_lists((rows_hbm, cols_hbm), (rows_ref, cols_ref), list_sems)
    copies = []
    for c in range(CHUNKS):
        part = pl.ds(c * chunk, min(chunk, half - c * chunk))
        copies.append(pltpu.make_async_copy(tiles_ref.at[part], held.at[part], sems.at[c]))

        @pl.when(c * chunk < live)
        def _():
            copies[c].start()

    chunk_rest = -(-rest.shape[0] // CHUNKS)
    rest_copies = []
    for c in range(CHUNKS):
        start = c * chunk_rest
        length = min(chunk_rest, rest.shape[0] - start)
        copy = pltpu.make_async_copy(
            tiles_ref.at[pl.ds(half + start, length)],
            rest.at[pl.ds(start, length)],
            sems.at[CHUNKS + c],
        )
        rest_copies.append((half + start, copy))

        @pl.when(half + start < live)
        def _():
            copy.start()

    def clear(index, carry):
        total[index] = jnp.zeros((tile, tile), F32)
        return carry

    lax.fori_loop(0, total.shape[0], clear, 0, unroll=4)
    for copy in lists:
        copy.wait()
    for c in range(CHUNKS):
        start, stop = c * chunk, min((c + 1) * chunk, half)

        @pl.when(start < live)
        def _():
            copies[c].wait()
            add_tiles(
                rows_dev, (rows_ref, cols_ref), held, 0, start, jnp.minimum(live, stop), total
            )

    for start, copy in rest_copies:

        @pl.when(start < live)
        def _():
            copy.wait()


def dense_kernel(
    rows_dev, count_ref, rows_hbm, cols_hbm, rest, total_in, joined_ref, out_ref, total, *scratch
):
    rows_ref, cols_ref, list_sems = scratch
    live = count_ref[0]
    half = rows_ref.shape[0] - rest.shape[0]
    tile = total.shape[1]
    row_blocks = out_ref.shape[2] // tile

    @pl.when(half < live)
    def _():
        lists = copy_lists((rows_hbm, cols_hbm), (rows_ref, cols_ref), list_sems)
        for copy in lists:
            copy.wait()
        add_tiles(rows_dev, (rows_ref, cols_ref), rest, half, half, live, total)

    def part(index, carry):
        start = pl.multiple_of(index * tile, tile)
        for b in range(row_blocks):
            value = total[index * row_blocks + b].T
            high = value.astype(BF16)
            low = (value - high.astype(F32)).astype(BF16)
            out_ref[0, pl.ds(start, tile), pl.ds(b * tile, tile)] = high
            out_ref[1, pl.ds(start, tile), pl.ds(b * tile, tile)] = low
        return carry

    lax.fori_loop(0, total.shape[0] // row_blocks, part, 0)


def join_kernel(order, *refs):
    for k, ref in zip(order, refs):
        refs[-1][k] = ref[...]


def apply_dense(directions, matrix):
    rounded = jnp.concatenate([direction.astype(BF16) for direction in directions], axis=1)
    high, low = [
        jnp.dot(rounded, matrix[part], preferred_element_type=F32) for part in range(2)
    ]
    return high + low


def message_kernel(
    signs_hbm, weight_hbm, scale_hbm, out_ref, scale_out, signs_ref, weight_ref, scale_ref, sems
):
    copies = copy_lists(
        (signs_hbm, weight_hbm, scale_hbm), (signs_ref, weight_ref, scale_ref), sems
    )
    for copy in copies:
        copy.wait()
    size, width = signs_ref.shape
    out_ref[:size] = signs_ref[...].astype(F32).astype(BF16)
    row_ids = lax.broadcasted_iota(jnp.int32, (TAIL, width), 0)
    tail = jnp.zeros((TAIL, width), F32)
    for i, part in enumerate(split(weight_ref[...].reshape(1, width))):
        tail = jnp.where(row_ids == i, part.astype(F32), tail)
    out_ref[size:] = tail.astype(BF16)
    scale = scale_ref[...].reshape(1, size)
    scale = jnp.concatenate([scale, jnp.zeros((1, LANES - size), F32)], axis=1)
    rows = lax.broadcasted_iota(jnp.int32, (size, LANES), 0)
    lanes = lax.broadcasted_iota(jnp.int32, (size, LANES), 1)
    column = jnp.sum(jnp.where(rows == lanes, scale, 0.0), axis=1, keepdims=True)
    scale_out[...] = jnp.broadcast_to(column, (size, LANES))


def right_side_of(message, scale):
    size, width = message.shape
    size = size - TAIL
    tail = message[size:].astype(F32)
    weight = (tail[0:1] + tail[1:2]) + tail[2:3]
    scale = jnp.concatenate([scale] * (width // LANES), axis=1)
    return message[:size].astype(F32) * weight * scale


def first_kernel(
    even_ref, far_even_ref, odd_ref, scale_ref, matrix, out_ref, ends_ref, odd_out_ref
):
    pieces = 2 * even_ref.shape[0]
    odd_out_ref[...] = odd_ref[...]
    scale = scale_ref[...]
    values = [
        right_side_of((odd_ref if k % 2 else even_ref)[k // 2], scale) for k in range(pieces)
    ]
    ends_ref[0] = values[0]
    ends_ref[1] = right_side_of(far_even_ref[0], scale)
    rows = 2 * values[0].shape[1]
    joined = jnp.concatenate(values, axis=1)
    out_ref[:, rows:] = gram_parts(joined, joined)
    out_ref[:, :rows] = apply_dense(values, matrix)


def collect_kernel(
    even_ref, odd_ref, far_even_ref, far_odd_ref, scale_ref, residual_ref, direction_ref
):
    pieces = 2 * even_ref.shape[0]
    scale = scale_ref[...]
    for k in range(pieces):
        near = right_side_of((odd_ref if k % 2 else even_ref)[k // 2], scale)
        far = right_side_of((far_odd_ref if k % 2 else far_even_ref)[k // 2], scale)
        residual_ref[0, k] = near
        residual_ref[1, k] = far
        direction_ref[k] = near
        if k == 0:
            direction_ref[pieces] = far


def add_halves(mine_ref, other_ref, width):
    near = mine_ref[:, :width] + other_ref[:, width : 2 * width]
    far = mine_ref[:, width : 2 * width] + other_ref[:, :width]
    return near, far


def image_kernel(first, mine_ref, other_ref, near_ref, far_ref, *refs):
    out_ref, norm_ref = refs if first else (refs[0], None)
    core = lax.axis_index("col")
    size, width = near_ref.shape[1:]
    near, far = add_halves(mine_ref, other_ref, width)
    if first:
        norm_ref[...] = finish(mine_ref[:, 2 * width :] + other_ref[:, 2 * width :])
    parts = width // LANES
    for i in range(parts):
        lanes = slice(i * LANES, (i + 1) * LANES)
        for place, half in ((core, near), (1 - core, far)):
            at = pl.multiple_of((place * parts + i) * size, size)
            out_ref[pl.ds(at, size)] = half[:, lanes]
    products = symmetric_parts(near, near_ref[0]) + symmetric_parts(
        far, far_ref[far_ref.shape[0] - 1]
    )
    out_ref[2 * parts * size :] = pack(finish(products))


def inverse_kernel(norm_ref, out_ref):
    norm = norm_ref[...]
    size = norm.shape[0]
    norm = 0.5 * (norm + jnp.concatenate([norm[:, :size].T, norm[:, size:]], axis=1))
    unit = lax.broadcasted_iota(jnp.int32, norm.shape, 0) == lax.broadcasted_iota(
        jnp.int32, norm.shape, 1
    )
    out_ref[...] = solve_wide(jnp.where(unit, 1.0, 0.0), pltpu.roll(norm, size, 1))


def pick(refs, places, core, rows):
    if places[0] == places[1]:
        return refs[places[0]][rows]
    return jnp.where(core == 0, refs[places[0]][rows], refs[places[1]][rows])


def step_kernel(used, places, with_solution, last, *refs):
    images, refs = refs[:used], refs[used:]
    direction_ref, residual_ref, norm_ref, inverse_ref, matrix = refs[:5]
    refs = refs[5:]
    if with_solution:
        solution_ref, refs = refs[0], refs[1:]
    out_ref, new_direction, new_residual, new_norm, new_solution = refs
    core = lax.axis_index("col")
    pieces = len(places)
    size, width = direction_ref.shape[1:]
    parts = width // LANES

    def image(k, half):
        found = []
        for i in range(parts):
            at = pl.multiple_of((half * parts + i) * size, size)
            found.append(pick(images, places[k], core, pl.ds(at, size)))
        return jnp.concatenate(found, axis=1)

    behind = slice(2 * parts * size, None)
    products = add_up([pick(images, pair, core, behind) for pair in places])
    inverse = stack(inverse_ref[:, :size])
    alpha = stack(solve_wide(norm_ref[...], unpack(products, size, 1))[:, :size])
    residuals = [
        [residual_ref[side, k] - times(alpha, image(k, half)) for k in range(pieces)]
        for side, half in enumerate((core, 1 - core))
    ]
    joined = [jnp.concatenate(values, axis=1) for values in residuals]
    next_norm = finish(gram_parts(joined[0], joined[0]) + gram_parts(joined[1], joined[1]))
    new_norm[...] = next_norm
    step = times(alpha, direction_ref[0])
    new_solution[...] = solution_ref[...] + step if with_solution else step
    beta = stack_leading(times(inverse, next_norm)[:, :size])
    directions = [
        residual + times_leading(beta, direction_ref[k])
        for k, residual in enumerate(residuals[0] + residuals[1][:1])
    ]
    if last:
        new_residual[...] = residuals[0][0]
        new_direction[0] = directions[0]
        new_direction[1] = directions[pieces]
    else:
        for k in range(pieces):
            new_residual[0, k] = residuals[0][k]
            new_residual[1, k] = residuals[1][k]
        for k in range(pieces + 1):
            new_direction[k] = directions[k]
    out_ref[...] = apply_dense(directions[:pieces], matrix)


def last_image_kernel(mine_ref, other_ref, direction_ref, near_ref, gram_ref):
    near, far = add_halves(mine_ref, other_ref, direction_ref.shape[2])
    near_ref[...] = near
    products = symmetric_parts(near, direction_ref[0]) + symmetric_parts(far, direction_ref[1])
    gram_ref[...] = pack(finish(products))


def last_kernel(used, places, *refs):
    image_ref, direction_ref, residual_ref, norm_ref, solution_ref = refs[used:-2]
    new_solution, new_residual = refs[-2:]
    core = lax.axis_index("col")
    size = image_ref.shape[0]
    products = add_up([pick(refs, pair, core, slice(None)) for pair in places])
    alpha = stack(solve_wide(norm_ref[...], unpack(products, size, 1))[:, :size])
    new_solution[...] = solution_ref[...] + times(alpha, direction_ref[0])
    new_residual[...] = residual_ref[...] - times(alpha, image_ref[...])


def shape(*dims, dtype=F32):
    return jax.ShapeDtypeStruct(dims, dtype)


def per_device(tiles, tile_rows, tile_cols, tile_count, signs, vertex_weight, column_scale):
    sketch, rows_dev = signs.shape
    tile = tiles.shape[1]
    pieces = lax.axis_size("row")
    col_devices = lax.axis_size("col")
    group = col_devices * rows_dev
    depth = pieces * rows_dev

    def swap(value, mask):
        return lax.ppermute(value, "row", [(i, i ^ mask) for i in range(pieces)])

    def across(value):
        return lax.ppermute(
            value, "col", [(i, (i + 1) % col_devices) for i in range(col_devices)]
        )

    def exchange(value, turns=((7, 5), (3, 6), (2, 4), (1, 1))):
        if pieces != 8:
            found = [value] + [swap(value, k) for k in range(1, pieces)]
            return found, [(k, k) for k in range(pieces)]
        fetched = []
        passed = []
        places = {0: (0, 0)}
        for turn, masks in enumerate(turns, 1):
            pairs = [
                (i * 2 + core, (i ^ mask) * 2 + core)
                for core, mask in enumerate(masks)
                for i in range(pieces)
            ]
            fetched.append(lax.ppermute(value, ("row", "col"), pairs))
            if masks[0] == masks[1]:
                places[masks[0]] = (turn, turn)
            else:
                passed.append(across(fetched[-1]))
                places[masks[0]] = (turn, turn + len(turns))
                places[masks[1]] = (turn + len(turns), turn)
        return [value, *fetched, *passed], [places[k] for k in range(pieces)]

    height = sketch + TAIL
    given = (signs, vertex_weight, column_scale)
    message, scale = pl.pallas_call(
        message_kernel,
        out_shape=(shape(height, rows_dev, dtype=BF16), shape(sketch, LANES)),
        in_specs=[HBM] * 3,
        out_specs=(VMEM, VMEM),
        scratch_shapes=[
            *[pltpu.VMEM(x.shape, x.dtype) for x in given],
            pltpu.SemaphoreType.DMA((len(given),)),
        ],
        compiler_params=params(),
        name="message",
    )(*[pltpu.with_memory_space_constraint(x, pltpu.HBM) for x in given])
    even = [message] + [swap(message, k) for k in range(2, pieces, 2)]

    matrix = shape(2, depth, group, dtype=BF16)
    total = shape(depth // tile * (group // tile), tile, tile)
    slots = tiles.shape[0]
    half = slots // 2
    rest = shape(slots - half, tile, tile, dtype=BF16)
    lists = [pltpu.with_memory_space_constraint(x, pltpu.HBM) for x in (tile_rows, tile_cols)]
    lists_scratch = [pltpu.SMEM(x.shape, jnp.int32) for x in lists]
    cost = pl.CostEstimate(
        flops=4 * tiles.size, bytes_accessed=4 * tiles.size, transcendentals=0
    )
    blocks_sum, others = pl.pallas_call(
        functools.partial(gather_kernel, rows_dev),
        out_shape=(total, rest),
        in_specs=[SMEM] + [HBM] * 3,
        out_specs=(VMEM, VMEM),
        scratch_shapes=[
            pltpu.VMEM((half, tile, tile), BF16),
            *lists_scratch,
            pltpu.SemaphoreType.DMA((2 * CHUNKS,)),
            pltpu.SemaphoreType.DMA((len(lists),)),
        ],
        compiler_params=params(tiles, total),
        cost_estimate=cost,
        name="gather",
    )(tile_count, *lists, pltpu.with_memory_space_constraint(tiles, pltpu.HBM))
    joined = shape(pieces // 2, height, rows_dev, dtype=BF16)
    order = [*range(pieces // 4, pieces // 2), *range(1, pieces // 4), 0]
    even = pl.pallas_call(
        functools.partial(join_kernel, order),
        out_shape=joined,
        in_specs=[VMEM] * (pieces // 2) + [ANY],
        out_specs=VMEM,
        compiler_params=params(joined, joined),
        name="join",
    )(*[even[k] for k in order], blocks_sum)
    odd = swap(even, 1)
    far_even = across(even)
    dense, _ = pl.pallas_call(
        functools.partial(dense_kernel, rows_dev),
        out_shape=(matrix, total),
        in_specs=[SMEM] + [HBM] * 2 + [VMEM, VMEM, ANY],
        out_specs=(VMEM, VMEM),
        scratch_shapes=[*lists_scratch, pltpu.SemaphoreType.DMA((len(lists),))],
        input_output_aliases={4: 1},
        compiler_params=params(rest, total, total, matrix),
        cost_estimate=cost,
        name="dense",
    )(tile_count, *lists, others, blocks_sum, even)

    held = shape(2, pieces, sketch, rows_dev)
    state = shape(pieces + 1, sketch, rows_dev)
    small = shape(sketch, LANES)
    piece = shape(sketch, rows_dev)
    packed = shape(sketch * sketch // LANES, LANES)
    payload = shape(2 * sketch * (rows_dev // LANES) + packed.shape[0], LANES)

    partial_sum, ends, odd = pl.pallas_call(
        first_kernel,
        out_shape=(shape(sketch, group + LANES), shape(2, sketch, rows_dev), joined),
        in_specs=[VMEM] * 5,
        out_specs=(VMEM,) * 3,
        compiler_params=params(matrix, state, state),
        name="first",
    )(even, far_even, odd, scale, dense)
    norm = None
    solution = None
    direction = None
    for iteration in range(ITERS - 1):
        first = iteration == 0
        last = iteration == ITERS - 2
        sums = (partial_sum, across(partial_sum))
        given = (ends, ends) if first else (direction, direction)
        outs = pl.pallas_call(
            functools.partial(image_kernel, first),
            out_shape=(payload, small) if first else (payload,),
            in_specs=[VMEM] * 4,
            out_specs=(VMEM, VMEM) if first else (VMEM,),
            compiler_params=params(state, payload),
            name="image",
        )(*sums, *given)
        found, places = exchange(outs[0])
        if first:
            norm = outs[1]
            residual, direction = pl.pallas_call(
                collect_kernel,
                out_shape=(held, state),
                in_specs=[VMEM] * 5,
                out_specs=(VMEM, VMEM),
                compiler_params=params(held, held, state),
                name="collect",
            )(even, odd, far_even, across(odd), scale)
        inverse = pl.pallas_call(
            inverse_kernel,
            out_shape=small,
            in_specs=[VMEM],
            out_specs=VMEM,
            compiler_params=params(),
            name="inverse",
        )(norm)
        given = () if first else (solution,)
        partial_sum, direction, residual, norm, solution = pl.pallas_call(
            functools.partial(step_kernel, len(found), places, not first, last),
            out_shape=(
                shape(sketch, group),
                shape(2, sketch, rows_dev) if last else state,
                piece if last else held,
                small,
                piece,
            ),
            in_specs=[VMEM] * (len(found) + 5 + len(given)),
            out_specs=(VMEM,) * 5,
            compiler_params=params(matrix, held, held, held, held, state),
            name="step",
        )(*found, direction, residual, norm, inverse, dense, *given)
    near, gram = pl.pallas_call(
        last_image_kernel,
        out_shape=(piece, packed),
        in_specs=[VMEM] * 3,
        out_specs=(VMEM, VMEM),
        compiler_params=params(state),
        name="last_image",
    )(partial_sum, across(partial_sum), direction)
    found, places = exchange(gram, ((6, 7), (3, 5), (2, 4), (1, 1)))
    return pl.pallas_call(
        functools.partial(last_kernel, len(found), places),
        out_shape=(piece, piece),
        in_specs=[VMEM] * (len(found) + 5),
        out_specs=(VMEM, VMEM),
        compiler_params=params(state, state),
        name="last",
    )(*found, near, direction, residual, norm, solution)


def solution(mesh):
    return jax.shard_map(
        per_device,
        mesh=mesh,
        in_specs=(
            P(("row", "col"), None, None),
            P(("row", "col")),
            P(("row", "col")),
            P(("row", "col")),
            P("rhs", ("row", "col")),
            P(("row", "col")),
            P("rhs"),
        ),
        out_specs=(P("rhs", ("row", "col")), P("rhs", ("row", "col"))),
        check_vma=False,
    )
```

```python
import functools

import jax
import jax.numpy as jnp
from jax import lax
from jax.experimental import pallas as pl
from jax.experimental.pallas import tpu as pltpu
from jax.sharding import PartitionSpec as P

ITERS = 3
LANES = 128
PIVOTS = 16
TAIL = 16
UNROLL = 4
CHUNKS = 5
F32 = jnp.float32
BF16 = jnp.bfloat16
SPARE_BYTES = 4 * 1024 * 1024

VMEM = pl.BlockSpec(memory_space=pltpu.VMEM)
SMEM = pl.BlockSpec(memory_space=pltpu.SMEM)
HBM = pl.BlockSpec(memory_space=pltpu.HBM)
ANY = pl.BlockSpec(memory_space=pl.ANY)


def params(*arrays):
    used = sum(a.size * jnp.dtype(a.dtype).itemsize for a in arrays)
    return pltpu.CompilerParams(vmem_limit_bytes=used + SPARE_BYTES)


def split(value):
    high = value.astype(BF16)
    rest = value - high.astype(F32)
    middle = rest.astype(BF16)
    low = (rest - middle.astype(F32)).astype(BF16)
    return high, middle, low


def stack(left):
    high, middle, low = [part.astype(F32) for part in split(left)]
    parts = jnp.concatenate([high, high, middle, high, middle, low], axis=0)
    return parts.T.astype(BF16)


def times(stacked, right):
    high, middle, low = split(right)
    parts = jnp.concatenate([high, middle, high, low, middle, high], axis=0)
    return jnp.dot(stacked, parts, preferred_element_type=F32)


def stack_leading(left):
    high, middle, _ = [part.astype(F32) for part in split(left)]
    return jnp.concatenate([high, high, middle], axis=0).T.astype(BF16)


def times_leading(stacked, right):
    high, middle, _ = split(right)
    parts = jnp.concatenate([high, middle, high], axis=0)
    return jnp.dot(stacked, parts, preferred_element_type=F32)


def gram_parts(left, right):
    size, width = left.shape
    filler = jnp.zeros((LANES - 3 * size, width), BF16)
    every = lax.dot_general(
        jnp.concatenate(split(left), axis=0),
        jnp.concatenate([*split(right), filler], axis=0),
        (((1,), (1,)), ((), ())),
        preferred_element_type=F32,
    )
    return every[2 * size :] + every[size : 2 * size] + every[:size]


def symmetric_parts(left, right):
    return 0.5 * (gram_parts(left, right) + gram_parts(right, left))


def finish(parts, place=0):
    size = parts.shape[0]

    def block(index):
        shift = (place - index) * size % LANES
        return pltpu.roll(parts, shift, 1) if shift else parts

    return block(2) + block(1) + block(0)


def pack(wide):
    rows = wide.shape[0]
    folds = LANES // rows
    height = rows // folds
    lanes = lax.broadcasted_iota(jnp.int32, wide.shape, 1)
    wide = jnp.where(lanes < rows, wide, 0.0)
    total = wide[:height]
    for i in range(1, folds):
        total = total + pltpu.roll(wide[i * height : (i + 1) * height], i * rows, 1)
    return total


def unpack(folded, size, place=0):
    parts = []
    for i in range(LANES // size):
        shift = (place - i) * size % LANES
        parts.append(pltpu.roll(folded, shift, 1) if shift else folded)
    return jnp.concatenate(parts, axis=0)


def solve_wide(target, matrix):
    size = matrix.shape[0]
    row_ids = lax.broadcasted_iota(jnp.int32, (size, LANES), 0)
    lane_ids = lax.broadcasted_iota(jnp.int32, (size, LANES), 1)
    work = jnp.where(lane_ids < size, target, matrix)
    for base in range(0, size, PIVOTS):
        columns = [
            jnp.broadcast_to(work[:, size + base + i : size + base + i + 1], (size, LANES))
            for i in range(PIVOTS)
        ]
        for i in range(PIVOTS):
            pivot = base + i
            here = row_ids == pivot
            inverse = pltpu.reciprocal(columns[i][pivot : pivot + 1, :], full_range=False)
            row = work[pivot : pivot + 1, :] * inverse
            work = jnp.where(here, row, work - columns[i] * row)
            for later in range(i + 1, PIVOTS):
                entry = columns[later][pivot : pivot + 1, :] * inverse
                columns[later] = jnp.where(here, entry, columns[later] - columns[i] * entry)
    return work


def add_up(values):
    values = list(values)
    while len(values) > 1:
        pairs = [values[i] + values[i + 1] for i in range(0, len(values) - 1, 2)]
        values = pairs + values[len(values) - len(values) % 2 :]
    return values[0]


def add_tiles(rows_dev, lists, tiles, first_tile, start, stop, total):
    rows_ref, cols_ref = lists
    tile = total.shape[1]
    slots = rows_ref.shape[0]
    blocks = rows_dev // tile
    row_place = lax.axis_index("row")
    col_place = lax.axis_index("col")
    col_devices = lax.axis_size("col")
    row_blocks = col_devices * blocks

    def place(slot):
        row = rows_ref[slot]
        column = cols_ref[slot]
        side = lax.rem(row // blocks + col_devices - col_place, col_devices)
        owner = column // (blocks * col_devices)
        column_at = (owner ^ row_place) * blocks + lax.rem(column, blocks)
        return column_at * row_blocks + side * blocks + lax.rem(row, blocks)

    def after(slot):
        return place(jnp.minimum(slot, slots - 1))

    def add(turn, places):
        slot = start + UNROLL * turn
        values = [tiles[slot + i - first_tile].astype(F32) for i in range(UNROLL)]
        following = tuple(after(slot + UNROLL + i) for i in range(UNROLL))
        for at, value in zip(places, values):
            total[at] = total[at] + value
        return following

    def add_one(slot, at):
        value = tiles[slot - first_tile].astype(F32)
        following = after(slot + 1)
        total[at] = total[at] + value
        return following

    turns = (stop - start) // UNROLL
    places = lax.fori_loop(0, turns, add, tuple(after(start + i) for i in range(UNROLL)))
    lax.fori_loop(start + UNROLL * turns, stop, add_one, places[0])


def copy_lists(hbm_refs, smem_refs, sems):
    copies = [
        pltpu.make_async_copy(source, target, sems.at[i])
        for i, (source, target) in enumerate(zip(hbm_refs, smem_refs))
    ]
    for copy in copies:
        copy.start()
    return copies


def gather_kernel(rows_dev, count_ref, rows_hbm, cols_hbm, tiles_ref, total, rest, *scratch):
    held, rows_ref, cols_ref, sems, list_sems = scratch
    live = count_ref[0]
    half = held.shape[0]
    slots, tile = tiles_ref.shape[:2]
    chunk = -(-half // CHUNKS)
    lists = copy_lists((rows_hbm, cols_hbm), (rows_ref, cols_ref), list_sems)
    copies = []
    for c in range(CHUNKS):
        part = pl.ds(c * chunk, min(chunk, half - c * chunk))
        copies.append(pltpu.make_async_copy(tiles_ref.at[part], held.at[part], sems.at[c]))

        @pl.when(c * chunk < live)
        def _():
            copies[c].start()

    chunk_rest = -(-rest.shape[0] // CHUNKS)
    rest_copies = []
    for c in range(CHUNKS):
        start = c * chunk_rest
        length = min(chunk_rest, rest.shape[0] - start)
        copy = pltpu.make_async_copy(
            tiles_ref.at[pl.ds(half + start, length)],
            rest.at[pl.ds(start, length)],
            sems.at[CHUNKS + c],
        )
        rest_copies.append((half + start, copy))

        @pl.when(half + start < live)
        def _():
            copy.start()

    def clear(index, carry):
        total[index] = jnp.zeros((tile, tile), F32)
        return carry

    lax.fori_loop(0, total.shape[0], clear, 0, unroll=4)
    for copy in lists:
        copy.wait()
    for c in range(CHUNKS):
        start, stop = c * chunk, min((c + 1) * chunk, half)

        @pl.when(start < live)
        def _():
            copies[c].wait()
            add_tiles(
                rows_dev, (rows_ref, cols_ref), held, 0, start, jnp.minimum(live, stop), total
            )

    for start, copy in rest_copies:

        @pl.when(start < live)
        def _():
            copy.wait()


def dense_kernel(
    rows_dev, count_ref, rows_hbm, cols_hbm, rest, total_in, joined_ref, out_ref, total, *scratch
):
    rows_ref, cols_ref, list_sems = scratch
    live = count_ref[0]
    half = rows_ref.shape[0] - rest.shape[0]
    tile = total.shape[1]
    row_blocks = out_ref.shape[2] // tile

    @pl.when(half < live)
    def _():
        lists = copy_lists((rows_hbm, cols_hbm), (rows_ref, cols_ref), list_sems)
        for copy in lists:
            copy.wait()
        add_tiles(rows_dev, (rows_ref, cols_ref), rest, half, half, live, total)

    def part(index, carry):
        start = pl.multiple_of(index * tile, tile)
        for b in range(row_blocks):
            value = total[index * row_blocks + b].T
            high = value.astype(BF16)
            low = (value - high.astype(F32)).astype(BF16)
            out_ref[0, pl.ds(start, tile), pl.ds(b * tile, tile)] = high
            out_ref[1, pl.ds(start, tile), pl.ds(b * tile, tile)] = low
        return carry

    lax.fori_loop(0, total.shape[0] // row_blocks, part, 0)


def join_kernel(order, *refs):
    for k, ref in zip(order, refs):
        refs[-1][k] = ref[...]


def apply_dense(directions, matrix):
    rounded = jnp.concatenate([direction.astype(BF16) for direction in directions], axis=1)
    high, low = [
        jnp.dot(rounded, matrix[part], preferred_element_type=F32) for part in range(2)
    ]
    return high + low


def message_kernel(
    signs_hbm, weight_hbm, scale_hbm, out_ref, scale_out, signs_ref, weight_ref, scale_ref, sems
):
    copies = copy_lists(
        (signs_hbm, weight_hbm, scale_hbm), (signs_ref, weight_ref, scale_ref), sems
    )
    for copy in copies:
        copy.wait()
    size, width = signs_ref.shape
    out_ref[:size] = signs_ref[...].astype(F32).astype(BF16)
    row_ids = lax.broadcasted_iota(jnp.int32, (TAIL, width), 0)
    tail = jnp.zeros((TAIL, width), F32)
    for i, part in enumerate(split(weight_ref[...].reshape(1, width))):
        tail = jnp.where(row_ids == i, part.astype(F32), tail)
    out_ref[size:] = tail.astype(BF16)
    scale = scale_ref[...].reshape(1, size)
    scale = jnp.concatenate([scale, jnp.zeros((1, LANES - size), F32)], axis=1)
    rows = lax.broadcasted_iota(jnp.int32, (size, LANES), 0)
    lanes = lax.broadcasted_iota(jnp.int32, (size, LANES), 1)
    column = jnp.sum(jnp.where(rows == lanes, scale, 0.0), axis=1, keepdims=True)
    scale_out[...] = jnp.broadcast_to(column, (size, LANES))


def right_side_of(message, scale):
    size, width = message.shape
    size = size - TAIL
    tail = message[size:].astype(F32)
    weight = (tail[0:1] + tail[1:2]) + tail[2:3]
    scale = jnp.concatenate([scale] * (width // LANES), axis=1)
    return message[:size].astype(F32) * weight * scale


def first_kernel(
    even_ref, far_even_ref, odd_ref, scale_ref, matrix, out_ref, ends_ref, odd_out_ref
):
    pieces = 2 * even_ref.shape[0]
    odd_out_ref[...] = odd_ref[...]
    scale = scale_ref[...]
    values = [
        right_side_of((odd_ref if k % 2 else even_ref)[k // 2], scale) for k in range(pieces)
    ]
    ends_ref[0] = values[0]
    ends_ref[1] = right_side_of(far_even_ref[0], scale)
    rows = 2 * values[0].shape[1]
    joined = jnp.concatenate(values, axis=1)
    out_ref[:, rows:] = gram_parts(joined, joined)
    out_ref[:, :rows] = apply_dense(values, matrix)


def collect_kernel(
    even_ref, odd_ref, far_even_ref, far_odd_ref, scale_ref, residual_ref, direction_ref
):
    pieces = 2 * even_ref.shape[0]
    scale = scale_ref[...]
    for k in range(pieces):
        near = right_side_of((odd_ref if k % 2 else even_ref)[k // 2], scale)
        far = right_side_of((far_odd_ref if k % 2 else far_even_ref)[k // 2], scale)
        residual_ref[0, k] = near
        residual_ref[1, k] = far
        direction_ref[k] = near
        if k == 0:
            direction_ref[pieces] = far


def add_halves(mine_ref, other_ref, width):
    near = mine_ref[:, :width] + other_ref[:, width : 2 * width]
    far = mine_ref[:, width : 2 * width] + other_ref[:, :width]
    return near, far


def image_kernel(first, mine_ref, other_ref, near_ref, far_ref, *refs):
    out_ref, norm_ref = refs if first else (refs[0], None)
    core = lax.axis_index("col")
    size, width = near_ref.shape[1:]
    near, far = add_halves(mine_ref, other_ref, width)
    if first:
        norm_ref[...] = finish(mine_ref[:, 2 * width :] + other_ref[:, 2 * width :])
    parts = width // LANES
    for i in range(parts):
        lanes = slice(i * LANES, (i + 1) * LANES)
        for place, half in ((core, near), (1 - core, far)):
            at = pl.multiple_of((place * parts + i) * size, size)
            out_ref[pl.ds(at, size)] = half[:, lanes]
    products = symmetric_parts(near, near_ref[0]) + symmetric_parts(
        far, far_ref[far_ref.shape[0] - 1]
    )
    out_ref[2 * parts * size :] = pack(finish(products))


def inverse_kernel(norm_ref, out_ref):
    norm = norm_ref[...]
    size = norm.shape[0]
    norm = 0.5 * (norm + jnp.concatenate([norm[:, :size].T, norm[:, size:]], axis=1))
    unit = lax.broadcasted_iota(jnp.int32, norm.shape, 0) == lax.broadcasted_iota(
        jnp.int32, norm.shape, 1
    )
    out_ref[...] = solve_wide(jnp.where(unit, 1.0, 0.0), pltpu.roll(norm, size, 1))


def pick(refs, places, core, rows):
    if places[0] == places[1]:
        return refs[places[0]][rows]
    return jnp.where(core == 0, refs[places[0]][rows], refs[places[1]][rows])


def step_kernel(used, places, with_solution, last, *refs):
    images, refs = refs[:used], refs[used:]
    direction_ref, residual_ref, norm_ref, inverse_ref, matrix = refs[:5]
    refs = refs[5:]
    if with_solution:
        solution_ref, refs = refs[0], refs[1:]
    out_ref, new_direction, new_residual, new_norm, new_solution = refs
    core = lax.axis_index("col")
    pieces = len(places)
    size, width = direction_ref.shape[1:]
    parts = width // LANES

    def image(k, half):
        found = []
        for i in range(parts):
            at = pl.multiple_of((half * parts + i) * size, size)
            found.append(pick(images, places[k], core, pl.ds(at, size)))
        return jnp.concatenate(found, axis=1)

    behind = slice(2 * parts * size, None)
    products = add_up([pick(images, pair, core, behind) for pair in places])
    inverse = stack(inverse_ref[:, :size])
    alpha = stack(solve_wide(norm_ref[...], unpack(products, size, 1))[:, :size])
    residuals = [
        [residual_ref[side, k] - times(alpha, image(k, half)) for k in range(pieces)]
        for side, half in enumerate((core, 1 - core))
    ]
    joined = [jnp.concatenate(values, axis=1) for values in residuals]
    next_norm = finish(gram_parts(joined[0], joined[0]) + gram_parts(joined[1], joined[1]))
    new_norm[...] = next_norm
    step = times(alpha, direction_ref[0])
    new_solution[...] = solution_ref[...] + step if with_solution else step
    beta = stack_leading(times(inverse, next_norm)[:, :size])
    directions = [
        residual + times_leading(beta, direction_ref[k])
        for k, residual in enumerate(residuals[0] + residuals[1][:1])
    ]
    if last:
        new_residual[...] = residuals[0][0]
        new_direction[0] = directions[0]
        new_direction[1] = directions[pieces]
    else:
        for k in range(pieces):
            new_residual[0, k] = residuals[0][k]
            new_residual[1, k] = residuals[1][k]
        for k in range(pieces + 1):
            new_direction[k] = directions[k]
    out_ref[...] = apply_dense(directions[:pieces], matrix)


def last_image_kernel(mine_ref, other_ref, direction_ref, near_ref, gram_ref):
    near, far = add_halves(mine_ref, other_ref, direction_ref.shape[2])
    near_ref[...] = near
    products = symmetric_parts(near, direction_ref[0]) + symmetric_parts(far, direction_ref[1])
    gram_ref[...] = pack(finish(products))


def last_kernel(used, places, *refs):
    image_ref, direction_ref, residual_ref, norm_ref, solution_ref = refs[used:-2]
    new_solution, new_residual = refs[-2:]
    core = lax.axis_index("col")
    size = image_ref.shape[0]
    products = add_up([pick(refs, pair, core, slice(None)) for pair in places])
    alpha = stack(solve_wide(norm_ref[...], unpack(products, size, 1))[:, :size])
    new_solution[...] = solution_ref[...] + times(alpha, direction_ref[0])
    new_residual[...] = residual_ref[...] - times(alpha, image_ref[...])


def shape(*dims, dtype=F32):
    return jax.ShapeDtypeStruct(dims, dtype)


def per_device(tiles, tile_rows, tile_cols, tile_count, signs, vertex_weight, column_scale):
    sketch, rows_dev = signs.shape
    tile = tiles.shape[1]
    pieces = lax.axis_size("row")
    col_devices = lax.axis_size("col")
    group = col_devices * rows_dev
    depth = pieces * rows_dev

    def swap(value, mask):
        return lax.ppermute(value, "row", [(i, i ^ mask) for i in range(pieces)])

    def across(value):
        return lax.ppermute(
            value, "col", [(i, (i + 1) % col_devices) for i in range(col_devices)]
        )

    def exchange(value, turns=((7, 5), (3, 6), (2, 4), (1, 1))):
        if pieces != 8:
            found = [value] + [swap(value, k) for k in range(1, pieces)]
            return found, [(k, k) for k in range(pieces)]
        fetched = []
        passed = []
        places = {0: (0, 0)}
        for turn, masks in enumerate(turns, 1):
            pairs = [
                (i * 2 + core, (i ^ mask) * 2 + core)
                for core, mask in enumerate(masks)
                for i in range(pieces)
            ]
            fetched.append(lax.ppermute(value, ("row", "col"), pairs))
            if masks[0] == masks[1]:
                places[masks[0]] = (turn, turn)
            else:
                passed.append(across(fetched[-1]))
                places[masks[0]] = (turn, turn + len(turns))
                places[masks[1]] = (turn + len(turns), turn)
        return [value, *fetched, *passed], [places[k] for k in range(pieces)]

    height = sketch + TAIL
    given = (signs, vertex_weight, column_scale)
    message, scale = pl.pallas_call(
        message_kernel,
        out_shape=(shape(height, rows_dev, dtype=BF16), shape(sketch, LANES)),
        in_specs=[HBM] * 3,
        out_specs=(VMEM, VMEM),
        scratch_shapes=[
            *[pltpu.VMEM(x.shape, x.dtype) for x in given],
            pltpu.SemaphoreType.DMA((len(given),)),
        ],
        compiler_params=params(),
        name="message",
    )(*[pltpu.with_memory_space_constraint(x, pltpu.HBM) for x in given])
    even = [message] + [swap(message, k) for k in range(2, pieces, 2)]

    matrix = shape(2, depth, group, dtype=BF16)
    total = shape(depth // tile * (group // tile), tile, tile)
    slots = tiles.shape[0]
    half = slots // 2
    rest = shape(slots - half, tile, tile, dtype=BF16)
    lists = [pltpu.with_memory_space_constraint(x, pltpu.HBM) for x in (tile_rows, tile_cols)]
    lists_scratch = [pltpu.SMEM(x.shape, jnp.int32) for x in lists]
    cost = pl.CostEstimate(
        flops=4 * tiles.size, bytes_accessed=4 * tiles.size, transcendentals=0
    )
    blocks_sum, others = pl.pallas_call(
        functools.partial(gather_kernel, rows_dev),
        out_shape=(total, rest),
        in_specs=[SMEM] + [HBM] * 3,
        out_specs=(VMEM, VMEM),
        scratch_shapes=[
            pltpu.VMEM((half, tile, tile), BF16),
            *lists_scratch,
            pltpu.SemaphoreType.DMA((2 * CHUNKS,)),
            pltpu.SemaphoreType.DMA((len(lists),)),
        ],
        compiler_params=params(tiles, total),
        cost_estimate=cost,
        name="gather",
    )(tile_count, *lists, pltpu.with_memory_space_constraint(tiles, pltpu.HBM))
    joined = shape(pieces // 2, height, rows_dev, dtype=BF16)
    order = [*range(pieces // 4, pieces // 2), *range(1, pieces // 4), 0]
    even = pl.pallas_call(
        functools.partial(join_kernel, order),
        out_shape=joined,
        in_specs=[VMEM] * (pieces // 2) + [ANY],
        out_specs=VMEM,
        compiler_params=params(joined, joined),
        name="join",
    )(*[even[k] for k in order], blocks_sum)
    odd = swap(even, 1)
    far_even = across(even)
    dense, _ = pl.pallas_call(
        functools.partial(dense_kernel, rows_dev),
        out_shape=(matrix, total),
        in_specs=[SMEM] + [HBM] * 2 + [VMEM, VMEM, ANY],
        out_specs=(VMEM, VMEM),
        scratch_shapes=[*lists_scratch, pltpu.SemaphoreType.DMA((len(lists),))],
        input_output_aliases={4: 1},
        compiler_params=params(rest, total, total, matrix),
        cost_estimate=cost,
        name="dense",
    )(tile_count, *lists, others, blocks_sum, even)

    held = shape(2, pieces, sketch, rows_dev)
    state = shape(pieces + 1, sketch, rows_dev)
    small = shape(sketch, LANES)
    piece = shape(sketch, rows_dev)
    packed = shape(sketch * sketch // LANES, LANES)
    payload = shape(2 * sketch * (rows_dev // LANES) + packed.shape[0], LANES)

    partial_sum, ends, odd = pl.pallas_call(
        first_kernel,
        out_shape=(shape(sketch, group + LANES), shape(2, sketch, rows_dev), joined),
        in_specs=[VMEM] * 5,
        out_specs=(VMEM,) * 3,
        compiler_params=params(matrix, state, state),
        name="first",
    )(even, far_even, odd, scale, dense)
    norm = None
    solution = None
    direction = None
    for iteration in range(ITERS - 1):
        first = iteration == 0
        last = iteration == ITERS - 2
        sums = (partial_sum, across(partial_sum))
        given = (ends, ends) if first else (direction, direction)
        outs = pl.pallas_call(
            functools.partial(image_kernel, first),
            out_shape=(payload, small) if first else (payload,),
            in_specs=[VMEM] * 4,
            out_specs=(VMEM, VMEM) if first else (VMEM,),
            compiler_params=params(state, payload),
            name="image",
        )(*sums, *given)
        found, places = exchange(outs[0])
        if first:
            norm = outs[1]
            residual, direction = pl.pallas_call(
                collect_kernel,
                out_shape=(held, state),
                in_specs=[VMEM] * 5,
                out_specs=(VMEM, VMEM),
                compiler_params=params(held, held, state),
                name="collect",
            )(even, odd, far_even, across(odd), scale)
        inverse = pl.pallas_call(
            inverse_kernel,
            out_shape=small,
            in_specs=[VMEM],
            out_specs=VMEM,
            compiler_params=params(),
            name="inverse",
        )(norm)
        given = () if first else (solution,)
        partial_sum, direction, residual, norm, solution = pl.pallas_call(
            functools.partial(step_kernel, len(found), places, not first, last),
            out_shape=(
                shape(sketch, group),
                shape(2, sketch, rows_dev) if last else state,
                piece if last else held,
                small,
                piece,
            ),
            in_specs=[VMEM] * (len(found) + 5 + len(given)),
            out_specs=(VMEM,) * 5,
            compiler_params=params(matrix, held, held, held, held, state),
            name="step",
        )(*found, direction, residual, norm, inverse, dense, *given)
    near, gram = pl.pallas_call(
        last_image_kernel,
        out_shape=(piece, packed),
        in_specs=[VMEM] * 3,
        out_specs=(VMEM, VMEM),
        compiler_params=params(state),
        name="last_image",
    )(partial_sum, across(partial_sum), direction)
    found, places = exchange(gram, ((6, 7), (3, 5), (2, 4), (1, 1)))
    return pl.pallas_call(
        functools.partial(last_kernel, len(found), places),
        out_shape=(piece, piece),
        in_specs=[VMEM] * (len(found) + 5),
        out_specs=(VMEM, VMEM),
        compiler_params=params(state, state),
        name="last",
    )(*found, near, direction, residual, norm, solution)


def solution(mesh):
    return jax.shard_map(
        per_device,
        mesh=mesh,
        in_specs=(
            P(("row", "col"), None, None),
            P(("row", "col")),
            P(("row", "col")),
            P(("row", "col")),
            P("rhs", ("row", "col")),
            P(("row", "col")),
            P("rhs"),
        ),
        out_specs=(P("rhs", ("row", "col")), P("rhs", ("row", "col"))),
        check_vma=False,
    )
```

```python
import functools

import jax
import jax.numpy as jnp
from jax import lax
from jax.experimental import pallas as pl
from jax.experimental.pallas import tpu as pltpu
from jax.sharding import PartitionSpec as P

ITERS = 3
LANES = 128
PIVOTS = 16
TAIL = 16
CHUNKS = 4
F32 = jnp.float32
BF16 = jnp.bfloat16
SPARE_BYTES = 4 * 1024 * 1024

VMEM = pl.BlockSpec(memory_space=pltpu.VMEM)
SMEM = pl.BlockSpec(memory_space=pltpu.SMEM)
HBM = pl.BlockSpec(memory_space=pltpu.HBM)
ANY = pl.BlockSpec(memory_space=pl.ANY)


def params(*arrays):
    used = sum(a.size * jnp.dtype(a.dtype).itemsize for a in arrays)
    return pltpu.CompilerParams(vmem_limit_bytes=used + SPARE_BYTES)


def split(value):
    high = value.astype(BF16)
    rest = value - high.astype(F32)
    middle = rest.astype(BF16)
    low = (rest - middle.astype(F32)).astype(BF16)
    return high, middle, low


def stack(left):
    high, middle, low = [part.astype(F32) for part in split(left)]
    parts = jnp.concatenate([high, high, middle, high, middle, low], axis=0)
    return parts.T.astype(BF16)


def times(stacked, right):
    high, middle, low = split(right)
    parts = jnp.concatenate([high, middle, high, low, middle, high], axis=0)
    return jnp.dot(stacked, parts, preferred_element_type=F32)


def stack_leading(left):
    high, middle, _ = [part.astype(F32) for part in split(left)]
    return jnp.concatenate([high, high, middle], axis=0).T.astype(BF16)


def times_leading(stacked, right):
    high, middle, _ = split(right)
    parts = jnp.concatenate([high, middle, high], axis=0)
    return jnp.dot(stacked, parts, preferred_element_type=F32)


def gram_parts(left, right):
    size, width = left.shape
    filler = jnp.zeros((LANES - 3 * size, width), BF16)
    every = lax.dot_general(
        jnp.concatenate(split(left), axis=0),
        jnp.concatenate([*split(right), filler], axis=0),
        (((1,), (1,)), ((), ())),
        preferred_element_type=F32,
    )
    return every[2 * size :] + every[size : 2 * size] + every[:size]


def symmetric_parts(left, right):
    return 0.5 * (gram_parts(left, right) + gram_parts(right, left))


def finish(parts, place=0):
    size = parts.shape[0]

    def block(index):
        shift = (place - index) * size % LANES
        return pltpu.roll(parts, shift, 1) if shift else parts

    return block(2) + block(1) + block(0)


def pack(wide):
    rows = wide.shape[0]
    folds = LANES // rows
    height = rows // folds
    lanes = lax.broadcasted_iota(jnp.int32, wide.shape, 1)
    wide = jnp.where(lanes < rows, wide, 0.0)
    total = wide[:height]
    for i in range(1, folds):
        total = total + pltpu.roll(wide[i * height : (i + 1) * height], i * rows, 1)
    return total


def unpack(folded, size, place=0):
    parts = []
    for i in range(LANES // size):
        shift = (place - i) * size % LANES
        parts.append(pltpu.roll(folded, shift, 1) if shift else folded)
    return jnp.concatenate(parts, axis=0)


def solve_wide(target, matrix):
    size = matrix.shape[0]
    row_ids = lax.broadcasted_iota(jnp.int32, (size, LANES), 0)
    lane_ids = lax.broadcasted_iota(jnp.int32, (size, LANES), 1)
    work = jnp.where(lane_ids < size, target, matrix)
    for base in range(0, size, PIVOTS):
        columns = [
            jnp.broadcast_to(work[:, size + base + i : size + base + i + 1], (size, LANES))
            for i in range(PIVOTS)
        ]
        for i in range(PIVOTS):
            pivot = base + i
            here = row_ids == pivot
            inverse = pltpu.reciprocal(columns[i][pivot : pivot + 1, :], full_range=False)
            row = work[pivot : pivot + 1, :] * inverse
            work = jnp.where(here, row, work - columns[i] * row)
            for later in range(i + 1, PIVOTS):
                entry = columns[later][pivot : pivot + 1, :] * inverse
                columns[later] = jnp.where(here, entry, columns[later] - columns[i] * entry)
    return work


def add_up(values):
    values = list(values)
    while len(values) > 1:
        pairs = [values[i] + values[i + 1] for i in range(0, len(values) - 1, 2)]
        values = pairs + values[len(values) - len(values) % 2 :]
    return values[0]


def add_tiles(rows_dev, lists, tiles, first_tile, start, stop, total):
    rows_ref, cols_ref = lists
    tile = total.shape[1]
    slots = rows_ref.shape[0]
    blocks = rows_dev // tile
    row_place = lax.axis_index("row")
    col_place = lax.axis_index("col")
    col_devices = lax.axis_size("col")
    row_blocks = col_devices * blocks

    def place(slot):
        row = rows_ref[slot]
        column = cols_ref[slot]
        side = lax.rem(row // blocks + col_devices - col_place, col_devices)
        owner = column // (blocks * col_devices)
        column_at = (owner ^ row_place) * blocks + lax.rem(column, blocks)
        return column_at * row_blocks + side * blocks + lax.rem(row, blocks)

    def after(slot):
        return place(jnp.minimum(slot, slots - 1))

    def add(turn, places):
        slot = start + 2 * turn
        values = [tiles[slot + i - first_tile].astype(F32) for i in range(2)]
        following = (after(slot + 2), after(slot + 3))
        for at, value in zip(places, values):
            total[at] = total[at] + value
        return following

    places = lax.fori_loop(0, (stop - start) // 2, add, (after(start), after(start + 1)))

    @pl.when(lax.rem(stop - start, 2) == 1)
    def _():
        total[places[0]] = total[places[0]] + tiles[stop - 1 - first_tile].astype(F32)


def copy_lists(hbm_refs, smem_refs, sems):
    copies = [
        pltpu.make_async_copy(source, target, sems.at[i])
        for i, (source, target) in enumerate(zip(hbm_refs, smem_refs))
    ]
    for copy in copies:
        copy.start()
    return copies


def gather_kernel(rows_dev, count_ref, rows_hbm, cols_hbm, tiles_ref, total, rest, *scratch):
    held, rows_ref, cols_ref, sems, list_sems = scratch
    live = count_ref[0]
    half = held.shape[0]
    slots, tile = tiles_ref.shape[:2]
    chunk = -(-half // CHUNKS)
    lists = copy_lists((rows_hbm, cols_hbm), (rows_ref, cols_ref), list_sems)
    copies = []
    for c in range(CHUNKS):
        part = pl.ds(c * chunk, min(chunk, half - c * chunk))
        copies.append(pltpu.make_async_copy(tiles_ref.at[part], held.at[part], sems.at[c]))

        @pl.when(c * chunk < live)
        def _():
            copies[c].start()

    chunk_rest = -(-rest.shape[0] // CHUNKS)
    rest_copies = []
    for c in range(CHUNKS):
        start = c * chunk_rest
        length = min(chunk_rest, rest.shape[0] - start)
        copy = pltpu.make_async_copy(
            tiles_ref.at[pl.ds(half + start, length)],
            rest.at[pl.ds(start, length)],
            sems.at[CHUNKS + c],
        )
        rest_copies.append((half + start, copy))

        @pl.when(half + start < live)
        def _():
            copy.start()

    def clear(index, carry):
        total[index] = jnp.zeros((tile, tile), F32)
        return carry

    lax.fori_loop(0, total.shape[0], clear, 0, unroll=4)
    for copy in lists:
        copy.wait()
    for c in range(CHUNKS):
        start, stop = c * chunk, min((c + 1) * chunk, half)

        @pl.when(start < live)
        def _():
            copies[c].wait()
            add_tiles(
                rows_dev, (rows_ref, cols_ref), held, 0, start, jnp.minimum(live, stop), total
            )

    for start, copy in rest_copies:

        @pl.when(start < live)
        def _():
            copy.wait()


def dense_kernel(
    rows_dev, count_ref, rows_hbm, cols_hbm, rest, total_in, joined_ref, out_ref, total, *scratch
):
    rows_ref, cols_ref, list_sems = scratch
    live = count_ref[0]
    half = rows_ref.shape[0] - rest.shape[0]
    tile = total.shape[1]
    row_blocks = out_ref.shape[2] // tile

    @pl.when(half < live)
    def _():
        lists = copy_lists((rows_hbm, cols_hbm), (rows_ref, cols_ref), list_sems)
        for copy in lists:
            copy.wait()
        add_tiles(rows_dev, (rows_ref, cols_ref), rest, half, half, live, total)

    def part(index, carry):
        start = pl.multiple_of(index * tile, tile)
        for b in range(row_blocks):
            value = total[index * row_blocks + b].T
            high = value.astype(BF16)
            low = (value - high.astype(F32)).astype(BF16)
            out_ref[0, pl.ds(start, tile), pl.ds(b * tile, tile)] = high
            out_ref[1, pl.ds(start, tile), pl.ds(b * tile, tile)] = low
        return carry

    lax.fori_loop(0, total.shape[0] // row_blocks, part, 0)


def join_kernel(order, *refs):
    for k, ref in zip(order, refs):
        refs[-1][k] = ref[...]


def apply_dense(directions, matrix):
    rounded = jnp.concatenate([direction.astype(BF16) for direction in directions], axis=1)
    high, low = [
        jnp.dot(rounded, matrix[part], preferred_element_type=F32) for part in range(2)
    ]
    return high + low


def message_kernel(
    signs_hbm, weight_hbm, scale_hbm, out_ref, scale_out, signs_ref, weight_ref, scale_ref, sems
):
    copies = copy_lists(
        (signs_hbm, weight_hbm, scale_hbm), (signs_ref, weight_ref, scale_ref), sems
    )
    for copy in copies:
        copy.wait()
    size, width = signs_ref.shape
    out_ref[:size] = signs_ref[...].astype(F32).astype(BF16)
    row_ids = lax.broadcasted_iota(jnp.int32, (TAIL, width), 0)
    tail = jnp.zeros((TAIL, width), F32)
    for i, part in enumerate(split(weight_ref[...].reshape(1, width))):
        tail = jnp.where(row_ids == i, part.astype(F32), tail)
    out_ref[size:] = tail.astype(BF16)
    scale = scale_ref[...].reshape(1, size)
    scale = jnp.concatenate([scale, jnp.zeros((1, LANES - size), F32)], axis=1)
    rows = lax.broadcasted_iota(jnp.int32, (size, LANES), 0)
    lanes = lax.broadcasted_iota(jnp.int32, (size, LANES), 1)
    column = jnp.sum(jnp.where(rows == lanes, scale, 0.0), axis=1, keepdims=True)
    scale_out[...] = jnp.broadcast_to(column, (size, LANES))


def right_side_of(message, scale):
    size, width = message.shape
    size = size - TAIL
    tail = message[size:].astype(F32)
    weight = (tail[0:1] + tail[1:2]) + tail[2:3]
    scale = jnp.concatenate([scale] * (width // LANES), axis=1)
    return message[:size].astype(F32) * weight * scale


def first_kernel(
    even_ref, far_even_ref, odd_ref, scale_ref, matrix, out_ref, ends_ref, odd_out_ref
):
    pieces = 2 * even_ref.shape[0]
    odd_out_ref[...] = odd_ref[...]
    scale = scale_ref[...]
    values = [
        right_side_of((odd_ref if k % 2 else even_ref)[k // 2], scale) for k in range(pieces)
    ]
    ends_ref[0] = values[0]
    ends_ref[1] = right_side_of(far_even_ref[0], scale)
    rows = 2 * values[0].shape[1]
    joined = jnp.concatenate(values, axis=1)
    out_ref[:, rows:] = gram_parts(joined, joined)
    out_ref[:, :rows] = apply_dense(values, matrix)


def collect_kernel(
    even_ref, odd_ref, far_even_ref, far_odd_ref, scale_ref, residual_ref, direction_ref
):
    pieces = 2 * even_ref.shape[0]
    scale = scale_ref[...]
    for k in range(pieces):
        near = right_side_of((odd_ref if k % 2 else even_ref)[k // 2], scale)
        far = right_side_of((far_odd_ref if k % 2 else far_even_ref)[k // 2], scale)
        residual_ref[0, k] = near
        residual_ref[1, k] = far
        direction_ref[k] = near
        if k == 0:
            direction_ref[pieces] = far


def add_halves(mine_ref, other_ref, width):
    near = mine_ref[:, :width] + other_ref[:, width : 2 * width]
    far = mine_ref[:, width : 2 * width] + other_ref[:, :width]
    return near, far


def image_kernel(first, mine_ref, other_ref, near_ref, far_ref, *refs):
    out_ref, norm_ref = refs if first else (refs[0], None)
    core = lax.axis_index("col")
    size, width = near_ref.shape[1:]
    near, far = add_halves(mine_ref, other_ref, width)
    if first:
        norm_ref[...] = finish(mine_ref[:, 2 * width :] + other_ref[:, 2 * width :])
    parts = width // LANES
    for i in range(parts):
        lanes = slice(i * LANES, (i + 1) * LANES)
        for place, half in ((core, near), (1 - core, far)):
            at = pl.multiple_of((place * parts + i) * size, size)
            out_ref[pl.ds(at, size)] = half[:, lanes]
    products = symmetric_parts(near, near_ref[0]) + symmetric_parts(
        far, far_ref[far_ref.shape[0] - 1]
    )
    out_ref[2 * parts * size :] = pack(finish(products))


def inverse_kernel(norm_ref, out_ref):
    norm = norm_ref[...]
    size = norm.shape[0]
    norm = 0.5 * (norm + jnp.concatenate([norm[:, :size].T, norm[:, size:]], axis=1))
    unit = lax.broadcasted_iota(jnp.int32, norm.shape, 0) == lax.broadcasted_iota(
        jnp.int32, norm.shape, 1
    )
    out_ref[...] = solve_wide(jnp.where(unit, 1.0, 0.0), pltpu.roll(norm, size, 1))


def pick(refs, places, core, rows):
    if places[0] == places[1]:
        return refs[places[0]][rows]
    return jnp.where(core == 0, refs[places[0]][rows], refs[places[1]][rows])


def step_kernel(used, places, with_solution, last, *refs):
    images, refs = refs[:used], refs[used:]
    direction_ref, residual_ref, norm_ref, inverse_ref, matrix = refs[:5]
    refs = refs[5:]
    if with_solution:
        solution_ref, refs = refs[0], refs[1:]
    out_ref, new_direction, new_residual, new_norm, new_solution = refs
    core = lax.axis_index("col")
    pieces = len(places)
    size, width = direction_ref.shape[1:]
    parts = width // LANES

    def image(k, half):
        found = []
        for i in range(parts):
            at = pl.multiple_of((half * parts + i) * size, size)
            found.append(pick(images, places[k], core, pl.ds(at, size)))
        return jnp.concatenate(found, axis=1)

    behind = slice(2 * parts * size, None)
    products = add_up([pick(images, pair, core, behind) for pair in places])
    inverse = stack(inverse_ref[:, :size])
    alpha = stack(solve_wide(norm_ref[...], unpack(products, size, 1))[:, :size])
    residuals = [
        [residual_ref[side, k] - times(alpha, image(k, half)) for k in range(pieces)]
        for side, half in enumerate((core, 1 - core))
    ]
    joined = [jnp.concatenate(values, axis=1) for values in residuals]
    next_norm = finish(gram_parts(joined[0], joined[0]) + gram_parts(joined[1], joined[1]))
    new_norm[...] = next_norm
    step = times(alpha, direction_ref[0])
    new_solution[...] = solution_ref[...] + step if with_solution else step
    beta = stack_leading(times(inverse, next_norm)[:, :size])
    directions = [
        residual + times_leading(beta, direction_ref[k])
        for k, residual in enumerate(residuals[0] + residuals[1][:1])
    ]
    if last:
        new_residual[...] = residuals[0][0]
        new_direction[0] = directions[0]
        new_direction[1] = directions[pieces]
    else:
        for k in range(pieces):
            new_residual[0, k] = residuals[0][k]
            new_residual[1, k] = residuals[1][k]
        for k in range(pieces + 1):
            new_direction[k] = directions[k]
    out_ref[...] = apply_dense(directions[:pieces], matrix)


def last_image_kernel(mine_ref, other_ref, direction_ref, near_ref, gram_ref):
    near, far = add_halves(mine_ref, other_ref, direction_ref.shape[2])
    near_ref[...] = near
    products = symmetric_parts(near, direction_ref[0]) + symmetric_parts(far, direction_ref[1])
    gram_ref[...] = pack(finish(products))


def last_kernel(used, places, *refs):
    image_ref, direction_ref, residual_ref, norm_ref, solution_ref = refs[used:-2]
    new_solution, new_residual = refs[-2:]
    core = lax.axis_index("col")
    size = image_ref.shape[0]
    products = add_up([pick(refs, pair, core, slice(None)) for pair in places])
    alpha = stack(solve_wide(norm_ref[...], unpack(products, size, 1))[:, :size])
    new_solution[...] = solution_ref[...] + times(alpha, direction_ref[0])
    new_residual[...] = residual_ref[...] - times(alpha, image_ref[...])


def shape(*dims, dtype=F32):
    return jax.ShapeDtypeStruct(dims, dtype)


def per_device(tiles, tile_rows, tile_cols, tile_count, signs, vertex_weight, column_scale):
    sketch, rows_dev = signs.shape
    tile = tiles.shape[1]
    pieces = lax.axis_size("row")
    col_devices = lax.axis_size("col")
    group = col_devices * rows_dev
    depth = pieces * rows_dev

    def swap(value, mask):
        return lax.ppermute(value, "row", [(i, i ^ mask) for i in range(pieces)])

    def across(value):
        return lax.ppermute(
            value, "col", [(i, (i + 1) % col_devices) for i in range(col_devices)]
        )

    def exchange(value, turns=((7, 5), (3, 6), (2, 4), (1, 1))):
        if pieces != 8:
            found = [value] + [swap(value, k) for k in range(1, pieces)]
            return found, [(k, k) for k in range(pieces)]
        fetched = []
        passed = []
        places = {0: (0, 0)}
        for turn, masks in enumerate(turns, 1):
            pairs = [
                (i * 2 + core, (i ^ mask) * 2 + core)
                for core, mask in enumerate(masks)
                for i in range(pieces)
            ]
            fetched.append(lax.ppermute(value, ("row", "col"), pairs))
            if masks[0] == masks[1]:
                places[masks[0]] = (turn, turn)
            else:
                passed.append(across(fetched[-1]))
                places[masks[0]] = (turn, turn + len(turns))
                places[masks[1]] = (turn + len(turns), turn)
        return [value, *fetched, *passed], [places[k] for k in range(pieces)]

    height = sketch + TAIL
    given = (signs, vertex_weight, column_scale)
    message, scale = pl.pallas_call(
        message_kernel,
        out_shape=(shape(height, rows_dev, dtype=BF16), shape(sketch, LANES)),
        in_specs=[HBM] * 3,
        out_specs=(VMEM, VMEM),
        scratch_shapes=[
            *[pltpu.VMEM(x.shape, x.dtype) for x in given],
            pltpu.SemaphoreType.DMA((len(given),)),
        ],
        compiler_params=params(),
        name="message",
    )(*[pltpu.with_memory_space_constraint(x, pltpu.HBM) for x in given])
    even = [message] + [swap(message, k) for k in range(2, pieces, 2)]

    matrix = shape(2, depth, group, dtype=BF16)
    total = shape(depth // tile * (group // tile), tile, tile)
    slots = tiles.shape[0]
    half = slots // 2 // (2 * CHUNKS) * (2 * CHUNKS)
    rest = shape(slots - half, tile, tile, dtype=BF16)
    lists = [pltpu.with_memory_space_constraint(x, pltpu.HBM) for x in (tile_rows, tile_cols)]
    lists_scratch = [pltpu.SMEM(x.shape, jnp.int32) for x in lists]
    cost = pl.CostEstimate(
        flops=4 * tiles.size, bytes_accessed=4 * tiles.size, transcendentals=0
    )
    blocks_sum, others = pl.pallas_call(
        functools.partial(gather_kernel, rows_dev),
        out_shape=(total, rest),
        in_specs=[SMEM] + [HBM] * 3,
        out_specs=(VMEM, VMEM),
        scratch_shapes=[
            pltpu.VMEM((half, tile, tile), BF16),
            *lists_scratch,
            pltpu.SemaphoreType.DMA((2 * CHUNKS,)),
            pltpu.SemaphoreType.DMA((len(lists),)),
        ],
        compiler_params=params(tiles, total),
        cost_estimate=cost,
        name="gather",
    )(tile_count, *lists, pltpu.with_memory_space_constraint(tiles, pltpu.HBM))
    joined = shape(pieces // 2, height, rows_dev, dtype=BF16)
    order = [*range(pieces // 4, pieces // 2), *range(1, pieces // 4), 0]
    even = pl.pallas_call(
        functools.partial(join_kernel, order),
        out_shape=joined,
        in_specs=[VMEM] * (pieces // 2) + [ANY],
        out_specs=VMEM,
        compiler_params=params(joined, joined),
        name="join",
    )(*[even[k] for k in order], blocks_sum)
    odd = swap(even, 1)
    far_even = across(even)
    dense, _ = pl.pallas_call(
        functools.partial(dense_kernel, rows_dev),
        out_shape=(matrix, total),
        in_specs=[SMEM] + [HBM] * 2 + [VMEM, VMEM, ANY],
        out_specs=(VMEM, VMEM),
        scratch_shapes=[*lists_scratch, pltpu.SemaphoreType.DMA((len(lists),))],
        input_output_aliases={4: 1},
        compiler_params=params(rest, total, total, matrix),
        cost_estimate=cost,
        name="dense",
    )(tile_count, *lists, others, blocks_sum, even)

    held = shape(2, pieces, sketch, rows_dev)
    state = shape(pieces + 1, sketch, rows_dev)
    small = shape(sketch, LANES)
    piece = shape(sketch, rows_dev)
    packed = shape(sketch * sketch // LANES, LANES)
    payload = shape(2 * sketch * (rows_dev // LANES) + packed.shape[0], LANES)

    partial_sum, ends, odd = pl.pallas_call(
        first_kernel,
        out_shape=(shape(sketch, group + LANES), shape(2, sketch, rows_dev), joined),
        in_specs=[VMEM] * 5,
        out_specs=(VMEM,) * 3,
        compiler_params=params(matrix, state, state),
        name="first",
    )(even, far_even, odd, scale, dense)
    norm = None
    solution = None
    direction = None
    for iteration in range(ITERS - 1):
        first = iteration == 0
        last = iteration == ITERS - 2
        sums = (partial_sum, across(partial_sum))
        given = (ends, ends) if first else (direction, direction)
        outs = pl.pallas_call(
            functools.partial(image_kernel, first),
            out_shape=(payload, small) if first else (payload,),
            in_specs=[VMEM] * 4,
            out_specs=(VMEM, VMEM) if first else (VMEM,),
            compiler_params=params(state, payload),
            name="image",
        )(*sums, *given)
        found, places = exchange(outs[0])
        if first:
            norm = outs[1]
            residual, direction = pl.pallas_call(
                collect_kernel,
                out_shape=(held, state),
                in_specs=[VMEM] * 5,
                out_specs=(VMEM, VMEM),
                compiler_params=params(held, held, state),
                name="collect",
            )(even, odd, far_even, across(odd), scale)
        inverse = pl.pallas_call(
            inverse_kernel,
            out_shape=small,
            in_specs=[VMEM],
            out_specs=VMEM,
            compiler_params=params(),
            name="inverse",
        )(norm)
        given = () if first else (solution,)
        partial_sum, direction, residual, norm, solution = pl.pallas_call(
            functools.partial(step_kernel, len(found), places, not first, last),
            out_shape=(
                shape(sketch, group),
                shape(2, sketch, rows_dev) if last else state,
                piece if last else held,
                small,
                piece,
            ),
            in_specs=[VMEM] * (len(found) + 5 + len(given)),
            out_specs=(VMEM,) * 5,
            compiler_params=params(matrix, held, held, held, held, state),
            name="step",
        )(*found, direction, residual, norm, inverse, dense, *given)
    near, gram = pl.pallas_call(
        last_image_kernel,
        out_shape=(piece, packed),
        in_specs=[VMEM] * 3,
        out_specs=(VMEM, VMEM),
        compiler_params=params(state),
        name="last_image",
    )(partial_sum, across(partial_sum), direction)
    found, places = exchange(gram, ((6, 7), (3, 5), (2, 4), (1, 1)))
    return pl.pallas_call(
        functools.partial(last_kernel, len(found), places),
        out_shape=(piece, piece),
        in_specs=[VMEM] * (len(found) + 5),
        out_specs=(VMEM, VMEM),
        compiler_params=params(state, state),
        name="last",
    )(*found, near, direction, residual, norm, solution)


def solution(mesh):
    return jax.shard_map(
        per_device,
        mesh=mesh,
        in_specs=(
            P(("row", "col"), None, None),
            P(("row", "col")),
            P(("row", "col")),
            P(("row", "col")),
            P("rhs", ("row", "col")),
            P(("row", "col")),
            P("rhs"),
        ),
        out_specs=(P("rhs", ("row", "col")), P("rhs", ("row", "col"))),
        check_vma=False,
    )
```

```python
import functools

import jax
import jax.numpy as jnp
from jax import lax
from jax.experimental import pallas as pl
from jax.experimental.pallas import tpu as pltpu
from jax.sharding import PartitionSpec as P

ITERS = 3
LANES = 128
PIVOTS = 16
TAIL = 16
CHUNKS = 4
F32 = jnp.float32
BF16 = jnp.bfloat16
SPARE_BYTES = 4 * 1024 * 1024

VMEM = pl.BlockSpec(memory_space=pltpu.VMEM)
SMEM = pl.BlockSpec(memory_space=pltpu.SMEM)
HBM = pl.BlockSpec(memory_space=pltpu.HBM)
ANY = pl.BlockSpec(memory_space=pl.ANY)


def params(*arrays):
    used = sum(a.size * jnp.dtype(a.dtype).itemsize for a in arrays)
    return pltpu.CompilerParams(vmem_limit_bytes=used + SPARE_BYTES)


def split(value):
    high = value.astype(BF16)
    rest = value - high.astype(F32)
    middle = rest.astype(BF16)
    low = (rest - middle.astype(F32)).astype(BF16)
    return high, middle, low


def stack(left):
    high, middle, low = [part.astype(F32) for part in split(left)]
    parts = jnp.concatenate([high, high, middle, high, middle, low], axis=0)
    return parts.T.astype(BF16)


def times(stacked, right):
    high, middle, low = split(right)
    parts = jnp.concatenate([high, middle, high, low, middle, high], axis=0)
    return jnp.dot(stacked, parts, preferred_element_type=F32)


def stack_leading(left):
    high, middle, _ = [part.astype(F32) for part in split(left)]
    return jnp.concatenate([high, high, middle], axis=0).T.astype(BF16)


def times_leading(stacked, right):
    high, middle, _ = split(right)
    parts = jnp.concatenate([high, middle, high], axis=0)
    return jnp.dot(stacked, parts, preferred_element_type=F32)


def gram_parts(left, right):
    size, width = left.shape
    filler = jnp.zeros((LANES - 3 * size, width), BF16)
    every = lax.dot_general(
        jnp.concatenate(split(left), axis=0),
        jnp.concatenate([*split(right), filler], axis=0),
        (((1,), (1,)), ((), ())),
        preferred_element_type=F32,
    )
    return every[2 * size :] + every[size : 2 * size] + every[:size]


def symmetric_parts(left, right):
    return 0.5 * (gram_parts(left, right) + gram_parts(right, left))


def finish(parts, place=0):
    size = parts.shape[0]

    def block(index):
        shift = (place - index) * size % LANES
        return pltpu.roll(parts, shift, 1) if shift else parts

    return block(2) + block(1) + block(0)


def pack(wide):
    rows = wide.shape[0]
    folds = LANES // rows
    height = rows // folds
    lanes = lax.broadcasted_iota(jnp.int32, wide.shape, 1)
    wide = jnp.where(lanes < rows, wide, 0.0)
    total = wide[:height]
    for i in range(1, folds):
        total = total + pltpu.roll(wide[i * height : (i + 1) * height], i * rows, 1)
    return total


def unpack(folded, size, place=0):
    parts = []
    for i in range(LANES // size):
        shift = (place - i) * size % LANES
        parts.append(pltpu.roll(folded, shift, 1) if shift else folded)
    return jnp.concatenate(parts, axis=0)


def solve_wide(target, matrix):
    size = matrix.shape[0]
    row_ids = lax.broadcasted_iota(jnp.int32, (size, LANES), 0)
    lane_ids = lax.broadcasted_iota(jnp.int32, (size, LANES), 1)
    work = jnp.where(lane_ids < size, target, matrix)
    for base in range(0, size, PIVOTS):
        columns = [
            jnp.broadcast_to(work[:, size + base + i : size + base + i + 1], (size, LANES))
            for i in range(PIVOTS)
        ]
        for i in range(PIVOTS):
            pivot = base + i
            here = row_ids == pivot
            inverse = pltpu.reciprocal(columns[i][pivot : pivot + 1, :], full_range=False)
            row = work[pivot : pivot + 1, :] * inverse
            work = jnp.where(here, row, work - columns[i] * row)
            for later in range(i + 1, PIVOTS):
                entry = columns[later][pivot : pivot + 1, :] * inverse
                columns[later] = jnp.where(here, entry, columns[later] - columns[i] * entry)
    return work


def add_up(values):
    values = list(values)
    while len(values) > 1:
        pairs = [values[i] + values[i + 1] for i in range(0, len(values) - 1, 2)]
        values = pairs + values[len(values) - len(values) % 2 :]
    return values[0]


def add_tiles(rows_dev, lists, tiles, first_tile, start, stop, total):
    rows_ref, cols_ref = lists
    tile = total.shape[1]
    slots = rows_ref.shape[0]
    blocks = rows_dev // tile
    row_place = lax.axis_index("row")
    col_place = lax.axis_index("col")
    col_devices = lax.axis_size("col")
    row_blocks = col_devices * blocks

    def place(slot):
        row = rows_ref[slot]
        column = cols_ref[slot]
        side = lax.rem(row // blocks + col_devices - col_place, col_devices)
        owner = column // (blocks * col_devices)
        column_at = (owner ^ row_place) * blocks + lax.rem(column, blocks)
        return column_at * row_blocks + side * blocks + lax.rem(row, blocks)

    def after(slot):
        return place(jnp.minimum(slot, slots - 1))

    def add(turn, places):
        slot = start + 2 * turn
        values = [tiles[slot + i - first_tile].astype(F32) for i in range(2)]
        following = (after(slot + 2), after(slot + 3))
        for at, value in zip(places, values):
            total[at] = total[at] + value
        return following

    places = lax.fori_loop(0, (stop - start) // 2, add, (after(start), after(start + 1)))

    @pl.when(lax.rem(stop - start, 2) == 1)
    def _():
        total[places[0]] = total[places[0]] + tiles[stop - 1 - first_tile].astype(F32)


def copy_lists(hbm_refs, smem_refs, sems):
    copies = [
        pltpu.make_async_copy(source, target, sems.at[i])
        for i, (source, target) in enumerate(zip(hbm_refs, smem_refs))
    ]
    for copy in copies:
        copy.start()
    return copies


def gather_kernel(rows_dev, count_ref, rows_hbm, cols_hbm, tiles_ref, total, rest, *scratch):
    held, rows_ref, cols_ref, sems, list_sems = scratch
    live = count_ref[0]
    half = held.shape[0]
    slots, tile = tiles_ref.shape[:2]
    chunk = -(-half // CHUNKS)
    lists = copy_lists((rows_hbm, cols_hbm), (rows_ref, cols_ref), list_sems)
    copies = []
    for c in range(CHUNKS):
        part = pl.ds(c * chunk, min(chunk, half - c * chunk))
        copies.append(pltpu.make_async_copy(tiles_ref.at[part], held.at[part], sems.at[c]))

        @pl.when(c * chunk < live)
        def _():
            copies[c].start()

    chunk_rest = -(-rest.shape[0] // CHUNKS)
    rest_copies = []
    for c in range(CHUNKS):
        start = c * chunk_rest
        length = min(chunk_rest, rest.shape[0] - start)
        copy = pltpu.make_async_copy(
            tiles_ref.at[pl.ds(half + start, length)],
            rest.at[pl.ds(start, length)],
            sems.at[CHUNKS + c],
        )
        rest_copies.append((half + start, copy))

        @pl.when(half + start < live)
        def _():
            copy.start()

    def clear(index, carry):
        total[index] = jnp.zeros((tile, tile), F32)
        return carry

    lax.fori_loop(0, total.shape[0], clear, 0, unroll=4)
    for copy in lists:
        copy.wait()
    for c in range(CHUNKS):
        start, stop = c * chunk, min((c + 1) * chunk, half)

        @pl.when(start < live)
        def _():
            copies[c].wait()
            add_tiles(
                rows_dev, (rows_ref, cols_ref), held, 0, start, jnp.minimum(live, stop), total
            )

    for start, copy in rest_copies:

        @pl.when(start < live)
        def _():
            copy.wait()


def dense_kernel(
    rows_dev, count_ref, rows_hbm, cols_hbm, rest, total_in, joined_ref, out_ref, total, *scratch
):
    rows_ref, cols_ref, list_sems = scratch
    live = count_ref[0]
    half = rows_ref.shape[0] - rest.shape[0]
    tile = total.shape[1]
    row_blocks = out_ref.shape[2] // tile

    @pl.when(half < live)
    def _():
        lists = copy_lists((rows_hbm, cols_hbm), (rows_ref, cols_ref), list_sems)
        for copy in lists:
            copy.wait()
        add_tiles(rows_dev, (rows_ref, cols_ref), rest, half, half, live, total)

    def part(index, carry):
        start = pl.multiple_of(index * tile, tile)
        for b in range(row_blocks):
            value = total[index * row_blocks + b].T
            high = value.astype(BF16)
            low = (value - high.astype(F32)).astype(BF16)
            out_ref[0, pl.ds(start, tile), pl.ds(b * tile, tile)] = high
            out_ref[1, pl.ds(start, tile), pl.ds(b * tile, tile)] = low
        return carry

    lax.fori_loop(0, total.shape[0] // row_blocks, part, 0)


def join_kernel(order, *refs):
    for k, ref in zip(order, refs):
        refs[-1][k] = ref[...]


def apply_dense(directions, matrix):
    rounded = jnp.concatenate([direction.astype(BF16) for direction in directions], axis=1)
    high, low = [
        jnp.dot(rounded, matrix[part], preferred_element_type=F32) for part in range(2)
    ]
    return high + low


def message_kernel(
    signs_hbm, weight_hbm, scale_hbm, out_ref, scale_out, signs_ref, weight_ref, scale_ref, sems
):
    copies = copy_lists(
        (signs_hbm, weight_hbm, scale_hbm), (signs_ref, weight_ref, scale_ref), sems
    )
    for copy in copies:
        copy.wait()
    size, width = signs_ref.shape
    out_ref[:size] = signs_ref[...].astype(F32).astype(BF16)
    row_ids = lax.broadcasted_iota(jnp.int32, (TAIL, width), 0)
    tail = jnp.zeros((TAIL, width), F32)
    for i, part in enumerate(split(weight_ref[...].reshape(1, width))):
        tail = jnp.where(row_ids == i, part.astype(F32), tail)
    out_ref[size:] = tail.astype(BF16)
    scale = scale_ref[...].reshape(1, size)
    scale = jnp.concatenate([scale, jnp.zeros((1, LANES - size), F32)], axis=1)
    rows = lax.broadcasted_iota(jnp.int32, (size, LANES), 0)
    lanes = lax.broadcasted_iota(jnp.int32, (size, LANES), 1)
    column = jnp.sum(jnp.where(rows == lanes, scale, 0.0), axis=1, keepdims=True)
    scale_out[...] = jnp.broadcast_to(column, (size, LANES))


def right_side_of(message, scale):
    size, width = message.shape
    size = size - TAIL
    tail = message[size:].astype(F32)
    weight = (tail[0:1] + tail[1:2]) + tail[2:3]
    scale = jnp.concatenate([scale] * (width // LANES), axis=1)
    return message[:size].astype(F32) * weight * scale


def first_kernel(
    even_ref, far_even_ref, odd_ref, scale_ref, matrix, out_ref, ends_ref, odd_out_ref
):
    pieces = 2 * even_ref.shape[0]
    odd_out_ref[...] = odd_ref[...]
    scale = scale_ref[...]
    values = [
        right_side_of((odd_ref if k % 2 else even_ref)[k // 2], scale) for k in range(pieces)
    ]
    ends_ref[0] = values[0]
    ends_ref[1] = right_side_of(far_even_ref[0], scale)
    rows = 2 * values[0].shape[1]
    joined = jnp.concatenate(values, axis=1)
    out_ref[:, rows:] = gram_parts(joined, joined)
    out_ref[:, :rows] = apply_dense(values, matrix)


def collect_kernel(
    even_ref, odd_ref, far_even_ref, far_odd_ref, scale_ref, residual_ref, direction_ref
):
    pieces = 2 * even_ref.shape[0]
    scale = scale_ref[...]
    for k in range(pieces):
        near = right_side_of((odd_ref if k % 2 else even_ref)[k // 2], scale)
        far = right_side_of((far_odd_ref if k % 2 else far_even_ref)[k // 2], scale)
        residual_ref[0, k] = near
        residual_ref[1, k] = far
        direction_ref[k] = near
        if k == 0:
            direction_ref[pieces] = far


def add_halves(mine_ref, other_ref, width):
    near = mine_ref[:, :width] + other_ref[:, width : 2 * width]
    far = mine_ref[:, width : 2 * width] + other_ref[:, :width]
    return near, far


def image_kernel(first, mine_ref, other_ref, near_ref, far_ref, *refs):
    out_ref, norm_ref = refs if first else (refs[0], None)
    core = lax.axis_index("col")
    size, width = near_ref.shape[1:]
    near, far = add_halves(mine_ref, other_ref, width)
    if first:
        norm_ref[...] = finish(mine_ref[:, 2 * width :] + other_ref[:, 2 * width :])
    parts = width // LANES
    for i in range(parts):
        lanes = slice(i * LANES, (i + 1) * LANES)
        for place, half in ((core, near), (1 - core, far)):
            at = pl.multiple_of((place * parts + i) * size, size)
            out_ref[pl.ds(at, size)] = half[:, lanes]
    products = symmetric_parts(near, near_ref[0]) + symmetric_parts(
        far, far_ref[far_ref.shape[0] - 1]
    )
    out_ref[2 * parts * size :] = pack(finish(products))


def inverse_kernel(norm_ref, out_ref):
    norm = norm_ref[...]
    size = norm.shape[0]
    norm = 0.5 * (norm + jnp.concatenate([norm[:, :size].T, norm[:, size:]], axis=1))
    unit = lax.broadcasted_iota(jnp.int32, norm.shape, 0) == lax.broadcasted_iota(
        jnp.int32, norm.shape, 1
    )
    out_ref[...] = solve_wide(jnp.where(unit, 1.0, 0.0), pltpu.roll(norm, size, 1))


def pick(refs, places, core, rows):
    if places[0] == places[1]:
        return refs[places[0]][rows]
    return jnp.where(core == 0, refs[places[0]][rows], refs[places[1]][rows])


def step_kernel(used, places, with_solution, last, *refs):
    images, refs = refs[:used], refs[used:]
    direction_ref, residual_ref, norm_ref, inverse_ref, matrix = refs[:5]
    refs = refs[5:]
    if with_solution:
        solution_ref, refs = refs[0], refs[1:]
    out_ref, new_direction, new_residual, new_norm, new_solution = refs
    core = lax.axis_index("col")
    pieces = len(places)
    size, width = direction_ref.shape[1:]
    parts = width // LANES

    def image(k, half):
        found = []
        for i in range(parts):
            at = pl.multiple_of((half * parts + i) * size, size)
            found.append(pick(images, places[k], core, pl.ds(at, size)))
        return jnp.concatenate(found, axis=1)

    behind = slice(2 * parts * size, None)
    products = add_up([pick(images, pair, core, behind) for pair in places])
    inverse = stack(inverse_ref[:, :size])
    alpha = stack(solve_wide(norm_ref[...], unpack(products, size, 1))[:, :size])
    residuals = [
        [residual_ref[side, k] - times(alpha, image(k, half)) for k in range(pieces)]
        for side, half in enumerate((core, 1 - core))
    ]
    joined = [jnp.concatenate(values, axis=1) for values in residuals]
    next_norm = finish(gram_parts(joined[0], joined[0]) + gram_parts(joined[1], joined[1]))
    new_norm[...] = next_norm
    step = times(alpha, direction_ref[0])
    new_solution[...] = solution_ref[...] + step if with_solution else step
    beta = stack_leading(times(inverse, next_norm)[:, :size])
    directions = [
        residual + times_leading(beta, direction_ref[k])
        for k, residual in enumerate(residuals[0] + residuals[1][:1])
    ]
    if last:
        new_residual[...] = residuals[0][0]
        new_direction[0] = directions[0]
        new_direction[1] = directions[pieces]
    else:
        for k in range(pieces):
            new_residual[0, k] = residuals[0][k]
            new_residual[1, k] = residuals[1][k]
        for k in range(pieces + 1):
            new_direction[k] = directions[k]
    out_ref[...] = apply_dense(directions[:pieces], matrix)


def last_image_kernel(mine_ref, other_ref, direction_ref, near_ref, gram_ref):
    near, far = add_halves(mine_ref, other_ref, direction_ref.shape[2])
    near_ref[...] = near
    products = symmetric_parts(near, direction_ref[0]) + symmetric_parts(far, direction_ref[1])
    gram_ref[...] = pack(finish(products))


def last_kernel(used, places, *refs):
    image_ref, direction_ref, residual_ref, norm_ref, solution_ref = refs[used:-2]
    new_solution, new_residual = refs[-2:]
    core = lax.axis_index("col")
    size = image_ref.shape[0]
    products = add_up([pick(refs, pair, core, slice(None)) for pair in places])
    alpha = stack(solve_wide(norm_ref[...], unpack(products, size, 1))[:, :size])
    new_solution[...] = solution_ref[...] + times(alpha, direction_ref[0])
    new_residual[...] = residual_ref[...] - times(alpha, image_ref[...])


def shape(*dims, dtype=F32):
    return jax.ShapeDtypeStruct(dims, dtype)


def per_device(tiles, tile_rows, tile_cols, tile_count, signs, vertex_weight, column_scale):
    sketch, rows_dev = signs.shape
    tile = tiles.shape[1]
    pieces = lax.axis_size("row")
    col_devices = lax.axis_size("col")
    group = col_devices * rows_dev
    depth = pieces * rows_dev

    def swap(value, mask):
        return lax.ppermute(value, "row", [(i, i ^ mask) for i in range(pieces)])

    def across(value):
        return lax.ppermute(
            value, "col", [(i, (i + 1) % col_devices) for i in range(col_devices)]
        )

    def exchange(value, turns=((7, 6), (3, 5), (2, 4), (1, 1))):
        if pieces != 8:
            found = [value] + [swap(value, k) for k in range(1, pieces)]
            return found, [(k, k) for k in range(pieces)]
        fetched = []
        passed = []
        places = {0: (0, 0)}
        for turn, masks in enumerate(turns, 1):
            pairs = [
                (i * 2 + core, (i ^ mask) * 2 + core)
                for core, mask in enumerate(masks)
                for i in range(pieces)
            ]
            fetched.append(lax.ppermute(value, ("row", "col"), pairs))
            if masks[0] == masks[1]:
                places[masks[0]] = (turn, turn)
            else:
                passed.append(across(fetched[-1]))
                places[masks[0]] = (turn, turn + len(turns))
                places[masks[1]] = (turn + len(turns), turn)
        return [value, *fetched, *passed], [places[k] for k in range(pieces)]

    height = sketch + TAIL
    given = (signs, vertex_weight, column_scale)
    message, scale = pl.pallas_call(
        message_kernel,
        out_shape=(shape(height, rows_dev, dtype=BF16), shape(sketch, LANES)),
        in_specs=[HBM] * 3,
        out_specs=(VMEM, VMEM),
        scratch_shapes=[
            *[pltpu.VMEM(x.shape, x.dtype) for x in given],
            pltpu.SemaphoreType.DMA((len(given),)),
        ],
        compiler_params=params(),
        name="message",
    )(*[pltpu.with_memory_space_constraint(x, pltpu.HBM) for x in given])
    even = [message] + [swap(message, k) for k in range(2, pieces, 2)]

    matrix = shape(2, depth, group, dtype=BF16)
    total = shape(depth // tile * (group // tile), tile, tile)
    slots = tiles.shape[0]
    half = slots // 2 // (2 * CHUNKS) * (2 * CHUNKS)
    rest = shape(slots - half, tile, tile, dtype=BF16)
    lists = [pltpu.with_memory_space_constraint(x, pltpu.HBM) for x in (tile_rows, tile_cols)]
    lists_scratch = [pltpu.SMEM(x.shape, jnp.int32) for x in lists]
    cost = pl.CostEstimate(
        flops=4 * tiles.size, bytes_accessed=4 * tiles.size, transcendentals=0
    )
    blocks_sum, others = pl.pallas_call(
        functools.partial(gather_kernel, rows_dev),
        out_shape=(total, rest),
        in_specs=[SMEM] + [HBM] * 3,
        out_specs=(VMEM, VMEM),
        scratch_shapes=[
            pltpu.VMEM((half, tile, tile), BF16),
            *lists_scratch,
            pltpu.SemaphoreType.DMA((2 * CHUNKS,)),
            pltpu.SemaphoreType.DMA((len(lists),)),
        ],
        compiler_params=params(tiles, total),
        cost_estimate=cost,
        name="gather",
    )(tile_count, *lists, pltpu.with_memory_space_constraint(tiles, pltpu.HBM))
    joined = shape(pieces // 2, height, rows_dev, dtype=BF16)
    order = [*range(pieces // 4, pieces // 2), *range(1, pieces // 4), 0]
    even = pl.pallas_call(
        functools.partial(join_kernel, order),
        out_shape=joined,
        in_specs=[VMEM] * (pieces // 2) + [ANY],
        out_specs=VMEM,
        compiler_params=params(joined, joined),
        name="join",
    )(*[even[k] for k in order], blocks_sum)
    odd = swap(even, 1)
    far_even = across(even)
    dense, _ = pl.pallas_call(
        functools.partial(dense_kernel, rows_dev),
        out_shape=(matrix, total),
        in_specs=[SMEM] + [HBM] * 2 + [VMEM, VMEM, ANY],
        out_specs=(VMEM, VMEM),
        scratch_shapes=[*lists_scratch, pltpu.SemaphoreType.DMA((len(lists),))],
        input_output_aliases={4: 1},
        compiler_params=params(rest, total, total, matrix),
        cost_estimate=cost,
        name="dense",
    )(tile_count, *lists, others, blocks_sum, even)

    held = shape(2, pieces, sketch, rows_dev)
    state = shape(pieces + 1, sketch, rows_dev)
    small = shape(sketch, LANES)
    piece = shape(sketch, rows_dev)
    packed = shape(sketch * sketch // LANES, LANES)
    payload = shape(2 * sketch * (rows_dev // LANES) + packed.shape[0], LANES)

    partial_sum, ends, odd = pl.pallas_call(
        first_kernel,
        out_shape=(shape(sketch, group + LANES), shape(2, sketch, rows_dev), joined),
        in_specs=[VMEM] * 5,
        out_specs=(VMEM,) * 3,
        compiler_params=params(matrix, state, state),
        name="first",
    )(even, far_even, odd, scale, dense)
    norm = None
    solution = None
    direction = None
    for iteration in range(ITERS - 1):
        first = iteration == 0
        last = iteration == ITERS - 2
        sums = (partial_sum, across(partial_sum))
        given = (ends, ends) if first else (direction, direction)
        outs = pl.pallas_call(
            functools.partial(image_kernel, first),
            out_shape=(payload, small) if first else (payload,),
            in_specs=[VMEM] * 4,
            out_specs=(VMEM, VMEM) if first else (VMEM,),
            compiler_params=params(state, payload),
            name="image",
        )(*sums, *given)
        found, places = exchange(outs[0])
        if first:
            norm = outs[1]
            residual, direction = pl.pallas_call(
                collect_kernel,
                out_shape=(held, state),
                in_specs=[VMEM] * 5,
                out_specs=(VMEM, VMEM),
                compiler_params=params(held, held, state),
                name="collect",
            )(even, odd, far_even, across(odd), scale)
        inverse = pl.pallas_call(
            inverse_kernel,
            out_shape=small,
            in_specs=[VMEM],
            out_specs=VMEM,
            compiler_params=params(),
            name="inverse",
        )(norm)
        given = () if first else (solution,)
        partial_sum, direction, residual, norm, solution = pl.pallas_call(
            functools.partial(step_kernel, len(found), places, not first, last),
            out_shape=(
                shape(sketch, group),
                shape(2, sketch, rows_dev) if last else state,
                piece if last else held,
                small,
                piece,
            ),
            in_specs=[VMEM] * (len(found) + 5 + len(given)),
            out_specs=(VMEM,) * 5,
            compiler_params=params(matrix, held, held, held, held, state),
            name="step",
        )(*found, direction, residual, norm, inverse, dense, *given)
    near, gram = pl.pallas_call(
        last_image_kernel,
        out_shape=(piece, packed),
        in_specs=[VMEM] * 3,
        out_specs=(VMEM, VMEM),
        compiler_params=params(state),
        name="last_image",
    )(partial_sum, across(partial_sum), direction)
    found, places = exchange(gram, ((6, 7), (3, 5), (2, 4), (1, 1)))
    return pl.pallas_call(
        functools.partial(last_kernel, len(found), places),
        out_shape=(piece, piece),
        in_specs=[VMEM] * (len(found) + 5),
        out_specs=(VMEM, VMEM),
        compiler_params=params(state, state),
        name="last",
    )(*found, near, direction, residual, norm, solution)


def solution(mesh):
    return jax.shard_map(
        per_device,
        mesh=mesh,
        in_specs=(
            P(("row", "col"), None, None),
            P(("row", "col")),
            P(("row", "col")),
            P(("row", "col")),
            P("rhs", ("row", "col")),
            P(("row", "col")),
            P("rhs"),
        ),
        out_specs=(P("rhs", ("row", "col")), P("rhs", ("row", "col"))),
        check_vma=False,
    )
```
